32 devices in a mesh: chan: 8 (over z, y), seg: 4 (over x, core).
Axes of the slice: x: 2, y: 2, z: 4, core: 2. Of those that a mesh axis runs over, the one named last changes fastest.
Arguments:
- recording: float32 [1024, 16384], P('chan', 'seg'), may hold values from -60 to 60
- filter_taps: float32 [64], replicated, may hold values from -0.75 to 0.75
- offsets: int32 [4], replicated, may hold values from -64 to 64, as said below
- loop_partner: int32 [8, 3], replicated, may hold values from 0 to 7, as said below
- loop_count: int32 [8], replicated, may hold values from 0 to 3, as said below
Outputs:
- near_corr: float32 [1024, 4, 256], P('chan', 'seg')
- loop_corr: float32 [8, 3, 128, 256], P('chan', None, 'seg')
The draws below stay inside these ranges and needn't reach their ends.
Inputs may be any that keep to these rules, and one draw needn't show every extreme that they name: 4 distinct nonzero offsets; both -64 and 64 are among them. `loop_partner`: slots at or beyond a block's loop_count are ignored. `loop_count`: some block uses all 3 slots.
All inputs are finite; a program needn't handle non-finite values.
Results may differ from the reference program's by a relative error of at most 0.004.
Values may be sent and summed in bfloat16 or wider, within the bound.
No kernel may reach another device: no remote copies, remote signals or barrier semaphores. Data moves between devices by JAX's collectives and lax.ppermute only.
A program may use at most 64 MiB of HBM per device.

```python
import math
import jax
import jax.numpy as jnp
from jax import lax

C_DEV = 128
NOFF = 4
NFFT = 1024
LAGS = 256
TAPS = 64
DECIM = 4
SPAN = 64
MAXLB = 3
HALFBAND = 10
BINS = 512
CHANNELS = 1024
NBLK = 8
SEGS = 4
TIMES = 16384


def draw_recording(key, part):
    scale_key = jax.random.fold_in(key, 1)
    noise_key = jax.random.fold_in(key, 2)
    scales = jnp.exp(jax.random.uniform(scale_key, (CHANNELS, 1), jnp.float32, 0.0, math.log(10.0)))
    noise_part = jnp.clip(jax.random.normal(noise_key, (CHANNELS, TIMES), jnp.float32), -6.0, 6.0)
    return scales * noise_part


def draw_offsets(key, part):
    steps_up = jnp.arange(1, SPAN, dtype=jnp.int32)
    candidates = jnp.concatenate([steps_up, -steps_up])
    shuffled = jax.random.permutation(jax.random.fold_in(key, 5), candidates)
    chosen = jnp.concatenate([jnp.array([SPAN, -SPAN], jnp.int32), shuffled[:NOFF - 2]])
    return jax.random.permutation(jax.random.fold_in(key, 6), chosen).astype(jnp.int32)


def draw_loop_partner(key, part):
    jumps = jax.random.randint(jax.random.fold_in(key, 7), (NBLK, MAXLB), 0, NBLK - 1)
    own_ids = jnp.arange(NBLK, dtype=jnp.int32)[:, None]
    return ((own_ids + 1 + jumps) % NBLK).astype(jnp.int32)


def draw_loop_count(key, part):
    raw_counts = jax.random.randint(jax.random.fold_in(key, 11), (NBLK,), -3, MAXLB + 1)
    counts = jnp.maximum(raw_counts, 0)
    chosen = jax.random.randint(jax.random.fold_in(key, 12), (), 0, NBLK)
    counts = jnp.where(jnp.arange(NBLK, dtype=jnp.int32) == chosen, MAXLB, counts)
    return counts.astype(jnp.int32)


def noise(key, extent, width, limit, held_as=jnp.bfloat16):
    result = jax.random.normal(key, extent, jnp.float32) * width
    return jnp.minimum(jnp.maximum(result, -limit), limit).astype(held_as)


def setup_inputs(seed: int = 0) -> dict:
    key_list = jax.random.split(jax.random.key(seed), 6)
    recording = draw_recording(jax.random.fold_in(key_list[5], 71), 0)
    filter_taps = noise(key_list[1], (TAPS,), TAPS ** -0.5, 0.75, jnp.float32)
    offsets = draw_offsets(jax.random.fold_in(key_list[5], 71), 0)
    loop_partner = draw_loop_partner(jax.random.fold_in(key_list[5], 71), 0)
    loop_count = draw_loop_count(jax.random.fold_in(key_list[5], 71), 0)
    return dict(recording=recording, filter_taps=filter_taps, offsets=offsets, loop_partner=loop_partner, loop_count=loop_count)


WATER = 0.2

def decimate(extended, filter_taps):
    row_count = extended.shape[0]
    lead_rows = TAPS // DECIM
    grouped = extended.reshape(row_count, -1, DECIM)
    out_len = grouped.shape[1] - lead_rows
    summed = jnp.zeros((row_count, out_len), jnp.float32)
    for tap_group in range(lead_rows):
        tap_vec = filter_taps[DECIM * tap_group:DECIM * tap_group + DECIM][::-1]
        window = grouped[:, lead_rows - tap_group:lead_rows - tap_group + out_len, :]
        summed = summed + jnp.einsum('cmp,p->cm', window, tap_vec, precision=lax.Precision.HIGHEST)
    return summed

def forward_table(nblocks):
    bin_width = BINS // nblocks
    column = jnp.arange(2 * BINS, dtype=jnp.int32)
    block_id = column // (2 * bin_width)
    is_imag = column // bin_width % 2
    bin_index = block_id * bin_width + column % bin_width
    sample = jnp.arange(NFFT, dtype=jnp.int32)
    phase_idx = sample[:, None] * bin_index[None, :] % NFFT
    angles = phase_idx.astype(jnp.float32) * (2.0 * math.pi / NFFT)
    return jnp.where(is_imag[None, :] == 1, -jnp.sin(angles), jnp.cos(angles))

def inverse_table(nblocks, total_segs):
    bin_width = BINS // nblocks
    column = jnp.arange(2 * BINS, dtype=jnp.int32)
    block_id = column // (2 * bin_width)
    is_imag = column // bin_width % 2
    bin_index = block_id * bin_width + column % bin_width
    lag_index = jnp.arange(LAGS, dtype=jnp.int32) - LAGS // 2
    phase_idx = bin_index[:, None] * lag_index[None, :] % NFFT
    angles = phase_idx.astype(jnp.float32) * (2.0 * math.pi / NFFT)
    weights = jnp.where(bin_index == 0, 1.0, 2.0) / math.sqrt(2.0 * BINS * total_segs)
    return jnp.where(is_imag[:, None] == 1, -jnp.sin(angles), jnp.cos(angles)) * weights[:, None]

def band_matrix():
    bin_ids = jnp.arange(BINS, dtype=jnp.int32)
    inside = (jnp.abs(bin_ids[:, None] - bin_ids[None, :]) <= HALFBAND).astype(jnp.float32)
    return inside / lax.optimization_barrier(jnp.sum(inside, axis=0, keepdims=True))

def whiten(pieces, nblocks):
    row_count = pieces.shape[0]
    bin_width = BINS // nblocks
    spectrum = jnp.dot(pieces, forward_table(nblocks), precision=lax.Precision.HIGHEST, preferred_element_type=jnp.float32)
    parted = spectrum.reshape(row_count, nblocks, 2, bin_width)
    amplitude = jnp.sqrt(parted[:, :, 0] * parted[:, :, 0] + parted[:, :, 1] * parted[:, :, 1]).reshape(row_count, BINS)
    smoothed = jnp.dot(amplitude, band_matrix(), precision=lax.Precision.HIGHEST, preferred_element_type=jnp.float32)
    level_mean = lax.optimization_barrier(jnp.mean(amplitude, axis=1, keepdims=True))
    divisor = smoothed + WATER * level_mean + 1e-06
    whitened = parted / divisor.reshape(row_count, nblocks, 1, bin_width)
    return whitened.reshape(row_count, 2 * BINS).astype(jnp.bfloat16)

def cross(own, partner, nblocks, form):
    full_width = own.shape[-1]
    bin_width = full_width // (2 * nblocks)
    own_parts = own.astype(jnp.float32).reshape(own.shape[:-1] + (nblocks, 2, bin_width))
    far_parts = partner.astype(jnp.float32).reshape(partner.shape[:-1] + (nblocks, 2, bin_width))
    own_real = own_parts[..., 0, :]
    own_imag = own_parts[..., 1, :]
    far_real = far_parts[..., 0, :]
    far_imag = far_parts[..., 1, :]
    high = lax.Precision.HIGHEST
    real_part = jnp.einsum(form, own_real, far_real, precision=high) + jnp.einsum(form, own_imag, far_imag, precision=high)
    imag_part = jnp.einsum(form, own_imag, far_real, precision=high) - jnp.einsum(form, own_real, far_imag, precision=high)
    joined = jnp.stack([real_part, imag_part], axis=-2)
    return joined.reshape(joined.shape[:-3] + (full_width,))

def to_lags(pair_spec, inverse):
    lead_shape = pair_spec.shape[:-1]
    lag_rows = jnp.dot(pair_spec.reshape(-1, pair_spec.shape[-1]), inverse, precision=lax.Precision.HIGHEST, preferred_element_type=jnp.float32)
    return lag_rows.reshape(lead_shape + (LAGS,))

def reference(recording, filter_taps, offsets, loop_partner, loop_count):
    chan_blocks = recording.reshape(NBLK, C_DEV, TIMES)

    def block_spectra(block_rec):
        padded = jnp.concatenate([jnp.zeros((C_DEV, TAPS), jnp.float32), block_rec], axis=1)
        decimated = decimate(padded, filter_taps)
        pieces = decimated.reshape(C_DEV, SEGS, NFFT)
        pieces = pieces - lax.optimization_barrier(jnp.mean(pieces, axis=2, keepdims=True))
        return whiten(pieces.reshape(C_DEV * SEGS, NFFT), 1).reshape(C_DEV, SEGS, 2 * BINS)
    whitened = lax.map(block_spectra, chan_blocks)
    flat_white = whitened.reshape(CHANNELS, SEGS, 2 * BINS)
    inverse = inverse_table(1, SEGS)

    def near_block(block_id):
        channel_ids = block_id * C_DEV + jnp.arange(C_DEV, dtype=jnp.int32)
        partner_ids = (channel_ids[None, :] + offsets[:, None]) % CHANNELS
        pair_spec = cross(flat_white[channel_ids], flat_white[partner_ids], 1, 'csnt,pcsnt->cpnt')
        return to_lags(pair_spec, inverse)
    block_ids = jnp.arange(NBLK, dtype=jnp.int32)
    near_corr = lax.map(near_block, block_ids).reshape(CHANNELS, NOFF, LAGS)

    def loop_block(block_id):
        partner = whitened[loop_partner[block_id]][:, ::-1]
        live_slots = (jnp.arange(MAXLB, dtype=jnp.int32) < loop_count[block_id]).astype(jnp.float32)
        pair_spec = cross(whitened[block_id], partner, 1, 'csnt,kcsnt->kcnt') * live_slots[:, None, None]
        return to_lags(pair_spec, inverse)
    loop_corr = lax.map(loop_block, block_ids)
    return (near_corr, loop_corr)
```

```python
import functools
import math

import jax
import jax.numpy as jnp
import numpy as np
from jax import lax
from jax.experimental import pallas as pl
from jax.experimental.pallas import tpu as pltpu
from jax.sharding import PartitionSpec as P

NFFT = 1024
LAGS = 256
TAPS = 64
DECIM = 4
HALFBAND = 10
BINS = 512
WATER = 0.2

LANES = 128
GROUP = 16
GROUPS = BINS // GROUP
OUT_BLOCK = 128
HALF = NFFT // 2

F32 = jnp.float32
BF16 = jnp.bfloat16


def bin_order():
    return np.concatenate([np.arange(0, BINS, 2), np.arange(1, BINS, 2)])


def split_np(table):
    high = table.astype(jnp.bfloat16)
    low = (table - high.astype(np.float64)).astype(jnp.bfloat16)
    return high, low


def forward_table():
    bins = bin_order().reshape(GROUPS, 1, GROUP)
    sample = np.arange(HALF)
    angles = (bins[..., None] * sample % NFFT) * (2.0 * np.pi / NFFT)
    rows = np.concatenate([np.cos(angles), -np.sin(angles)], axis=1)
    rows = rows * (bins != 0)[..., None]
    return rows.reshape(2, BINS, HALF)


def inverse_table(total_segs, order):
    lag = np.arange(LAGS) - LAGS // 2
    bins, part = order
    angles = (bins[None, :] * lag[:, None] % NFFT) * (2.0 * np.pi / NFFT)
    weights = np.where(bins == 0, 1.0, 2.0) / math.sqrt(2.0 * BINS * total_segs)
    return np.where(part[None, :] == 1, -np.sin(angles), np.cos(angles)) * weights[None, :]


def band_table():
    bins = bin_order()
    return (np.abs(bins[:, None] - bins[None, :]) <= HALFBAND).astype(jnp.bfloat16)


def split(value):
    high = value.astype(BF16)
    return high, (value - high.astype(F32)).astype(BF16)


def mm(a, b):
    return jnp.dot(a, b, preferred_element_type=F32)


def mm_nt(a, b):
    return lax.dot_general(a, b, (((1,), (1,)), ((), ())), preferred_element_type=F32)


def tap_rows(base_ref, rows):
    width = base_ref.shape[1]
    spread = jnp.broadcast_to(base_ref[0:1, :], (rows, width))
    return pltpu.roll(spread, 0, 1, stride=DECIM, stride_axis=0)


def spectrum_kernel(rec_ref, base_ref, tab_ref, spec_ref, mean_ref):
    length = rec_ref.shape[1]
    total = rec_ref[:, 0:LANES]
    for t in range(1, length // LANES):
        total = total + rec_ref[:, t * LANES : (t + 1) * LANES]
    mean = jnp.sum(total, axis=1, keepdims=True) * (1.0 / length)
    mean_ref[...] = jnp.broadcast_to(mean, mean_ref.shape)
    taps_high, taps_low = split(tap_rows(base_ref, OUT_BLOCK))
    taps_both = jnp.concatenate([taps_high, taps_low], axis=0)
    step = OUT_BLOCK * DECIM
    pieces = []
    for j in range(length // step):
        skip = LANES if j == 0 else 0
        window = rec_ref[:, j * step - LANES + skip : (j + 1) * step] - mean
        high, low = split(window)
        both = mm_nt(taps_both[:, skip:], high)
        pieces.append(both[:OUT_BLOCK] + both[OUT_BLOCK:] + mm_nt(taps_high[:, skip:], low))
    decimated = jnp.concatenate(pieces, axis=0)
    first, second = decimated[:HALF], decimated[HALF:]
    for parity, folded in enumerate((first + second, first - second)):
        high, low = split(folded)
        wide = mm(tab_ref[0, parity], jnp.concatenate([high, low], axis=1))
        rows = wide[:, :LANES] + wide[:, LANES:] + mm(tab_ref[1, parity], high)
        spec_ref[parity * BINS : (parity + 1) * BINS, :] = rows


def whiten_kernel(spec_ref, rim_ref, mean_ref, base_ref, edge_ref, band_ref, white_ref):
    head = tap_rows(base_ref, GROUP)[:, :LANES]
    rim = rim_ref[...] - mean_ref[...]
    history = lax.dot_general(
        head, rim, (((1,), (1,)), ((), ())),
        precision=lax.Precision.HIGHEST, preferred_element_type=F32,
    )
    high, low = split(history)
    stacked = jnp.concatenate([high, high, low], axis=0)
    spec = spec_ref[...] + mm(edge_ref[:, : 3 * GROUP], stacked)
    parted = spec.reshape(GROUPS, 2, GROUP, LANES)
    real, imag = parted[:, 0], parted[:, 1]
    amplitude = jnp.sqrt(real * real + imag * imag).reshape(BINS, LANES)
    high, low = split(amplitude)
    wide = mm(band_ref[...], jnp.concatenate([high, low], axis=1))
    row = lax.broadcasted_iota(jnp.int32, (BINS, LANES), 0)
    bins = jnp.where(row < BINS // 2, 2 * row, 2 * row - (BINS - 1))
    count = jnp.minimum(bins, HALFBAND) + jnp.minimum(BINS - 1 - bins, HALFBAND) + 1
    smoothed = (wide[:, :LANES] + wide[:, LANES:]) / count.astype(F32)
    level = jnp.sum(amplitude, axis=0, keepdims=True) * (1.0 / BINS)
    scale = 1.0 / (smoothed + WATER * level + 1e-06)
    white = parted * scale.reshape(GROUPS, 1, GROUP, LANES)
    white_ref[...] = white.astype(BF16)


def cross_kernel(offs_ref, partner_ref, count_ref, white_ref, out_ref, turned_ref):
    blocks, segs, _, bins, _ = white_ref.shape
    owners = out_ref.shape[1]
    noff = offs_ref.shape[0]
    slots = partner_ref.shape[1]
    near_tiles = noff // owners
    share = LANES // owners
    rows = segs * 2 * bins
    lane_in = lax.broadcasted_iota(jnp.int32, (LANES, LANES), 0)
    lane_out = lax.broadcasted_iota(jnp.int32, (LANES, LANES), 1)
    flip = (lane_in + lane_out == LANES - 1).astype(BF16)
    turned = mm(white_ref[...].reshape(blocks * rows, LANES), flip)
    turned_ref[...] = turned.reshape(turned_ref.shape)
    lane = lax.broadcasted_iota(jnp.int32, (rows, LANES), 1)
    pair_lane = lane[: 2 * bins]

    def products(own, far):
        real = jnp.sum(own[:, 0] * far[:, 0] + own[:, 1] * far[:, 1], axis=0)
        imag = jnp.sum(own[:, 1] * far[:, 0] - own[:, 0] * far[:, 1], axis=0)
        return real, imag

    def one_block(b, carry):
        flat = white_ref[b].astype(F32).reshape(rows, LANES)
        own = flat.reshape(segs, 2, bins, LANES)
        for o in range(noff):
            offset = offs_ref[o]
            ahead = offset > 0
            other = jnp.where(ahead, b + 1, b - 1)
            other = jnp.where(other < 0, blocks - 1, jnp.where(other >= blocks, 0, other))
            turn = jnp.where(ahead, offset, LANES + offset)
            mine = (lane >= turn) == ahead
            beside = white_ref[other].astype(F32).reshape(rows, LANES)
            far = pltpu.roll(jnp.where(mine, flat, beside), LANES - turn, 1)
            real, imag = products(own, far.reshape(own.shape))
            out_ref[b, o // near_tiles, o % near_tiles, 0] = real.astype(BF16)
            out_ref[b, o // near_tiles, o % near_tiles, 1] = imag.astype(BF16)
        live_count = count_ref[b]
        pairs = []
        for k in range(slots):
            partner = jnp.clip(partner_ref[b, k], 0, blocks - 1)
            live = (k < live_count).astype(F32)
            real, imag = products(own * live, turned_ref[partner])
            pairs.append(jnp.concatenate([real, imag], axis=0))
        for q in range(owners):
            packed = jnp.zeros_like(pairs[0])
            for k in range(slots):
                shift = (share * (k - q)) % LANES
                moved = pltpu.roll(pairs[k], shift, 1) if shift else pairs[k]
                inside = (pair_lane >= share * k) & (pair_lane < share * (k + 1))
                packed = jnp.where(inside, moved, packed)
            packed = packed.reshape(2, bins, LANES).astype(BF16)
            out_ref[b, q, near_tiles] = packed
        return carry

    lax.fori_loop(0, blocks, one_block, 0)


def lag_kernel(spec_ref, inv_ref, near_ref, loop_ref):
    tiles = spec_ref.shape[1]
    depth = inv_ref.shape[1]
    columns = [spec_ref[:, t].reshape(depth, LANES) for t in range(tiles)]
    both = mm(inv_ref[...], jnp.concatenate(columns, axis=1))
    lags = both[:LAGS] + both[LAGS:]
    for t in range(tiles - 1):
        near_ref[:, t, :] = lags[:, t * LANES : (t + 1) * LANES].T
    loop = lags[:, (tiles - 1) * LANES :].T
    loop_ref[...] = loop[: loop_ref.shape[0]]


def vmem(count):
    return [pl.BlockSpec(memory_space=pltpu.VMEM)] * count


def smem(count):
    return [pl.BlockSpec(memory_space=pltpu.SMEM)] * count


PARAMS = pltpu.CompilerParams(vmem_limit_bytes=48 * 1024 * 1024)


def cross_plain(white, offsets, loop_partner, loop_count, owners):
    blocks, segs, _, bins, chans = white.shape
    slots = loop_partner.shape[1]
    wide = white.astype(F32)
    flat = jnp.moveaxis(wide, 0, 3).reshape(segs, 2, bins, blocks * chans)

    def products(own, far):
        real = jnp.sum(own[:, 0] * far[:, 0] + own[:, 1] * far[:, 1], axis=0)
        imag = jnp.sum(own[:, 1] * far[:, 0] - own[:, 0] * far[:, 1], axis=0)
        return jnp.stack([real, imag])

    near = [products(flat, jnp.roll(flat, -offsets[o], axis=3)) for o in range(offsets.shape[0])]
    near = jnp.stack(near).reshape(owners, -1, 2, bins, blocks, chans)
    near = jnp.moveaxis(near, 4, 0)
    loops = []
    for k in range(slots):
        far = jnp.flip(wide[loop_partner[:, k]], axis=4)
        live = (k < loop_count).astype(F32)[:, None, None]
        pair = products(jnp.moveaxis(wide, 0, 2), jnp.moveaxis(far, 0, 2)) * live[None]
        loops.append(pair.reshape(2, blocks, bins, owners, chans // owners))
    loop = jnp.stack(loops)
    loop = jnp.transpose(loop, (2, 4, 1, 3, 0, 5))
    loop = loop.reshape(blocks, owners, 1, 2, bins, slots * (chans // owners))
    spare = chans - loop.shape[-1]
    loop = jnp.pad(loop, ((0, 0),) * 5 + ((0, spare),))
    return jnp.concatenate([near, loop], axis=2).astype(BF16)


def body(recording, filter_taps, offsets, loop_partner, loop_count):
    chan_count = lax.axis_size("chan")
    seg_count = lax.axis_size("seg")
    devices = chan_count * seg_count
    bins = BINS // devices
    chans, length = recording.shape
    noff, slots = offsets.shape[0], loop_partner.shape[1]
    share = chans // seg_count
    tiles = noff // seg_count + 1
    assert length == NFFT * DECIM and chans == LANES
    assert slots * share <= LANES and noff % seg_count == 0

    route = [(i, i + 1) for i in range(seg_count - 1)]
    rim = lax.ppermute(recording[:, length - LANES :], "seg", route)

    width = LANES + OUT_BLOCK * DECIM
    start = LANES + DECIM - TAPS
    base = jnp.pad(filter_taps[::-1], (start, width - start - TAPS))
    base = jnp.broadcast_to(base[None, :], (8, width))
    forward = forward_table()
    table = np.stack(split_np(forward))
    spec, mean = pl.pallas_call(
        spectrum_kernel,
        out_shape=[
            jax.ShapeDtypeStruct((2 * BINS, LANES), F32),
            jax.ShapeDtypeStruct((LANES, LANES), F32),
        ],
        in_specs=vmem(3),
        out_specs=vmem(2),
        compiler_params=PARAMS,
        cost_estimate=pl.CostEstimate(
            flops=1_000_000_000, bytes_accessed=5_000_000, transcendentals=0
        ),
        name="filter_and_transform",
    )(recording, base, table)

    first = forward.reshape(2 * BINS, HALF)[:, :GROUP]
    high, low = split_np(first)
    edge = np.concatenate([high, low, high], axis=1)
    edge = np.pad(edge.astype(np.float32), ((0, 0), (0, LANES - 3 * GROUP))).astype(jnp.bfloat16)
    white = pl.pallas_call(
        whiten_kernel,
        out_shape=jax.ShapeDtypeStruct((GROUPS, 2, GROUP, LANES), BF16),
        in_specs=vmem(6),
        out_specs=pl.BlockSpec(memory_space=pltpu.VMEM),
        compiler_params=PARAMS,
        name="whiten",
    )(spec, rim, mean, base, edge, band_table())

    if bins != GROUP:
        white = jnp.moveaxis(white, 1, 0).reshape(2, devices, bins, LANES)
        white = jnp.moveaxis(white, 0, 1)
    moved = lax.all_to_all(white, ("chan", "seg"), 0, 0, tiled=True)
    moved = moved.reshape(chan_count, seg_count, 2, bins, LANES)
    if bins % GROUP == 0:
        crossed = pl.pallas_call(
            cross_kernel,
            out_shape=jax.ShapeDtypeStruct(
                (chan_count, seg_count, tiles, 2, bins, LANES), BF16
            ),
            in_specs=smem(3) + vmem(1),
            out_specs=pl.BlockSpec(memory_space=pltpu.VMEM),
            scratch_shapes=[pltpu.VMEM((chan_count, seg_count, 2, bins, LANES), F32)],
            compiler_params=PARAMS,
            name="cross_spectra",
        )(offsets, loop_partner, loop_count, moved)
    else:
        crossed = cross_plain(moved, offsets, loop_partner, loop_count, seg_count)
    crossed = crossed.reshape(devices, tiles, 2, bins, LANES)
    summed = lax.all_to_all(crossed, ("chan", "seg"), 0, 0, tiled=True)

    if bins % GROUP:
        summed = jnp.transpose(summed, (1, 2, 0, 3, 4)).reshape(1, tiles, 2, BINS, LANES)
    sources, rows = summed.shape[0], summed.shape[3]
    order = np.broadcast_to(bin_order().reshape(sources, 1, rows), (sources, 2, rows))
    part = np.broadcast_to(np.arange(2).reshape(1, 2, 1), order.shape)
    inverse = inverse_table(seg_count, (order.reshape(-1), part.reshape(-1)))
    inverse = np.concatenate(split_np(inverse), axis=0)
    near, loop = pl.pallas_call(
        lag_kernel,
        out_shape=[
            jax.ShapeDtypeStruct((chans, tiles - 1, LAGS), F32),
            jax.ShapeDtypeStruct((slots * share, LAGS), F32),
        ],
        in_specs=vmem(2),
        out_specs=vmem(2),
        compiler_params=PARAMS,
        name="lags",
    )(summed, inverse)
    return near, loop.reshape(1, slots, share, LAGS)


def solution(mesh):
    in_specs = (P("chan", "seg"), P(), P(), P(), P())
    out_specs = (P("chan", "seg", None), P("chan", None, "seg", None))
    return jax.shard_map(body, mesh=mesh, in_specs=in_specs, out_specs=out_specs, check_vma=False)
```

```python
import functools
import math

import jax
import jax.numpy as jnp
import numpy as np
from jax import lax
from jax.experimental import pallas as pl
from jax.experimental.pallas import tpu as pltpu
from jax.sharding import PartitionSpec as P

NFFT = 1024
LAGS = 256
TAPS = 64
DECIM = 4
HALFBAND = 10
BINS = 512
WATER = 0.2

LANES = 128
GROUP = 16
GROUPS = BINS // GROUP
OUT_BLOCK = 128
HALF = NFFT // 2

F32 = jnp.float32
BF16 = jnp.bfloat16


def bin_order():
    return np.concatenate([np.arange(0, BINS, 2), np.arange(1, BINS, 2)])


def split_np(table):
    high = table.astype(jnp.bfloat16)
    low = (table - high.astype(np.float64)).astype(jnp.bfloat16)
    return high, low


def forward_table():
    bins = bin_order().reshape(GROUPS, 1, GROUP)
    sample = np.arange(HALF)
    angles = (bins[..., None] * sample % NFFT) * (2.0 * np.pi / NFFT)
    rows = np.concatenate([np.cos(angles), -np.sin(angles)], axis=1)
    rows = rows * (bins != 0)[..., None]
    return rows.reshape(2, BINS, HALF)


def inverse_table(total_segs, order):
    lag = np.arange(LAGS) - LAGS // 2
    bins, part = order
    angles = (bins[None, :] * lag[:, None] % NFFT) * (2.0 * np.pi / NFFT)
    weights = np.where(bins == 0, 1.0, 2.0) / math.sqrt(2.0 * BINS * total_segs)
    return np.where(part[None, :] == 1, -np.sin(angles), np.cos(angles)) * weights[None, :]


def band_table():
    bins = bin_order()
    return (np.abs(bins[:, None] - bins[None, :]) <= HALFBAND).astype(jnp.bfloat16)


def split(value):
    high = value.astype(BF16)
    return high, (value - high.astype(F32)).astype(BF16)


def mm(a, b):
    return jnp.dot(a, b, preferred_element_type=F32)


def mm_nt(a, b):
    return lax.dot_general(a, b, (((1,), (1,)), ((), ())), preferred_element_type=F32)


def tap_rows(taps_ref, rows):
    width = LANES + OUT_BLOCK * DECIM
    tap = lax.broadcasted_iota(jnp.int32, (TAPS, width), 0)
    column = lax.broadcasted_iota(jnp.int32, (TAPS, width), 1)
    placed = jnp.where(column == LANES + DECIM - 1 - tap, taps_ref[...], 0.0)
    spread = jnp.broadcast_to(jnp.sum(placed, axis=0, keepdims=True), (rows, width))
    return pltpu.roll(spread, 0, 1, stride=DECIM, stride_axis=0)


def spectrum_kernel(rec_hbm, taps_ref, tab_hbm, spec_ref, mean_ref, rec_ref, tab_ref, sems):
    length = rec_ref.shape[1]
    step = OUT_BLOCK * DECIM
    blocks = length // step
    copies = []
    for j in range(blocks):
        part = pl.ds(j * step, step)
        copies.append(
            pltpu.make_async_copy(rec_hbm.at[:, part], rec_ref.at[:, part], sems.at[j])
        )
    for t in range(4):
        place = (t // 2, t % 2)
        copies.append(
            pltpu.make_async_copy(tab_hbm.at[place], tab_ref.at[place], sems.at[blocks + t])
        )
    for copy in copies:
        copy.start()
    taps_high, taps_low = split(tap_rows(taps_ref, OUT_BLOCK))
    taps_both = jnp.concatenate([taps_high, taps_low], axis=0)
    pieces = []
    for j in range(blocks):
        copies[j].wait()
        skip = LANES if j == 0 else 0
        window = rec_ref[:, j * step - LANES + skip : (j + 1) * step]
        if j == 0:
            mean = jnp.sum(window, axis=1, keepdims=True) * (1.0 / step)
        high, low = split(window - mean)
        both = mm_nt(taps_both[:, skip:], high)
        pieces.append(both[:OUT_BLOCK] + both[OUT_BLOCK:] + mm_nt(taps_high[:, skip:], low))
    mean_ref[...] = jnp.broadcast_to(mean, mean_ref.shape)
    decimated = jnp.concatenate(pieces, axis=0)
    decimated = decimated - jnp.sum(decimated, axis=0, keepdims=True) * (1.0 / NFFT)
    first, second = decimated[:HALF], decimated[HALF:]
    for copy in copies[blocks:]:
        copy.wait()
    for parity, folded in enumerate((first + second, first - second)):
        high, low = split(folded)
        wide = mm(tab_ref[0, parity], jnp.concatenate([high, low], axis=1))
        rows = wide[:, :LANES] + wide[:, LANES:] + mm(tab_ref[1, parity], high)
        spec_ref[parity * BINS : (parity + 1) * BINS, :] = rows


def whiten_kernel(spec_ref, rim_ref, mean_ref, taps_ref, edge_ref, band_ref, white_ref):
    head = tap_rows(taps_ref, GROUP)[:, :LANES]
    rim = rim_ref[...] - mean_ref[...]
    history = lax.dot_general(
        head, rim, (((1,), (1,)), ((), ())),
        precision=lax.Precision.HIGHEST, preferred_element_type=F32,
    )
    high, low = split(history)
    stacked = jnp.concatenate([high, high, low], axis=0)
    spec = spec_ref[...] + mm(edge_ref[:, : 3 * GROUP], stacked)
    parted = spec.reshape(GROUPS, 2, GROUP, LANES)
    real, imag = parted[:, 0], parted[:, 1]
    amplitude = jnp.sqrt(real * real + imag * imag).reshape(BINS, LANES)
    high, low = split(amplitude)
    wide = mm(band_ref[...], jnp.concatenate([high, low], axis=1))
    row = lax.broadcasted_iota(jnp.int32, (BINS, LANES), 0)
    bins = jnp.where(row < BINS // 2, 2 * row, 2 * row - (BINS - 1))
    count = jnp.minimum(bins, HALFBAND) + jnp.minimum(BINS - 1 - bins, HALFBAND) + 1
    smoothed = (wide[:, :LANES] + wide[:, LANES:]) / count.astype(F32)
    level = jnp.sum(amplitude, axis=0, keepdims=True) * (1.0 / BINS)
    scale = 1.0 / (smoothed + WATER * level + 1e-06)
    white = parted * scale.reshape(GROUPS, 1, GROUP, LANES)
    white_ref[...] = white.astype(BF16)


def cross_kernel(offs_ref, partner_ref, count_ref, white_ref, out_ref, turned_ref):
    blocks, segs, _, bins, _ = white_ref.shape
    owners = out_ref.shape[1]
    noff = offs_ref.shape[0]
    slots = partner_ref.shape[1]
    near_tiles = noff // owners
    share = LANES // owners
    rows = segs * 2 * bins
    lane_in = lax.broadcasted_iota(jnp.int32, (LANES, LANES), 0)
    lane_out = lax.broadcasted_iota(jnp.int32, (LANES, LANES), 1)
    flip = (lane_in + lane_out == LANES - 1).astype(BF16)
    turned = mm(white_ref[...].reshape(blocks * rows, LANES), flip)
    turned_ref[...] = turned.reshape(turned_ref.shape)
    lane = lax.broadcasted_iota(jnp.int32, (rows, LANES), 1)
    pair_lane = lane[: 2 * bins]

    def products(own, far):
        real = jnp.sum(own[:, 0] * far[:, 0] + own[:, 1] * far[:, 1], axis=0)
        imag = jnp.sum(own[:, 1] * far[:, 0] - own[:, 0] * far[:, 1], axis=0)
        return real, imag

    def one_block(b, carry):
        flat = white_ref[b].astype(F32).reshape(rows, LANES)
        own = flat.reshape(segs, 2, bins, LANES)
        for o in range(noff):
            offset = offs_ref[o]
            ahead = offset > 0
            other = jnp.where(ahead, b + 1, b - 1)
            other = jnp.where(other < 0, blocks - 1, jnp.where(other >= blocks, 0, other))
            turn = jnp.where(ahead, offset, LANES + offset)
            mine = (lane >= turn) == ahead
            beside = white_ref[other].astype(F32).reshape(rows, LANES)
            far = pltpu.roll(jnp.where(mine, flat, beside), LANES - turn, 1)
            real, imag = products(own, far.reshape(own.shape))
            out_ref[b, o // near_tiles, o % near_tiles, 0] = real.astype(BF16)
            out_ref[b, o // near_tiles, o % near_tiles, 1] = imag.astype(BF16)
        live_count = count_ref[b]
        pairs = []
        for k in range(slots):
            partner = jnp.clip(partner_ref[b, k], 0, blocks - 1)
            live = (k < live_count).astype(F32)
            real, imag = products(own * live, turned_ref[partner])
            pairs.append(jnp.concatenate([real, imag], axis=0))
        for q in range(owners):
            packed = jnp.zeros_like(pairs[0])
            for k in range(slots):
                shift = (share * (k - q)) % LANES
                moved = pltpu.roll(pairs[k], shift, 1) if shift else pairs[k]
                inside = (pair_lane >= share * k) & (pair_lane < share * (k + 1))
                packed = jnp.where(inside, moved, packed)
            packed = packed.reshape(2, bins, LANES).astype(BF16)
            out_ref[b, q, near_tiles] = packed
        return carry

    lax.fori_loop(0, blocks, one_block, 0)


def lag_kernel(spec_ref, inv_ref, near_ref, loop_ref):
    tiles = spec_ref.shape[1]
    depth = inv_ref.shape[1]
    columns = [spec_ref[:, t].reshape(depth, LANES) for t in range(tiles)]
    both = mm(inv_ref[...], jnp.concatenate(columns, axis=1))
    lags = both[:LAGS] + both[LAGS:]
    for t in range(tiles - 1):
        near_ref[:, t, :] = lags[:, t * LANES : (t + 1) * LANES].T
    loop = lags[:, (tiles - 1) * LANES :].T
    loop_ref[...] = loop[: loop_ref.shape[0]]


def vmem(count):
    return [pl.BlockSpec(memory_space=pltpu.VMEM)] * count


def in_hbm(array):
    return pltpu.with_memory_space_constraint(array, pltpu.HBM)


def smem(count):
    return [pl.BlockSpec(memory_space=pltpu.SMEM)] * count


PARAMS = pltpu.CompilerParams(vmem_limit_bytes=32 * 1024 * 1024)


def cross_plain(white, offsets, loop_partner, loop_count, owners):
    blocks, segs, _, bins, chans = white.shape
    slots = loop_partner.shape[1]
    wide = white.astype(F32)
    flat = jnp.moveaxis(wide, 0, 3).reshape(segs, 2, bins, blocks * chans)

    def products(own, far):
        real = jnp.sum(own[:, 0] * far[:, 0] + own[:, 1] * far[:, 1], axis=0)
        imag = jnp.sum(own[:, 1] * far[:, 0] - own[:, 0] * far[:, 1], axis=0)
        return jnp.stack([real, imag])

    near = [products(flat, jnp.roll(flat, -offsets[o], axis=3)) for o in range(offsets.shape[0])]
    near = jnp.stack(near).reshape(owners, -1, 2, bins, blocks, chans)
    near = jnp.moveaxis(near, 4, 0)
    loops = []
    for k in range(slots):
        far = jnp.flip(wide[loop_partner[:, k]], axis=4)
        live = (k < loop_count).astype(F32)[:, None, None]
        pair = products(jnp.moveaxis(wide, 0, 2), jnp.moveaxis(far, 0, 2)) * live[None]
        loops.append(pair.reshape(2, blocks, bins, owners, chans // owners))
    loop = jnp.stack(loops)
    loop = jnp.transpose(loop, (2, 4, 1, 3, 0, 5))
    loop = loop.reshape(blocks, owners, 1, 2, bins, slots * (chans // owners))
    spare = chans - loop.shape[-1]
    loop = jnp.pad(loop, ((0, 0),) * 5 + ((0, spare),))
    return jnp.concatenate([near, loop], axis=2).astype(BF16)


def body(recording, filter_taps, offsets, loop_partner, loop_count):
    chan_count = lax.axis_size("chan")
    seg_count = lax.axis_size("seg")
    devices = chan_count * seg_count
    bins = BINS // devices
    chans, length = recording.shape
    noff, slots = offsets.shape[0], loop_partner.shape[1]
    share = chans // seg_count
    tiles = noff // seg_count + 1
    assert length == NFFT * DECIM and chans == LANES
    assert slots * share <= LANES and noff % seg_count == 0

    route = [(i, i + 1) for i in range(seg_count - 1)]
    rim = lax.ppermute(recording[:, length - LANES :], "seg", route)

    taps = filter_taps.reshape(TAPS, 1)
    forward = forward_table()
    table = np.stack(split_np(forward))
    spec, mean = pl.pallas_call(
        spectrum_kernel,
        out_shape=[
            jax.ShapeDtypeStruct((2 * BINS, LANES), F32),
            jax.ShapeDtypeStruct((LANES, LANES), F32),
        ],
        in_specs=[
            pl.BlockSpec(memory_space=pltpu.HBM),
            pl.BlockSpec(memory_space=pltpu.VMEM),
            pl.BlockSpec(memory_space=pltpu.HBM),
        ],
        out_specs=vmem(2),
        scratch_shapes=[
            pltpu.VMEM((chans, length), F32),
            pltpu.VMEM((2, 2, HALF, HALF), BF16),
            pltpu.SemaphoreType.DMA((length // (OUT_BLOCK * DECIM) + 4,)),
        ],
        compiler_params=PARAMS,
        cost_estimate=pl.CostEstimate(
            flops=1_000_000_000, bytes_accessed=5_000_000, transcendentals=0
        ),
        name="filter_and_transform",
    )(in_hbm(recording), taps, in_hbm(jnp.asarray(table)))

    first = forward.reshape(2 * BINS, HALF)[:, :GROUP]
    high, low = split_np(first)
    edge = np.concatenate([high, low, high], axis=1)
    edge = np.pad(edge.astype(np.float32), ((0, 0), (0, LANES - 3 * GROUP))).astype(jnp.bfloat16)
    white = pl.pallas_call(
        whiten_kernel,
        out_shape=jax.ShapeDtypeStruct((GROUPS, 2, GROUP, LANES), BF16),
        in_specs=vmem(6),
        out_specs=pl.BlockSpec(memory_space=pltpu.VMEM),
        compiler_params=PARAMS,
        name="whiten",
    )(spec, rim, mean, taps, edge, band_table())

    if bins != GROUP:
        white = jnp.moveaxis(white, 1, 0).reshape(2, devices, bins, LANES)
        white = jnp.moveaxis(white, 0, 1)
    moved = lax.all_to_all(white, ("chan", "seg"), 0, 0, tiled=True)
    moved = moved.reshape(chan_count, seg_count, 2, bins, LANES)
    if bins % GROUP == 0:
        crossed = pl.pallas_call(
            cross_kernel,
            out_shape=jax.ShapeDtypeStruct(
                (chan_count, seg_count, tiles, 2, bins, LANES), BF16
            ),
            in_specs=smem(3) + vmem(1),
            out_specs=pl.BlockSpec(memory_space=pltpu.VMEM),
            scratch_shapes=[pltpu.VMEM((chan_count, seg_count, 2, bins, LANES), F32)],
            compiler_params=PARAMS,
            name="cross_spectra",
        )(offsets, loop_partner, loop_count, moved)
    else:
        crossed = cross_plain(moved, offsets, loop_partner, loop_count, seg_count)
    crossed = crossed.reshape(devices, tiles, 2, bins, LANES)
    summed = lax.all_to_all(crossed, ("chan", "seg"), 0, 0, tiled=True)

    if bins % GROUP:
        summed = jnp.transpose(summed, (1, 2, 0, 3, 4)).reshape(1, tiles, 2, BINS, LANES)
    sources, rows = summed.shape[0], summed.shape[3]
    order = np.broadcast_to(bin_order().reshape(sources, 1, rows), (sources, 2, rows))
    part = np.broadcast_to(np.arange(2).reshape(1, 2, 1), order.shape)
    inverse = inverse_table(seg_count, (order.reshape(-1), part.reshape(-1)))
    inverse = np.concatenate(split_np(inverse), axis=0)
    near, loop = pl.pallas_call(
        lag_kernel,
        out_shape=[
            jax.ShapeDtypeStruct((chans, tiles - 1, LAGS), F32),
            jax.ShapeDtypeStruct((slots * share, LAGS), F32),
        ],
        in_specs=vmem(2),
        out_specs=vmem(2),
        compiler_params=PARAMS,
        name="lags",
    )(summed, inverse)
    return near, loop.reshape(1, slots, share, LAGS)


def solution(mesh):
    in_specs = (P("chan", "seg"), P(), P(), P(), P())
    out_specs = (P("chan", "seg", None), P("chan", None, "seg", None))
    return jax.shard_map(body, mesh=mesh, in_specs=in_specs, out_specs=out_specs, check_vma=False)
```

```python
import functools
import math

import jax
import jax.numpy as jnp
import numpy as np
from jax import lax
from jax.experimental import pallas as pl
from jax.experimental.pallas import tpu as pltpu
from jax.sharding import PartitionSpec as P

NFFT = 1024
LAGS = 256
TAPS = 64
DECIM = 4
HALFBAND = 10
BINS = 512
WATER = 0.2

LANES = 128
GROUP = 16
GROUPS = BINS // GROUP
OUT_BLOCK = 128
STEP = OUT_BLOCK * DECIM
RADIX = 4
DEPTH = NFFT // RADIX
FAR_BINS = BINS // RADIX

F32 = jnp.float32
BF16 = jnp.bfloat16
MIB = 1024 * 1024
PARAMS = pltpu.CompilerParams(vmem_limit_bytes=32 * MIB)


def bin_order():
    return np.concatenate([np.arange(r, BINS, RADIX) for r in range(RADIX)])


def split_np(table):
    high = table.astype(jnp.bfloat16)
    low = (table - high.astype(np.float64)).astype(jnp.bfloat16)
    return high, low


def short_table():
    bins = np.arange(FAR_BINS).reshape(-1, 1, GROUP, 1)
    angles = (bins * np.arange(DEPTH) % DEPTH) * (2.0 * np.pi / DEPTH)
    rows = np.concatenate([np.cos(angles), np.sin(angles)], axis=1).reshape(-1, DEPTH)
    high, low = split_np(rows)
    return np.concatenate([high, high, low], axis=1)


def twiddle_table():
    angles = np.arange(DEPTH)[:, None] * np.arange(1, RADIX) * (2.0 * np.pi / NFFT)
    columns = np.stack([np.cos(angles), np.sin(angles)], axis=2).reshape(DEPTH, -1)
    return np.pad(columns, ((0, 0), (0, LANES - columns.shape[1]))).astype(np.float32)


def edge_table():
    bins = bin_order().reshape(GROUPS, 1, GROUP, 1)
    angles = (bins * np.arange(GROUP) % NFFT) * (2.0 * np.pi / NFFT)
    rows = np.concatenate([np.cos(angles), -np.sin(angles)], axis=1) * (bins != 0)
    high, low = split_np(rows.reshape(2 * BINS, GROUP))
    table = np.concatenate([high, high, low], axis=1)
    return np.pad(table.astype(np.float32), ((0, 0), (0, LANES - 3 * GROUP))).astype(jnp.bfloat16)


def inverse_table(total_segs, bins, part):
    lag = np.arange(LAGS) - LAGS // 2
    angles = (bins[None, :] * lag[:, None] % NFFT) * (2.0 * np.pi / NFFT)
    weights = np.where(bins == 0, 1.0, 2.0) / math.sqrt(2.0 * BINS * total_segs)
    return np.where(part[None, :] == 1, -np.sin(angles), np.cos(angles)) * weights[None, :]


def band_tables():
    bins = bin_order()
    inside = np.abs(bins[:, None] - bins[None, :]) <= HALFBAND
    share = np.broadcast_to(1.0 / inside.sum(axis=1, keepdims=True), (BINS, LANES))
    return inside.astype(jnp.bfloat16), share.astype(np.float32)


def split(value):
    high = value.astype(BF16)
    return high, (value - high.astype(F32)).astype(BF16)


def mm(a, b):
    return jnp.dot(a, b, preferred_element_type=F32)


def mm_nt(a, b):
    return lax.dot_general(a, b, (((1,), (1,)), ((), ())), preferred_element_type=F32)


def tap_rows(taps_ref, rows):
    width = LANES + STEP
    square = (TAPS, TAPS)
    diagonal = lax.broadcasted_iota(jnp.int32, square, 0) == lax.broadcasted_iota(jnp.int32, square, 1)
    column_taps = jnp.sum(jnp.where(diagonal, taps_ref[...], 0.0), axis=1, keepdims=True)
    tap = lax.broadcasted_iota(jnp.int32, (TAPS, width), 0)
    column = lax.broadcasted_iota(jnp.int32, (TAPS, width), 1)
    placed = jnp.where(column == LANES + DECIM - 1 - tap, column_taps, 0.0)
    spread = jnp.broadcast_to(jnp.sum(placed, axis=0, keepdims=True), (rows, width))
    return pltpu.roll(spread, 0, 1, stride=DECIM, stride_axis=0)


def spectrum_kernel(
    taps_ref, rec_hbm, tab_hbm, twist_hbm, spec_ref, mean_ref, rec_ref, tab_ref, twist_ref, sems
):
    blocks = rec_ref.shape[1] // STEP
    copies = []
    for j in range(blocks):
        part = pl.ds(j * STEP, STEP)
        copies.append((rec_hbm.at[:, part], rec_ref.at[:, part]))
    copies = copies + [(twist_hbm, twist_ref), (tab_hbm, tab_ref)]
    copies = [pltpu.make_async_copy(*c, sems.at[i]) for i, c in enumerate(copies)]
    for copy in copies:
        copy.start()
    taps_high, taps_low = split(tap_rows(taps_ref, OUT_BLOCK))
    taps = jnp.concatenate([taps_high, taps_high, taps_low], axis=1)
    before = [jnp.zeros((LANES, LANES), BF16)] * 2
    windows, pieces = [], []
    for j in range(blocks):
        copies[j].wait()
        chunk = rec_ref[:, j * STEP : (j + 1) * STEP]
        if j == 0:
            mean = jnp.sum(chunk, axis=1, keepdims=True) * (1.0 / STEP)
        high, low = split(chunk - mean)
        windows.append(jnp.concatenate([before[0], high, before[1], low, before[0], high], axis=1))
        before = [high[:, STEP - LANES :], low[:, STEP - LANES :]]
        if j % 2:
            pair = mm_nt(taps, jnp.concatenate(windows[-2:], axis=0))
            pieces.append(jnp.concatenate([pair[:, :LANES], pair[:, LANES:]], axis=0))
    mean_ref[...] = jnp.broadcast_to(mean, mean_ref.shape)
    even, odd = pieces[0] + pieces[2], pieces[1] + pieces[3]
    a, b = pieces[0] - pieces[2], pieces[1] - pieces[3]
    whole, half = even + odd, even - odd
    whole = whole - jnp.sum(whole, axis=0, keepdims=True) * (1.0 / DEPTH)
    copies[blocks].wait()
    c1, s1, c2, s2, c3, s3 = [twist_ref[:, i : i + 1] for i in range(6)]
    inputs = [
        whole,
        a * c1 - b * s1,
        -(a * s1 + b * c1),
        half * c2,
        -(half * s2),
        a * c3 + b * s3,
        b * c3 - a * s3,
    ]
    parts = [split(value) for value in inputs]
    high = jnp.concatenate([p[0] for p in parts], axis=1)
    low = jnp.concatenate([p[1] for p in parts], axis=1)
    copies[blocks + 1].wait()
    out = mm(tab_ref[...], jnp.concatenate([high, low, high], axis=0))
    out = out.reshape(FAR_BINS // GROUP, 2, GROUP, out.shape[1])
    rows = 2 * FAR_BINS
    for r in range(RADIX):
        first = max(2 * r - 1, 0) * LANES
        real_in = out[..., first : first + LANES]
        if r == 0:
            real, imag = real_in[:, 0], -real_in[:, 1]
        else:
            imag_in = out[..., first + LANES : first + 2 * LANES]
            real, imag = real_in[:, 0] + imag_in[:, 1], imag_in[:, 0] - real_in[:, 1]
        both = jnp.stack([real, imag], axis=1).reshape(rows, LANES)
        spec_ref[r * rows : (r + 1) * rows, :] = both


def whiten_kernel(
    spec_ref, rim_ref, mean_ref, taps_ref, edge_ref, band_ref, share_ref, white_ref
):
    head_high, head_low = split(tap_rows(taps_ref, GROUP)[:, :LANES])
    rim_high, rim_low = split(rim_ref[...] - mean_ref[...])
    history = mm_nt(
        jnp.concatenate([head_high, head_high, head_low], axis=1),
        jnp.concatenate([rim_high, rim_low, rim_high], axis=1),
    )
    high, low = split(history)
    stacked = jnp.concatenate([high, low, high], axis=0)
    spec = spec_ref[...] + mm(edge_ref[:, : 3 * GROUP], stacked)
    parted = spec.reshape(GROUPS, 2, GROUP, LANES)
    real, imag = parted[:, 0], parted[:, 1]
    amplitude = jnp.sqrt(real * real + imag * imag).reshape(BINS, LANES)
    high, low = split(amplitude)
    wide = mm(band_ref[...], jnp.concatenate([high, low], axis=1))
    smoothed = (wide[:, :LANES] + wide[:, LANES:]) * share_ref[...]
    level = jnp.sum(amplitude, axis=0, keepdims=True) * (1.0 / BINS)
    scale = 1.0 / (smoothed + (WATER * level + 1e-06))
    white = parted * scale.reshape(GROUPS, 1, GROUP, LANES)
    white_ref[...] = white.astype(BF16)


def moves_kernel(offs_ref, moves_ref):
    noff = offs_ref.shape[0]
    source = lax.broadcasted_iota(jnp.int32, (3 * LANES, LANES), 0)
    channel = lax.broadcasted_iota(jnp.int32, (3 * LANES, LANES), 1)
    for o in range(noff):
        hit = source == channel + (LANES + offs_ref[o])
        moves_ref[:, o * LANES : (o + 1) * LANES] = hit.astype(F32).astype(BF16)


def pack_matrix(owners):
    share = LANES // owners
    matrix = np.zeros((owners, owners, share, owners, owners, share), np.float32)
    for group in range(owners):
        for owner in range(owners):
            matrix[group, owner, :, owner, group, :] = np.eye(share)
    return matrix.reshape(owners * LANES, owners * LANES).astype(jnp.bfloat16)


def cross_kernel(
    partner_ref, count_ref, moves_ref, flip_ref, pack_ref, white_ref, out_ref, turned_ref
):
    blocks, segs, _, bins, _ = white_ref.shape
    owners = out_ref.shape[1]
    slots = partner_ref.shape[1]
    noff = moves_ref.shape[1] // LANES
    near_each = noff // owners
    rows = segs * 2 * bins
    packed_rows = 2 * bins // owners
    flats = [white_ref[b].reshape(rows, LANES) for b in range(blocks)]
    every = jnp.concatenate(flats, axis=0)
    turned_ref[...] = mm(every, flip_ref[...]).reshape(turned_ref.shape)
    before = jnp.concatenate(flats[-1:] + flats[:-1], axis=0)
    after = jnp.concatenate(flats[1:] + flats[:1], axis=0)
    moved = mm(jnp.concatenate([before, every, after], axis=1), moves_ref[...])

    def products(own, far):
        own = own.reshape(segs, 2, bins, LANES)
        far = far.reshape(segs, 2, bins, LANES)
        real = jnp.sum(own[:, 0] * far[:, 0] + own[:, 1] * far[:, 1], axis=0)
        imag = jnp.sum(own[:, 1] * far[:, 0] - own[:, 0] * far[:, 1], axis=0)
        return jnp.concatenate([real, imag], axis=0)

    near, loops = [], []
    for b in range(blocks):
        own = flats[b].astype(F32)
        far = moved[b * rows : (b + 1) * rows]
        near.append([products(own, far[:, o * LANES : (o + 1) * LANES]) for o in range(noff)])
        for k in range(slots):
            partner = jnp.clip(partner_ref[b, k], 0, blocks - 1)
            live = (k < count_ref[b]).astype(F32)
            pair = products(own, turned_ref[partner]) * live
            groups = [pair[g * packed_rows : (g + 1) * packed_rows] for g in range(owners)]
            loops.append(jnp.concatenate(groups, axis=1))
    packed = mm(jnp.concatenate(loops, axis=0).astype(BF16), pack_ref[...])
    depth = slots * packed_rows
    for b in range(blocks):
        for q in range(owners):
            tail = packed[b * depth : (b + 1) * depth, q * LANES : (q + 1) * LANES]
            mine = near[b][q * near_each : (q + 1) * near_each] + [tail]
            out_ref[b, q] = jnp.concatenate(mine, axis=0).astype(BF16)


def lag_kernel(slots, spec_ref, inv_ref, near_ref, loop_ref):
    sources = spec_ref.shape[0]
    rows = inv_ref.shape[1] // sources
    near_each = near_ref.shape[1]
    share = loop_ref.shape[0] // slots
    owners = LANES // share
    step = rows // owners
    columns = [
        spec_ref[:, t * rows : (t + 1) * rows].reshape(sources * rows, LANES)
        for t in range(near_each)
    ]
    loop = spec_ref[:, near_each * rows :].astype(F32)
    lane = lax.broadcasted_iota(jnp.int32, (sources, step, LANES), 2)
    for k in range(slots):
        tile = loop[:, k * step : (k + 1) * step]
        groups = [
            jnp.where((lane >= g * share) & (lane < (g + 1) * share), tile, 0.0)
            for g in range(owners)
        ]
        columns.append(jnp.concatenate(groups, axis=1).astype(BF16).reshape(sources * rows, LANES))
    both = mm(inv_ref[...], jnp.concatenate(columns, axis=1))
    lags = both[:LAGS] + both[LAGS:]
    for t in range(near_each):
        near_ref[:, t, :] = lags[:, t * LANES : (t + 1) * LANES].T
    for k in range(slots):
        first = (near_each + k) * LANES
        turned = lags[:, first : first + LANES].T
        loop_ref[k * share : (k + 1) * share] = sum(
            turned[g * share : (g + 1) * share] for g in range(owners)
        )


def vmem(count):
    return [pl.BlockSpec(memory_space=pltpu.VMEM)] * count


def smem(count):
    return [pl.BlockSpec(memory_space=pltpu.SMEM)] * count


def hbm(count):
    return [pl.BlockSpec(memory_space=pltpu.HBM)] * count


def in_hbm(array):
    return pltpu.with_memory_space_constraint(jnp.asarray(array), pltpu.HBM)


def finish_plain(white, offsets, loop_partner, loop_count, owners, total_segs):
    blocks, segs, _, bins, chans = white.shape
    devices = blocks * owners
    noff, slots = offsets.shape[0], loop_partner.shape[1]
    share = chans // owners
    wide = white.astype(F32)
    flat = jnp.moveaxis(wide, 0, 3).reshape(segs, 2, bins, blocks * chans)

    def products(own, far):
        real = jnp.sum(own[:, 0] * far[:, 0] + own[:, 1] * far[:, 1], axis=0)
        imag = jnp.sum(own[:, 1] * far[:, 0] - own[:, 0] * far[:, 1], axis=0)
        return jnp.stack([real, imag]).astype(BF16)

    near = [products(flat, jnp.roll(flat, -offsets[o], axis=3)) for o in range(noff)]
    near = jnp.stack(near).reshape(owners, noff // owners, 2, bins, blocks, chans)
    near = jnp.moveaxis(near, 4, 0).reshape(devices, noff // owners, 2 * bins, chans)
    loops = []
    for k in range(slots):
        far = jnp.flip(wide[loop_partner[:, k]], axis=4)
        live = (k < loop_count).astype(BF16)[:, None, None]
        pair = products(jnp.moveaxis(wide, 0, 2), jnp.moveaxis(far, 0, 2)) * live[None]
        loops.append(pair.reshape(2, blocks, bins, owners, share))
    loop = jnp.transpose(jnp.stack(loops), (2, 4, 0, 1, 3, 5))
    loop = loop.reshape(devices, slots, 2 * bins, share)
    order = np.repeat(bin_order().reshape(devices, 1, bins), 2, axis=1).reshape(-1)
    part = np.broadcast_to(np.arange(2).reshape(1, 2, 1), (devices, 2, bins)).reshape(-1)
    inverse = inverse_table(total_segs, order, part).astype(np.float32)
    inverse = inverse.reshape(LAGS, devices, 2 * bins)
    results = []
    for array in (near, loop):
        summed = lax.all_to_all(array, ("chan", "seg"), 0, 0, tiled=True).astype(F32)
        lags = jnp.einsum("dtvc,ldv->tcl", summed, inverse, precision=lax.Precision.HIGHEST)
        results.append(lags)
    return jnp.moveaxis(results[0], 0, 1), results[1][None]


def body(recording, filter_taps, offsets, loop_partner, loop_count):
    chan_count = lax.axis_size("chan")
    seg_count = lax.axis_size("seg")
    devices = chan_count * seg_count
    bins = BINS // devices
    chans, length = recording.shape
    noff, slots = offsets.shape[0], loop_partner.shape[1]
    share = chans // seg_count
    near_each = noff // seg_count
    assert length == NFFT * DECIM and chans == LANES and noff % seg_count == 0

    route = [(i, i + 1) for i in range(seg_count - 1)]
    rim = lax.ppermute(recording[:, length - LANES :], "seg", route)
    taps = filter_taps.reshape(1, TAPS)
    spec, mean = pl.pallas_call(
        spectrum_kernel,
        out_shape=[
            jax.ShapeDtypeStruct((2 * BINS, LANES), F32),
            jax.ShapeDtypeStruct((LANES, LANES), F32),
        ],
        in_specs=vmem(1) + hbm(3),
        out_specs=vmem(2),
        scratch_shapes=[
            pltpu.VMEM((chans, length), F32),
            pltpu.VMEM((2 * FAR_BINS, 3 * DEPTH), BF16),
            pltpu.VMEM((DEPTH, LANES), F32),
            pltpu.SemaphoreType.DMA((length // STEP + 2,)),
        ],
        compiler_params=PARAMS,
        cost_estimate=pl.CostEstimate(
            flops=1_000_000_000, bytes_accessed=5_000_000, transcendentals=0
        ),
        name="filter_and_transform",
    )(taps, in_hbm(recording), in_hbm(short_table()), in_hbm(twiddle_table()))

    band, band_share = band_tables()
    white = pl.pallas_call(
        whiten_kernel,
        out_shape=jax.ShapeDtypeStruct((GROUPS, 2, GROUP, LANES), BF16),
        in_specs=vmem(7),
        out_specs=pl.BlockSpec(memory_space=pltpu.VMEM),
        compiler_params=PARAMS,
        name="whiten",
    )(spec, rim, mean, taps, edge_table(), band, band_share)

    white, offsets = lax.optimization_barrier((white, offsets))
    if bins != GROUP:
        white = jnp.moveaxis(white, 1, 0).reshape(2, devices, bins, LANES)
        white = jnp.moveaxis(white, 0, 1)
    moved = lax.all_to_all(white, ("chan", "seg"), 0, 0, tiled=True)
    moved = moved.reshape(chan_count, seg_count, 2, bins, LANES)
    if bins % GROUP or 2 * bins % (8 * seg_count):
        return finish_plain(moved, offsets, loop_partner, loop_count, seg_count, seg_count)

    moves = pl.pallas_call(
        moves_kernel,
        out_shape=jax.ShapeDtypeStruct((3 * LANES, noff * LANES), BF16),
        in_specs=smem(1),
        out_specs=pl.BlockSpec(memory_space=pltpu.VMEM),
        compiler_params=PARAMS,
        name="offset_moves",
    )(offsets)
    flip = np.eye(LANES, dtype=np.float32)[::-1].astype(jnp.bfloat16)
    out_rows = near_each * 2 * bins + slots * (2 * bins // seg_count)
    crossed = pl.pallas_call(
        cross_kernel,
        out_shape=jax.ShapeDtypeStruct((chan_count, seg_count, out_rows, LANES), BF16),
        in_specs=smem(2) + vmem(4),
        out_specs=pl.BlockSpec(memory_space=pltpu.VMEM),
        scratch_shapes=[pltpu.VMEM((chan_count, seg_count * 2 * bins, LANES), F32)],
        compiler_params=PARAMS,
        name="cross_spectra",
    )(loop_partner, loop_count, moves, flip, pack_matrix(seg_count), moved)
    crossed = crossed.reshape(devices, out_rows, LANES)
    summed = lax.all_to_all(crossed, ("chan", "seg"), 0, 0, tiled=True)

    order = np.repeat(bin_order().reshape(devices, 1, bins), 2, axis=1).reshape(-1)
    part = np.broadcast_to(np.arange(2).reshape(1, 2, 1), (devices, 2, bins)).reshape(-1)
    inverse = np.concatenate(split_np(inverse_table(seg_count, order, part)), axis=0)
    near, loop = pl.pallas_call(
        functools.partial(lag_kernel, slots),
        out_shape=[
            jax.ShapeDtypeStruct((chans, near_each, LAGS), F32),
            jax.ShapeDtypeStruct((slots * share, LAGS), F32),
        ],
        in_specs=vmem(2),
        out_specs=vmem(2),
        compiler_params=PARAMS,
        name="lags",
    )(summed, inverse)
    return near, loop.reshape(1, slots, share, LAGS)


def solution(mesh):
    in_specs = (P("chan", "seg"), P(), P(), P(), P())
    out_specs = (P("chan", "seg", None), P("chan", None, "seg", None))
    return jax.shard_map(body, mesh=mesh, in_specs=in_specs, out_specs=out_specs, check_vma=False)
```

```python
import functools
import math

import jax
import jax.numpy as jnp
import numpy as np
from jax import lax
from jax.experimental import pallas as pl
from jax.experimental.pallas import tpu as pltpu
from jax.sharding import PartitionSpec as P

NFFT = 1024
LAGS = 256
TAPS = 64
DECIM = 4
HALFBAND = 10
BINS = 512
WATER = 0.2

LANES = 128
GROUP = 16
GROUPS = BINS // GROUP
OUT_BLOCK = 128
STEP = OUT_BLOCK * DECIM
RADIX = 4
DEPTH = NFFT // RADIX
FAR_BINS = BINS // RADIX

F32 = jnp.float32
BF16 = jnp.bfloat16
MIB = 1024 * 1024
PARAMS = pltpu.CompilerParams(vmem_limit_bytes=32 * MIB)


def bin_order():
    return np.concatenate([np.arange(r, BINS, RADIX) for r in range(RADIX)])


def split_np(table):
    high = table.astype(jnp.bfloat16)
    low = (table - high.astype(np.float64)).astype(jnp.bfloat16)
    return high, low


def short_table():
    bins = np.arange(FAR_BINS).reshape(-1, 1, GROUP, 1)
    angles = (bins * np.arange(DEPTH) % DEPTH) * (2.0 * np.pi / DEPTH)
    rows = np.concatenate([np.cos(angles), np.sin(angles)], axis=1).reshape(-1, DEPTH)
    high, low = split_np(rows)
    return np.concatenate([high, high, low], axis=1)


def twiddle_table():
    angles = np.arange(DEPTH)[:, None] * np.arange(1, RADIX) * (2.0 * np.pi / NFFT)
    columns = np.stack([np.cos(angles), np.sin(angles)], axis=2).reshape(DEPTH, -1)
    return np.pad(columns, ((0, 0), (0, LANES - columns.shape[1]))).astype(np.float32)


def edge_table():
    bins = bin_order().reshape(GROUPS, 1, GROUP, 1)
    angles = (bins * np.arange(GROUP) % NFFT) * (2.0 * np.pi / NFFT)
    rows = np.concatenate([np.cos(angles), -np.sin(angles)], axis=1) * (bins != 0)
    high, low = split_np(rows.reshape(2 * BINS, GROUP))
    table = np.concatenate([high, high, low], axis=1)
    return np.pad(table.astype(np.float32), ((0, 0), (0, LANES - 3 * GROUP))).astype(jnp.bfloat16)


def inverse_table(total_segs, bins, part):
    lag = np.arange(LAGS) - LAGS // 2
    angles = (bins[None, :] * lag[:, None] % NFFT) * (2.0 * np.pi / NFFT)
    weights = np.where(bins == 0, 1.0, 2.0) / math.sqrt(2.0 * BINS * total_segs)
    return np.where(part[None, :] == 1, -np.sin(angles), np.cos(angles)) * weights[None, :]


def band_tables():
    bins = bin_order()
    inside = np.abs(bins[:, None] - bins[None, :]) <= HALFBAND
    share = np.broadcast_to(1.0 / inside.sum(axis=1, keepdims=True), (BINS, LANES))
    return inside.astype(jnp.bfloat16), share.astype(np.float32)


def split(value):
    high = value.astype(BF16)
    return high, (value - high.astype(F32)).astype(BF16)


def mm(a, b):
    return jnp.dot(a, b, preferred_element_type=F32)


def mm_nt(a, b):
    return lax.dot_general(a, b, (((1,), (1,)), ((), ())), preferred_element_type=F32)


def tap_rows(taps):
    width = LANES + STEP
    square = (TAPS, TAPS)
    diagonal = lax.broadcasted_iota(jnp.int32, square, 0) == lax.broadcasted_iota(jnp.int32, square, 1)
    column_taps = jnp.sum(jnp.where(diagonal, taps, 0.0), axis=1, keepdims=True)
    tap = lax.broadcasted_iota(jnp.int32, (TAPS, width), 0)
    column = lax.broadcasted_iota(jnp.int32, (TAPS, width), 1)
    placed = jnp.where(column == LANES + DECIM - 1 - tap, column_taps, 0.0)
    spread = jnp.broadcast_to(jnp.sum(placed, axis=0, keepdims=True), (OUT_BLOCK, width))
    return pltpu.roll(spread, 0, 1, stride=DECIM, stride_axis=0)


def spectrum_kernel(
    taps_hbm,
    rec_hbm,
    tab_hbm,
    twist_hbm,
    spec_ref,
    mean_ref,
    head_ref,
    taps_ref,
    rec_ref,
    tab_ref,
    twist_ref,
    sems,
):
    blocks = rec_ref.shape[1] // STEP
    copies = [(taps_hbm, taps_ref)]
    for j in range(blocks):
        part = pl.ds(j * STEP, STEP)
        copies.append((rec_hbm.at[:, part], rec_ref.at[:, part]))
    copies = copies + [(twist_hbm, twist_ref), (tab_hbm, tab_ref)]
    copies = [pltpu.make_async_copy(*c, sems.at[i]) for i, c in enumerate(copies)]
    for copy in copies:
        copy.start()
    copies[0].wait()
    table = tap_rows(taps_ref[...])
    head_ref[...] = table[:GROUP, :LANES]
    taps_high, taps_low = split(table.T)
    taps_both = jnp.concatenate([taps_high, taps_low], axis=1)
    before = [jnp.zeros((LANES, LANES), BF16)] * 2
    outputs = []
    for j in range(blocks):
        copies[1 + j].wait()
        chunk = rec_ref[:, j * STEP : (j + 1) * STEP]
        if j == 0:
            mean = jnp.sum(chunk, axis=1, keepdims=True) * (1.0 / STEP)
        high, low = split(chunk - mean)
        wide = mm(jnp.concatenate([before[0], high], axis=1), taps_both)
        rest = mm(jnp.concatenate([before[1], low], axis=1), taps_high)
        outputs.append((wide[:, :LANES] + wide[:, LANES:] + rest).T)
        before = [high[:, STEP - LANES :], low[:, STEP - LANES :]]
    pieces = [jnp.concatenate(outputs[j : j + 2], axis=0) for j in range(0, blocks, 2)]
    mean_ref[...] = jnp.broadcast_to(mean, mean_ref.shape)
    even, odd = pieces[0] + pieces[2], pieces[1] + pieces[3]
    a, b = pieces[0] - pieces[2], pieces[1] - pieces[3]
    whole, half = even + odd, even - odd
    whole = whole - jnp.sum(whole, axis=0, keepdims=True) * (1.0 / DEPTH)
    copies[blocks + 1].wait()
    c1, s1, c2, s2, c3, s3 = [twist_ref[:, i : i + 1] for i in range(6)]
    inputs = [
        whole,
        a * c1 - b * s1,
        -(a * s1 + b * c1),
        half * c2,
        -(half * s2),
        a * c3 + b * s3,
        b * c3 - a * s3,
    ]
    parts = [split(value) for value in inputs]
    high = jnp.concatenate([p[0] for p in parts], axis=1)
    low = jnp.concatenate([p[1] for p in parts], axis=1)
    copies[blocks + 2].wait()
    out = mm(tab_ref[...], jnp.concatenate([high, low, high], axis=0))
    out = out.reshape(FAR_BINS // GROUP, 2, GROUP, out.shape[1])
    rows = 2 * FAR_BINS
    for r in range(RADIX):
        first = max(2 * r - 1, 0) * LANES
        real_in = out[..., first : first + LANES]
        if r == 0:
            real, imag = real_in[:, 0], -real_in[:, 1]
        else:
            imag_in = out[..., first + LANES : first + 2 * LANES]
            real, imag = real_in[:, 0] + imag_in[:, 1], imag_in[:, 0] - real_in[:, 1]
        both = jnp.stack([real, imag], axis=1).reshape(rows, LANES)
        spec_ref[r * rows : (r + 1) * rows, :] = both


def whiten_kernel(
    spec_ref, rim_ref, mean_ref, head_ref, edge_ref, band_ref, share_ref, white_ref
):
    head_high, head_low = split(head_ref[...])
    rim_high, rim_low = split(rim_ref[...] - mean_ref[...])
    history = mm_nt(
        jnp.concatenate([head_high, head_high, head_low], axis=1),
        jnp.concatenate([rim_high, rim_low, rim_high], axis=1),
    )
    high, low = split(history)
    stacked = jnp.concatenate([high, low, high], axis=0)
    spec = spec_ref[...] + mm(edge_ref[:, : 3 * GROUP], stacked)
    parted = spec.reshape(GROUPS, 2, GROUP, LANES)
    real, imag = parted[:, 0], parted[:, 1]
    amplitude = jnp.sqrt(real * real + imag * imag).reshape(BINS, LANES)
    high, low = split(amplitude)
    wide = mm(band_ref[...], jnp.concatenate([high, low], axis=1))
    smoothed = (wide[:, :LANES] + wide[:, LANES:]) * share_ref[...]
    level = jnp.sum(amplitude, axis=0, keepdims=True) * (1.0 / BINS)
    scale = 1.0 / (smoothed + (WATER * level + 1e-06))
    white = parted * scale.reshape(GROUPS, 1, GROUP, LANES)
    white_ref[...] = white.astype(BF16)


def moves_kernel(offs_ref, moves_ref):
    noff = offs_ref.shape[0]
    source = lax.broadcasted_iota(jnp.int32, (3 * LANES, LANES), 0)
    channel = lax.broadcasted_iota(jnp.int32, (3 * LANES, LANES), 1)
    for o in range(noff):
        hit = source == channel + (LANES + offs_ref[o])
        moves_ref[:, o * LANES : (o + 1) * LANES] = hit.astype(F32).astype(BF16)


def pack_matrix(owners):
    share = LANES // owners
    matrix = np.zeros((owners, owners, share, owners, owners, share), np.float32)
    for group in range(owners):
        for owner in range(owners):
            matrix[group, owner, :, owner, group, :] = np.eye(share)
    return matrix.reshape(owners * LANES, owners * LANES).astype(jnp.bfloat16)


def cross_kernel(
    partner_ref, count_ref, moves_ref, flip_ref, pack_ref, white_ref, out_ref, turned_ref
):
    blocks, segs, _, bins, _ = white_ref.shape
    owners = out_ref.shape[1]
    slots = partner_ref.shape[1]
    noff = moves_ref.shape[1] // LANES
    near_each = noff // owners
    rows = segs * 2 * bins
    packed_rows = 2 * bins // owners
    flats = [white_ref[b].reshape(rows, LANES) for b in range(blocks)]
    every = jnp.concatenate(flats, axis=0)
    turned_ref[...] = mm(every, flip_ref[...]).reshape(turned_ref.shape)
    before = jnp.concatenate(flats[-1:] + flats[:-1], axis=0)
    after = jnp.concatenate(flats[1:] + flats[:1], axis=0)
    moved = mm(jnp.concatenate([before, every, after], axis=1), moves_ref[...])

    def products(own, far):
        own = own.reshape(segs, 2, bins, LANES)
        far = far.reshape(segs, 2, bins, LANES)
        real = jnp.sum(own[:, 0] * far[:, 0] + own[:, 1] * far[:, 1], axis=0)
        imag = jnp.sum(own[:, 1] * far[:, 0] - own[:, 0] * far[:, 1], axis=0)
        return jnp.concatenate([real, imag], axis=0)

    near, loops = [], []
    for b in range(blocks):
        own = flats[b].astype(F32)
        far = moved[b * rows : (b + 1) * rows]
        near.append([products(own, far[:, o * LANES : (o + 1) * LANES]) for o in range(noff)])
        for k in range(slots):
            partner = jnp.clip(partner_ref[b, k], 0, blocks - 1)
            live = (k < count_ref[b]).astype(F32)
            pair = products(own, turned_ref[partner]) * live
            groups = [pair[g * packed_rows : (g + 1) * packed_rows] for g in range(owners)]
            loops.append(jnp.concatenate(groups, axis=1))
    packed = mm(jnp.concatenate(loops, axis=0).astype(BF16), pack_ref[...])
    depth = slots * packed_rows
    for b in range(blocks):
        for q in range(owners):
            tail = packed[b * depth : (b + 1) * depth, q * LANES : (q + 1) * LANES]
            mine = near[b][q * near_each : (q + 1) * near_each] + [tail]
            out_ref[b, q] = jnp.concatenate(mine, axis=0).astype(BF16)


def lag_kernel(slots, spec_ref, inv_ref, near_ref, loop_ref):
    sources = spec_ref.shape[0]
    rows = inv_ref.shape[1] // sources
    near_each = near_ref.shape[1]
    share = loop_ref.shape[0] // slots
    owners = LANES // share
    step = rows // owners
    columns = [
        spec_ref[:, t * rows : (t + 1) * rows].reshape(sources * rows, LANES)
        for t in range(near_each)
    ]
    loop = spec_ref[:, near_each * rows :].astype(F32)
    lane = lax.broadcasted_iota(jnp.int32, (sources, step, LANES), 2)
    for k in range(slots):
        tile = loop[:, k * step : (k + 1) * step]
        groups = [
            jnp.where((lane >= g * share) & (lane < (g + 1) * share), tile, 0.0)
            for g in range(owners)
        ]
        columns.append(jnp.concatenate(groups, axis=1).astype(BF16).reshape(sources * rows, LANES))
    both = mm(inv_ref[...], jnp.concatenate(columns, axis=1))
    lags = both[:LAGS] + both[LAGS:]
    for t in range(near_each):
        near_ref[:, t, :] = lags[:, t * LANES : (t + 1) * LANES].T
    for k in range(slots):
        first = (near_each + k) * LANES
        turned = lags[:, first : first + LANES].T
        loop_ref[k * share : (k + 1) * share] = sum(
            turned[g * share : (g + 1) * share] for g in range(owners)
        )


def vmem(count):
    return [pl.BlockSpec(memory_space=pltpu.VMEM)] * count


def smem(count):
    return [pl.BlockSpec(memory_space=pltpu.SMEM)] * count


def hbm(count):
    return [pl.BlockSpec(memory_space=pltpu.HBM)] * count


def in_hbm(array):
    return pltpu.with_memory_space_constraint(jnp.asarray(array), pltpu.HBM)


def finish_plain(white, offsets, loop_partner, loop_count, owners, total_segs):
    blocks, segs, _, bins, chans = white.shape
    devices = blocks * owners
    noff, slots = offsets.shape[0], loop_partner.shape[1]
    share = chans // owners
    wide = white.astype(F32)
    flat = jnp.moveaxis(wide, 0, 3).reshape(segs, 2, bins, blocks * chans)

    def products(own, far):
        real = jnp.sum(own[:, 0] * far[:, 0] + own[:, 1] * far[:, 1], axis=0)
        imag = jnp.sum(own[:, 1] * far[:, 0] - own[:, 0] * far[:, 1], axis=0)
        return jnp.stack([real, imag]).astype(BF16)

    near = [products(flat, jnp.roll(flat, -offsets[o], axis=3)) for o in range(noff)]
    near = jnp.stack(near).reshape(owners, noff // owners, 2, bins, blocks, chans)
    near = jnp.moveaxis(near, 4, 0).reshape(devices, noff // owners, 2 * bins, chans)
    loops = []
    for k in range(slots):
        far = jnp.flip(wide[loop_partner[:, k]], axis=4)
        live = (k < loop_count).astype(BF16)[:, None, None]
        pair = products(jnp.moveaxis(wide, 0, 2), jnp.moveaxis(far, 0, 2)) * live[None]
        loops.append(pair.reshape(2, blocks, bins, owners, share))
    loop = jnp.transpose(jnp.stack(loops), (2, 4, 0, 1, 3, 5))
    loop = loop.reshape(devices, slots, 2 * bins, share)
    order = np.repeat(bin_order().reshape(devices, 1, bins), 2, axis=1).reshape(-1)
    part = np.broadcast_to(np.arange(2).reshape(1, 2, 1), (devices, 2, bins)).reshape(-1)
    inverse = inverse_table(total_segs, order, part).astype(np.float32)
    inverse = inverse.reshape(LAGS, devices, 2 * bins)
    results = []
    for array in (near, loop):
        summed = lax.all_to_all(array, ("chan", "seg"), 0, 0, tiled=True).astype(F32)
        lags = jnp.einsum("dtvc,ldv->tcl", summed, inverse, precision=lax.Precision.HIGHEST)
        results.append(lags)
    return jnp.moveaxis(results[0], 0, 1), results[1][None]


def body(recording, filter_taps, offsets, loop_partner, loop_count):
    chan_count = lax.axis_size("chan")
    seg_count = lax.axis_size("seg")
    devices = chan_count * seg_count
    bins = BINS // devices
    chans, length = recording.shape
    noff, slots = offsets.shape[0], loop_partner.shape[1]
    share = chans // seg_count
    near_each = noff // seg_count
    assert length == NFFT * DECIM and chans == LANES and noff % seg_count == 0

    route = [(i, i + 1) for i in range(seg_count - 1)]
    rim = lax.ppermute(recording[:, length - LANES :], "seg", route)
    taps = filter_taps.reshape(1, TAPS)
    spec, mean, head = pl.pallas_call(
        spectrum_kernel,
        out_shape=[
            jax.ShapeDtypeStruct((2 * BINS, LANES), F32),
            jax.ShapeDtypeStruct((LANES, LANES), F32),
            jax.ShapeDtypeStruct((GROUP, LANES), F32),
        ],
        in_specs=hbm(4),
        out_specs=vmem(3),
        scratch_shapes=[
            pltpu.VMEM((1, TAPS), F32),
            pltpu.VMEM((chans, length), F32),
            pltpu.VMEM((2 * FAR_BINS, 3 * DEPTH), BF16),
            pltpu.VMEM((DEPTH, LANES), F32),
            pltpu.SemaphoreType.DMA((length // STEP + 3,)),
        ],
        compiler_params=PARAMS,
        cost_estimate=pl.CostEstimate(
            flops=1_000_000_000, bytes_accessed=5_000_000, transcendentals=0
        ),
        name="filter_and_transform",
    )(in_hbm(taps), in_hbm(recording), in_hbm(short_table()), in_hbm(twiddle_table()))

    band, band_share = band_tables()
    white = pl.pallas_call(
        whiten_kernel,
        out_shape=jax.ShapeDtypeStruct((GROUPS, 2, GROUP, LANES), BF16),
        in_specs=vmem(7),
        out_specs=pl.BlockSpec(memory_space=pltpu.VMEM),
        compiler_params=PARAMS,
        name="whiten",
    )(spec, rim, mean, head, edge_table(), band, band_share)

    white, offsets = lax.optimization_barrier((white, offsets))
    if bins != GROUP:
        white = jnp.moveaxis(white, 1, 0).reshape(2, devices, bins, LANES)
        white = jnp.moveaxis(white, 0, 1)
    moved = lax.all_to_all(white, ("chan", "seg"), 0, 0, tiled=True)
    moved = moved.reshape(chan_count, seg_count, 2, bins, LANES)
    if bins % GROUP or 2 * bins % (8 * seg_count):
        return finish_plain(moved, offsets, loop_partner, loop_count, seg_count, seg_count)

    moves = pl.pallas_call(
        moves_kernel,
        out_shape=jax.ShapeDtypeStruct((3 * LANES, noff * LANES), BF16),
        in_specs=smem(1),
        out_specs=pl.BlockSpec(memory_space=pltpu.VMEM),
        compiler_params=PARAMS,
        name="offset_moves",
    )(offsets)
    flip = np.eye(LANES, dtype=np.float32)[::-1].astype(jnp.bfloat16)
    out_rows = near_each * 2 * bins + slots * (2 * bins // seg_count)
    crossed = pl.pallas_call(
        cross_kernel,
        out_shape=jax.ShapeDtypeStruct((chan_count, seg_count, out_rows, LANES), BF16),
        in_specs=smem(2) + vmem(4),
        out_specs=pl.BlockSpec(memory_space=pltpu.VMEM),
        scratch_shapes=[pltpu.VMEM((chan_count, seg_count * 2 * bins, LANES), F32)],
        compiler_params=PARAMS,
        name="cross_spectra",
    )(loop_partner, loop_count, moves, flip, pack_matrix(seg_count), moved)
    crossed = crossed.reshape(devices, out_rows, LANES)
    summed = lax.all_to_all(crossed, ("chan", "seg"), 0, 0, tiled=True)

    order = np.repeat(bin_order().reshape(devices, 1, bins), 2, axis=1).reshape(-1)
    part = np.broadcast_to(np.arange(2).reshape(1, 2, 1), (devices, 2, bins)).reshape(-1)
    inverse = np.concatenate(split_np(inverse_table(seg_count, order, part)), axis=0)
    near, loop = pl.pallas_call(
        functools.partial(lag_kernel, slots),
        out_shape=[
            jax.ShapeDtypeStruct((chans, near_each, LAGS), F32),
            jax.ShapeDtypeStruct((slots * share, LAGS), F32),
        ],
        in_specs=vmem(2),
        out_specs=vmem(2),
        compiler_params=PARAMS,
        name="lags",
    )(summed, inverse)
    return near, loop.reshape(1, slots, share, LAGS)


def solution(mesh):
    in_specs = (P("chan", "seg"), P(), P(), P(), P())
    out_specs = (P("chan", "seg", None), P("chan", None, "seg", None))
    return jax.shard_map(body, mesh=mesh, in_specs=in_specs, out_specs=out_specs, check_vma=False)
```

```python
import functools
import math

import jax
import jax.numpy as jnp
import numpy as np
from jax import lax
from jax.experimental import pallas as pl
from jax.experimental.pallas import tpu as pltpu
from jax.sharding import PartitionSpec as P

NFFT = 1024
LAGS = 256
TAPS = 64
DECIM = 4
HALFBAND = 10
BINS = 512
WATER = 0.2

LANES = 128
GROUP = 16
GROUPS = BINS // GROUP
OUT_BLOCK = 128
STEP = OUT_BLOCK * DECIM
RADIX = 4
DEPTH = NFFT // RADIX
FAR_BINS = BINS // RADIX

F32 = jnp.float32
BF16 = jnp.bfloat16
MIB = 1024 * 1024
PARAMS = pltpu.CompilerParams(vmem_limit_bytes=32 * MIB)


def bin_order():
    return np.concatenate([np.arange(r, BINS, RADIX) for r in range(RADIX)])


def split_np(table):
    high = table.astype(jnp.bfloat16)
    low = (table - high.astype(np.float64)).astype(jnp.bfloat16)
    return high, low


def short_table():
    bins = np.arange(FAR_BINS).reshape(-1, 1, GROUP, 1)
    angles = (bins * np.arange(DEPTH) % DEPTH) * (2.0 * np.pi / DEPTH)
    rows = np.concatenate([np.cos(angles), np.sin(angles)], axis=1).reshape(-1, DEPTH)
    high, low = split_np(rows)
    return np.concatenate([high, high, low], axis=1)


def twiddle_table():
    angles = np.arange(DEPTH)[:, None] * np.arange(1, RADIX) * (2.0 * np.pi / NFFT)
    columns = np.stack([np.cos(angles), np.sin(angles)], axis=2).reshape(DEPTH, -1)
    return np.pad(columns, ((0, 0), (0, LANES - columns.shape[1]))).astype(np.float32)


def edge_table():
    bins = bin_order().reshape(GROUPS, 1, GROUP, 1)
    angles = (bins * np.arange(GROUP) % NFFT) * (2.0 * np.pi / NFFT)
    rows = np.concatenate([np.cos(angles), -np.sin(angles)], axis=1) * (bins != 0)
    high, low = split_np(rows.reshape(2 * BINS, GROUP))
    table = np.concatenate([high, high, low], axis=1)
    return np.pad(table.astype(np.float32), ((0, 0), (0, LANES - 3 * GROUP))).astype(jnp.bfloat16)


def inverse_table(total_segs, bins, part):
    lag = np.arange(LAGS) - LAGS // 2
    angles = (bins[None, :] * lag[:, None] % NFFT) * (2.0 * np.pi / NFFT)
    weights = np.where(bins == 0, 1.0, 2.0) / math.sqrt(2.0 * BINS * total_segs)
    return np.where(part[None, :] == 1, -np.sin(angles), np.cos(angles)) * weights[None, :]


def band_tables():
    bins = bin_order()
    inside = np.abs(bins[:, None] - bins[None, :]) <= HALFBAND
    share = np.broadcast_to(1.0 / inside.sum(axis=1, keepdims=True), (BINS, LANES))
    return inside.astype(jnp.bfloat16), share.astype(np.float32)


def split(value):
    high = value.astype(BF16)
    return high, (value - high.astype(F32)).astype(BF16)


def mm(a, b):
    return jnp.dot(a, b, preferred_element_type=F32)


def mm_nt(a, b):
    return lax.dot_general(a, b, (((1,), (1,)), ((), ())), preferred_element_type=F32)


def tap_rows(taps):
    width = LANES + STEP
    square = (TAPS, TAPS)
    diagonal = lax.broadcasted_iota(jnp.int32, square, 0) == lax.broadcasted_iota(jnp.int32, square, 1)
    column_taps = jnp.sum(jnp.where(diagonal, taps, 0.0), axis=1, keepdims=True)
    tap = lax.broadcasted_iota(jnp.int32, (TAPS, width), 0)
    column = lax.broadcasted_iota(jnp.int32, (TAPS, width), 1)
    placed = jnp.where(column == LANES + DECIM - 1 - tap, column_taps, 0.0)
    spread = jnp.broadcast_to(jnp.sum(placed, axis=0, keepdims=True), (OUT_BLOCK, width))
    return pltpu.roll(spread, 0, 1, stride=DECIM, stride_axis=0)


def spectrum_kernel(
    taps_hbm,
    rec_hbm,
    tab_hbm,
    twist_hbm,
    spec_ref,
    mean_ref,
    head_ref,
    taps_ref,
    rec_ref,
    tab_ref,
    twist_ref,
    sems,
):
    blocks = rec_ref.shape[1] // STEP
    copies = [(taps_hbm, taps_ref)]
    for j in range(blocks):
        part = pl.ds(j * STEP, STEP)
        copies.append((rec_hbm.at[:, part], rec_ref.at[:, part]))
    copies = copies + [(twist_hbm, twist_ref), (tab_hbm, tab_ref)]
    copies = [pltpu.make_async_copy(*c, sems.at[i]) for i, c in enumerate(copies)]
    for copy in copies:
        copy.start()
    copies[0].wait()
    table = tap_rows(taps_ref[...])
    head_ref[...] = table[:GROUP, :LANES]
    taps_high, taps_low = split(table.T)
    taps_both = jnp.concatenate([taps_high, taps_low], axis=1)
    before = [jnp.zeros((LANES, LANES), BF16)] * 2
    outputs = []
    for first in range(0, blocks, blocks // 2):
        windows = ([], [])
        for j in range(first, first + blocks // 2):
            copies[1 + j].wait()
        for j in range(first, first + blocks // 2):
            chunk = rec_ref[:, j * STEP : (j + 1) * STEP]
            if j == 0:
                mean = jnp.sum(chunk, axis=1, keepdims=True) * (1.0 / STEP)
            for i, value in enumerate(split(chunk - mean)):
                windows[i].append(jnp.concatenate([before[i], value], axis=1))
                before[i] = value[:, STEP - LANES :]
        wide = mm(jnp.concatenate(windows[0], axis=0), taps_both)
        rest = mm(jnp.concatenate(windows[1], axis=0), taps_high)
        total = wide[:, :LANES] + wide[:, LANES:] + rest
        outputs += [total[t * LANES : (t + 1) * LANES].T for t in range(blocks // 2)]
    pieces = [jnp.concatenate(outputs[j : j + 2], axis=0) for j in range(0, blocks, 2)]
    mean_ref[...] = jnp.broadcast_to(mean, mean_ref.shape)
    even, odd = pieces[0] + pieces[2], pieces[1] + pieces[3]
    a, b = pieces[0] - pieces[2], pieces[1] - pieces[3]
    whole, half = even + odd, even - odd
    whole = whole - jnp.sum(whole, axis=0, keepdims=True) * (1.0 / DEPTH)
    copies[blocks + 1].wait()
    c1, s1, c2, s2, c3, s3 = [twist_ref[:, i : i + 1] for i in range(6)]
    inputs = [
        whole,
        a * c1 - b * s1,
        -(a * s1 + b * c1),
        half * c2,
        -(half * s2),
        a * c3 + b * s3,
        b * c3 - a * s3,
    ]
    parts = [split(value) for value in inputs]
    high = jnp.concatenate([p[0] for p in parts], axis=1)
    low = jnp.concatenate([p[1] for p in parts], axis=1)
    copies[blocks + 2].wait()
    out = mm(tab_ref[...], jnp.concatenate([high, low, high], axis=0))
    out = out.reshape(FAR_BINS // GROUP, 2, GROUP, out.shape[1])
    rows = 2 * FAR_BINS
    for r in range(RADIX):
        first = max(2 * r - 1, 0) * LANES
        real_in = out[..., first : first + LANES]
        if r == 0:
            real, imag = real_in[:, 0], -real_in[:, 1]
        else:
            imag_in = out[..., first + LANES : first + 2 * LANES]
            real, imag = real_in[:, 0] + imag_in[:, 1], imag_in[:, 0] - real_in[:, 1]
        both = jnp.stack([real, imag], axis=1).reshape(rows, LANES)
        spec_ref[r * rows : (r + 1) * rows, :] = both


def whiten_kernel(
    spec_ref, rim_ref, mean_ref, head_ref, edge_ref, band_ref, share_ref, white_ref
):
    head_high, head_low = split(head_ref[...])
    rim_high, rim_low = split(rim_ref[...] - mean_ref[...])
    history = mm_nt(
        jnp.concatenate([head_high, head_high, head_low], axis=1),
        jnp.concatenate([rim_high, rim_low, rim_high], axis=1),
    )
    high, low = split(history)
    stacked = jnp.concatenate([high, low, high], axis=0)
    spec = spec_ref[...] + mm(edge_ref[:, : 3 * GROUP], stacked)
    parted = spec.reshape(GROUPS, 2, GROUP, LANES)
    real, imag = parted[:, 0], parted[:, 1]
    amplitude = jnp.sqrt(real * real + imag * imag).reshape(BINS, LANES)
    high, low = split(amplitude)
    wide = mm(band_ref[...], jnp.concatenate([high, low], axis=1))
    smoothed = (wide[:, :LANES] + wide[:, LANES:]) * share_ref[...]
    level = jnp.sum(amplitude, axis=0, keepdims=True) * (1.0 / BINS)
    scale = 1.0 / (smoothed + (WATER * level + 1e-06))
    white = parted * scale.reshape(GROUPS, 1, GROUP, LANES)
    white_ref[...] = white.astype(BF16)


def moves_kernel(offs_ref, moves_ref):
    noff = offs_ref.shape[0]
    source = lax.broadcasted_iota(jnp.int32, (3 * LANES, LANES), 0)
    channel = lax.broadcasted_iota(jnp.int32, (3 * LANES, LANES), 1)
    for o in range(noff):
        hit = source == channel + (LANES + offs_ref[o])
        moves_ref[:, o * LANES : (o + 1) * LANES] = hit.astype(F32).astype(BF16)


def pack_matrix(owners):
    share = LANES // owners
    matrix = np.zeros((owners, owners, share, owners, owners, share), np.float32)
    for group in range(owners):
        for owner in range(owners):
            matrix[group, owner, :, owner, group, :] = np.eye(share)
    return matrix.reshape(owners * LANES, owners * LANES).astype(jnp.bfloat16)


def cross_kernel(
    partner_ref, count_ref, moves_ref, flip_ref, pack_ref, white_ref, out_ref, turned_ref
):
    blocks, segs, _, bins, _ = white_ref.shape
    owners = out_ref.shape[1]
    slots = partner_ref.shape[1]
    noff = moves_ref.shape[1] // LANES
    near_each = noff // owners
    rows = segs * 2 * bins
    packed_rows = 2 * bins // owners
    flats = [white_ref[b].reshape(rows, LANES) for b in range(blocks)]
    every = jnp.concatenate(flats, axis=0)
    turned_ref[...] = mm(every, flip_ref[...]).reshape(turned_ref.shape)
    before = jnp.concatenate(flats[-1:] + flats[:-1], axis=0)
    after = jnp.concatenate(flats[1:] + flats[:1], axis=0)
    moved = mm(jnp.concatenate([before, every, after], axis=1), moves_ref[...])

    def products(own, far):
        own = own.reshape(segs, 2, bins, LANES)
        far = far.reshape(segs, 2, bins, LANES)
        real = jnp.sum(own[:, 0] * far[:, 0] + own[:, 1] * far[:, 1], axis=0)
        imag = jnp.sum(own[:, 1] * far[:, 0] - own[:, 0] * far[:, 1], axis=0)
        return jnp.concatenate([real, imag], axis=0)

    near, loops = [], []
    for b in range(blocks):
        own = flats[b].astype(F32)
        far = moved[b * rows : (b + 1) * rows]
        near.append([products(own, far[:, o * LANES : (o + 1) * LANES]) for o in range(noff)])
        for k in range(slots):
            partner = jnp.clip(partner_ref[b, k], 0, blocks - 1)
            live = (k < count_ref[b]).astype(F32)
            pair = products(own, turned_ref[partner]) * live
            groups = [pair[g * packed_rows : (g + 1) * packed_rows] for g in range(owners)]
            loops.append(jnp.concatenate(groups, axis=1))
    packed = mm(jnp.concatenate(loops, axis=0).astype(BF16), pack_ref[...])
    depth = slots * packed_rows
    for b in range(blocks):
        for q in range(owners):
            tail = packed[b * depth : (b + 1) * depth, q * LANES : (q + 1) * LANES]
            mine = near[b][q * near_each : (q + 1) * near_each] + [tail]
            out_ref[b, q] = jnp.concatenate(mine, axis=0).astype(BF16)


def lag_kernel(slots, spec_ref, inv_ref, near_ref, loop_ref):
    sources = spec_ref.shape[0]
    rows = inv_ref.shape[1] // sources
    near_each = near_ref.shape[1]
    share = loop_ref.shape[0] // slots
    owners = LANES // share
    step = rows // owners
    columns = [
        spec_ref[:, t * rows : (t + 1) * rows].reshape(sources * rows, LANES)
        for t in range(near_each)
    ]
    loop = spec_ref[:, near_each * rows :].astype(F32)
    lane = lax.broadcasted_iota(jnp.int32, (sources, step, LANES), 2)
    for k in range(slots):
        tile = loop[:, k * step : (k + 1) * step]
        groups = [
            jnp.where((lane >= g * share) & (lane < (g + 1) * share), tile, 0.0)
            for g in range(owners)
        ]
        columns.append(jnp.concatenate(groups, axis=1).astype(BF16).reshape(sources * rows, LANES))
    both = mm(inv_ref[...], jnp.concatenate(columns, axis=1))
    lags = both[:LAGS] + both[LAGS:]
    for t in range(near_each):
        near_ref[:, t, :] = lags[:, t * LANES : (t + 1) * LANES].T
    for k in range(slots):
        first = (near_each + k) * LANES
        turned = lags[:, first : first + LANES].T
        loop_ref[k * share : (k + 1) * share] = sum(
            turned[g * share : (g + 1) * share] for g in range(owners)
        )


def vmem(count):
    return [pl.BlockSpec(memory_space=pltpu.VMEM)] * count


def smem(count):
    return [pl.BlockSpec(memory_space=pltpu.SMEM)] * count


def hbm(count):
    return [pl.BlockSpec(memory_space=pltpu.HBM)] * count


def in_hbm(array):
    return pltpu.with_memory_space_constraint(jnp.asarray(array), pltpu.HBM)


def finish_plain(white, offsets, loop_partner, loop_count, owners, total_segs):
    blocks, segs, _, bins, chans = white.shape
    devices = blocks * owners
    noff, slots = offsets.shape[0], loop_partner.shape[1]
    share = chans // owners
    wide = white.astype(F32)
    flat = jnp.moveaxis(wide, 0, 3).reshape(segs, 2, bins, blocks * chans)

    def products(own, far):
        real = jnp.sum(own[:, 0] * far[:, 0] + own[:, 1] * far[:, 1], axis=0)
        imag = jnp.sum(own[:, 1] * far[:, 0] - own[:, 0] * far[:, 1], axis=0)
        return jnp.stack([real, imag]).astype(BF16)

    near = [products(flat, jnp.roll(flat, -offsets[o], axis=3)) for o in range(noff)]
    near = jnp.stack(near).reshape(owners, noff // owners, 2, bins, blocks, chans)
    near = jnp.moveaxis(near, 4, 0).reshape(devices, noff // owners, 2 * bins, chans)
    loops = []
    for k in range(slots):
        far = jnp.flip(wide[loop_partner[:, k]], axis=4)
        live = (k < loop_count).astype(BF16)[:, None, None]
        pair = products(jnp.moveaxis(wide, 0, 2), jnp.moveaxis(far, 0, 2)) * live[None]
        loops.append(pair.reshape(2, blocks, bins, owners, share))
    loop = jnp.transpose(jnp.stack(loops), (2, 4, 0, 1, 3, 5))
    loop = loop.reshape(devices, slots, 2 * bins, share)
    order = np.repeat(bin_order().reshape(devices, 1, bins), 2, axis=1).reshape(-1)
    part = np.broadcast_to(np.arange(2).reshape(1, 2, 1), (devices, 2, bins)).reshape(-1)
    inverse = inverse_table(total_segs, order, part).astype(np.float32)
    inverse = inverse.reshape(LAGS, devices, 2 * bins)
    results = []
    for array in (near, loop):
        summed = lax.all_to_all(array, ("chan", "seg"), 0, 0, tiled=True).astype(F32)
        lags = jnp.einsum("dtvc,ldv->tcl", summed, inverse, precision=lax.Precision.HIGHEST)
        results.append(lags)
    return jnp.moveaxis(results[0], 0, 1), results[1][None]


def body(recording, filter_taps, offsets, loop_partner, loop_count):
    chan_count = lax.axis_size("chan")
    seg_count = lax.axis_size("seg")
    devices = chan_count * seg_count
    bins = BINS // devices
    chans, length = recording.shape
    noff, slots = offsets.shape[0], loop_partner.shape[1]
    share = chans // seg_count
    near_each = noff // seg_count
    assert length == NFFT * DECIM and chans == LANES and noff % seg_count == 0

    route = [(i, i + 1) for i in range(seg_count - 1)]
    rim = lax.ppermute(recording[:, length - LANES :], "seg", route)
    taps = filter_taps.reshape(1, TAPS)
    spec, mean, head = pl.pallas_call(
        spectrum_kernel,
        out_shape=[
            jax.ShapeDtypeStruct((2 * BINS, LANES), F32),
            jax.ShapeDtypeStruct((LANES, LANES), F32),
            jax.ShapeDtypeStruct((GROUP, LANES), F32),
        ],
        in_specs=hbm(4),
        out_specs=vmem(3),
        scratch_shapes=[
            pltpu.VMEM((1, TAPS), F32),
            pltpu.VMEM((chans, length), F32),
            pltpu.VMEM((2 * FAR_BINS, 3 * DEPTH), BF16),
            pltpu.VMEM((DEPTH, LANES), F32),
            pltpu.SemaphoreType.DMA((length // STEP + 3,)),
        ],
        compiler_params=PARAMS,
        cost_estimate=pl.CostEstimate(
            flops=1_000_000_000, bytes_accessed=5_000_000, transcendentals=0
        ),
        name="filter_and_transform",
    )(in_hbm(taps), in_hbm(recording), in_hbm(short_table()), in_hbm(twiddle_table()))

    band, band_share = band_tables()
    white = pl.pallas_call(
        whiten_kernel,
        out_shape=jax.ShapeDtypeStruct((GROUPS, 2, GROUP, LANES), BF16),
        in_specs=vmem(7),
        out_specs=pl.BlockSpec(memory_space=pltpu.VMEM),
        compiler_params=PARAMS,
        name="whiten",
    )(spec, rim, mean, head, edge_table(), band, band_share)

    white, offsets = lax.optimization_barrier((white, offsets))
    if bins != GROUP:
        white = jnp.moveaxis(white, 1, 0).reshape(2, devices, bins, LANES)
        white = jnp.moveaxis(white, 0, 1)
    moved = lax.all_to_all(white, ("chan", "seg"), 0, 0, tiled=True)
    moved = moved.reshape(chan_count, seg_count, 2, bins, LANES)
    if bins % GROUP or 2 * bins % (8 * seg_count):
        return finish_plain(moved, offsets, loop_partner, loop_count, seg_count, seg_count)

    moves = pl.pallas_call(
        moves_kernel,
        out_shape=jax.ShapeDtypeStruct((3 * LANES, noff * LANES), BF16),
        in_specs=smem(1),
        out_specs=pl.BlockSpec(memory_space=pltpu.VMEM),
        compiler_params=PARAMS,
        name="offset_moves",
    )(offsets)
    flip = np.eye(LANES, dtype=np.float32)[::-1].astype(jnp.bfloat16)
    out_rows = near_each * 2 * bins + slots * (2 * bins // seg_count)
    crossed = pl.pallas_call(
        cross_kernel,
        out_shape=jax.ShapeDtypeStruct((chan_count, seg_count, out_rows, LANES), BF16),
        in_specs=smem(2) + vmem(4),
        out_specs=pl.BlockSpec(memory_space=pltpu.VMEM),
        scratch_shapes=[pltpu.VMEM((chan_count, seg_count * 2 * bins, LANES), F32)],
        compiler_params=PARAMS,
        name="cross_spectra",
    )(loop_partner, loop_count, moves, flip, pack_matrix(seg_count), moved)
    crossed = crossed.reshape(devices, out_rows, LANES)
    summed = lax.all_to_all(crossed, ("chan", "seg"), 0, 0, tiled=True)

    order = np.repeat(bin_order().reshape(devices, 1, bins), 2, axis=1).reshape(-1)
    part = np.broadcast_to(np.arange(2).reshape(1, 2, 1), (devices, 2, bins)).reshape(-1)
    inverse = np.concatenate(split_np(inverse_table(seg_count, order, part)), axis=0)
    near, loop = pl.pallas_call(
        functools.partial(lag_kernel, slots),
        out_shape=[
            jax.ShapeDtypeStruct((chans, near_each, LAGS), F32),
            jax.ShapeDtypeStruct((slots * share, LAGS), F32),
        ],
        in_specs=vmem(2),
        out_specs=vmem(2),
        compiler_params=PARAMS,
        name="lags",
    )(summed, inverse)
    return near, loop.reshape(1, slots, share, LAGS)


def solution(mesh):
    in_specs = (P("chan", "seg"), P(), P(), P(), P())
    out_specs = (P("chan", "seg", None), P("chan", None, "seg", None))
    return jax.shard_map(body, mesh=mesh, in_specs=in_specs, out_specs=out_specs, check_vma=False)
```

```python
import functools
import math

import jax
import jax.numpy as jnp
import numpy as np
from jax import lax
from jax.experimental import pallas as pl
from jax.experimental.pallas import tpu as pltpu
from jax.sharding import PartitionSpec as P

NFFT = 1024
LAGS = 256
TAPS = 64
DECIM = 4
HALFBAND = 10
BINS = 512
WATER = 0.2

LANES = 128
GROUP = 16
GROUPS = BINS // GROUP
OUT_BLOCK = 128
STEP = OUT_BLOCK * DECIM
RADIX = 4
DEPTH = NFFT // RADIX
FAR_BINS = BINS // RADIX

F32 = jnp.float32
BF16 = jnp.bfloat16
MIB = 1024 * 1024
PARAMS = pltpu.CompilerParams(vmem_limit_bytes=32 * MIB)


def bin_order():
    return np.concatenate([np.arange(r, BINS, RADIX) for r in range(RADIX)])


def split_np(table):
    high = table.astype(jnp.bfloat16)
    low = (table - high.astype(np.float64)).astype(jnp.bfloat16)
    return high, low


def short_table():
    bins = np.arange(FAR_BINS).reshape(-1, 1, GROUP, 1)
    angles = (bins * np.arange(DEPTH) % DEPTH) * (2.0 * np.pi / DEPTH)
    rows = np.concatenate([np.cos(angles), np.sin(angles)], axis=1).reshape(-1, DEPTH)
    high, low = split_np(rows)
    return np.concatenate([high, high, low], axis=1)


def twiddle_table():
    angles = np.arange(DEPTH)[:, None] * np.arange(1, RADIX) * (2.0 * np.pi / NFFT)
    columns = np.stack([np.cos(angles), np.sin(angles)], axis=2).reshape(DEPTH, -1)
    return np.pad(columns, ((0, 0), (0, LANES - columns.shape[1]))).astype(np.float32)


def edge_table():
    bins = bin_order().reshape(GROUPS, 1, GROUP, 1)
    angles = (bins * np.arange(GROUP) % NFFT) * (2.0 * np.pi / NFFT)
    rows = np.concatenate([np.cos(angles), -np.sin(angles)], axis=1) * (bins != 0)
    high, low = split_np(rows.reshape(2 * BINS, GROUP))
    table = np.concatenate([high, high, low], axis=1)
    return np.pad(table.astype(np.float32), ((0, 0), (0, LANES - 3 * GROUP))).astype(jnp.bfloat16)


def inverse_table(total_segs, bins, part):
    lag = np.arange(LAGS) - LAGS // 2
    angles = (bins[None, :] * lag[:, None] % NFFT) * (2.0 * np.pi / NFFT)
    weights = np.where(bins == 0, 1.0, 2.0) / math.sqrt(2.0 * BINS * total_segs)
    return np.where(part[None, :] == 1, -np.sin(angles), np.cos(angles)) * weights[None, :]


def band_tables():
    bins = bin_order()
    inside = np.abs(bins[:, None] - bins[None, :]) <= HALFBAND
    share = np.broadcast_to(1.0 / inside.sum(axis=1, keepdims=True), (BINS, LANES))
    return inside.astype(jnp.bfloat16), share.astype(np.float32)


def split(value):
    high = value.astype(BF16)
    return high, (value - high.astype(F32)).astype(BF16)


def mm(a, b):
    return jnp.dot(a, b, preferred_element_type=F32)


def mm_nt(a, b):
    return lax.dot_general(a, b, (((1,), (1,)), ((), ())), preferred_element_type=F32)


def tap_rows(taps):
    width = LANES + STEP
    square = (TAPS, TAPS)
    diagonal = lax.broadcasted_iota(jnp.int32, square, 0) == lax.broadcasted_iota(jnp.int32, square, 1)
    column_taps = jnp.sum(jnp.where(diagonal, taps, 0.0), axis=1, keepdims=True)
    tap = lax.broadcasted_iota(jnp.int32, (TAPS, width), 0)
    column = lax.broadcasted_iota(jnp.int32, (TAPS, width), 1)
    placed = jnp.where(column == LANES + DECIM - 1 - tap, column_taps, 0.0)
    spread = jnp.broadcast_to(jnp.sum(placed, axis=0, keepdims=True), (OUT_BLOCK, width))
    return pltpu.roll(spread, 0, 1, stride=DECIM, stride_axis=0)


def spectrum_kernel(
    taps_hbm,
    rec_hbm,
    tab_hbm,
    twist_hbm,
    spec_ref,
    mean_ref,
    head_ref,
    taps_ref,
    rec_ref,
    tab_ref,
    twist_ref,
    sems,
):
    blocks = rec_ref.shape[1] // STEP
    copies = [(taps_hbm, taps_ref)]
    for j in range(blocks):
        part = pl.ds(j * STEP, STEP)
        copies.append((rec_hbm.at[:, part], rec_ref.at[:, part]))
    copies = copies + [(twist_hbm, twist_ref), (tab_hbm, tab_ref)]
    copies = [pltpu.make_async_copy(*c, sems.at[i]) for i, c in enumerate(copies)]
    for copy in copies:
        copy.start()
    copies[0].wait()
    table = tap_rows(taps_ref[...])
    head_ref[...] = table[:GROUP, :LANES]
    taps_high, taps_low = split(table.T)
    taps_both = jnp.concatenate([taps_high, taps_low], axis=1)
    before = [jnp.zeros((LANES, LANES), BF16)] * 2
    outputs = []
    for first in range(0, blocks, blocks // 2):
        windows = ([], [])
        for j in range(first, first + blocks // 2):
            copies[1 + j].wait()
        for j in range(first, first + blocks // 2):
            chunk = rec_ref[:, j * STEP : (j + 1) * STEP]
            if j == 0:
                mean = jnp.sum(chunk, axis=1, keepdims=True) * (1.0 / STEP)
            for i, value in enumerate(split(chunk - mean)):
                windows[i].append(jnp.concatenate([before[i], value], axis=1))
                before[i] = value[:, STEP - LANES :]
        wide = mm(jnp.concatenate(windows[0], axis=0), taps_both)
        rest = mm(jnp.concatenate(windows[1], axis=0), taps_high)
        total = wide[:, :LANES] + wide[:, LANES:] + rest
        outputs += [total[t * LANES : (t + 1) * LANES].T for t in range(blocks // 2)]
    pieces = [jnp.concatenate(outputs[j : j + 2], axis=0) for j in range(0, blocks, 2)]
    mean_ref[...] = jnp.broadcast_to(mean, mean_ref.shape)
    even, odd = pieces[0] + pieces[2], pieces[1] + pieces[3]
    a, b = pieces[0] - pieces[2], pieces[1] - pieces[3]
    whole, half = even + odd, even - odd
    whole = whole - jnp.sum(whole, axis=0, keepdims=True) * (1.0 / DEPTH)
    copies[blocks + 1].wait()
    c1, s1, c2, s2, c3, s3 = [twist_ref[:, i : i + 1] for i in range(6)]
    inputs = [
        whole,
        a * c1 - b * s1,
        -(a * s1 + b * c1),
        half * c2,
        -(half * s2),
        a * c3 + b * s3,
        b * c3 - a * s3,
    ]
    parts = [split(value) for value in inputs]
    high = jnp.concatenate([p[0] for p in parts], axis=1)
    low = jnp.concatenate([p[1] for p in parts], axis=1)
    copies[blocks + 2].wait()
    out = mm(tab_ref[...], jnp.concatenate([high, low, high], axis=0))
    out = out.reshape(FAR_BINS // GROUP, 2, GROUP, out.shape[1])
    rows = 2 * FAR_BINS
    for r in range(RADIX):
        first = max(2 * r - 1, 0) * LANES
        real_in = out[..., first : first + LANES]
        if r == 0:
            real, imag = real_in[:, 0], -real_in[:, 1]
        else:
            imag_in = out[..., first + LANES : first + 2 * LANES]
            real, imag = real_in[:, 0] + imag_in[:, 1], imag_in[:, 0] - real_in[:, 1]
        both = jnp.stack([real, imag], axis=1).reshape(rows, LANES)
        spec_ref[r * rows : (r + 1) * rows, :] = both


def whiten_kernel(
    rims_hbm, spec_ref, mean_ref, head_ref, edge_ref, band_ref, share_ref, white_ref, rim_ref, sem
):
    place = lax.axis_index("seg")
    copy = pltpu.make_async_copy(rims_hbm.at[jnp.maximum(place - 1, 0)], rim_ref, sem)
    copy.start()
    head_high, head_low = split(head_ref[...])
    copy.wait()
    rim = jnp.where(place > 0, rim_ref[...], 0.0)
    rim_high, rim_low = split(rim - mean_ref[...])
    history = mm_nt(
        jnp.concatenate([head_high, head_high, head_low], axis=1),
        jnp.concatenate([rim_high, rim_low, rim_high], axis=1),
    )
    high, low = split(history)
    stacked = jnp.concatenate([high, low, high], axis=0)
    spec = spec_ref[...] + mm(edge_ref[:, : 3 * GROUP], stacked)
    parted = spec.reshape(GROUPS, 2, GROUP, LANES)
    real, imag = parted[:, 0], parted[:, 1]
    amplitude = jnp.sqrt(real * real + imag * imag).reshape(BINS, LANES)
    high, low = split(amplitude)
    wide = mm(band_ref[...], jnp.concatenate([high, low], axis=1))
    smoothed = (wide[:, :LANES] + wide[:, LANES:]) * share_ref[...]
    level = jnp.sum(amplitude, axis=0, keepdims=True) * (1.0 / BINS)
    scale = 1.0 / (smoothed + (WATER * level + 1e-06))
    white = parted * scale.reshape(GROUPS, 1, GROUP, LANES)
    white_ref[...] = white.astype(BF16)


def moves_kernel(offs_ref, moves_ref):
    noff = offs_ref.shape[0]
    source = lax.broadcasted_iota(jnp.int32, (3 * LANES, LANES), 0)
    channel = lax.broadcasted_iota(jnp.int32, (3 * LANES, LANES), 1)
    for o in range(noff):
        hit = source == channel + (LANES + offs_ref[o])
        moves_ref[:, o * LANES : (o + 1) * LANES] = hit.astype(F32).astype(BF16)


def pack_matrix(owners):
    share = LANES // owners
    matrix = np.zeros((owners, owners, share, owners, owners, share), np.float32)
    for group in range(owners):
        for owner in range(owners):
            matrix[group, owner, :, owner, group, :] = np.eye(share)
    return matrix.reshape(owners * LANES, owners * LANES).astype(jnp.bfloat16)


def cross_kernel(
    partner_ref, count_ref, moves_ref, flip_ref, pack_ref, white_ref, out_ref, turned_ref
):
    blocks, segs, _, bins, _ = white_ref.shape
    owners = out_ref.shape[1]
    slots = partner_ref.shape[1]
    noff = moves_ref.shape[1] // LANES
    near_each = noff // owners
    rows = segs * 2 * bins
    packed_rows = 2 * bins // owners
    flats = [white_ref[b].reshape(rows, LANES) for b in range(blocks)]
    every = jnp.concatenate(flats, axis=0)
    turned_ref[...] = mm(every, flip_ref[...]).reshape(turned_ref.shape)
    before = jnp.concatenate(flats[-1:] + flats[:-1], axis=0)
    after = jnp.concatenate(flats[1:] + flats[:1], axis=0)
    moved = mm(jnp.concatenate([before, every, after], axis=1), moves_ref[...])

    def products(own, far):
        own = own.reshape(segs, 2, bins, LANES)
        far = far.reshape(segs, 2, bins, LANES)
        real = jnp.sum(own[:, 0] * far[:, 0] + own[:, 1] * far[:, 1], axis=0)
        imag = jnp.sum(own[:, 1] * far[:, 0] - own[:, 0] * far[:, 1], axis=0)
        return jnp.concatenate([real, imag], axis=0)

    near, loops = [], []
    for b in range(blocks):
        own = flats[b].astype(F32)
        far = moved[b * rows : (b + 1) * rows]
        near.append([products(own, far[:, o * LANES : (o + 1) * LANES]) for o in range(noff)])
        for k in range(slots):
            partner = jnp.clip(partner_ref[b, k], 0, blocks - 1)
            live = (k < count_ref[b]).astype(F32)
            pair = products(own, turned_ref[partner]) * live
            groups = [pair[g * packed_rows : (g + 1) * packed_rows] for g in range(owners)]
            loops.append(jnp.concatenate(groups, axis=1))
    packed = mm(jnp.concatenate(loops, axis=0).astype(BF16), pack_ref[...])
    depth = slots * packed_rows
    for b in range(blocks):
        for q in range(owners):
            tail = packed[b * depth : (b + 1) * depth, q * LANES : (q + 1) * LANES]
            mine = near[b][q * near_each : (q + 1) * near_each] + [tail]
            out_ref[b, q] = jnp.concatenate(mine, axis=0).astype(BF16)


def lag_kernel(slots, spec_ref, inv_ref, near_ref, loop_ref):
    sources = spec_ref.shape[0]
    rows = inv_ref.shape[1] // sources
    near_each = near_ref.shape[1]
    share = loop_ref.shape[0] // slots
    owners = LANES // share
    step = rows // owners
    columns = [
        spec_ref[:, t * rows : (t + 1) * rows].reshape(sources * rows, LANES)
        for t in range(near_each)
    ]
    loop = spec_ref[:, near_each * rows :].astype(F32)
    lane = lax.broadcasted_iota(jnp.int32, (sources, step, LANES), 2)
    for k in range(slots):
        tile = loop[:, k * step : (k + 1) * step]
        groups = [
            jnp.where((lane >= g * share) & (lane < (g + 1) * share), tile, 0.0)
            for g in range(owners)
        ]
        columns.append(jnp.concatenate(groups, axis=1).astype(BF16).reshape(sources * rows, LANES))
    both = mm(inv_ref[...], jnp.concatenate(columns, axis=1))
    lags = both[:LAGS] + both[LAGS:]
    for t in range(near_each):
        near_ref[:, t, :] = lags[:, t * LANES : (t + 1) * LANES].T
    for k in range(slots):
        first = (near_each + k) * LANES
        turned = lags[:, first : first + LANES].T
        loop_ref[k * share : (k + 1) * share] = sum(
            turned[g * share : (g + 1) * share] for g in range(owners)
        )


def vmem(count):
    return [pl.BlockSpec(memory_space=pltpu.VMEM)] * count


def smem(count):
    return [pl.BlockSpec(memory_space=pltpu.SMEM)] * count


def hbm(count):
    return [pl.BlockSpec(memory_space=pltpu.HBM)] * count


def in_hbm(array):
    return pltpu.with_memory_space_constraint(jnp.asarray(array), pltpu.HBM)


def finish_plain(white, offsets, loop_partner, loop_count, owners, total_segs):
    blocks, segs, _, bins, chans = white.shape
    devices = blocks * owners
    noff, slots = offsets.shape[0], loop_partner.shape[1]
    share = chans // owners
    wide = white.astype(F32)
    flat = jnp.moveaxis(wide, 0, 3).reshape(segs, 2, bins, blocks * chans)

    def products(own, far):
        real = jnp.sum(own[:, 0] * far[:, 0] + own[:, 1] * far[:, 1], axis=0)
        imag = jnp.sum(own[:, 1] * far[:, 0] - own[:, 0] * far[:, 1], axis=0)
        return jnp.stack([real, imag]).astype(BF16)

    near = [products(flat, jnp.roll(flat, -offsets[o], axis=3)) for o in range(noff)]
    near = jnp.stack(near).reshape(owners, noff // owners, 2, bins, blocks, chans)
    near = jnp.moveaxis(near, 4, 0).reshape(devices, noff // owners, 2 * bins, chans)
    loops = []
    for k in range(slots):
        far = jnp.flip(wide[loop_partner[:, k]], axis=4)
        live = (k < loop_count).astype(BF16)[:, None, None]
        pair = products(jnp.moveaxis(wide, 0, 2), jnp.moveaxis(far, 0, 2)) * live[None]
        loops.append(pair.reshape(2, blocks, bins, owners, share))
    loop = jnp.transpose(jnp.stack(loops), (2, 4, 0, 1, 3, 5))
    loop = loop.reshape(devices, slots, 2 * bins, share)
    order = np.repeat(bin_order().reshape(devices, 1, bins), 2, axis=1).reshape(-1)
    part = np.broadcast_to(np.arange(2).reshape(1, 2, 1), (devices, 2, bins)).reshape(-1)
    inverse = inverse_table(total_segs, order, part).astype(np.float32)
    inverse = inverse.reshape(LAGS, devices, 2 * bins)
    results = []
    for array in (near, loop):
        summed = lax.all_to_all(array, ("chan", "seg"), 0, 0, tiled=True).astype(F32)
        lags = jnp.einsum("dtvc,ldv->tcl", summed, inverse, precision=lax.Precision.HIGHEST)
        results.append(lags)
    return jnp.moveaxis(results[0], 0, 1), results[1][None]


def body(recording, filter_taps, offsets, loop_partner, loop_count):
    chan_count = lax.axis_size("chan")
    seg_count = lax.axis_size("seg")
    devices = chan_count * seg_count
    bins = BINS // devices
    chans, length = recording.shape
    noff, slots = offsets.shape[0], loop_partner.shape[1]
    share = chans // seg_count
    near_each = noff // seg_count
    assert length == NFFT * DECIM and chans == LANES and noff % seg_count == 0

    rims = lax.all_gather(recording[:, length - LANES :], "seg")
    taps = filter_taps.reshape(1, TAPS)
    spec, mean, head = pl.pallas_call(
        spectrum_kernel,
        out_shape=[
            jax.ShapeDtypeStruct((2 * BINS, LANES), F32),
            jax.ShapeDtypeStruct((LANES, LANES), F32),
            jax.ShapeDtypeStruct((GROUP, LANES), F32),
        ],
        in_specs=hbm(4),
        out_specs=vmem(3),
        scratch_shapes=[
            pltpu.VMEM((1, TAPS), F32),
            pltpu.VMEM((chans, length), F32),
            pltpu.VMEM((2 * FAR_BINS, 3 * DEPTH), BF16),
            pltpu.VMEM((DEPTH, LANES), F32),
            pltpu.SemaphoreType.DMA((length // STEP + 3,)),
        ],
        compiler_params=PARAMS,
        cost_estimate=pl.CostEstimate(
            flops=1_000_000_000, bytes_accessed=5_000_000, transcendentals=0
        ),
        name="filter_and_transform",
    )(in_hbm(taps), in_hbm(recording), in_hbm(short_table()), in_hbm(twiddle_table()))

    band, band_share = band_tables()
    white = pl.pallas_call(
        whiten_kernel,
        out_shape=jax.ShapeDtypeStruct((GROUPS, 2, GROUP, LANES), BF16),
        in_specs=hbm(1) + vmem(6),
        out_specs=pl.BlockSpec(memory_space=pltpu.VMEM),
        scratch_shapes=[pltpu.VMEM((chans, LANES), F32), pltpu.SemaphoreType.DMA],
        compiler_params=PARAMS,
        name="whiten",
    )(in_hbm(rims), spec, mean, head, edge_table(), band, band_share)

    white, offsets = lax.optimization_barrier((white, offsets))
    if bins != GROUP:
        white = jnp.moveaxis(white, 1, 0).reshape(2, devices, bins, LANES)
        white = jnp.moveaxis(white, 0, 1)
    moved = lax.all_to_all(white, ("chan", "seg"), 0, 0, tiled=True)
    moved = moved.reshape(chan_count, seg_count, 2, bins, LANES)
    if bins % GROUP or 2 * bins % (8 * seg_count):
        return finish_plain(moved, offsets, loop_partner, loop_count, seg_count, seg_count)

    moves = pl.pallas_call(
        moves_kernel,
        out_shape=jax.ShapeDtypeStruct((3 * LANES, noff * LANES), BF16),
        in_specs=smem(1),
        out_specs=pl.BlockSpec(memory_space=pltpu.VMEM),
        compiler_params=PARAMS,
        name="offset_moves",
    )(offsets)
    flip = np.eye(LANES, dtype=np.float32)[::-1].astype(jnp.bfloat16)
    out_rows = near_each * 2 * bins + slots * (2 * bins // seg_count)
    crossed = pl.pallas_call(
        cross_kernel,
        out_shape=jax.ShapeDtypeStruct((chan_count, seg_count, out_rows, LANES), BF16),
        in_specs=smem(2) + vmem(4),
        out_specs=pl.BlockSpec(memory_space=pltpu.VMEM),
        scratch_shapes=[pltpu.VMEM((chan_count, seg_count * 2 * bins, LANES), F32)],
        compiler_params=PARAMS,
        name="cross_spectra",
    )(loop_partner, loop_count, moves, flip, pack_matrix(seg_count), moved)
    crossed = crossed.reshape(devices, out_rows, LANES)
    summed = lax.all_to_all(crossed, ("chan", "seg"), 0, 0, tiled=True)

    order = np.repeat(bin_order().reshape(devices, 1, bins), 2, axis=1).reshape(-1)
    part = np.broadcast_to(np.arange(2).reshape(1, 2, 1), (devices, 2, bins)).reshape(-1)
    inverse = np.concatenate(split_np(inverse_table(seg_count, order, part)), axis=0)
    near, loop = pl.pallas_call(
        functools.partial(lag_kernel, slots),
        out_shape=[
            jax.ShapeDtypeStruct((chans, near_each, LAGS), F32),
            jax.ShapeDtypeStruct((slots * share, LAGS), F32),
        ],
        in_specs=vmem(2),
        out_specs=vmem(2),
        compiler_params=PARAMS,
        name="lags",
    )(summed, inverse)
    return near, loop.reshape(1, slots, share, LAGS)


def solution(mesh):
    in_specs = (P("chan", "seg"), P(), P(), P(), P())
    out_specs = (P("chan", "seg", None), P("chan", None, "seg", None))
    return jax.shard_map(body, mesh=mesh, in_specs=in_specs, out_specs=out_specs, check_vma=False)
```

```python
import functools
import math

import jax
import jax.numpy as jnp
import numpy as np
from jax import lax
from jax.experimental import pallas as pl
from jax.experimental.pallas import tpu as pltpu
from jax.sharding import PartitionSpec as P

NFFT = 1024
LAGS = 256
TAPS = 64
DECIM = 4
HALFBAND = 10
BINS = 512
WATER = 0.2

LANES = 128
GROUP = 16
GROUPS = BINS // GROUP
OUT_BLOCK = 128
STEP = OUT_BLOCK * DECIM
RADIX = 4
DEPTH = NFFT // RADIX
FAR_BINS = BINS // RADIX

F32 = jnp.float32
BF16 = jnp.bfloat16
MIB = 1024 * 1024
PARAMS = pltpu.CompilerParams(vmem_limit_bytes=32 * MIB)


def bin_order():
    return np.concatenate([np.arange(r, BINS, RADIX) for r in range(RADIX)])


def split_np(table):
    high = table.astype(jnp.bfloat16)
    low = (table - high.astype(np.float64)).astype(jnp.bfloat16)
    return high, low


def short_table():
    bins = np.arange(FAR_BINS).reshape(-1, 1, GROUP, 1)
    angles = (bins * np.arange(DEPTH) % DEPTH) * (2.0 * np.pi / DEPTH)
    rows = np.concatenate([np.cos(angles), np.sin(angles)], axis=1).reshape(-1, DEPTH)
    high, low = split_np(rows)
    return np.concatenate([high, high, low], axis=1)


def twiddle_table():
    angles = np.arange(DEPTH)[:, None] * np.arange(1, RADIX) * (2.0 * np.pi / NFFT)
    columns = np.stack([np.cos(angles), np.sin(angles)], axis=2).reshape(DEPTH, -1)
    return np.pad(columns, ((0, 0), (0, LANES - columns.shape[1]))).astype(np.float32)


def edge_table():
    bins = bin_order().reshape(GROUPS, 1, GROUP, 1)
    angles = (bins * np.arange(GROUP) % NFFT) * (2.0 * np.pi / NFFT)
    rows = np.concatenate([np.cos(angles), -np.sin(angles)], axis=1) * (bins != 0)
    high, low = split_np(rows.reshape(2 * BINS, GROUP))
    table = np.concatenate([high, high, low], axis=1)
    return np.pad(table.astype(np.float32), ((0, 0), (0, LANES - 3 * GROUP))).astype(jnp.bfloat16)


def inverse_table(total_segs, bins, part):
    lag = np.arange(LAGS) - LAGS // 2
    angles = (bins[None, :] * lag[:, None] % NFFT) * (2.0 * np.pi / NFFT)
    weights = np.where(bins == 0, 1.0, 2.0) / math.sqrt(2.0 * BINS * total_segs)
    return np.where(part[None, :] == 1, -np.sin(angles), np.cos(angles)) * weights[None, :]


def band_tables():
    bins = bin_order()
    inside = np.abs(bins[:, None] - bins[None, :]) <= HALFBAND
    share = np.broadcast_to(1.0 / inside.sum(axis=1, keepdims=True), (BINS, LANES))
    return inside.astype(jnp.bfloat16), share.astype(np.float32)


def split(value):
    high = value.astype(BF16)
    return high, (value - high.astype(F32)).astype(BF16)


def mm(a, b):
    return jnp.dot(a, b, preferred_element_type=F32)


def mm_nt(a, b):
    return lax.dot_general(a, b, (((1,), (1,)), ((), ())), preferred_element_type=F32)


def tap_rows(taps):
    width = LANES + STEP
    square = (TAPS, TAPS)
    diagonal = lax.broadcasted_iota(jnp.int32, square, 0) == lax.broadcasted_iota(jnp.int32, square, 1)
    column_taps = jnp.sum(jnp.where(diagonal, taps, 0.0), axis=1, keepdims=True)
    tap = lax.broadcasted_iota(jnp.int32, (TAPS, width), 0)
    column = lax.broadcasted_iota(jnp.int32, (TAPS, width), 1)
    placed = jnp.where(column == LANES + DECIM - 1 - tap, column_taps, 0.0)
    spread = jnp.broadcast_to(jnp.sum(placed, axis=0, keepdims=True), (OUT_BLOCK, width))
    return pltpu.roll(spread, 0, 1, stride=DECIM, stride_axis=0)


def rim_kernel(rec_hbm, rim_ref, sem):
    length = rec_hbm.shape[1]
    copy = pltpu.make_async_copy(rec_hbm.at[:, pl.ds(length - LANES, LANES)], rim_ref, sem)
    copy.start()
    copy.wait()


def spectrum_kernel(taps_ref, rec_ref, tab_ref, twist_ref, spec_ref, mean_ref, head_ref):
    blocks = rec_ref.shape[1] // STEP
    table = tap_rows(taps_ref[...])
    head_ref[...] = table[:GROUP, :LANES]
    taps_high, taps_low = split(table.T)
    taps_both = jnp.concatenate([taps_high, taps_low], axis=1)
    before = [jnp.zeros((LANES, LANES), BF16)] * 2
    outputs = []
    for first in range(0, blocks, blocks // 2):
        windows = ([], [])
        for j in range(first, first + blocks // 2):
            chunk = rec_ref[:, j * STEP : (j + 1) * STEP]
            if j == 0:
                mean = jnp.sum(chunk, axis=1, keepdims=True) * (1.0 / STEP)
            for i, value in enumerate(split(chunk - mean)):
                windows[i].append(jnp.concatenate([before[i], value], axis=1))
                before[i] = value[:, STEP - LANES :]
        wide = mm(jnp.concatenate(windows[0], axis=0), taps_both)
        rest = mm(jnp.concatenate(windows[1], axis=0), taps_high)
        total = wide[:, :LANES] + wide[:, LANES:] + rest
        outputs += [total[t * LANES : (t + 1) * LANES].T for t in range(blocks // 2)]
    pieces = [jnp.concatenate(outputs[j : j + 2], axis=0) for j in range(0, blocks, 2)]
    mean_ref[...] = jnp.broadcast_to(mean, mean_ref.shape)
    even, odd = pieces[0] + pieces[2], pieces[1] + pieces[3]
    a, b = pieces[0] - pieces[2], pieces[1] - pieces[3]
    whole, half = even + odd, even - odd
    whole = whole - jnp.sum(whole, axis=0, keepdims=True) * (1.0 / DEPTH)
    c1, s1, c2, s2, c3, s3 = [twist_ref[:, i : i + 1] for i in range(6)]
    inputs = [
        whole,
        a * c1 - b * s1,
        -(a * s1 + b * c1),
        half * c2,
        -(half * s2),
        a * c3 + b * s3,
        b * c3 - a * s3,
    ]
    parts = [split(value) for value in inputs]
    high = jnp.concatenate([p[0] for p in parts], axis=1)
    low = jnp.concatenate([p[1] for p in parts], axis=1)
    out = mm(tab_ref[...], jnp.concatenate([high, low, high], axis=0))
    out = out.reshape(FAR_BINS // GROUP, 2, GROUP, out.shape[1])
    rows = 2 * FAR_BINS
    for r in range(RADIX):
        first = max(2 * r - 1, 0) * LANES
        real_in = out[..., first : first + LANES]
        if r == 0:
            real, imag = real_in[:, 0], -real_in[:, 1]
        else:
            imag_in = out[..., first + LANES : first + 2 * LANES]
            real, imag = real_in[:, 0] + imag_in[:, 1], imag_in[:, 0] - real_in[:, 1]
        both = jnp.stack([real, imag], axis=1).reshape(rows, LANES)
        spec_ref[r * rows : (r + 1) * rows, :] = both


def whiten_kernel(
    spec_ref, rim_ref, mean_ref, head_ref, edge_ref, band_ref, share_ref, white_ref
):
    head_high, head_low = split(head_ref[...])
    rim_high, rim_low = split(rim_ref[...] - mean_ref[...])
    history = mm_nt(
        jnp.concatenate([head_high, head_high, head_low], axis=1),
        jnp.concatenate([rim_high, rim_low, rim_high], axis=1),
    )
    high, low = split(history)
    stacked = jnp.concatenate([high, low, high], axis=0)
    spec = spec_ref[...] + mm(edge_ref[:, : 3 * GROUP], stacked)
    parted = spec.reshape(GROUPS, 2, GROUP, LANES)
    real, imag = parted[:, 0], parted[:, 1]
    amplitude = jnp.sqrt(real * real + imag * imag).reshape(BINS, LANES)
    high, low = split(amplitude)
    wide = mm(band_ref[...], jnp.concatenate([high, low], axis=1))
    smoothed = (wide[:, :LANES] + wide[:, LANES:]) * share_ref[...]
    level = jnp.sum(amplitude, axis=0, keepdims=True) * (1.0 / BINS)
    scale = 1.0 / (smoothed + (WATER * level + 1e-06))
    white = parted * scale.reshape(GROUPS, 1, GROUP, LANES)
    white_ref[...] = white.astype(BF16)


def moves_kernel(offs_ref, moves_ref):
    noff = offs_ref.shape[0]
    source = lax.broadcasted_iota(jnp.int32, (3 * LANES, LANES), 0)
    channel = lax.broadcasted_iota(jnp.int32, (3 * LANES, LANES), 1)
    for o in range(noff):
        hit = source == channel + (LANES + offs_ref[o])
        moves_ref[:, o * LANES : (o + 1) * LANES] = hit.astype(F32).astype(BF16)


def pack_matrix(owners):
    share = LANES // owners
    matrix = np.zeros((owners, owners, share, owners, owners, share), np.float32)
    for group in range(owners):
        for owner in range(owners):
            matrix[group, owner, :, owner, group, :] = np.eye(share)
    return matrix.reshape(owners * LANES, owners * LANES).astype(jnp.bfloat16)


def cross_kernel(
    partner_ref, count_ref, moves_ref, flip_ref, pack_ref, white_ref, out_ref, turned_ref
):
    blocks, segs, _, bins, _ = white_ref.shape
    owners = out_ref.shape[1]
    slots = partner_ref.shape[1]
    noff = moves_ref.shape[1] // LANES
    near_each = noff // owners
    rows = segs * 2 * bins
    packed_rows = 2 * bins // owners
    flats = [white_ref[b].reshape(rows, LANES) for b in range(blocks)]
    every = jnp.concatenate(flats, axis=0)
    turned_ref[...] = mm(every, flip_ref[...]).reshape(turned_ref.shape)
    before = jnp.concatenate(flats[-1:] + flats[:-1], axis=0)
    after = jnp.concatenate(flats[1:] + flats[:1], axis=0)
    moved = mm(jnp.concatenate([before, every, after], axis=1), moves_ref[...])

    def products(own, far):
        own = own.reshape(segs, 2, bins, LANES)
        far = far.reshape(segs, 2, bins, LANES)
        real = jnp.sum(own[:, 0] * far[:, 0] + own[:, 1] * far[:, 1], axis=0)
        imag = jnp.sum(own[:, 1] * far[:, 0] - own[:, 0] * far[:, 1], axis=0)
        return jnp.concatenate([real, imag], axis=0)

    near, loops = [], []
    for b in range(blocks):
        own = flats[b].astype(F32)
        far = moved[b * rows : (b + 1) * rows]
        near.append([products(own, far[:, o * LANES : (o + 1) * LANES]) for o in range(noff)])
        for k in range(slots):
            partner = jnp.clip(partner_ref[b, k], 0, blocks - 1)
            live = (k < count_ref[b]).astype(F32)
            pair = products(own, turned_ref[partner]) * live
            groups = [pair[g * packed_rows : (g + 1) * packed_rows] for g in range(owners)]
            loops.append(jnp.concatenate(groups, axis=1))
    packed = mm(jnp.concatenate(loops, axis=0).astype(BF16), pack_ref[...])
    depth = slots * packed_rows
    for b in range(blocks):
        for q in range(owners):
            tail = packed[b * depth : (b + 1) * depth, q * LANES : (q + 1) * LANES]
            mine = near[b][q * near_each : (q + 1) * near_each] + [tail]
            out_ref[b, q] = jnp.concatenate(mine, axis=0).astype(BF16)


def lag_kernel(slots, spec_ref, inv_ref, near_ref, loop_ref):
    sources = spec_ref.shape[0]
    rows = inv_ref.shape[1] // sources
    near_each = near_ref.shape[1]
    share = loop_ref.shape[0] // slots
    owners = LANES // share
    step = rows // owners
    columns = [
        spec_ref[:, t * rows : (t + 1) * rows].reshape(sources * rows, LANES)
        for t in range(near_each)
    ]
    loop = spec_ref[:, near_each * rows :].astype(F32)
    lane = lax.broadcasted_iota(jnp.int32, (sources, step, LANES), 2)
    for k in range(slots):
        tile = loop[:, k * step : (k + 1) * step]
        groups = [
            jnp.where((lane >= g * share) & (lane < (g + 1) * share), tile, 0.0)
            for g in range(owners)
        ]
        columns.append(jnp.concatenate(groups, axis=1).astype(BF16).reshape(sources * rows, LANES))
    both = mm(inv_ref[...], jnp.concatenate(columns, axis=1))
    lags = both[:LAGS] + both[LAGS:]
    for t in range(near_each):
        near_ref[:, t, :] = lags[:, t * LANES : (t + 1) * LANES].T
    for k in range(slots):
        first = (near_each + k) * LANES
        turned = lags[:, first : first + LANES].T
        loop_ref[k * share : (k + 1) * share] = sum(
            turned[g * share : (g + 1) * share] for g in range(owners)
        )


def vmem(count):
    return [pl.BlockSpec(memory_space=pltpu.VMEM)] * count


def smem(count):
    return [pl.BlockSpec(memory_space=pltpu.SMEM)] * count


def hbm(count):
    return [pl.BlockSpec(memory_space=pltpu.HBM)] * count


def in_hbm(array):
    return pltpu.with_memory_space_constraint(jnp.asarray(array), pltpu.HBM)


def finish_plain(white, offsets, loop_partner, loop_count, owners, total_segs):
    blocks, segs, _, bins, chans = white.shape
    devices = blocks * owners
    noff, slots = offsets.shape[0], loop_partner.shape[1]
    share = chans // owners
    wide = white.astype(F32)
    flat = jnp.moveaxis(wide, 0, 3).reshape(segs, 2, bins, blocks * chans)

    def products(own, far):
        real = jnp.sum(own[:, 0] * far[:, 0] + own[:, 1] * far[:, 1], axis=0)
        imag = jnp.sum(own[:, 1] * far[:, 0] - own[:, 0] * far[:, 1], axis=0)
        return jnp.stack([real, imag]).astype(BF16)

    near = [products(flat, jnp.roll(flat, -offsets[o], axis=3)) for o in range(noff)]
    near = jnp.stack(near).reshape(owners, noff // owners, 2, bins, blocks, chans)
    near = jnp.moveaxis(near, 4, 0).reshape(devices, noff // owners, 2 * bins, chans)
    loops = []
    for k in range(slots):
        far = jnp.flip(wide[loop_partner[:, k]], axis=4)
        live = (k < loop_count).astype(BF16)[:, None, None]
        pair = products(jnp.moveaxis(wide, 0, 2), jnp.moveaxis(far, 0, 2)) * live[None]
        loops.append(pair.reshape(2, blocks, bins, owners, share))
    loop = jnp.transpose(jnp.stack(loops), (2, 4, 0, 1, 3, 5))
    loop = loop.reshape(devices, slots, 2 * bins, share)
    order = np.repeat(bin_order().reshape(devices, 1, bins), 2, axis=1).reshape(-1)
    part = np.broadcast_to(np.arange(2).reshape(1, 2, 1), (devices, 2, bins)).reshape(-1)
    inverse = inverse_table(total_segs, order, part).astype(np.float32)
    inverse = inverse.reshape(LAGS, devices, 2 * bins)
    results = []
    for array in (near, loop):
        summed = lax.all_to_all(array, ("chan", "seg"), 0, 0, tiled=True).astype(F32)
        lags = jnp.einsum("dtvc,ldv->tcl", summed, inverse, precision=lax.Precision.HIGHEST)
        results.append(lags)
    return jnp.moveaxis(results[0], 0, 1), results[1][None]


def body(recording, filter_taps, offsets, loop_partner, loop_count):
    chan_count = lax.axis_size("chan")
    seg_count = lax.axis_size("seg")
    devices = chan_count * seg_count
    bins = BINS // devices
    chans, length = recording.shape
    noff, slots = offsets.shape[0], loop_partner.shape[1]
    share = chans // seg_count
    near_each = noff // seg_count
    assert length == NFFT * DECIM and chans == LANES and noff % seg_count == 0

    route = [(i, i + 1) for i in range(seg_count - 1)]
    rim = pl.pallas_call(
        rim_kernel,
        out_shape=jax.ShapeDtypeStruct((chans, LANES), F32),
        in_specs=hbm(1),
        out_specs=pl.BlockSpec(memory_space=pltpu.VMEM),
        scratch_shapes=[pltpu.SemaphoreType.DMA],
        compiler_params=PARAMS,
        cost_estimate=pl.CostEstimate(
            flops=10_000_000_000, bytes_accessed=20_000_000, transcendentals=0
        ),
        name="history",
    )(in_hbm(recording))
    rim = lax.ppermute(rim, "seg", route)
    taps = filter_taps.reshape(1, TAPS)
    spec, mean, head = pl.pallas_call(
        spectrum_kernel,
        out_shape=[
            jax.ShapeDtypeStruct((2 * BINS, LANES), F32),
            jax.ShapeDtypeStruct((LANES, LANES), F32),
            jax.ShapeDtypeStruct((GROUP, LANES), F32),
        ],
        in_specs=vmem(4),
        out_specs=vmem(3),
        compiler_params=PARAMS,
        cost_estimate=pl.CostEstimate(
            flops=1_000_000_000, bytes_accessed=5_000_000, transcendentals=0
        ),
        name="filter_and_transform",
    )(taps, recording, short_table(), twiddle_table())

    band, band_share = band_tables()
    white = pl.pallas_call(
        whiten_kernel,
        out_shape=jax.ShapeDtypeStruct((GROUPS, 2, GROUP, LANES), BF16),
        in_specs=vmem(7),
        out_specs=pl.BlockSpec(memory_space=pltpu.VMEM),
        compiler_params=PARAMS,
        name="whiten",
    )(spec, rim, mean, head, edge_table(), band, band_share)

    white, offsets = lax.optimization_barrier((white, offsets))
    if bins != GROUP:
        white = jnp.moveaxis(white, 1, 0).reshape(2, devices, bins, LANES)
        white = jnp.moveaxis(white, 0, 1)
    moved = lax.all_to_all(white, ("chan", "seg"), 0, 0, tiled=True)
    moved = moved.reshape(chan_count, seg_count, 2, bins, LANES)
    if bins % GROUP or 2 * bins % (8 * seg_count):
        return finish_plain(moved, offsets, loop_partner, loop_count, seg_count, seg_count)

    moves = pl.pallas_call(
        moves_kernel,
        out_shape=jax.ShapeDtypeStruct((3 * LANES, noff * LANES), BF16),
        in_specs=smem(1),
        out_specs=pl.BlockSpec(memory_space=pltpu.VMEM),
        compiler_params=PARAMS,
        name="offset_moves",
    )(offsets)
    flip = np.eye(LANES, dtype=np.float32)[::-1].astype(jnp.bfloat16)
    out_rows = near_each * 2 * bins + slots * (2 * bins // seg_count)
    crossed = pl.pallas_call(
        cross_kernel,
        out_shape=jax.ShapeDtypeStruct((chan_count, seg_count, out_rows, LANES), BF16),
        in_specs=smem(2) + vmem(4),
        out_specs=pl.BlockSpec(memory_space=pltpu.VMEM),
        scratch_shapes=[pltpu.VMEM((chan_count, seg_count * 2 * bins, LANES), F32)],
        compiler_params=PARAMS,
        name="cross_spectra",
    )(loop_partner, loop_count, moves, flip, pack_matrix(seg_count), moved)
    crossed = crossed.reshape(devices, out_rows, LANES)
    summed = lax.all_to_all(crossed, ("chan", "seg"), 0, 0, tiled=True)

    order = np.repeat(bin_order().reshape(devices, 1, bins), 2, axis=1).reshape(-1)
    part = np.broadcast_to(np.arange(2).reshape(1, 2, 1), (devices, 2, bins)).reshape(-1)
    inverse = np.concatenate(split_np(inverse_table(seg_count, order, part)), axis=0)
    near, loop = pl.pallas_call(
        functools.partial(lag_kernel, slots),
        out_shape=[
            jax.ShapeDtypeStruct((chans, near_each, LAGS), F32),
            jax.ShapeDtypeStruct((slots * share, LAGS), F32),
        ],
        in_specs=vmem(2),
        out_specs=vmem(2),
        compiler_params=PARAMS,
        name="lags",
    )(summed, inverse)
    return near, loop.reshape(1, slots, share, LAGS)


def solution(mesh):
    in_specs = (P("chan", "seg"), P(), P(), P(), P())
    out_specs = (P("chan", "seg", None), P("chan", None, "seg", None))
    return jax.shard_map(body, mesh=mesh, in_specs=in_specs, out_specs=out_specs, check_vma=False)
```

```python
import functools
import math

import jax
import jax.numpy as jnp
import numpy as np
from jax import lax
from jax.experimental import pallas as pl
from jax.experimental.pallas import tpu as pltpu
from jax.sharding import PartitionSpec as P

NFFT = 1024
LAGS = 256
TAPS = 64
DECIM = 4
HALFBAND = 10
SPAN = 64
BINS = 512
WATER = 0.2

LANES = 128
GROUP = 16
GROUPS = BINS // GROUP
OUT_BLOCK = 128
STEP = OUT_BLOCK * DECIM
RADIX = 4
DEPTH = NFFT // RADIX
FAR_BINS = BINS // RADIX

F32 = jnp.float32
BF16 = jnp.bfloat16
MIB = 1024 * 1024
PARAMS = pltpu.CompilerParams(vmem_limit_bytes=32 * MIB)


def bin_order():
    return np.concatenate([np.arange(r, BINS, RADIX) for r in range(RADIX)])


def split_np(table):
    high = table.astype(jnp.bfloat16)
    low = (table - high.astype(np.float64)).astype(jnp.bfloat16)
    return high, low


def short_table():
    bins = np.arange(FAR_BINS).reshape(-1, 1, GROUP, 1)
    angles = (bins * np.arange(DEPTH) % DEPTH) * (2.0 * np.pi / DEPTH)
    rows = np.concatenate([np.cos(angles), np.sin(angles)], axis=1).reshape(-1, DEPTH)
    high, low = split_np(rows)
    return np.concatenate([high, high, low], axis=1)


def twiddle_table():
    angles = np.arange(DEPTH)[:, None] * np.arange(1, RADIX) * (2.0 * np.pi / NFFT)
    columns = np.stack([np.cos(angles), np.sin(angles)], axis=2).reshape(DEPTH, -1)
    return np.pad(columns, ((0, 0), (0, LANES - columns.shape[1]))).astype(np.float32)


def edge_table():
    bins = bin_order().reshape(GROUPS, 1, GROUP, 1)
    angles = (bins * np.arange(GROUP) % NFFT) * (2.0 * np.pi / NFFT)
    rows = np.concatenate([np.cos(angles), -np.sin(angles)], axis=1) * (bins != 0)
    high, low = split_np(rows.reshape(2 * BINS, GROUP))
    table = np.concatenate([high, high, low], axis=1)
    return np.pad(table.astype(np.float32), ((0, 0), (0, LANES - 3 * GROUP))).astype(jnp.bfloat16)


def inverse_table(total_segs, bins, part):
    lag = np.arange(LAGS) - LAGS // 2
    angles = (bins[None, :] * lag[:, None] % NFFT) * (2.0 * np.pi / NFFT)
    weights = np.where(bins == 0, 1.0, 2.0) / math.sqrt(2.0 * BINS * total_segs)
    return np.where(part[None, :] == 1, -np.sin(angles), np.cos(angles)) * weights[None, :]


def band_tables():
    bins = bin_order()
    inside = np.abs(bins[:, None] - bins[None, :]) <= HALFBAND
    share = np.broadcast_to(1.0 / inside.sum(axis=1, keepdims=True), (BINS, LANES))
    return inside.astype(jnp.bfloat16), share.astype(np.float32)


def split(value):
    high = value.astype(BF16)
    return high, (value - high.astype(F32)).astype(BF16)


def mm(a, b):
    return jnp.dot(a, b, preferred_element_type=F32)


def mm_nt(a, b):
    return lax.dot_general(a, b, (((1,), (1,)), ((), ())), preferred_element_type=F32)


def tap_rows(taps):
    width = LANES + STEP
    square = (TAPS, TAPS)
    diagonal = lax.broadcasted_iota(jnp.int32, square, 0) == lax.broadcasted_iota(jnp.int32, square, 1)
    column_taps = jnp.sum(jnp.where(diagonal, taps, 0.0), axis=1, keepdims=True)
    tap = lax.broadcasted_iota(jnp.int32, (TAPS, width), 0)
    column = lax.broadcasted_iota(jnp.int32, (TAPS, width), 1)
    placed = jnp.where(column == LANES + DECIM - 1 - tap, column_taps, 0.0)
    spread = jnp.broadcast_to(jnp.sum(placed, axis=0, keepdims=True), (OUT_BLOCK, width))
    return pltpu.roll(spread, 0, 1, stride=DECIM, stride_axis=0)


def rim_kernel(rec_hbm, rim_ref, tail_ref, sem):
    length = rec_hbm.shape[1]
    copy = pltpu.make_async_copy(rec_hbm.at[:, pl.ds(length - LANES, LANES)], tail_ref, sem)
    copy.start()
    copy.wait()
    upper, lower = tail_ref[: LANES // 2], tail_ref[LANES // 2 :]
    lane = lax.broadcasted_iota(jnp.int32, lower.shape, 1)
    rim_ref[...] = jnp.where(lane < TAPS, pltpu.roll(upper, LANES - TAPS, 1), lower)


def spectrum_kernel(taps_ref, rec_ref, tab_ref, twist_ref, spec_ref, mean_ref, head_ref):
    blocks = rec_ref.shape[1] // STEP
    table = tap_rows(taps_ref[...])
    head_ref[...] = table[:GROUP, :LANES]
    taps_high, taps_low = split(table.T)
    taps_both = jnp.concatenate([taps_high, taps_low], axis=1)
    before = [jnp.zeros((LANES, LANES), BF16)] * 2
    outputs = []
    for first in range(0, blocks, blocks // 2):
        windows = ([], [])
        for j in range(first, first + blocks // 2):
            chunk = rec_ref[:, j * STEP : (j + 1) * STEP]
            if j == 0:
                mean = jnp.sum(chunk, axis=1, keepdims=True) * (1.0 / STEP)
            for i, value in enumerate(split(chunk - mean)):
                windows[i].append(jnp.concatenate([before[i], value], axis=1))
                before[i] = value[:, STEP - LANES :]
        wide = mm(jnp.concatenate(windows[0], axis=0), taps_both)
        rest = mm(jnp.concatenate(windows[1], axis=0), taps_high)
        total = wide[:, :LANES] + wide[:, LANES:] + rest
        outputs += [total[t * LANES : (t + 1) * LANES].T for t in range(blocks // 2)]
    pieces = [jnp.concatenate(outputs[j : j + 2], axis=0) for j in range(0, blocks, 2)]
    mean_ref[...] = jnp.broadcast_to(mean, mean_ref.shape)
    even, odd = pieces[0] + pieces[2], pieces[1] + pieces[3]
    a, b = pieces[0] - pieces[2], pieces[1] - pieces[3]
    whole, half = even + odd, even - odd
    whole = whole - jnp.sum(whole, axis=0, keepdims=True) * (1.0 / DEPTH)
    c1, s1, c2, s2, c3, s3 = [twist_ref[:, i : i + 1] for i in range(6)]
    inputs = [
        whole,
        a * c1 - b * s1,
        -(a * s1 + b * c1),
        half * c2,
        -(half * s2),
        a * c3 + b * s3,
        b * c3 - a * s3,
    ]
    parts = [split(value) for value in inputs]
    high = jnp.concatenate([p[0] for p in parts], axis=1)
    low = jnp.concatenate([p[1] for p in parts], axis=1)
    out = mm(tab_ref[...], jnp.concatenate([high, low, high], axis=0))
    out = out.reshape(FAR_BINS // GROUP, 2, GROUP, out.shape[1])
    rows = 2 * FAR_BINS
    for r in range(RADIX):
        first = max(2 * r - 1, 0) * LANES
        real_in = out[..., first : first + LANES]
        if r == 0:
            real, imag = real_in[:, 0], -real_in[:, 1]
        else:
            imag_in = out[..., first + LANES : first + 2 * LANES]
            real, imag = real_in[:, 0] + imag_in[:, 1], imag_in[:, 0] - real_in[:, 1]
        both = jnp.stack([real, imag], axis=1).reshape(rows, LANES)
        spec_ref[r * rows : (r + 1) * rows, :] = both


def whiten_kernel(
    spec_ref, rim_ref, mean_ref, head_ref, edge_ref, band_ref, share_ref, white_ref
):
    head_high, head_low = split(head_ref[...])
    rim = jnp.concatenate([pltpu.roll(rim_ref[...], LANES - TAPS, 1), rim_ref[...]], axis=0)
    rim_high, rim_low = split(rim - mean_ref[...])
    history = mm_nt(
        jnp.concatenate([head_high, head_high, head_low], axis=1),
        jnp.concatenate([rim_high, rim_low, rim_high], axis=1),
    )
    high, low = split(history)
    stacked = jnp.concatenate([high, low, high], axis=0)
    spec = spec_ref[...] + mm(edge_ref[:, : 3 * GROUP], stacked)
    parted = spec.reshape(GROUPS, 2, GROUP, LANES)
    real, imag = parted[:, 0], parted[:, 1]
    amplitude = jnp.sqrt(real * real + imag * imag).reshape(BINS, LANES)
    high, low = split(amplitude)
    wide = mm(band_ref[...], jnp.concatenate([high, low], axis=1))
    smoothed = (wide[:, :LANES] + wide[:, LANES:]) * share_ref[...]
    level = jnp.sum(amplitude, axis=0, keepdims=True) * (1.0 / BINS)
    scale = 1.0 / (smoothed + (WATER * level + 1e-06))
    white = parted * scale.reshape(GROUPS, 1, GROUP, LANES)
    white_ref[...] = white.astype(BF16)


def moves_kernel(offs_ref, moves_ref):
    noff = offs_ref.shape[0]
    row = lax.broadcasted_iota(jnp.int32, (2 * LANES, LANES), 0)
    channel = lax.broadcasted_iota(jnp.int32, (2 * LANES, LANES), 1)
    source = jnp.where(row < LANES + SPAN, row, row - 2 * LANES)
    for o in range(noff):
        hit = source == channel + offs_ref[o]
        moves_ref[:, o * LANES : (o + 1) * LANES] = hit.astype(F32).astype(BF16)


def pack_matrix(owners):
    share = LANES // owners
    matrix = np.zeros((owners, owners, share, owners, owners, share), np.float32)
    for group in range(owners):
        for owner in range(owners):
            matrix[group, owner, :, owner, group, :] = np.eye(share)
    return matrix.reshape(owners * LANES, owners * LANES).astype(jnp.bfloat16)


def cross_kernel(
    partner_ref, count_ref, moves_ref, flip_ref, pack_ref, white_ref, out_ref, turned_ref
):
    blocks, segs, _, bins, _ = white_ref.shape
    owners = out_ref.shape[1]
    slots = partner_ref.shape[1]
    noff = moves_ref.shape[1] // LANES
    near_each = noff // owners
    rows = segs * 2 * bins
    packed_rows = 2 * bins // owners
    flats = [white_ref[b].reshape(rows, LANES) for b in range(blocks)]
    every = jnp.concatenate(flats, axis=0)
    turned_ref[...] = mm(every, flip_ref[...]).reshape(turned_ref.shape)
    before = jnp.concatenate(flats[-1:] + flats[:-1], axis=0)
    after = jnp.concatenate(flats[1:] + flats[:1], axis=0)
    lane = lax.broadcasted_iota(jnp.int32, every.shape, 1)
    edge = jnp.where(lane < SPAN, after.astype(F32), before.astype(F32)).astype(BF16)
    moved = mm(jnp.concatenate([every, edge], axis=1), moves_ref[...])

    def products(own, far):
        own = own.reshape(segs, 2, bins, LANES)
        far = far.reshape(segs, 2, bins, LANES)
        real = jnp.sum(own[:, 0] * far[:, 0] + own[:, 1] * far[:, 1], axis=0)
        imag = jnp.sum(own[:, 1] * far[:, 0] - own[:, 0] * far[:, 1], axis=0)
        return jnp.concatenate([real, imag], axis=0)

    near, loops = [], []
    for b in range(blocks):
        own = flats[b].astype(F32)
        far = moved[b * rows : (b + 1) * rows]
        near.append([products(own, far[:, o * LANES : (o + 1) * LANES]) for o in range(noff)])
        for k in range(slots):
            partner = jnp.clip(partner_ref[b, k], 0, blocks - 1)
            live = (k < count_ref[b]).astype(F32)
            pair = products(own, turned_ref[partner]) * live
            groups = [pair[g * packed_rows : (g + 1) * packed_rows] for g in range(owners)]
            loops.append(jnp.concatenate(groups, axis=1))
    packed = mm(jnp.concatenate(loops, axis=0).astype(BF16), pack_ref[...])
    depth = slots * packed_rows
    for b in range(blocks):
        for q in range(owners):
            tail = packed[b * depth : (b + 1) * depth, q * LANES : (q + 1) * LANES]
            mine = near[b][q * near_each : (q + 1) * near_each] + [tail]
            out_ref[b, q] = jnp.concatenate(mine, axis=0).astype(BF16)


def lag_kernel(slots, spec_ref, inv_ref, near_ref, loop_ref):
    sources = spec_ref.shape[0]
    rows = inv_ref.shape[1] // sources
    near_each = near_ref.shape[1]
    share = loop_ref.shape[0] // slots
    owners = LANES // share
    step = rows // owners
    columns = [
        spec_ref[:, t * rows : (t + 1) * rows].reshape(sources * rows, LANES)
        for t in range(near_each)
    ]
    loop = spec_ref[:, near_each * rows :].astype(F32)
    lane = lax.broadcasted_iota(jnp.int32, (sources, step, LANES), 2)
    for k in range(slots):
        tile = loop[:, k * step : (k + 1) * step]
        groups = [
            jnp.where((lane >= g * share) & (lane < (g + 1) * share), tile, 0.0)
            for g in range(owners)
        ]
        columns.append(jnp.concatenate(groups, axis=1).astype(BF16).reshape(sources * rows, LANES))
    both = mm(inv_ref[...], jnp.concatenate(columns, axis=1))
    lags = both[:LAGS] + both[LAGS:]
    for t in range(near_each):
        near_ref[:, t, :] = lags[:, t * LANES : (t + 1) * LANES].T
    for k in range(slots):
        first = (near_each + k) * LANES
        turned = lags[:, first : first + LANES].T
        loop_ref[k * share : (k + 1) * share] = sum(
            turned[g * share : (g + 1) * share] for g in range(owners)
        )


def vmem(count):
    return [pl.BlockSpec(memory_space=pltpu.VMEM)] * count


def smem(count):
    return [pl.BlockSpec(memory_space=pltpu.SMEM)] * count


def hbm(count):
    return [pl.BlockSpec(memory_space=pltpu.HBM)] * count


def in_hbm(array):
    return pltpu.with_memory_space_constraint(jnp.asarray(array), pltpu.HBM)


def finish_plain(white, offsets, loop_partner, loop_count, owners, total_segs):
    blocks, segs, _, bins, chans = white.shape
    devices = blocks * owners
    noff, slots = offsets.shape[0], loop_partner.shape[1]
    share = chans // owners
    wide = white.astype(F32)
    flat = jnp.moveaxis(wide, 0, 3).reshape(segs, 2, bins, blocks * chans)

    def products(own, far):
        real = jnp.sum(own[:, 0] * far[:, 0] + own[:, 1] * far[:, 1], axis=0)
        imag = jnp.sum(own[:, 1] * far[:, 0] - own[:, 0] * far[:, 1], axis=0)
        return jnp.stack([real, imag]).astype(BF16)

    near = [products(flat, jnp.roll(flat, -offsets[o], axis=3)) for o in range(noff)]
    near = jnp.stack(near).reshape(owners, noff // owners, 2, bins, blocks, chans)
    near = jnp.moveaxis(near, 4, 0).reshape(devices, noff // owners, 2 * bins, chans)
    loops = []
    for k in range(slots):
        far = jnp.flip(wide[loop_partner[:, k]], axis=4)
        live = (k < loop_count).astype(BF16)[:, None, None]
        pair = products(jnp.moveaxis(wide, 0, 2), jnp.moveaxis(far, 0, 2)) * live[None]
        loops.append(pair.reshape(2, blocks, bins, owners, share))
    loop = jnp.transpose(jnp.stack(loops), (2, 4, 0, 1, 3, 5))
    loop = loop.reshape(devices, slots, 2 * bins, share)
    order = np.repeat(bin_order().reshape(devices, 1, bins), 2, axis=1).reshape(-1)
    part = np.broadcast_to(np.arange(2).reshape(1, 2, 1), (devices, 2, bins)).reshape(-1)
    inverse = inverse_table(total_segs, order, part).astype(np.float32)
    inverse = inverse.reshape(LAGS, devices, 2 * bins)
    results = []
    for array in (near, loop):
        summed = lax.all_to_all(array, ("chan", "seg"), 0, 0, tiled=True).astype(F32)
        lags = jnp.einsum("dtvc,ldv->tcl", summed, inverse, precision=lax.Precision.HIGHEST)
        results.append(lags)
    return jnp.moveaxis(results[0], 0, 1), results[1][None]


def body(recording, filter_taps, offsets, loop_partner, loop_count):
    chan_count = lax.axis_size("chan")
    seg_count = lax.axis_size("seg")
    devices = chan_count * seg_count
    bins = BINS // devices
    chans, length = recording.shape
    noff, slots = offsets.shape[0], loop_partner.shape[1]
    share = chans // seg_count
    near_each = noff // seg_count
    assert length == NFFT * DECIM and chans == LANES and noff % seg_count == 0

    route = [(i, i + 1) for i in range(seg_count - 1)]
    rim = pl.pallas_call(
        rim_kernel,
        out_shape=jax.ShapeDtypeStruct((chans // 2, LANES), F32),
        in_specs=hbm(1),
        out_specs=pl.BlockSpec(memory_space=pltpu.VMEM),
        scratch_shapes=[pltpu.VMEM((chans, LANES), F32), pltpu.SemaphoreType.DMA],
        compiler_params=PARAMS,
        cost_estimate=pl.CostEstimate(
            flops=10_000_000_000, bytes_accessed=20_000_000, transcendentals=0
        ),
        name="history",
    )(in_hbm(recording))
    rim = lax.ppermute(rim, "seg", route)
    taps = filter_taps.reshape(1, TAPS)
    spec, mean, head = pl.pallas_call(
        spectrum_kernel,
        out_shape=[
            jax.ShapeDtypeStruct((2 * BINS, LANES), F32),
            jax.ShapeDtypeStruct((LANES, LANES), F32),
            jax.ShapeDtypeStruct((GROUP, LANES), F32),
        ],
        in_specs=vmem(4),
        out_specs=vmem(3),
        compiler_params=PARAMS,
        cost_estimate=pl.CostEstimate(
            flops=1_000_000_000, bytes_accessed=5_000_000, transcendentals=0
        ),
        name="filter_and_transform",
    )(taps, recording, short_table(), twiddle_table())

    band, band_share = band_tables()
    white = pl.pallas_call(
        whiten_kernel,
        out_shape=jax.ShapeDtypeStruct((GROUPS, 2, GROUP, LANES), BF16),
        in_specs=vmem(7),
        out_specs=pl.BlockSpec(memory_space=pltpu.VMEM),
        compiler_params=PARAMS,
        name="whiten",
    )(spec, rim, mean, head, edge_table(), band, band_share)

    white, offsets = lax.optimization_barrier((white, offsets))
    if bins != GROUP:
        white = jnp.moveaxis(white, 1, 0).reshape(2, devices, bins, LANES)
        white = jnp.moveaxis(white, 0, 1)
    moved = lax.all_to_all(white, ("chan", "seg"), 0, 0, tiled=True)
    moved = moved.reshape(chan_count, seg_count, 2, bins, LANES)
    if bins % GROUP or 2 * bins % (8 * seg_count):
        return finish_plain(moved, offsets, loop_partner, loop_count, seg_count, seg_count)

    moves = pl.pallas_call(
        moves_kernel,
        out_shape=jax.ShapeDtypeStruct((2 * LANES, noff * LANES), BF16),
        in_specs=smem(1),
        out_specs=pl.BlockSpec(memory_space=pltpu.VMEM),
        compiler_params=PARAMS,
        name="offset_moves",
    )(offsets)
    flip = np.eye(LANES, dtype=np.float32)[::-1].astype(jnp.bfloat16)
    out_rows = near_each * 2 * bins + slots * (2 * bins // seg_count)
    crossed = pl.pallas_call(
        cross_kernel,
        out_shape=jax.ShapeDtypeStruct((chan_count, seg_count, out_rows, LANES), BF16),
        in_specs=smem(2) + vmem(4),
        out_specs=pl.BlockSpec(memory_space=pltpu.VMEM),
        scratch_shapes=[pltpu.VMEM((chan_count, seg_count * 2 * bins, LANES), F32)],
        compiler_params=PARAMS,
        name="cross_spectra",
    )(loop_partner, loop_count, moves, flip, pack_matrix(seg_count), moved)
    crossed = crossed.reshape(devices, out_rows, LANES)
    summed = lax.all_to_all(crossed, ("chan", "seg"), 0, 0, tiled=True)

    order = np.repeat(bin_order().reshape(devices, 1, bins), 2, axis=1).reshape(-1)
    part = np.broadcast_to(np.arange(2).reshape(1, 2, 1), (devices, 2, bins)).reshape(-1)
    inverse = np.concatenate(split_np(inverse_table(seg_count, order, part)), axis=0)
    near, loop = pl.pallas_call(
        functools.partial(lag_kernel, slots),
        out_shape=[
            jax.ShapeDtypeStruct((chans, near_each, LAGS), F32),
            jax.ShapeDtypeStruct((slots * share, LAGS), F32),
        ],
        in_specs=vmem(2),
        out_specs=vmem(2),
        compiler_params=PARAMS,
        name="lags",
    )(summed, inverse)
    return near, loop.reshape(1, slots, share, LAGS)


def solution(mesh):
    in_specs = (P("chan", "seg"), P(), P(), P(), P())
    out_specs = (P("chan", "seg", None), P("chan", None, "seg", None))
    return jax.shard_map(body, mesh=mesh, in_specs=in_specs, out_specs=out_specs, check_vma=False)
```

```python
import functools
import math

import jax
import jax.numpy as jnp
import numpy as np
from jax import lax
from jax.experimental import pallas as pl
from jax.experimental.pallas import tpu as pltpu
from jax.sharding import PartitionSpec as P

NFFT = 1024
LAGS = 256
TAPS = 64
DECIM = 4
HALFBAND = 10
SPAN = 64
BINS = 512
WATER = 0.2

LANES = 128
GROUP = 16
GROUPS = BINS // GROUP
OUT_BLOCK = 128
STEP = OUT_BLOCK * DECIM
RADIX = 4
DEPTH = NFFT // RADIX
FAR_BINS = BINS // RADIX

F32 = jnp.float32
BF16 = jnp.bfloat16
MIB = 1024 * 1024
PARAMS = pltpu.CompilerParams(vmem_limit_bytes=32 * MIB)


def bin_order():
    return np.concatenate([np.arange(r, BINS, RADIX) for r in range(RADIX)])


def split_np(table):
    high = table.astype(jnp.bfloat16)
    low = (table - high.astype(np.float64)).astype(jnp.bfloat16)
    return high, low


def short_table():
    bins = np.arange(FAR_BINS).reshape(-1, 1, GROUP, 1)
    angles = (bins * np.arange(DEPTH) % DEPTH) * (2.0 * np.pi / DEPTH)
    rows = np.concatenate([np.cos(angles), np.sin(angles)], axis=1).reshape(-1, DEPTH)
    high, low = split_np(rows)
    return np.concatenate([high, high, low], axis=1)


def twiddle_table():
    angles = np.arange(DEPTH)[:, None] * np.arange(1, RADIX) * (2.0 * np.pi / NFFT)
    columns = np.stack([np.cos(angles), np.sin(angles)], axis=2).reshape(DEPTH, -1)
    return np.pad(columns, ((0, 0), (0, LANES - columns.shape[1]))).astype(np.float32)


def edge_table():
    bins = bin_order().reshape(GROUPS, 1, GROUP, 1)
    angles = (bins * np.arange(GROUP) % NFFT) * (2.0 * np.pi / NFFT)
    rows = np.concatenate([np.cos(angles), -np.sin(angles)], axis=1) * (bins != 0)
    high, low = split_np(rows.reshape(2 * BINS, GROUP))
    table = np.concatenate([high, high, low], axis=1)
    return np.pad(table.astype(np.float32), ((0, 0), (0, LANES - 3 * GROUP))).astype(jnp.bfloat16)


def inverse_table(total_segs, bins, part):
    lag = np.arange(LAGS) - LAGS // 2
    angles = (bins[None, :] * lag[:, None] % NFFT) * (2.0 * np.pi / NFFT)
    weights = np.where(bins == 0, 1.0, 2.0) / math.sqrt(2.0 * BINS * total_segs)
    return np.where(part[None, :] == 1, -np.sin(angles), np.cos(angles)) * weights[None, :]


def band_tables():
    bins = bin_order()
    inside = np.abs(bins[:, None] - bins[None, :]) <= HALFBAND
    share = np.broadcast_to(1.0 / inside.sum(axis=1, keepdims=True), (BINS, LANES))
    return inside.astype(jnp.bfloat16), share.astype(np.float32)


def split(value):
    high = value.astype(BF16)
    return high, (value - high.astype(F32)).astype(BF16)


def mm(a, b):
    return jnp.dot(a, b, preferred_element_type=F32)


def mm_nt(a, b):
    return lax.dot_general(a, b, (((1,), (1,)), ((), ())), preferred_element_type=F32)


def tap_rows(taps):
    width = LANES + STEP
    square = (TAPS, TAPS)
    diagonal = lax.broadcasted_iota(jnp.int32, square, 0) == lax.broadcasted_iota(jnp.int32, square, 1)
    column_taps = jnp.sum(jnp.where(diagonal, taps, 0.0), axis=1, keepdims=True)
    tap = lax.broadcasted_iota(jnp.int32, (TAPS, width), 0)
    column = lax.broadcasted_iota(jnp.int32, (TAPS, width), 1)
    placed = jnp.where(column == LANES + DECIM - 1 - tap, column_taps, 0.0)
    spread = jnp.broadcast_to(jnp.sum(placed, axis=0, keepdims=True), (OUT_BLOCK, width))
    return pltpu.roll(spread, 0, 1, stride=DECIM, stride_axis=0)


def rim_kernel(rec_hbm, rim_ref, tail_ref, sem):
    length = rec_hbm.shape[1]
    copy = pltpu.make_async_copy(rec_hbm.at[:, pl.ds(length - LANES, LANES)], tail_ref, sem)
    copy.start()
    copy.wait()
    upper, lower = tail_ref[: LANES // 2], tail_ref[LANES // 2 :]
    lane = lax.broadcasted_iota(jnp.int32, lower.shape, 1)
    rim_ref[...] = jnp.where(lane < TAPS, pltpu.roll(upper, LANES - TAPS, 1), lower)


def spectrum_kernel(taps_ref, rec_ref, tab_ref, twist_ref, spec_ref, mean_ref, head_ref):
    blocks = rec_ref.shape[1] // STEP
    table = tap_rows(taps_ref[...])
    head_ref[...] = table[:GROUP, :LANES]
    taps_high, taps_low = split(table.T)
    taps_both = jnp.concatenate([taps_high, taps_low], axis=1)
    before = [jnp.zeros((LANES, LANES), BF16)] * 2
    outputs = []
    for first in range(0, blocks, blocks // 2):
        windows = ([], [])
        for j in range(first, first + blocks // 2):
            chunk = rec_ref[:, j * STEP : (j + 1) * STEP]
            if j == 0:
                mean = jnp.sum(chunk, axis=1, keepdims=True) * (1.0 / STEP)
            for i, value in enumerate(split(chunk - mean)):
                windows[i].append(jnp.concatenate([before[i], value], axis=1))
                before[i] = value[:, STEP - LANES :]
        wide = mm(jnp.concatenate(windows[0], axis=0), taps_both)
        rest = mm(jnp.concatenate(windows[1], axis=0), taps_high)
        total = wide[:, :LANES] + wide[:, LANES:] + rest
        outputs += [total[t * LANES : (t + 1) * LANES].T for t in range(blocks // 2)]
    pieces = [jnp.concatenate(outputs[j : j + 2], axis=0) for j in range(0, blocks, 2)]
    mean_ref[...] = jnp.broadcast_to(mean, mean_ref.shape)
    even, odd = pieces[0] + pieces[2], pieces[1] + pieces[3]
    a, b = pieces[0] - pieces[2], pieces[1] - pieces[3]
    whole, half = even + odd, even - odd
    whole = whole - jnp.sum(whole, axis=0, keepdims=True) * (1.0 / DEPTH)
    c1, s1, c2, s2, c3, s3 = [twist_ref[:, i : i + 1] for i in range(6)]
    inputs = [
        whole,
        a * c1 - b * s1,
        -(a * s1 + b * c1),
        half * c2,
        -(half * s2),
        a * c3 + b * s3,
        b * c3 - a * s3,
    ]
    parts = [split(value) for value in inputs]
    high = jnp.concatenate([p[0] for p in parts], axis=1)
    low = jnp.concatenate([p[1] for p in parts], axis=1)
    out = mm(tab_ref[...], jnp.concatenate([high, low, high], axis=0))
    out = out.reshape(FAR_BINS // GROUP, 2, GROUP, out.shape[1])
    rows = 2 * FAR_BINS
    for r in range(RADIX):
        first = max(2 * r - 1, 0) * LANES
        real_in = out[..., first : first + LANES]
        if r == 0:
            real, imag = real_in[:, 0], -real_in[:, 1]
        else:
            imag_in = out[..., first + LANES : first + 2 * LANES]
            real, imag = real_in[:, 0] + imag_in[:, 1], imag_in[:, 0] - real_in[:, 1]
        both = jnp.stack([real, imag], axis=1).reshape(rows, LANES)
        spec_ref[r * rows : (r + 1) * rows, :] = both


def whiten_kernel(
    spec_ref, rim_ref, mean_ref, head_ref, edge_ref, band_ref, share_ref, white_ref
):
    head_high, head_low = split(head_ref[...])
    rim = jnp.concatenate([pltpu.roll(rim_ref[...], LANES - TAPS, 1), rim_ref[...]], axis=0)
    rim_high, rim_low = split(rim - mean_ref[...])
    history = mm_nt(
        jnp.concatenate([head_high, head_high, head_low], axis=1),
        jnp.concatenate([rim_high, rim_low, rim_high], axis=1),
    )
    high, low = split(history)
    stacked = jnp.concatenate([high, low, high], axis=0)
    spec = spec_ref[...] + mm(edge_ref[:, : 3 * GROUP], stacked)
    parted = spec.reshape(GROUPS, 2, GROUP, LANES)
    real, imag = parted[:, 0], parted[:, 1]
    amplitude = jnp.sqrt(real * real + imag * imag).reshape(BINS, LANES)
    high, low = split(amplitude)
    wide = mm(band_ref[...], jnp.concatenate([high, low], axis=1))
    smoothed = (wide[:, :LANES] + wide[:, LANES:]) * share_ref[...]
    level = jnp.sum(amplitude, axis=0, keepdims=True) * (1.0 / BINS)
    scale = 1.0 / (smoothed + (WATER * level + 1e-06))
    white = parted * scale.reshape(GROUPS, 1, GROUP, LANES)
    white_ref[...] = white.astype(BF16)


def moves_kernel(offs_ref, moves_ref):
    noff = offs_ref.shape[0]
    row = lax.broadcasted_iota(jnp.int32, (2 * LANES, LANES), 0)
    channel = lax.broadcasted_iota(jnp.int32, (2 * LANES, LANES), 1)
    source = jnp.where(row < LANES + SPAN, row, row - 2 * LANES)
    for o in range(noff):
        hit = source == channel + offs_ref[o]
        moves_ref[:, o * LANES : (o + 1) * LANES] = hit.astype(F32).astype(BF16)


def pack_matrix(owners):
    share = LANES // owners
    matrix = np.zeros((owners, owners, share, owners, owners, share), np.float32)
    for group in range(owners):
        for owner in range(owners):
            matrix[group, owner, :, owner, group, :] = np.eye(share)
    return matrix.reshape(owners * LANES, owners * LANES).astype(jnp.bfloat16)


def halo_kernel(white_ref, up_ref, down_ref):
    rows = white_ref.shape[0] * 2 * GROUP
    white = white_ref[...].reshape(rows, LANES).astype(F32)
    turned = pltpu.roll(white, SPAN, 1)
    half = rows // 2
    lane = lax.broadcasted_iota(jnp.int32, (half, LANES), 1)
    up_ref[...] = jnp.where(lane < SPAN, turned[:half], white[half:]).astype(BF16)
    down_ref[...] = jnp.where(lane < SPAN, white[:half], turned[half:]).astype(BF16)


def near_kernel(white_ref, before_ref, after_ref, moves_ref, inv_ref, out_ref):
    rows = white_ref.shape[0] * 2 * GROUP
    half = rows // 2
    noff = out_ref.shape[0]
    before, after = before_ref[...].astype(F32), after_ref[...].astype(F32)
    lane = lax.broadcasted_iota(jnp.int32, (half, LANES), 1)
    upper = jnp.where(lane < SPAN, after, pltpu.roll(before, SPAN, 1))
    lower = jnp.where(lane < SPAN, pltpu.roll(after, SPAN, 1), before)
    edge = jnp.concatenate([upper, lower], axis=0).astype(BF16)
    own = white_ref[...].reshape(rows, LANES)
    far = mm(jnp.concatenate([own, edge], axis=1), moves_ref[...])
    own = own.astype(F32).reshape(-1, 2, GROUP, LANES)
    columns = []
    for o in range(noff):
        other = far[:, o * LANES : (o + 1) * LANES].reshape(own.shape)
        real = own[:, 0] * other[:, 0] + own[:, 1] * other[:, 1]
        imag = own[:, 1] * other[:, 0] - own[:, 0] * other[:, 1]
        columns.append(jnp.stack([real, imag], axis=1).reshape(rows, LANES).astype(BF16))
    both = mm(inv_ref[...], jnp.concatenate(columns, axis=1))
    lags = both[:LAGS] + both[LAGS:]
    for o in range(noff):
        out_ref[o] = lags[:, o * LANES : (o + 1) * LANES]


def turn_kernel(lags_ref, near_ref):
    for t in range(lags_ref.shape[0]):
        near_ref[:, t, :] = lags_ref[t].T


def loop_kernel(partner_ref, count_ref, flip_ref, pack_ref, white_ref, out_ref, turned_ref):
    blocks, segs, _, bins, _ = white_ref.shape
    owners = out_ref.shape[1]
    slots = partner_ref.shape[1]
    rows = segs * 2 * bins
    packed_rows = 2 * bins // owners
    flats = [white_ref[b].reshape(rows, LANES) for b in range(blocks)]
    turned_ref[...] = mm(jnp.concatenate(flats, axis=0), flip_ref[...]).reshape(turned_ref.shape)
    loops = []
    for b in range(blocks):
        own = flats[b].astype(F32).reshape(segs, 2, bins, LANES)
        for k in range(slots):
            partner = jnp.clip(partner_ref[b, k], 0, blocks - 1)
            live = (k < count_ref[b]).astype(F32)
            far = turned_ref[partner].reshape(segs, 2, bins, LANES)
            real = jnp.sum(own[:, 0] * far[:, 0] + own[:, 1] * far[:, 1], axis=0)
            imag = jnp.sum(own[:, 1] * far[:, 0] - own[:, 0] * far[:, 1], axis=0)
            pair = jnp.concatenate([real, imag], axis=0) * live
            groups = [pair[g * packed_rows : (g + 1) * packed_rows] for g in range(owners)]
            loops.append(jnp.concatenate(groups, axis=1))
    packed = mm(jnp.concatenate(loops, axis=0).astype(BF16), pack_ref[...])
    depth = slots * packed_rows
    for b in range(blocks):
        for q in range(owners):
            tile = packed[b * depth : (b + 1) * depth, q * LANES : (q + 1) * LANES]
            out_ref[b, q] = tile.astype(BF16)


def loop_lag_kernel(slots, spec_ref, inv_ref, loop_ref):
    sources = spec_ref.shape[0]
    rows = inv_ref.shape[1] // sources
    share = loop_ref.shape[0] // slots
    owners = LANES // share
    step = rows // owners
    loop = spec_ref[...].astype(F32)
    lane = lax.broadcasted_iota(jnp.int32, (sources, step, LANES), 2)
    columns = []
    for k in range(slots):
        tile = loop[:, k * step : (k + 1) * step]
        groups = [
            jnp.where((lane >= g * share) & (lane < (g + 1) * share), tile, 0.0)
            for g in range(owners)
        ]
        columns.append(jnp.concatenate(groups, axis=1).astype(BF16).reshape(sources * rows, LANES))
    both = mm(inv_ref[...], jnp.concatenate(columns, axis=1))
    lags = both[:LAGS] + both[LAGS:]
    for k in range(slots):
        turned = lags[:, k * LANES : (k + 1) * LANES].T
        loop_ref[k * share : (k + 1) * share] = sum(
            turned[g * share : (g + 1) * share] for g in range(owners)
        )


def vmem(count):
    return [pl.BlockSpec(memory_space=pltpu.VMEM)] * count


def smem(count):
    return [pl.BlockSpec(memory_space=pltpu.SMEM)] * count


def hbm(count):
    return [pl.BlockSpec(memory_space=pltpu.HBM)] * count


def in_hbm(array):
    return pltpu.with_memory_space_constraint(jnp.asarray(array), pltpu.HBM)


def loops_plain(white, loop_partner, loop_count, owners, inverse):
    blocks, _, _, bins, chans = white.shape
    devices = blocks * owners
    slots = loop_partner.shape[1]
    share = chans // owners
    wide = white.astype(F32)
    loops = []
    for k in range(slots):
        far = jnp.flip(wide[loop_partner[:, k]], axis=4)
        live = (k < loop_count).astype(F32)[:, None, None]
        real = jnp.sum(wide[:, :, 0] * far[:, :, 0] + wide[:, :, 1] * far[:, :, 1], axis=1)
        imag = jnp.sum(wide[:, :, 1] * far[:, :, 0] - wide[:, :, 0] * far[:, :, 1], axis=1)
        pair = (jnp.stack([real, imag]) * live[None]).astype(BF16)
        loops.append(pair.reshape(2, blocks, bins, owners, share))
    loop = jnp.transpose(jnp.stack(loops), (2, 4, 0, 1, 3, 5))
    loop = loop.reshape(devices, slots, 2 * bins, share)
    summed = lax.all_to_all(loop, ("chan", "seg"), 0, 0, tiled=True).astype(F32)
    table = inverse.astype(np.float32).reshape(LAGS, devices, 2 * bins)
    lags = jnp.einsum("dtvc,ldv->tcl", summed, table, precision=lax.Precision.HIGHEST)
    return lags[None]


def body(recording, filter_taps, offsets, loop_partner, loop_count):
    chan_count = lax.axis_size("chan")
    seg_count = lax.axis_size("seg")
    devices = chan_count * seg_count
    bins = BINS // devices
    chans, length = recording.shape
    noff, slots = offsets.shape[0], loop_partner.shape[1]
    share = chans // seg_count
    near_each = noff // seg_count
    assert length == NFFT * DECIM and chans == LANES and noff % seg_count == 0

    route = [(i, i + 1) for i in range(seg_count - 1)]
    rim = pl.pallas_call(
        rim_kernel,
        out_shape=jax.ShapeDtypeStruct((chans // 2, LANES), F32),
        in_specs=hbm(1),
        out_specs=pl.BlockSpec(memory_space=pltpu.VMEM),
        scratch_shapes=[pltpu.VMEM((chans, LANES), F32), pltpu.SemaphoreType.DMA],
        compiler_params=PARAMS,
        cost_estimate=pl.CostEstimate(
            flops=10_000_000_000, bytes_accessed=20_000_000, transcendentals=0
        ),
        name="history",
    )(in_hbm(recording))
    rim = lax.ppermute(rim, "seg", route)
    taps = filter_taps.reshape(1, TAPS)
    spec, mean, head = pl.pallas_call(
        spectrum_kernel,
        out_shape=[
            jax.ShapeDtypeStruct((2 * BINS, LANES), F32),
            jax.ShapeDtypeStruct((LANES, LANES), F32),
            jax.ShapeDtypeStruct((GROUP, LANES), F32),
        ],
        in_specs=vmem(4),
        out_specs=vmem(3),
        compiler_params=PARAMS,
        cost_estimate=pl.CostEstimate(
            flops=1_000_000_000, bytes_accessed=5_000_000, transcendentals=0
        ),
        name="filter_and_transform",
    )(taps, recording, short_table(), twiddle_table())

    band, band_share = band_tables()
    white = pl.pallas_call(
        whiten_kernel,
        out_shape=jax.ShapeDtypeStruct((GROUPS, 2, GROUP, LANES), BF16),
        in_specs=vmem(7),
        out_specs=pl.BlockSpec(memory_space=pltpu.VMEM),
        compiler_params=PARAMS,
        name="whiten",
    )(spec, rim, mean, head, edge_table(), band, band_share)

    white, offsets = lax.optimization_barrier((white, offsets))
    spread = white
    if bins != GROUP:
        spread = jnp.moveaxis(white, 1, 0).reshape(2, devices, bins, LANES)
        spread = jnp.moveaxis(spread, 0, 1)
    moved = lax.all_to_all(spread, ("chan", "seg"), 0, 0, tiled=True)
    moved = moved.reshape(chan_count, seg_count, 2, bins, LANES)

    half = jax.ShapeDtypeStruct((BINS, LANES), BF16)
    up, down = pl.pallas_call(
        halo_kernel,
        out_shape=[half, half],
        in_specs=vmem(1),
        out_specs=vmem(2),
        compiler_params=PARAMS,
        name="halo",
    )(white)
    ring = [(i, (i + 1) % chan_count) for i in range(chan_count)]
    before = lax.ppermute(up, "chan", ring)
    after = lax.ppermute(down, "chan", [(j, i) for i, j in ring])
    moves = pl.pallas_call(
        moves_kernel,
        out_shape=jax.ShapeDtypeStruct((2 * LANES, noff * LANES), BF16),
        in_specs=smem(1),
        out_specs=pl.BlockSpec(memory_space=pltpu.VMEM),
        compiler_params=PARAMS,
        name="offset_moves",
    )(offsets)
    order = np.repeat(bin_order().reshape(GROUPS, 1, GROUP), 2, axis=1).reshape(-1)
    part = np.broadcast_to(np.arange(2).reshape(1, 2, 1), (GROUPS, 2, GROUP)).reshape(-1)
    inverse = np.concatenate(split_np(inverse_table(seg_count, order, part)), axis=0)
    lags = pl.pallas_call(
        near_kernel,
        out_shape=jax.ShapeDtypeStruct((noff, LAGS, LANES), F32),
        in_specs=vmem(5),
        out_specs=pl.BlockSpec(memory_space=pltpu.VMEM),
        compiler_params=PARAMS,
        name="near_lags",
    )(white, before, after, moves, inverse)
    lags = lax.psum_scatter(lags, "seg", scatter_dimension=0, tiled=True)

    if bins % GROUP or 2 * bins % (8 * seg_count):
        order = np.repeat(bin_order().reshape(devices, 1, bins), 2, axis=1).reshape(-1)
        part = np.broadcast_to(np.arange(2).reshape(1, 2, 1), (devices, 2, bins)).reshape(-1)
        loop_inverse = inverse_table(seg_count, order, part)
        loop = loops_plain(moved, loop_partner, loop_count, seg_count, loop_inverse)
    else:
        flip = np.eye(LANES, dtype=np.float32)[::-1].astype(jnp.bfloat16)
        out_rows = slots * (2 * bins // seg_count)
        crossed = pl.pallas_call(
            loop_kernel,
            out_shape=jax.ShapeDtypeStruct((chan_count, seg_count, out_rows, LANES), BF16),
            in_specs=smem(2) + vmem(3),
            out_specs=pl.BlockSpec(memory_space=pltpu.VMEM),
            scratch_shapes=[pltpu.VMEM((chan_count, seg_count * 2 * bins, LANES), F32)],
            compiler_params=PARAMS,
            name="loop_spectra",
        )(loop_partner, loop_count, flip, pack_matrix(seg_count), moved)
        crossed = crossed.reshape(devices, out_rows, LANES)
        summed = lax.all_to_all(crossed, ("chan", "seg"), 0, 0, tiled=True)
        loop = pl.pallas_call(
            functools.partial(loop_lag_kernel, slots),
            out_shape=jax.ShapeDtypeStruct((slots * share, LAGS), F32),
            in_specs=vmem(2),
            out_specs=pl.BlockSpec(memory_space=pltpu.VMEM),
            compiler_params=PARAMS,
            name="loop_lags",
        )(summed, inverse)
        loop = loop.reshape(1, slots, share, LAGS)
    near = pl.pallas_call(
        turn_kernel,
        out_shape=jax.ShapeDtypeStruct((chans, near_each, LAGS), F32),
        in_specs=vmem(1),
        out_specs=pl.BlockSpec(memory_space=pltpu.VMEM),
        compiler_params=PARAMS,
        name="near_turn",
    )(lags)
    return near, loop


def solution(mesh):
    in_specs = (P("chan", "seg"), P(), P(), P(), P())
    out_specs = (P("chan", "seg", None), P("chan", None, "seg", None))
    return jax.shard_map(body, mesh=mesh, in_specs=in_specs, out_specs=out_specs, check_vma=False)
```

```python
import functools
import math

import jax
import jax.numpy as jnp
import numpy as np
from jax import lax
from jax.experimental import pallas as pl
from jax.experimental.pallas import tpu as pltpu
from jax.sharding import PartitionSpec as P

NFFT = 1024
LAGS = 256
TAPS = 64
DECIM = 4
HALFBAND = 10
SPAN = 64
BINS = 512
WATER = 0.2

LANES = 128
GROUP = 16
GROUPS = BINS // GROUP
OUT_BLOCK = 128
STEP = OUT_BLOCK * DECIM
RADIX = 4
DEPTH = NFFT // RADIX
FAR_BINS = BINS // RADIX

F32 = jnp.float32
BF16 = jnp.bfloat16
MIB = 1024 * 1024
PARAMS = pltpu.CompilerParams(vmem_limit_bytes=32 * MIB)


def bin_order():
    return np.concatenate([np.arange(r, BINS, RADIX) for r in range(RADIX)])


def split_np(table):
    high = table.astype(jnp.bfloat16)
    low = (table - high.astype(np.float64)).astype(jnp.bfloat16)
    return high, low


def short_table():
    bins = np.arange(FAR_BINS).reshape(-1, 1, GROUP, 1)
    angles = (bins * np.arange(DEPTH) % DEPTH) * (2.0 * np.pi / DEPTH)
    rows = np.concatenate([np.cos(angles), np.sin(angles)], axis=1).reshape(-1, DEPTH)
    high, low = split_np(rows)
    return np.concatenate([high, high, low], axis=1)


def twiddle_table():
    angles = np.arange(DEPTH)[:, None] * np.arange(1, RADIX) * (2.0 * np.pi / NFFT)
    columns = np.stack([np.cos(angles), np.sin(angles)], axis=2).reshape(DEPTH, -1)
    return np.pad(columns, ((0, 0), (0, LANES - columns.shape[1]))).astype(np.float32)


def edge_table():
    bins = bin_order().reshape(GROUPS, 1, GROUP, 1)
    angles = (bins * np.arange(GROUP) % NFFT) * (2.0 * np.pi / NFFT)
    rows = np.concatenate([np.cos(angles), -np.sin(angles)], axis=1) * (bins != 0)
    high, low = split_np(rows.reshape(2 * BINS, GROUP))
    table = np.concatenate([high, high, low], axis=1)
    return np.pad(table.astype(np.float32), ((0, 0), (0, LANES - 3 * GROUP))).astype(jnp.bfloat16)


def inverse_table(total_segs, bins, part):
    lag = np.arange(LAGS) - LAGS // 2
    angles = (bins[None, :] * lag[:, None] % NFFT) * (2.0 * np.pi / NFFT)
    weights = np.where(bins == 0, 1.0, 2.0) / math.sqrt(2.0 * BINS * total_segs)
    return np.where(part[None, :] == 1, -np.sin(angles), np.cos(angles)) * weights[None, :]


def band_tables():
    bins = bin_order()
    inside = np.abs(bins[:, None] - bins[None, :]) <= HALFBAND
    share = np.broadcast_to(1.0 / inside.sum(axis=1, keepdims=True), (BINS, LANES))
    return inside.astype(jnp.bfloat16), share.astype(np.float32)


def split(value):
    high = value.astype(BF16)
    return high, (value - high.astype(F32)).astype(BF16)


def mm(a, b):
    return jnp.dot(a, b, preferred_element_type=F32)


def mm_nt(a, b):
    return lax.dot_general(a, b, (((1,), (1,)), ((), ())), preferred_element_type=F32)


def tap_rows(taps):
    width = LANES + STEP
    square = (TAPS, TAPS)
    diagonal = lax.broadcasted_iota(jnp.int32, square, 0) == lax.broadcasted_iota(jnp.int32, square, 1)
    column_taps = jnp.sum(jnp.where(diagonal, taps, 0.0), axis=1, keepdims=True)
    tap = lax.broadcasted_iota(jnp.int32, (TAPS, width), 0)
    column = lax.broadcasted_iota(jnp.int32, (TAPS, width), 1)
    placed = jnp.where(column == LANES + DECIM - 1 - tap, column_taps, 0.0)
    spread = jnp.broadcast_to(jnp.sum(placed, axis=0, keepdims=True), (OUT_BLOCK, width))
    return pltpu.roll(spread, 0, 1, stride=DECIM, stride_axis=0)


def rim_kernel(rec_hbm, rim_ref, tail_ref, sem):
    length = rec_hbm.shape[1]
    copy = pltpu.make_async_copy(rec_hbm.at[:, pl.ds(length - LANES, LANES)], tail_ref, sem)
    copy.start()
    copy.wait()
    upper, lower = tail_ref[: LANES // 2], tail_ref[LANES // 2 :]
    lane = lax.broadcasted_iota(jnp.int32, lower.shape, 1)
    rim_ref[...] = jnp.where(lane < TAPS, pltpu.roll(upper, LANES - TAPS, 1), lower)


def spectrum_kernel(taps_ref, rec_ref, tab_ref, twist_ref, spec_ref, mean_ref, head_ref):
    blocks = rec_ref.shape[1] // STEP
    table = tap_rows(taps_ref[...])
    head_ref[...] = table[:GROUP, :LANES]
    taps_high, taps_low = split(table.T)
    taps_both = jnp.concatenate([taps_high, taps_low], axis=1)
    before = [jnp.zeros((LANES, LANES), BF16)] * 2
    outputs = []
    for first in range(0, blocks, blocks // 2):
        windows = ([], [])
        for j in range(first, first + blocks // 2):
            chunk = rec_ref[:, j * STEP : (j + 1) * STEP]
            if j == 0:
                mean = jnp.sum(chunk, axis=1, keepdims=True) * (1.0 / STEP)
            for i, value in enumerate(split(chunk - mean)):
                windows[i].append(jnp.concatenate([before[i], value], axis=1))
                before[i] = value[:, STEP - LANES :]
        wide = mm(jnp.concatenate(windows[0], axis=0), taps_both)
        rest = mm(jnp.concatenate(windows[1], axis=0), taps_high)
        total = wide[:, :LANES] + wide[:, LANES:] + rest
        outputs += [total[t * LANES : (t + 1) * LANES].T for t in range(blocks // 2)]
    pieces = [jnp.concatenate(outputs[j : j + 2], axis=0) for j in range(0, blocks, 2)]
    mean_ref[...] = jnp.broadcast_to(mean, mean_ref.shape)
    even, odd = pieces[0] + pieces[2], pieces[1] + pieces[3]
    a, b = pieces[0] - pieces[2], pieces[1] - pieces[3]
    whole, half = even + odd, even - odd
    whole = whole - jnp.sum(whole, axis=0, keepdims=True) * (1.0 / DEPTH)
    c1, s1, c2, s2, c3, s3 = [twist_ref[:, i : i + 1] for i in range(6)]
    inputs = [
        whole,
        a * c1 - b * s1,
        -(a * s1 + b * c1),
        half * c2,
        -(half * s2),
        a * c3 + b * s3,
        b * c3 - a * s3,
    ]
    parts = [split(value) for value in inputs]
    high = jnp.concatenate([p[0] for p in parts], axis=1)
    low = jnp.concatenate([p[1] for p in parts], axis=1)
    out = mm(tab_ref[...], jnp.concatenate([high, low, high], axis=0))
    out = out.reshape(FAR_BINS // GROUP, 2, GROUP, out.shape[1])
    rows = 2 * FAR_BINS
    for r in range(RADIX):
        first = max(2 * r - 1, 0) * LANES
        real_in = out[..., first : first + LANES]
        if r == 0:
            real, imag = real_in[:, 0], -real_in[:, 1]
        else:
            imag_in = out[..., first + LANES : first + 2 * LANES]
            real, imag = real_in[:, 0] + imag_in[:, 1], imag_in[:, 0] - real_in[:, 1]
        both = jnp.stack([real, imag], axis=1).reshape(rows, LANES)
        spec_ref[r * rows : (r + 1) * rows, :] = both


def whiten_kernel(
    spec_ref,
    rim_ref,
    mean_ref,
    head_ref,
    edge_ref,
    band_ref,
    share_ref,
    white_ref,
    up_ref,
    down_ref,
):
    head_high, head_low = split(head_ref[...])
    rim = jnp.concatenate([pltpu.roll(rim_ref[...], LANES - TAPS, 1), rim_ref[...]], axis=0)
    rim_high, rim_low = split(rim - mean_ref[...])
    history = mm_nt(
        jnp.concatenate([head_high, head_high, head_low], axis=1),
        jnp.concatenate([rim_high, rim_low, rim_high], axis=1),
    )
    high, low = split(history)
    stacked = jnp.concatenate([high, low, high], axis=0)
    spec = spec_ref[...] + mm(edge_ref[:, : 3 * GROUP], stacked)
    parted = spec.reshape(GROUPS, 2, GROUP, LANES)
    real, imag = parted[:, 0], parted[:, 1]
    amplitude = jnp.sqrt(real * real + imag * imag).reshape(BINS, LANES)
    high, low = split(amplitude)
    wide = mm(band_ref[...], jnp.concatenate([high, low], axis=1))
    smoothed = (wide[:, :LANES] + wide[:, LANES:]) * share_ref[...]
    level = jnp.sum(amplitude, axis=0, keepdims=True) * (1.0 / BINS)
    scale = 1.0 / (smoothed + (WATER * level + 1e-06))
    white = parted * scale.reshape(GROUPS, 1, GROUP, LANES)
    white_ref[...] = white.astype(BF16)
    flat = white.reshape(2 * BINS, LANES)
    turned = pltpu.roll(flat, SPAN, 1)
    lane = lax.broadcasted_iota(jnp.int32, (BINS, LANES), 1)
    up_ref[...] = jnp.where(lane < SPAN, turned[:BINS], flat[BINS:]).astype(BF16)
    down_ref[...] = jnp.where(lane < SPAN, flat[:BINS], turned[BINS:]).astype(BF16)


def moves_kernel(offs_ref, moves_ref):
    noff = offs_ref.shape[0]
    row = lax.broadcasted_iota(jnp.int32, (2 * LANES, LANES), 0)
    channel = lax.broadcasted_iota(jnp.int32, (2 * LANES, LANES), 1)
    source = jnp.where(row < LANES + SPAN, row, row - 2 * LANES)
    for o in range(noff):
        hit = source == channel + offs_ref[o]
        moves_ref[:, o * LANES : (o + 1) * LANES] = hit.astype(F32).astype(BF16)


def pack_matrix(owners):
    share = LANES // owners
    matrix = np.zeros((owners, owners, share, owners, owners, share), np.float32)
    for group in range(owners):
        for owner in range(owners):
            matrix[group, owner, :, owner, group, :] = np.eye(share)
    return matrix.reshape(owners * LANES, owners * LANES).astype(jnp.bfloat16)


def near_kernel(white_ref, before_ref, after_ref, moves_ref, inv_ref, *refs):
    out_refs, lags_ref = refs[:-1], refs[-1]
    rows = white_ref.shape[0] * 2 * GROUP
    half = rows // 2
    noff = lags_ref.shape[0]
    before, after = before_ref[...].astype(F32), after_ref[...].astype(F32)
    lane = lax.broadcasted_iota(jnp.int32, (half, LANES), 1)
    upper = jnp.where(lane < SPAN, after, pltpu.roll(before, SPAN, 1))
    lower = jnp.where(lane < SPAN, pltpu.roll(after, SPAN, 1), before)
    edge = jnp.concatenate([upper, lower], axis=0).astype(BF16)
    own = white_ref[...].reshape(rows, LANES)
    far = mm(jnp.concatenate([own, edge], axis=1), moves_ref[...])
    own = own.astype(F32).reshape(-1, 2, GROUP, LANES)
    columns = []
    for o in range(noff):
        other = far[:, o * LANES : (o + 1) * LANES].reshape(own.shape)
        real = own[:, 0] * other[:, 0] + own[:, 1] * other[:, 1]
        imag = own[:, 1] * other[:, 0] - own[:, 0] * other[:, 1]
        columns.append(jnp.stack([real, imag], axis=1).reshape(rows, LANES).astype(BF16))
    both = mm(inv_ref[...], jnp.concatenate(columns, axis=1))
    lags = both[:LAGS] + both[LAGS:]
    for o in range(noff):
        lags_ref[o] = lags[:, o * LANES : (o + 1) * LANES]
    owners = len(out_refs)
    each = noff // owners
    place = lax.axis_index("seg")
    for r in range(owners):
        first = lax.rem(place + r, owners) * each
        out_refs[r][...] = lags_ref[pl.ds(first, each)].astype(BF16)


def turn_kernel(*refs):
    near_ref = refs[-1]
    total = sum(ref[...].astype(F32) for ref in refs[:-1])
    for t in range(near_ref.shape[1]):
        near_ref[:, t, :] = total[t].T


def loop_kernel(partner_ref, count_ref, flip_ref, pack_ref, white_ref, out_ref, turned_ref):
    blocks, segs, _, bins, _ = white_ref.shape
    owners = out_ref.shape[1]
    slots = partner_ref.shape[1]
    rows = segs * 2 * bins
    packed_rows = 2 * bins // owners
    flats = [white_ref[b].reshape(rows, LANES) for b in range(blocks)]
    turned_ref[...] = mm(jnp.concatenate(flats, axis=0), flip_ref[...]).reshape(turned_ref.shape)
    loops = []
    for b in range(blocks):
        own = flats[b].astype(F32).reshape(segs, 2, bins, LANES)
        for k in range(slots):
            partner = jnp.clip(partner_ref[b, k], 0, blocks - 1)
            live = (k < count_ref[b]).astype(F32)
            far = turned_ref[partner].reshape(segs, 2, bins, LANES)
            real = jnp.sum(own[:, 0] * far[:, 0] + own[:, 1] * far[:, 1], axis=0)
            imag = jnp.sum(own[:, 1] * far[:, 0] - own[:, 0] * far[:, 1], axis=0)
            pair = jnp.concatenate([real, imag], axis=0) * live
            groups = [pair[g * packed_rows : (g + 1) * packed_rows] for g in range(owners)]
            loops.append(jnp.concatenate(groups, axis=1))
    packed = mm(jnp.concatenate(loops, axis=0).astype(BF16), pack_ref[...])
    depth = slots * packed_rows
    for b in range(blocks):
        for q in range(owners):
            tile = packed[b * depth : (b + 1) * depth, q * LANES : (q + 1) * LANES]
            out_ref[b, q] = tile.astype(BF16)


def loop_lag_kernel(slots, spec_ref, inv_ref, loop_ref):
    sources = spec_ref.shape[0]
    rows = inv_ref.shape[1] // sources
    share = loop_ref.shape[0] // slots
    owners = LANES // share
    step = rows // owners
    loop = spec_ref[...].astype(F32)
    lane = lax.broadcasted_iota(jnp.int32, (sources, step, LANES), 2)
    columns = []
    for k in range(slots):
        tile = loop[:, k * step : (k + 1) * step]
        groups = [
            jnp.where((lane >= g * share) & (lane < (g + 1) * share), tile, 0.0)
            for g in range(owners)
        ]
        columns.append(jnp.concatenate(groups, axis=1).astype(BF16).reshape(sources * rows, LANES))
    both = mm(inv_ref[...], jnp.concatenate(columns, axis=1))
    lags = both[:LAGS] + both[LAGS:]
    for k in range(slots):
        turned = lags[:, k * LANES : (k + 1) * LANES].T
        loop_ref[k * share : (k + 1) * share] = sum(
            turned[g * share : (g + 1) * share] for g in range(owners)
        )


def vmem(count):
    return [pl.BlockSpec(memory_space=pltpu.VMEM)] * count


def smem(count):
    return [pl.BlockSpec(memory_space=pltpu.SMEM)] * count


def hbm(count):
    return [pl.BlockSpec(memory_space=pltpu.HBM)] * count


def in_hbm(array):
    return pltpu.with_memory_space_constraint(jnp.asarray(array), pltpu.HBM)


def loops_plain(white, loop_partner, loop_count, owners, inverse):
    blocks, _, _, bins, chans = white.shape
    devices = blocks * owners
    slots = loop_partner.shape[1]
    share = chans // owners
    wide = white.astype(F32)
    loops = []
    for k in range(slots):
        far = jnp.flip(wide[loop_partner[:, k]], axis=4)
        live = (k < loop_count).astype(F32)[:, None, None]
        real = jnp.sum(wide[:, :, 0] * far[:, :, 0] + wide[:, :, 1] * far[:, :, 1], axis=1)
        imag = jnp.sum(wide[:, :, 1] * far[:, :, 0] - wide[:, :, 0] * far[:, :, 1], axis=1)
        pair = (jnp.stack([real, imag]) * live[None]).astype(BF16)
        loops.append(pair.reshape(2, blocks, bins, owners, share))
    loop = jnp.transpose(jnp.stack(loops), (2, 4, 0, 1, 3, 5))
    loop = loop.reshape(devices, slots, 2 * bins, share)
    summed = lax.all_to_all(loop, ("chan", "seg"), 0, 0, tiled=True).astype(F32)
    table = inverse.astype(np.float32).reshape(LAGS, devices, 2 * bins)
    lags = jnp.einsum("dtvc,ldv->tcl", summed, table, precision=lax.Precision.HIGHEST)
    return lags[None]


def body(recording, filter_taps, offsets, loop_partner, loop_count):
    chan_count = lax.axis_size("chan")
    seg_count = lax.axis_size("seg")
    devices = chan_count * seg_count
    bins = BINS // devices
    chans, length = recording.shape
    noff, slots = offsets.shape[0], loop_partner.shape[1]
    share = chans // seg_count
    near_each = noff // seg_count
    assert length == NFFT * DECIM and chans == LANES and noff % seg_count == 0

    route = [(i, i + 1) for i in range(seg_count - 1)]
    rim = pl.pallas_call(
        rim_kernel,
        out_shape=jax.ShapeDtypeStruct((chans // 2, LANES), F32),
        in_specs=hbm(1),
        out_specs=pl.BlockSpec(memory_space=pltpu.VMEM),
        scratch_shapes=[pltpu.VMEM((chans, LANES), F32), pltpu.SemaphoreType.DMA],
        compiler_params=PARAMS,
        cost_estimate=pl.CostEstimate(
            flops=10_000_000_000, bytes_accessed=20_000_000, transcendentals=0
        ),
        name="history",
    )(in_hbm(recording))
    rim = lax.ppermute(rim, "seg", route)
    taps = filter_taps.reshape(1, TAPS)
    spec, mean, head = pl.pallas_call(
        spectrum_kernel,
        out_shape=[
            jax.ShapeDtypeStruct((2 * BINS, LANES), F32),
            jax.ShapeDtypeStruct((LANES, LANES), F32),
            jax.ShapeDtypeStruct((GROUP, LANES), F32),
        ],
        in_specs=vmem(4),
        out_specs=vmem(3),
        compiler_params=PARAMS,
        cost_estimate=pl.CostEstimate(
            flops=1_000_000_000, bytes_accessed=5_000_000, transcendentals=0
        ),
        name="filter_and_transform",
    )(taps, recording, short_table(), twiddle_table())

    band, band_share = band_tables()
    half = jax.ShapeDtypeStruct((BINS, LANES), BF16)
    white, up, down = pl.pallas_call(
        whiten_kernel,
        out_shape=[jax.ShapeDtypeStruct((GROUPS, 2, GROUP, LANES), BF16), half, half],
        in_specs=vmem(7),
        out_specs=vmem(3),
        compiler_params=PARAMS,
        name="whiten",
    )(spec, rim, mean, head, edge_table(), band, band_share)

    white, offsets = lax.optimization_barrier((white, offsets))
    spread = white
    if bins != GROUP:
        spread = jnp.moveaxis(white, 1, 0).reshape(2, devices, bins, LANES)
        spread = jnp.moveaxis(spread, 0, 1)
    moved = lax.all_to_all(spread, ("chan", "seg"), 0, 0, tiled=True)
    moved = moved.reshape(chan_count, seg_count, 2, bins, LANES)

    ring = [(i, (i + 1) % chan_count) for i in range(chan_count)]
    before = lax.ppermute(up, "chan", ring)
    after = lax.ppermute(down, "chan", [(j, i) for i, j in ring])
    moves = pl.pallas_call(
        moves_kernel,
        out_shape=jax.ShapeDtypeStruct((2 * LANES, noff * LANES), BF16),
        in_specs=smem(1),
        out_specs=pl.BlockSpec(memory_space=pltpu.VMEM),
        compiler_params=PARAMS,
        name="offset_moves",
    )(offsets)
    order = np.repeat(bin_order().reshape(GROUPS, 1, GROUP), 2, axis=1).reshape(-1)
    part = np.broadcast_to(np.arange(2).reshape(1, 2, 1), (GROUPS, 2, GROUP)).reshape(-1)
    inverse = np.concatenate(split_np(inverse_table(seg_count, order, part)), axis=0)
    lags = pl.pallas_call(
        near_kernel,
        out_shape=[jax.ShapeDtypeStruct((near_each, LAGS, LANES), BF16)] * seg_count,
        in_specs=vmem(5),
        out_specs=vmem(seg_count),
        scratch_shapes=[pltpu.VMEM((noff, LAGS, LANES), F32)],
        compiler_params=PARAMS,
        cost_estimate=pl.CostEstimate(
            flops=10_000_000_000, bytes_accessed=20_000_000, transcendentals=0
        ),
        name="near_lags",
    )(white, before, after, moves, inverse)
    lags = list(lags)
    for r in range(1, seg_count):
        route = [(i, (i + r) % seg_count) for i in range(seg_count)]
        lags[r] = lax.ppermute(lags[r], "seg", route)

    if bins % GROUP or 2 * bins % (8 * seg_count):
        order = np.repeat(bin_order().reshape(devices, 1, bins), 2, axis=1).reshape(-1)
        part = np.broadcast_to(np.arange(2).reshape(1, 2, 1), (devices, 2, bins)).reshape(-1)
        loop_inverse = inverse_table(seg_count, order, part)
        loop = loops_plain(moved, loop_partner, loop_count, seg_count, loop_inverse)
    else:
        flip = np.eye(LANES, dtype=np.float32)[::-1].astype(jnp.bfloat16)
        out_rows = slots * (2 * bins // seg_count)
        crossed = pl.pallas_call(
            loop_kernel,
            out_shape=jax.ShapeDtypeStruct((chan_count, seg_count, out_rows, LANES), BF16),
            in_specs=smem(2) + vmem(3),
            out_specs=pl.BlockSpec(memory_space=pltpu.VMEM),
            scratch_shapes=[pltpu.VMEM((chan_count, seg_count * 2 * bins, LANES), F32)],
            compiler_params=PARAMS,
            name="loop_spectra",
        )(loop_partner, loop_count, flip, pack_matrix(seg_count), moved)
        crossed = crossed.reshape(devices, out_rows, LANES)
        summed = lax.all_to_all(crossed, ("chan", "seg"), 0, 0, tiled=True)
        loop = pl.pallas_call(
            functools.partial(loop_lag_kernel, slots),
            out_shape=jax.ShapeDtypeStruct((slots * share, LAGS), F32),
            in_specs=vmem(2),
            out_specs=pl.BlockSpec(memory_space=pltpu.VMEM),
            compiler_params=PARAMS,
            name="loop_lags",
        )(summed, inverse)
        loop = loop.reshape(1, slots, share, LAGS)
    near = pl.pallas_call(
        turn_kernel,
        out_shape=jax.ShapeDtypeStruct((chans, near_each, LAGS), F32),
        in_specs=vmem(seg_count),
        out_specs=pl.BlockSpec(memory_space=pltpu.VMEM),
        compiler_params=PARAMS,
        name="near_turn",
    )(*lags)
    return near, loop


def solution(mesh):
    in_specs = (P("chan", "seg"), P(), P(), P(), P())
    out_specs = (P("chan", "seg", None), P("chan", None, "seg", None))
    return jax.shard_map(body, mesh=mesh, in_specs=in_specs, out_specs=out_specs, check_vma=False)
```

```python
import functools
import math

import jax
import jax.numpy as jnp
import numpy as np
from jax import lax
from jax.experimental import pallas as pl
from jax.experimental.pallas import tpu as pltpu
from jax.sharding import PartitionSpec as P

NFFT = 1024
LAGS = 256
TAPS = 64
DECIM = 4
HALFBAND = 10
SPAN = 64
BINS = 512
WATER = 0.2

LANES = 128
GROUP = 16
GROUPS = BINS // GROUP
OUT_BLOCK = 128
STEP = OUT_BLOCK * DECIM
RADIX = 4
DEPTH = NFFT // RADIX
FAR_BINS = BINS // RADIX

F32 = jnp.float32
BF16 = jnp.bfloat16
MIB = 1024 * 1024
PARAMS = pltpu.CompilerParams(vmem_limit_bytes=32 * MIB)


def bin_order():
    return np.concatenate([np.arange(r, BINS, RADIX) for r in range(RADIX)])


def split_np(table):
    high = table.astype(jnp.bfloat16)
    low = (table - high.astype(np.float64)).astype(jnp.bfloat16)
    return high, low


def short_table():
    bins = np.arange(FAR_BINS).reshape(-1, 1, GROUP, 1)
    angles = (bins * np.arange(DEPTH) % DEPTH) * (2.0 * np.pi / DEPTH)
    rows = np.concatenate([np.cos(angles), np.sin(angles)], axis=1).reshape(-1, DEPTH)
    high, low = split_np(rows)
    return np.concatenate([high, high, low], axis=1)


def twiddle_table():
    angles = np.arange(DEPTH)[:, None] * np.arange(1, RADIX) * (2.0 * np.pi / NFFT)
    columns = np.stack([np.cos(angles), np.sin(angles)], axis=2).reshape(DEPTH, -1)
    return np.pad(columns, ((0, 0), (0, LANES - columns.shape[1]))).astype(np.float32)


def edge_table():
    bins = bin_order().reshape(GROUPS, 1, GROUP, 1)
    angles = (bins * np.arange(GROUP) % NFFT) * (2.0 * np.pi / NFFT)
    rows = np.concatenate([np.cos(angles), -np.sin(angles)], axis=1) * (bins != 0)
    high, low = split_np(rows.reshape(2 * BINS, GROUP))
    table = np.concatenate([high, high, low], axis=1)
    return np.pad(table.astype(np.float32), ((0, 0), (0, LANES - 3 * GROUP))).astype(jnp.bfloat16)


def inverse_table(total_segs, bins, part):
    lag = np.arange(LAGS) - LAGS // 2
    angles = (bins[None, :] * lag[:, None] % NFFT) * (2.0 * np.pi / NFFT)
    weights = np.where(bins == 0, 1.0, 2.0) / math.sqrt(2.0 * BINS * total_segs)
    return np.where(part[None, :] == 1, -np.sin(angles), np.cos(angles)) * weights[None, :]


def band_tables():
    bins = bin_order()
    inside = np.abs(bins[:, None] - bins[None, :]) <= HALFBAND
    share = np.broadcast_to(1.0 / inside.sum(axis=1, keepdims=True), (BINS, LANES))
    return inside.astype(jnp.bfloat16), share.astype(np.float32)


def split(value):
    high = value.astype(BF16)
    return high, (value - high.astype(F32)).astype(BF16)


def mm(a, b):
    return jnp.dot(a, b, preferred_element_type=F32)


def mm_nt(a, b):
    return lax.dot_general(a, b, (((1,), (1,)), ((), ())), preferred_element_type=F32)


def tap_rows(taps):
    width = LANES + STEP
    square = (TAPS, TAPS)
    diagonal = lax.broadcasted_iota(jnp.int32, square, 0) == lax.broadcasted_iota(jnp.int32, square, 1)
    column_taps = jnp.sum(jnp.where(diagonal, taps, 0.0), axis=1, keepdims=True)
    tap = lax.broadcasted_iota(jnp.int32, (TAPS, width), 0)
    column = lax.broadcasted_iota(jnp.int32, (TAPS, width), 1)
    placed = jnp.where(column == LANES + DECIM - 1 - tap, column_taps, 0.0)
    spread = jnp.broadcast_to(jnp.sum(placed, axis=0, keepdims=True), (OUT_BLOCK, width))
    return pltpu.roll(spread, 0, 1, stride=DECIM, stride_axis=0)


def rim_kernel(rec_hbm, rim_ref, tail_ref, sem):
    length = rec_hbm.shape[1]
    copy = pltpu.make_async_copy(rec_hbm.at[:, pl.ds(length - LANES, LANES)], tail_ref, sem)
    copy.start()
    copy.wait()
    upper, lower = tail_ref[: LANES // 2], tail_ref[LANES // 2 :]
    lane = lax.broadcasted_iota(jnp.int32, lower.shape, 1)
    rim_ref[...] = jnp.where(lane < TAPS, pltpu.roll(upper, LANES - TAPS, 1), lower)


def spectrum_kernel(taps_ref, rec_ref, tab_ref, twist_ref, spec_ref, mean_ref, head_ref):
    blocks = rec_ref.shape[1] // STEP
    table = tap_rows(taps_ref[...])
    head_ref[...] = table[:GROUP, :LANES]
    taps_high, taps_low = split(table.T)
    taps_both = jnp.concatenate([taps_high, taps_low], axis=1)
    before = [jnp.zeros((LANES, LANES), BF16)] * 2
    outputs = []
    for first in range(0, blocks, blocks // 2):
        windows = ([], [])
        for j in range(first, first + blocks // 2):
            chunk = rec_ref[:, j * STEP : (j + 1) * STEP]
            if j == 0:
                mean = jnp.sum(chunk, axis=1, keepdims=True) * (1.0 / STEP)
            for i, value in enumerate(split(chunk - mean)):
                windows[i].append(jnp.concatenate([before[i], value], axis=1))
                before[i] = value[:, STEP - LANES :]
        wide = mm(jnp.concatenate(windows[0], axis=0), taps_both)
        rest = mm(jnp.concatenate(windows[1], axis=0), taps_high)
        total = wide[:, :LANES] + wide[:, LANES:] + rest
        outputs += [total[t * LANES : (t + 1) * LANES].T for t in range(blocks // 2)]
    pieces = [jnp.concatenate(outputs[j : j + 2], axis=0) for j in range(0, blocks, 2)]
    mean_ref[...] = jnp.broadcast_to(mean, mean_ref.shape)
    even, odd = pieces[0] + pieces[2], pieces[1] + pieces[3]
    a, b = pieces[0] - pieces[2], pieces[1] - pieces[3]
    whole, half = even + odd, even - odd
    whole = whole - jnp.sum(whole, axis=0, keepdims=True) * (1.0 / DEPTH)
    c1, s1, c2, s2, c3, s3 = [twist_ref[:, i : i + 1] for i in range(6)]
    inputs = [
        whole,
        a * c1 - b * s1,
        -(a * s1 + b * c1),
        half * c2,
        -(half * s2),
        a * c3 + b * s3,
        b * c3 - a * s3,
    ]
    parts = [split(value) for value in inputs]
    high = jnp.concatenate([p[0] for p in parts], axis=1)
    low = jnp.concatenate([p[1] for p in parts], axis=1)
    out = mm(tab_ref[...], jnp.concatenate([high, low, high], axis=0))
    out = out.reshape(FAR_BINS // GROUP, 2, GROUP, out.shape[1])
    rows = 2 * FAR_BINS
    for r in range(RADIX):
        first = max(2 * r - 1, 0) * LANES
        real_in = out[..., first : first + LANES]
        if r == 0:
            real, imag = real_in[:, 0], -real_in[:, 1]
        else:
            imag_in = out[..., first + LANES : first + 2 * LANES]
            real, imag = real_in[:, 0] + imag_in[:, 1], imag_in[:, 0] - real_in[:, 1]
        both = jnp.stack([real, imag], axis=1).reshape(rows, LANES)
        spec_ref[r * rows : (r + 1) * rows, :] = both


def whiten_kernel(
    spec_ref,
    rim_ref,
    mean_ref,
    head_ref,
    edge_ref,
    band_ref,
    share_ref,
    white_ref,
    up_ref,
    down_ref,
):
    head_high, head_low = split(head_ref[...])
    rim = jnp.concatenate([pltpu.roll(rim_ref[...], LANES - TAPS, 1), rim_ref[...]], axis=0)
    rim_high, rim_low = split(rim - mean_ref[...])
    history = mm_nt(
        jnp.concatenate([head_high, head_high, head_low], axis=1),
        jnp.concatenate([rim_high, rim_low, rim_high], axis=1),
    )
    high, low = split(history)
    stacked = jnp.concatenate([high, low, high], axis=0)
    spec = spec_ref[...] + mm(edge_ref[:, : 3 * GROUP], stacked)
    parted = spec.reshape(GROUPS, 2, GROUP, LANES)
    real, imag = parted[:, 0], parted[:, 1]
    amplitude = jnp.sqrt(real * real + imag * imag).reshape(BINS, LANES)
    high, low = split(amplitude)
    wide = mm(band_ref[...], jnp.concatenate([high, low], axis=1))
    smoothed = (wide[:, :LANES] + wide[:, LANES:]) * share_ref[...]
    level = jnp.sum(amplitude, axis=0, keepdims=True) * (1.0 / BINS)
    scale = 1.0 / (smoothed + (WATER * level + 1e-06))
    white = parted * scale.reshape(GROUPS, 1, GROUP, LANES)
    white_ref[...] = white.astype(BF16)
    flat = white.reshape(2 * BINS, LANES)
    turned = pltpu.roll(flat, SPAN, 1)
    lane = lax.broadcasted_iota(jnp.int32, (BINS, LANES), 1)
    up_ref[...] = jnp.where(lane < SPAN, turned[:BINS], flat[BINS:]).astype(BF16)
    down_ref[...] = jnp.where(lane < SPAN, flat[:BINS], turned[BINS:]).astype(BF16)


def moves_kernel(offs_ref, moves_ref):
    noff = offs_ref.shape[0]
    row = lax.broadcasted_iota(jnp.int32, (2 * LANES, LANES), 0)
    channel = lax.broadcasted_iota(jnp.int32, (2 * LANES, LANES), 1)
    source = jnp.where(row < LANES + SPAN, row, row - 2 * LANES)
    for o in range(noff):
        hit = source == channel + offs_ref[o]
        moves_ref[:, o * LANES : (o + 1) * LANES] = hit.astype(F32).astype(BF16)


def pack_matrix(owners):
    share = LANES // owners
    matrix = np.zeros((owners, owners, share, owners, owners, share), np.float32)
    for group in range(owners):
        for owner in range(owners):
            matrix[group, owner, :, owner, group, :] = np.eye(share)
    return matrix.reshape(owners * LANES, owners * LANES).astype(jnp.bfloat16)


def near_kernel(white_ref, before_ref, after_ref, moves_ref, inv_ref, *refs):
    out_refs, lags_ref = refs[:-1], refs[-1]
    rows = white_ref.shape[0] * 2 * GROUP
    half = rows // 2
    noff = lags_ref.shape[0]
    before, after = before_ref[...].astype(F32), after_ref[...].astype(F32)
    lane = lax.broadcasted_iota(jnp.int32, (half, LANES), 1)
    upper = jnp.where(lane < SPAN, after, pltpu.roll(before, SPAN, 1))
    lower = jnp.where(lane < SPAN, pltpu.roll(after, SPAN, 1), before)
    edge = jnp.concatenate([upper, lower], axis=0).astype(BF16)
    own = white_ref[...].reshape(rows, LANES)
    far = mm(jnp.concatenate([own, edge], axis=1), moves_ref[...])
    own = own.astype(F32).reshape(-1, 2, GROUP, LANES)
    columns = []
    for o in range(noff):
        other = far[:, o * LANES : (o + 1) * LANES].reshape(own.shape)
        real = own[:, 0] * other[:, 0] + own[:, 1] * other[:, 1]
        imag = own[:, 1] * other[:, 0] - own[:, 0] * other[:, 1]
        columns.append(jnp.stack([real, imag], axis=1).reshape(rows, LANES).astype(BF16))
    both = mm(inv_ref[...], jnp.concatenate(columns, axis=1))
    lags = both[:LAGS] + both[LAGS:]
    for o in range(noff):
        lags_ref[o] = lags[:, o * LANES : (o + 1) * LANES]
    owners = len(out_refs)
    each = noff // owners
    place = lax.axis_index("seg")
    for r in range(owners):
        first = lax.rem(place + r, owners) * each
        out_refs[r][...] = lags_ref[pl.ds(first, each)].astype(BF16)


def turn_kernel(*refs):
    near_ref = refs[-1]
    total = sum(ref[...].astype(F32) for ref in refs[:-1])
    for t in range(near_ref.shape[1]):
        near_ref[:, t, :] = total[t].T


def loop_kernel(partner_ref, count_ref, flip_ref, pack_ref, white_ref, out_ref, turned_ref):
    blocks, segs, _, bins, _ = white_ref.shape
    owners = out_ref.shape[1]
    slots = partner_ref.shape[1]
    rows = segs * 2 * bins
    packed_rows = 2 * bins // owners
    flats = [white_ref[b].reshape(rows, LANES) for b in range(blocks)]
    turned_ref[...] = mm(jnp.concatenate(flats, axis=0), flip_ref[...]).reshape(turned_ref.shape)
    loops = []
    for b in range(blocks):
        own = flats[b].astype(F32).reshape(segs, 2, bins, LANES)
        for k in range(slots):
            partner = jnp.clip(partner_ref[b, k], 0, blocks - 1)
            live = (k < count_ref[b]).astype(F32)
            far = turned_ref[partner].reshape(segs, 2, bins, LANES)
            real = jnp.sum(own[:, 0] * far[:, 0] + own[:, 1] * far[:, 1], axis=0)
            imag = jnp.sum(own[:, 1] * far[:, 0] - own[:, 0] * far[:, 1], axis=0)
            pair = jnp.concatenate([real, imag], axis=0) * live
            groups = [pair[g * packed_rows : (g + 1) * packed_rows] for g in range(owners)]
            loops.append(jnp.concatenate(groups, axis=1))
    packed = mm(jnp.concatenate(loops, axis=0).astype(BF16), pack_ref[...])
    depth = slots * packed_rows
    for b in range(blocks):
        for q in range(owners):
            tile = packed[b * depth : (b + 1) * depth, q * LANES : (q + 1) * LANES]
            out_ref[b, q] = tile.astype(BF16)


def loop_lag_kernel(slots, spec_ref, inv_ref, loop_ref):
    sources = spec_ref.shape[0]
    step = spec_ref.shape[1] // slots
    share = loop_ref.shape[0] // slots
    loop = spec_ref[...].astype(F32)
    rows = []
    for k in range(slots):
        turned = loop[:, k * step : (k + 1) * step].reshape(sources * step, LANES).T
        groups = [turned[g * share : (g + 1) * share] for g in range(LANES // share)]
        rows.append(jnp.concatenate(groups, axis=1))
    both = mm(jnp.concatenate(rows, axis=0).astype(BF16), inv_ref[...])
    loop_ref[...] = both[:, :LAGS] + both[:, LAGS:]


def vmem(count):
    return [pl.BlockSpec(memory_space=pltpu.VMEM)] * count


def smem(count):
    return [pl.BlockSpec(memory_space=pltpu.SMEM)] * count


def hbm(count):
    return [pl.BlockSpec(memory_space=pltpu.HBM)] * count


def in_hbm(array):
    return pltpu.with_memory_space_constraint(jnp.asarray(array), pltpu.HBM)


def loops_plain(white, loop_partner, loop_count, owners, inverse):
    blocks, _, _, bins, chans = white.shape
    devices = blocks * owners
    slots = loop_partner.shape[1]
    share = chans // owners
    wide = white.astype(F32)
    loops = []
    for k in range(slots):
        far = jnp.flip(wide[loop_partner[:, k]], axis=4)
        live = (k < loop_count).astype(F32)[:, None, None]
        real = jnp.sum(wide[:, :, 0] * far[:, :, 0] + wide[:, :, 1] * far[:, :, 1], axis=1)
        imag = jnp.sum(wide[:, :, 1] * far[:, :, 0] - wide[:, :, 0] * far[:, :, 1], axis=1)
        pair = (jnp.stack([real, imag]) * live[None]).astype(BF16)
        loops.append(pair.reshape(2, blocks, bins, owners, share))
    loop = jnp.transpose(jnp.stack(loops), (2, 4, 0, 1, 3, 5))
    loop = loop.reshape(devices, slots, 2 * bins, share)
    summed = lax.all_to_all(loop, ("chan", "seg"), 0, 0, tiled=True).astype(F32)
    table = inverse.astype(np.float32).reshape(LAGS, devices, 2 * bins)
    lags = jnp.einsum("dtvc,ldv->tcl", summed, table, precision=lax.Precision.HIGHEST)
    return lags[None]


def body(recording, filter_taps, offsets, loop_partner, loop_count):
    chan_count = lax.axis_size("chan")
    seg_count = lax.axis_size("seg")
    devices = chan_count * seg_count
    bins = BINS // devices
    chans, length = recording.shape
    noff, slots = offsets.shape[0], loop_partner.shape[1]
    share = chans // seg_count
    near_each = noff // seg_count
    assert length == NFFT * DECIM and chans == LANES and noff % seg_count == 0

    route = [(i, i + 1) for i in range(seg_count - 1)]
    rim = pl.pallas_call(
        rim_kernel,
        out_shape=jax.ShapeDtypeStruct((chans // 2, LANES), F32),
        in_specs=hbm(1),
        out_specs=pl.BlockSpec(memory_space=pltpu.VMEM),
        scratch_shapes=[pltpu.VMEM((chans, LANES), F32), pltpu.SemaphoreType.DMA],
        compiler_params=PARAMS,
        cost_estimate=pl.CostEstimate(
            flops=10_000_000_000, bytes_accessed=20_000_000, transcendentals=0
        ),
        name="history",
    )(in_hbm(recording))
    rim = lax.ppermute(rim, "seg", route)
    taps = filter_taps.reshape(1, TAPS)
    spec, mean, head = pl.pallas_call(
        spectrum_kernel,
        out_shape=[
            jax.ShapeDtypeStruct((2 * BINS, LANES), F32),
            jax.ShapeDtypeStruct((LANES, LANES), F32),
            jax.ShapeDtypeStruct((GROUP, LANES), F32),
        ],
        in_specs=vmem(4),
        out_specs=vmem(3),
        compiler_params=PARAMS,
        cost_estimate=pl.CostEstimate(
            flops=1_000_000_000, bytes_accessed=5_000_000, transcendentals=0
        ),
        name="filter_and_transform",
    )(taps, recording, short_table(), twiddle_table())

    band, band_share = band_tables()
    half = jax.ShapeDtypeStruct((BINS, LANES), BF16)
    white, up, down = pl.pallas_call(
        whiten_kernel,
        out_shape=[jax.ShapeDtypeStruct((GROUPS, 2, GROUP, LANES), BF16), half, half],
        in_specs=vmem(7),
        out_specs=vmem(3),
        compiler_params=PARAMS,
        name="whiten",
    )(spec, rim, mean, head, edge_table(), band, band_share)

    white, offsets = lax.optimization_barrier((white, offsets))
    spread = white
    if bins != GROUP:
        spread = jnp.moveaxis(white, 1, 0).reshape(2, devices, bins, LANES)
        spread = jnp.moveaxis(spread, 0, 1)
    moved = lax.all_to_all(spread, ("chan", "seg"), 0, 0, tiled=True)
    moved = moved.reshape(chan_count, seg_count, 2, bins, LANES)

    ring = [(i, (i + 1) % chan_count) for i in range(chan_count)]
    before = lax.ppermute(up, "chan", ring)
    after = lax.ppermute(down, "chan", [(j, i) for i, j in ring])
    moves = pl.pallas_call(
        moves_kernel,
        out_shape=jax.ShapeDtypeStruct((2 * LANES, noff * LANES), BF16),
        in_specs=smem(1),
        out_specs=pl.BlockSpec(memory_space=pltpu.VMEM),
        compiler_params=PARAMS,
        name="offset_moves",
    )(offsets)
    order = np.repeat(bin_order().reshape(GROUPS, 1, GROUP), 2, axis=1).reshape(-1)
    part = np.broadcast_to(np.arange(2).reshape(1, 2, 1), (GROUPS, 2, GROUP)).reshape(-1)
    inverse = np.concatenate(split_np(inverse_table(seg_count, order, part)), axis=0)
    lags = pl.pallas_call(
        near_kernel,
        out_shape=[jax.ShapeDtypeStruct((near_each, LAGS, LANES), BF16)] * seg_count,
        in_specs=vmem(5),
        out_specs=vmem(seg_count),
        scratch_shapes=[pltpu.VMEM((noff, LAGS, LANES), F32)],
        compiler_params=PARAMS,
        cost_estimate=pl.CostEstimate(
            flops=3_000_000_000, bytes_accessed=4_000_000, transcendentals=0
        ),
        name="near_lags",
    )(white, before, after, moves, inverse)
    moved, *lags = lax.optimization_barrier((moved, *lags))

    if bins % GROUP or 2 * bins % (8 * seg_count):
        order = np.repeat(bin_order().reshape(devices, 1, bins), 2, axis=1).reshape(-1)
        part = np.broadcast_to(np.arange(2).reshape(1, 2, 1), (devices, 2, bins)).reshape(-1)
        loop_inverse = inverse_table(seg_count, order, part)
        loop = loops_plain(moved, loop_partner, loop_count, seg_count, loop_inverse)
    else:
        flip = np.eye(LANES, dtype=np.float32)[::-1].astype(jnp.bfloat16)
        out_rows = slots * (2 * bins // seg_count)
        crossed = pl.pallas_call(
            loop_kernel,
            out_shape=jax.ShapeDtypeStruct((chan_count, seg_count, out_rows, LANES), BF16),
            in_specs=smem(2) + vmem(3),
            out_specs=pl.BlockSpec(memory_space=pltpu.VMEM),
            scratch_shapes=[pltpu.VMEM((chan_count, seg_count * 2 * bins, LANES), F32)],
            compiler_params=PARAMS,
            name="loop_spectra",
        )(loop_partner, loop_count, flip, pack_matrix(seg_count), moved)
        crossed, *lags = lax.optimization_barrier((crossed, *lags))
        crossed = crossed.reshape(devices, out_rows, LANES)
        summed = lax.all_to_all(crossed, ("chan", "seg"), 0, 0, tiled=True)
        columns = np.arange(2 * BINS).reshape(devices, seg_count, -1).swapaxes(0, 1).reshape(-1)
        loop_inverse = inverse_table(seg_count, order[columns], part[columns]).T
        loop_inverse = np.concatenate(split_np(loop_inverse), axis=1)
        loop = pl.pallas_call(
            functools.partial(loop_lag_kernel, slots),
            out_shape=jax.ShapeDtypeStruct((slots * share, LAGS), F32),
            in_specs=vmem(2),
            out_specs=pl.BlockSpec(memory_space=pltpu.VMEM),
            compiler_params=PARAMS,
            name="loop_lags",
        )(summed, loop_inverse)
        loop = loop.reshape(1, slots, share, LAGS)
    for r in range(1, seg_count):
        route = [(i, (i + r) % seg_count) for i in range(seg_count)]
        lags[r] = lax.ppermute(lags[r], "seg", route)
    near = pl.pallas_call(
        turn_kernel,
        out_shape=jax.ShapeDtypeStruct((chans, near_each, LAGS), F32),
        in_specs=vmem(seg_count),
        out_specs=pl.BlockSpec(memory_space=pltpu.VMEM),
        compiler_params=PARAMS,
        name="near_turn",
    )(*lags)
    return near, loop


def solution(mesh):
    in_specs = (P("chan", "seg"), P(), P(), P(), P())
    out_specs = (P("chan", "seg", None), P("chan", None, "seg", None))
    return jax.shard_map(body, mesh=mesh, in_specs=in_specs, out_specs=out_specs, check_vma=False)
```

```python
import functools
import math

import jax
import jax.numpy as jnp
import numpy as np
from jax import lax
from jax.experimental import pallas as pl
from jax.experimental.pallas import tpu as pltpu
from jax.sharding import PartitionSpec as P

NFFT = 1024
LAGS = 256
TAPS = 64
DECIM = 4
HALFBAND = 10
SPAN = 64
BINS = 512
WATER = 0.2

LANES = 128
GROUP = 16
GROUPS = BINS // GROUP
OUT_BLOCK = 128
STEP = OUT_BLOCK * DECIM
RADIX = 4
DEPTH = NFFT // RADIX
FAR_BINS = BINS // RADIX

F32 = jnp.float32
BF16 = jnp.bfloat16
MIB = 1024 * 1024
PARAMS = pltpu.CompilerParams(vmem_limit_bytes=32 * MIB)


def bin_order():
    return np.concatenate([np.arange(r, BINS, RADIX) for r in range(RADIX)])


def split_np(table):
    high = table.astype(jnp.bfloat16)
    low = (table - high.astype(np.float64)).astype(jnp.bfloat16)
    return high, low


def short_table():
    bins = np.arange(FAR_BINS).reshape(-1, 1, GROUP, 1)
    angles = (bins * np.arange(DEPTH) % DEPTH) * (2.0 * np.pi / DEPTH)
    rows = np.concatenate([np.cos(angles), np.sin(angles)], axis=1).reshape(-1, DEPTH)
    high, low = split_np(rows)
    return np.concatenate([high, high, low], axis=1)


def twiddle_table():
    angles = np.arange(DEPTH)[:, None] * np.arange(1, RADIX) * (2.0 * np.pi / NFFT)
    columns = np.stack([np.cos(angles), np.sin(angles)], axis=2).reshape(DEPTH, -1)
    return np.pad(columns, ((0, 0), (0, LANES - columns.shape[1]))).astype(np.float32)


def edge_table():
    bins = bin_order().reshape(GROUPS, 1, GROUP, 1)
    angles = (bins * np.arange(GROUP) % NFFT) * (2.0 * np.pi / NFFT)
    rows = np.concatenate([np.cos(angles), -np.sin(angles)], axis=1) * (bins != 0)
    high, low = split_np(rows.reshape(2 * BINS, GROUP))
    table = np.concatenate([high, high, low], axis=1)
    return np.pad(table.astype(np.float32), ((0, 0), (0, LANES - 3 * GROUP))).astype(jnp.bfloat16)


def inverse_table(total_segs, bins, part):
    lag = np.arange(LAGS) - LAGS // 2
    angles = (bins[None, :] * lag[:, None] % NFFT) * (2.0 * np.pi / NFFT)
    weights = np.where(bins == 0, 1.0, 2.0) / math.sqrt(2.0 * BINS * total_segs)
    return np.where(part[None, :] == 1, -np.sin(angles), np.cos(angles)) * weights[None, :]


def band_tables():
    bins = bin_order()
    inside = np.abs(bins[:, None] - bins[None, :]) <= HALFBAND
    share = np.broadcast_to(1.0 / inside.sum(axis=1, keepdims=True), (BINS, LANES))
    return inside.astype(jnp.bfloat16), share.astype(np.float32)


def split(value):
    high = value.astype(BF16)
    return high, (value - high.astype(F32)).astype(BF16)


def mm(a, b):
    return jnp.dot(a, b, preferred_element_type=F32)


def mm_nt(a, b):
    return lax.dot_general(a, b, (((1,), (1,)), ((), ())), preferred_element_type=F32)


def tap_rows(taps):
    width = LANES + STEP
    square = (TAPS, TAPS)
    diagonal = lax.broadcasted_iota(jnp.int32, square, 0) == lax.broadcasted_iota(jnp.int32, square, 1)
    column_taps = jnp.sum(jnp.where(diagonal, taps, 0.0), axis=1, keepdims=True)
    tap = lax.broadcasted_iota(jnp.int32, (TAPS, width), 0)
    column = lax.broadcasted_iota(jnp.int32, (TAPS, width), 1)
    placed = jnp.where(column == LANES + DECIM - 1 - tap, column_taps, 0.0)
    spread = jnp.broadcast_to(jnp.sum(placed, axis=0, keepdims=True), (OUT_BLOCK, width))
    return pltpu.roll(spread, 0, 1, stride=DECIM, stride_axis=0)


def rim_kernel(rec_hbm, rim_ref, tail_ref, sem):
    length = rec_hbm.shape[1]
    copy = pltpu.make_async_copy(rec_hbm.at[:, pl.ds(length - LANES, LANES)], tail_ref, sem)
    copy.start()
    copy.wait()
    upper, lower = tail_ref[: LANES // 2], tail_ref[LANES // 2 :]
    lane = lax.broadcasted_iota(jnp.int32, lower.shape, 1)
    rim_ref[...] = jnp.where(lane < TAPS, pltpu.roll(upper, LANES - TAPS, 1), lower)


def spectrum_kernel(taps_ref, rec_ref, tab_ref, twist_ref, spec_ref, mean_ref, head_ref):
    blocks = rec_ref.shape[1] // STEP
    table = tap_rows(taps_ref[...])
    head_ref[...] = table[:GROUP, :LANES]
    taps_high, taps_low = split(table.T)
    taps_both = jnp.concatenate([taps_high, taps_low], axis=1)
    before = [jnp.zeros((LANES, LANES), BF16)] * 2
    outputs = []
    for first in range(0, blocks, blocks // 2):
        windows = ([], [])
        for j in range(first, first + blocks // 2):
            chunk = rec_ref[:, j * STEP : (j + 1) * STEP]
            if j == 0:
                mean = jnp.sum(chunk, axis=1, keepdims=True) * (1.0 / STEP)
            for i, value in enumerate(split(chunk - mean)):
                windows[i].append(jnp.concatenate([before[i], value], axis=1))
                before[i] = value[:, STEP - LANES :]
        wide = mm(jnp.concatenate(windows[0], axis=0), taps_both)
        rest = mm(jnp.concatenate(windows[1], axis=0), taps_high)
        total = wide[:, :LANES] + wide[:, LANES:] + rest
        outputs += [total[t * LANES : (t + 1) * LANES].T for t in range(blocks // 2)]
    pieces = [jnp.concatenate(outputs[j : j + 2], axis=0) for j in range(0, blocks, 2)]
    mean_ref[...] = jnp.broadcast_to(mean, mean_ref.shape)
    even, odd = pieces[0] + pieces[2], pieces[1] + pieces[3]
    a, b = pieces[0] - pieces[2], pieces[1] - pieces[3]
    whole, half = even + odd, even - odd
    whole = whole - jnp.sum(whole, axis=0, keepdims=True) * (1.0 / DEPTH)
    c1, s1, c2, s2, c3, s3 = [twist_ref[:, i : i + 1] for i in range(6)]
    inputs = [
        whole,
        a * c1 - b * s1,
        -(a * s1 + b * c1),
        half * c2,
        -(half * s2),
        a * c3 + b * s3,
        b * c3 - a * s3,
    ]
    parts = [split(value) for value in inputs]
    high = jnp.concatenate([p[0] for p in parts], axis=1)
    low = jnp.concatenate([p[1] for p in parts], axis=1)
    out = mm(tab_ref[...], jnp.concatenate([high, low, high], axis=0))
    out = out.reshape(FAR_BINS // GROUP, 2, GROUP, out.shape[1])
    rows = 2 * FAR_BINS
    for r in range(RADIX):
        first = max(2 * r - 1, 0) * LANES
        real_in = out[..., first : first + LANES]
        if r == 0:
            real, imag = real_in[:, 0], -real_in[:, 1]
        else:
            imag_in = out[..., first + LANES : first + 2 * LANES]
            real, imag = real_in[:, 0] + imag_in[:, 1], imag_in[:, 0] - real_in[:, 1]
        both = jnp.stack([real, imag], axis=1).reshape(rows, LANES)
        spec_ref[r * rows : (r + 1) * rows, :] = both


def whiten_kernel(
    spec_ref,
    rim_ref,
    mean_ref,
    head_ref,
    edge_ref,
    band_ref,
    share_ref,
    white_ref,
    up_ref,
    down_ref,
):
    head_high, head_low = split(head_ref[...])
    rim = jnp.concatenate([pltpu.roll(rim_ref[...], LANES - TAPS, 1), rim_ref[...]], axis=0)
    rim_high, rim_low = split(rim - mean_ref[...])
    history = mm_nt(
        jnp.concatenate([head_high, head_high, head_low], axis=1),
        jnp.concatenate([rim_high, rim_low, rim_high], axis=1),
    )
    high, low = split(history)
    stacked = jnp.concatenate([high, low, high], axis=0)
    spec = spec_ref[...] + mm(edge_ref[:, : 3 * GROUP], stacked)
    parted = spec.reshape(GROUPS, 2, GROUP, LANES)
    real, imag = parted[:, 0], parted[:, 1]
    amplitude = jnp.sqrt(real * real + imag * imag).reshape(BINS, LANES)
    high, low = split(amplitude)
    wide = mm(band_ref[...], jnp.concatenate([high, low], axis=1))
    smoothed = (wide[:, :LANES] + wide[:, LANES:]) * share_ref[...]
    level = jnp.sum(amplitude, axis=0, keepdims=True) * (1.0 / BINS)
    scale = 1.0 / (smoothed + (WATER * level + 1e-06))
    white = parted * scale.reshape(GROUPS, 1, GROUP, LANES)
    white_ref[...] = white.astype(BF16)
    flat = white.reshape(2 * BINS, LANES)
    turned = pltpu.roll(flat, SPAN, 1)
    lane = lax.broadcasted_iota(jnp.int32, (BINS, LANES), 1)
    up_ref[...] = jnp.where(lane < SPAN, turned[:BINS], flat[BINS:]).astype(BF16)
    down_ref[...] = jnp.where(lane < SPAN, flat[:BINS], turned[BINS:]).astype(BF16)


def moves_kernel(offs_ref, moves_ref):
    noff = offs_ref.shape[0]
    row = lax.broadcasted_iota(jnp.int32, (2 * LANES, LANES), 0)
    channel = lax.broadcasted_iota(jnp.int32, (2 * LANES, LANES), 1)
    source = jnp.where(row < LANES + SPAN, row, row - 2 * LANES)
    for o in range(noff):
        hit = source == channel + offs_ref[o]
        moves_ref[:, o * LANES : (o + 1) * LANES] = hit.astype(F32).astype(BF16)


def pack_matrix(owners):
    share = LANES // owners
    matrix = np.zeros((owners, owners, share, owners, owners, share), np.float32)
    for group in range(owners):
        for owner in range(owners):
            matrix[group, owner, :, owner, group, :] = np.eye(share)
    return matrix.reshape(owners * LANES, owners * LANES).astype(jnp.bfloat16)


def partner_of(place, r, owners):
    return place ^ r if owners & (owners - 1) == 0 else (place + r) % owners


def near_kernel(white_ref, before_ref, after_ref, moves_ref, inv_ref, *refs):
    out_refs, lags_ref = refs[:-1], refs[-1]
    rows = white_ref.shape[0] * 2 * GROUP
    half = rows // 2
    noff = lags_ref.shape[0]
    before, after = before_ref[...].astype(F32), after_ref[...].astype(F32)
    lane = lax.broadcasted_iota(jnp.int32, (half, LANES), 1)
    upper = jnp.where(lane < SPAN, after, pltpu.roll(before, SPAN, 1))
    lower = jnp.where(lane < SPAN, pltpu.roll(after, SPAN, 1), before)
    edge = jnp.concatenate([upper, lower], axis=0).astype(BF16)
    own = white_ref[...].reshape(rows, LANES)
    far = mm(jnp.concatenate([own, edge], axis=1), moves_ref[...])
    own = own.astype(F32).reshape(-1, 2, GROUP, LANES)
    columns = []
    for o in range(noff):
        other = far[:, o * LANES : (o + 1) * LANES].reshape(own.shape)
        real = own[:, 0] * other[:, 0] + own[:, 1] * other[:, 1]
        imag = own[:, 1] * other[:, 0] - own[:, 0] * other[:, 1]
        columns.append(jnp.stack([real, imag], axis=1).reshape(rows, LANES).astype(BF16))
    both = mm(inv_ref[...], jnp.concatenate(columns, axis=1))
    lags = both[:LAGS] + both[LAGS:]
    for o in range(noff):
        lags_ref[o] = lags[:, o * LANES : (o + 1) * LANES]
    owners = len(out_refs)
    each = noff // owners
    place = lax.axis_index("seg")
    for r in range(owners):
        first = partner_of(place, r, owners) * each
        out_refs[r][...] = lags_ref[pl.ds(first, each)].astype(BF16)


def turn_kernel(*refs):
    near_ref = refs[-1]
    total = sum(ref[...].astype(F32) for ref in refs[:-1])
    for t in range(near_ref.shape[1]):
        near_ref[:, t, :] = total[t].T


def loop_kernel(partner_ref, count_ref, flip_ref, pack_ref, white_ref, out_ref, turned_ref):
    blocks, segs, _, bins, _ = white_ref.shape
    owners = out_ref.shape[1]
    slots = partner_ref.shape[1]
    rows = segs * 2 * bins
    packed_rows = 2 * bins // owners
    flats = [white_ref[b].reshape(rows, LANES) for b in range(blocks)]
    turned_ref[...] = mm(jnp.concatenate(flats, axis=0), flip_ref[...]).reshape(turned_ref.shape)
    loops = []
    for b in range(blocks):
        own = flats[b].astype(F32).reshape(segs, 2, bins, LANES)
        for k in range(slots):
            partner = jnp.clip(partner_ref[b, k], 0, blocks - 1)
            live = (k < count_ref[b]).astype(F32)
            far = turned_ref[partner].reshape(segs, 2, bins, LANES)
            real = jnp.sum(own[:, 0] * far[:, 0] + own[:, 1] * far[:, 1], axis=0)
            imag = jnp.sum(own[:, 1] * far[:, 0] - own[:, 0] * far[:, 1], axis=0)
            pair = jnp.concatenate([real, imag], axis=0) * live
            groups = [pair[g * packed_rows : (g + 1) * packed_rows] for g in range(owners)]
            loops.append(jnp.concatenate(groups, axis=1))
    packed = mm(jnp.concatenate(loops, axis=0).astype(BF16), pack_ref[...])
    depth = slots * packed_rows
    for b in range(blocks):
        for q in range(owners):
            tile = packed[b * depth : (b + 1) * depth, q * LANES : (q + 1) * LANES]
            out_ref[b, q] = tile.astype(BF16)


def loop_lag_kernel(slots, spec_ref, inv_ref, loop_ref):
    sources = spec_ref.shape[0]
    step = spec_ref.shape[1] // slots
    share = loop_ref.shape[0] // slots
    loop = spec_ref[...].astype(F32)
    rows = []
    for k in range(slots):
        turned = loop[:, k * step : (k + 1) * step].reshape(sources * step, LANES).T
        groups = [turned[g * share : (g + 1) * share] for g in range(LANES // share)]
        rows.append(jnp.concatenate(groups, axis=1))
    both = mm(jnp.concatenate(rows, axis=0).astype(BF16), inv_ref[...])
    loop_ref[...] = both[:, :LAGS] + both[:, LAGS:]


def vmem(count):
    return [pl.BlockSpec(memory_space=pltpu.VMEM)] * count


def smem(count):
    return [pl.BlockSpec(memory_space=pltpu.SMEM)] * count


def hbm(count):
    return [pl.BlockSpec(memory_space=pltpu.HBM)] * count


def in_hbm(array):
    return pltpu.with_memory_space_constraint(jnp.asarray(array), pltpu.HBM)


def loops_plain(white, loop_partner, loop_count, owners, inverse):
    blocks, _, _, bins, chans = white.shape
    devices = blocks * owners
    slots = loop_partner.shape[1]
    share = chans // owners
    wide = white.astype(F32)
    loops = []
    for k in range(slots):
        far = jnp.flip(wide[loop_partner[:, k]], axis=4)
        live = (k < loop_count).astype(F32)[:, None, None]
        real = jnp.sum(wide[:, :, 0] * far[:, :, 0] + wide[:, :, 1] * far[:, :, 1], axis=1)
        imag = jnp.sum(wide[:, :, 1] * far[:, :, 0] - wide[:, :, 0] * far[:, :, 1], axis=1)
        pair = (jnp.stack([real, imag]) * live[None]).astype(BF16)
        loops.append(pair.reshape(2, blocks, bins, owners, share))
    loop = jnp.transpose(jnp.stack(loops), (2, 4, 0, 1, 3, 5))
    loop = loop.reshape(devices, slots, 2 * bins, share)
    summed = lax.all_to_all(loop, ("chan", "seg"), 0, 0, tiled=True).astype(F32)
    table = inverse.astype(np.float32).reshape(LAGS, devices, 2 * bins)
    lags = jnp.einsum("dtvc,ldv->tcl", summed, table, precision=lax.Precision.HIGHEST)
    return lags[None]


def body(recording, filter_taps, offsets, loop_partner, loop_count):
    chan_count = lax.axis_size("chan")
    seg_count = lax.axis_size("seg")
    devices = chan_count * seg_count
    bins = BINS // devices
    chans, length = recording.shape
    noff, slots = offsets.shape[0], loop_partner.shape[1]
    share = chans // seg_count
    near_each = noff // seg_count
    assert length == NFFT * DECIM and chans == LANES and noff % seg_count == 0

    route = [(i, i + 1) for i in range(seg_count - 1)]
    rim = pl.pallas_call(
        rim_kernel,
        out_shape=jax.ShapeDtypeStruct((chans // 2, LANES), F32),
        in_specs=hbm(1),
        out_specs=pl.BlockSpec(memory_space=pltpu.VMEM),
        scratch_shapes=[pltpu.VMEM((chans, LANES), F32), pltpu.SemaphoreType.DMA],
        compiler_params=PARAMS,
        cost_estimate=pl.CostEstimate(
            flops=10_000_000_000, bytes_accessed=20_000_000, transcendentals=0
        ),
        name="history",
    )(in_hbm(recording))
    rim = lax.ppermute(rim, "seg", route)
    taps = filter_taps.reshape(1, TAPS)
    spec, mean, head = pl.pallas_call(
        spectrum_kernel,
        out_shape=[
            jax.ShapeDtypeStruct((2 * BINS, LANES), F32),
            jax.ShapeDtypeStruct((LANES, LANES), F32),
            jax.ShapeDtypeStruct((GROUP, LANES), F32),
        ],
        in_specs=vmem(4),
        out_specs=vmem(3),
        compiler_params=PARAMS,
        cost_estimate=pl.CostEstimate(
            flops=1_000_000_000, bytes_accessed=5_000_000, transcendentals=0
        ),
        name="filter_and_transform",
    )(taps, recording, short_table(), twiddle_table())

    band, band_share = band_tables()
    half = jax.ShapeDtypeStruct((BINS, LANES), BF16)
    white, up, down = pl.pallas_call(
        whiten_kernel,
        out_shape=[pltpu.VMEM((GROUPS, 2, GROUP, LANES), BF16), half, half],
        in_specs=vmem(7),
        out_specs=vmem(3),
        compiler_params=PARAMS,
        name="whiten",
    )(spec, rim, mean, head, edge_table(), band, band_share)

    white, offsets = lax.optimization_barrier((white, offsets))
    spread = white
    if bins != GROUP:
        spread = jnp.moveaxis(white, 1, 0).reshape(2, devices, bins, LANES)
        spread = jnp.moveaxis(spread, 0, 1)
    moved = lax.all_to_all(spread, ("chan", "seg"), 0, 0, tiled=True)
    moved = moved.reshape(chan_count, seg_count, 2, bins, LANES)

    ring = [(i, (i + 1) % chan_count) for i in range(chan_count)]
    before = lax.ppermute(up, "chan", ring)
    after = lax.ppermute(down, "chan", [(j, i) for i, j in ring])
    moves = pl.pallas_call(
        moves_kernel,
        out_shape=jax.ShapeDtypeStruct((2 * LANES, noff * LANES), BF16),
        in_specs=smem(1),
        out_specs=pl.BlockSpec(memory_space=pltpu.VMEM),
        compiler_params=PARAMS,
        name="offset_moves",
    )(offsets)
    order = np.repeat(bin_order().reshape(GROUPS, 1, GROUP), 2, axis=1).reshape(-1)
    part = np.broadcast_to(np.arange(2).reshape(1, 2, 1), (GROUPS, 2, GROUP)).reshape(-1)
    inverse = np.concatenate(split_np(inverse_table(seg_count, order, part)), axis=0)
    lags = pl.pallas_call(
        near_kernel,
        out_shape=[jax.ShapeDtypeStruct((near_each, LAGS, LANES), BF16)] * seg_count,
        in_specs=vmem(5),
        out_specs=vmem(seg_count),
        scratch_shapes=[pltpu.VMEM((noff, LAGS, LANES), F32)],
        compiler_params=PARAMS,
        cost_estimate=pl.CostEstimate(
            flops=20_000_000_000, bytes_accessed=20_000_000, transcendentals=0
        ),
        name="near_lags",
    )(white, before, after, moves, inverse)
    moved, *lags = lax.optimization_barrier((moved, *lags))

    if bins % GROUP or 2 * bins % (8 * seg_count):
        order = np.repeat(bin_order().reshape(devices, 1, bins), 2, axis=1).reshape(-1)
        part = np.broadcast_to(np.arange(2).reshape(1, 2, 1), (devices, 2, bins)).reshape(-1)
        loop_inverse = inverse_table(seg_count, order, part)
        loop = loops_plain(moved, loop_partner, loop_count, seg_count, loop_inverse)
    else:
        flip = np.eye(LANES, dtype=np.float32)[::-1].astype(jnp.bfloat16)
        out_rows = slots * (2 * bins // seg_count)
        crossed = pl.pallas_call(
            loop_kernel,
            out_shape=pltpu.VMEM((chan_count, seg_count, out_rows, LANES), BF16),
            in_specs=smem(2) + vmem(3),
            out_specs=pl.BlockSpec(memory_space=pltpu.VMEM),
            scratch_shapes=[pltpu.VMEM((chan_count, seg_count * 2 * bins, LANES), F32)],
            compiler_params=PARAMS,
            name="loop_spectra",
        )(loop_partner, loop_count, flip, pack_matrix(seg_count), moved)
        crossed, *lags = lax.optimization_barrier((crossed, *lags))
        crossed = crossed.reshape(devices, out_rows, LANES)
        summed = lax.all_to_all(crossed, ("chan", "seg"), 0, 0, tiled=True)
        columns = np.arange(2 * BINS).reshape(devices, seg_count, -1).swapaxes(0, 1).reshape(-1)
        loop_inverse = inverse_table(seg_count, order[columns], part[columns]).T
        loop_inverse = np.concatenate(split_np(loop_inverse), axis=1)
        loop = pl.pallas_call(
            functools.partial(loop_lag_kernel, slots),
            out_shape=jax.ShapeDtypeStruct((slots * share, LAGS), F32),
            in_specs=vmem(2),
            out_specs=pl.BlockSpec(memory_space=pltpu.VMEM),
            compiler_params=PARAMS,
            name="loop_lags",
        )(summed, loop_inverse)
        loop = loop.reshape(1, slots, share, LAGS)
    for r in range(seg_count - 1, 0, -1):
        route = [(i, partner_of(i, r, seg_count)) for i in range(seg_count)]
        lags[r] = lax.ppermute(lags[r], "seg", route)
    near = pl.pallas_call(
        turn_kernel,
        out_shape=jax.ShapeDtypeStruct((chans, near_each, LAGS), F32),
        in_specs=vmem(seg_count),
        out_specs=pl.BlockSpec(memory_space=pltpu.VMEM),
        compiler_params=PARAMS,
        name="near_turn",
    )(*lags)
    return near, loop


def solution(mesh):
    in_specs = (P("chan", "seg"), P(), P(), P(), P())
    out_specs = (P("chan", "seg", None), P("chan", None, "seg", None))
    return jax.shard_map(body, mesh=mesh, in_specs=in_specs, out_specs=out_specs, check_vma=False)
```

```python
import functools
import math

import jax
import jax.numpy as jnp
import numpy as np
from jax import lax
from jax.experimental import pallas as pl
from jax.experimental.pallas import tpu as pltpu
from jax.sharding import PartitionSpec as P

NFFT = 1024
LAGS = 256
TAPS = 64
DECIM = 4
HALFBAND = 10
SPAN = 64
BINS = 512
WATER = 0.2

LANES = 128
GROUP = 16
GROUPS = BINS // GROUP
OUT_BLOCK = 128
STEP = OUT_BLOCK * DECIM
RADIX = 4
DEPTH = NFFT // RADIX
FAR_BINS = BINS // RADIX

F32 = jnp.float32
BF16 = jnp.bfloat16
MIB = 1024 * 1024
PARAMS = pltpu.CompilerParams(vmem_limit_bytes=32 * MIB)


def bin_order():
    return np.concatenate([np.arange(r, BINS, RADIX) for r in range(RADIX)])


def split_np(table):
    high = table.astype(jnp.bfloat16)
    low = (table - high.astype(np.float64)).astype(jnp.bfloat16)
    return high, low


def short_table():
    bins = np.arange(FAR_BINS).reshape(-1, 1, GROUP, 1)
    angles = (bins * np.arange(DEPTH) % DEPTH) * (2.0 * np.pi / DEPTH)
    rows = np.concatenate([np.cos(angles), np.sin(angles)], axis=1).reshape(-1, DEPTH)
    high, low = split_np(rows)
    return np.concatenate([high, high, low], axis=1)


def twiddle_table():
    angles = np.arange(DEPTH)[:, None] * np.arange(1, RADIX) * (2.0 * np.pi / NFFT)
    columns = np.stack([np.cos(angles), np.sin(angles)], axis=2).reshape(DEPTH, -1)
    return np.pad(columns, ((0, 0), (0, LANES - columns.shape[1]))).astype(np.float32)


def edge_table():
    bins = bin_order().reshape(GROUPS, 1, GROUP, 1)
    angles = (bins * np.arange(GROUP) % NFFT) * (2.0 * np.pi / NFFT)
    rows = np.concatenate([np.cos(angles), -np.sin(angles)], axis=1) * (bins != 0)
    high, low = split_np(rows.reshape(2 * BINS, GROUP))
    table = np.concatenate([high, high, low], axis=1)
    return np.pad(table.astype(np.float32), ((0, 0), (0, LANES - 3 * GROUP))).astype(jnp.bfloat16)


def inverse_table(total_segs, bins, part):
    lag = np.arange(LAGS) - LAGS // 2
    angles = (bins[None, :] * lag[:, None] % NFFT) * (2.0 * np.pi / NFFT)
    weights = np.where(bins == 0, 1.0, 2.0) / math.sqrt(2.0 * BINS * total_segs)
    return np.where(part[None, :] == 1, -np.sin(angles), np.cos(angles)) * weights[None, :]


def band_tables():
    bins = bin_order()
    inside = np.abs(bins[:, None] - bins[None, :]) <= HALFBAND
    share = np.broadcast_to(1.0 / inside.sum(axis=1, keepdims=True), (BINS, LANES))
    return inside.astype(jnp.bfloat16), share.astype(np.float32)


def split(value):
    high = value.astype(BF16)
    return high, (value - high.astype(F32)).astype(BF16)


def mm(a, b):
    return jnp.dot(a, b, preferred_element_type=F32)


def mm_nt(a, b):
    return lax.dot_general(a, b, (((1,), (1,)), ((), ())), preferred_element_type=F32)


def tap_rows(taps):
    width = LANES + STEP
    square = (TAPS, TAPS)
    diagonal = lax.broadcasted_iota(jnp.int32, square, 0) == lax.broadcasted_iota(jnp.int32, square, 1)
    column_taps = jnp.sum(jnp.where(diagonal, taps, 0.0), axis=1, keepdims=True)
    tap = lax.broadcasted_iota(jnp.int32, (TAPS, width), 0)
    column = lax.broadcasted_iota(jnp.int32, (TAPS, width), 1)
    placed = jnp.where(column == LANES + DECIM - 1 - tap, column_taps, 0.0)
    spread = jnp.broadcast_to(jnp.sum(placed, axis=0, keepdims=True), (OUT_BLOCK, width))
    return pltpu.roll(spread, 0, 1, stride=DECIM, stride_axis=0)


def rim_kernel(rec_hbm, rim_ref, tail_ref, sem):
    length = rec_hbm.shape[1]
    copy = pltpu.make_async_copy(rec_hbm.at[:, pl.ds(length - LANES, LANES)], tail_ref, sem)
    copy.start()
    copy.wait()
    upper, lower = tail_ref[: LANES // 2], tail_ref[LANES // 2 :]
    lane = lax.broadcasted_iota(jnp.int32, lower.shape, 1)
    rim_ref[...] = jnp.where(lane < TAPS, pltpu.roll(upper, LANES - TAPS, 1), lower)


def spectrum_kernel(taps_ref, rec_ref, tab_ref, twist_ref, spec_ref, mean_ref, head_ref):
    blocks = rec_ref.shape[1] // STEP
    table = tap_rows(taps_ref[...])
    head_ref[...] = table[:GROUP, :LANES]
    taps_high, taps_low = split(table.T)
    taps_both = jnp.concatenate([taps_high, taps_low], axis=1)
    before = [jnp.zeros((LANES, LANES), BF16)] * 2
    outputs = []
    for first in range(0, blocks, blocks // 2):
        windows = ([], [])
        for j in range(first, first + blocks // 2):
            chunk = rec_ref[:, j * STEP : (j + 1) * STEP]
            if j == 0:
                mean = jnp.sum(chunk, axis=1, keepdims=True) * (1.0 / STEP)
            for i, value in enumerate(split(chunk - mean)):
                windows[i].append(jnp.concatenate([before[i], value], axis=1))
                before[i] = value[:, STEP - LANES :]
        wide = mm(jnp.concatenate(windows[0], axis=0), taps_both)
        rest = mm(jnp.concatenate(windows[1], axis=0), taps_high)
        total = wide[:, :LANES] + wide[:, LANES:] + rest
        outputs += [total[t * LANES : (t + 1) * LANES].T for t in range(blocks // 2)]
    pieces = [jnp.concatenate(outputs[j : j + 2], axis=0) for j in range(0, blocks, 2)]
    mean_ref[...] = jnp.broadcast_to(mean, mean_ref.shape)
    even, odd = pieces[0] + pieces[2], pieces[1] + pieces[3]
    a, b = pieces[0] - pieces[2], pieces[1] - pieces[3]
    whole, half = even + odd, even - odd
    whole = whole - jnp.sum(whole, axis=0, keepdims=True) * (1.0 / DEPTH)
    c1, s1, c2, s2, c3, s3 = [twist_ref[:, i : i + 1] for i in range(6)]
    inputs = [
        whole,
        a * c1 - b * s1,
        -(a * s1 + b * c1),
        half * c2,
        -(half * s2),
        a * c3 + b * s3,
        b * c3 - a * s3,
    ]
    parts = [split(value) for value in inputs]
    high = jnp.concatenate([p[0] for p in parts], axis=1)
    low = jnp.concatenate([p[1] for p in parts], axis=1)
    out = mm(tab_ref[...], jnp.concatenate([high, low, high], axis=0))
    out = out.reshape(FAR_BINS // GROUP, 2, GROUP, out.shape[1])
    rows = 2 * FAR_BINS
    for r in range(RADIX):
        first = max(2 * r - 1, 0) * LANES
        real_in = out[..., first : first + LANES]
        if r == 0:
            real, imag = real_in[:, 0], -real_in[:, 1]
        else:
            imag_in = out[..., first + LANES : first + 2 * LANES]
            real, imag = real_in[:, 0] + imag_in[:, 1], imag_in[:, 0] - real_in[:, 1]
        both = jnp.stack([real, imag], axis=1).reshape(rows, LANES)
        spec_ref[r * rows : (r + 1) * rows, :] = both


def whiten_kernel(
    spec_ref,
    rim_ref,
    mean_ref,
    head_ref,
    edge_ref,
    band_ref,
    share_ref,
    white_ref,
    up_ref,
    down_ref,
):
    head_high, head_low = split(head_ref[...])
    rim = jnp.concatenate([pltpu.roll(rim_ref[...], LANES - TAPS, 1), rim_ref[...]], axis=0)
    rim_high, rim_low = split(rim - mean_ref[...])
    history = mm_nt(
        jnp.concatenate([head_high, head_high, head_low], axis=1),
        jnp.concatenate([rim_high, rim_low, rim_high], axis=1),
    )
    high, low = split(history)
    stacked = jnp.concatenate([high, low, high], axis=0)
    spec = spec_ref[...] + mm(edge_ref[:, : 3 * GROUP], stacked)
    parted = spec.reshape(GROUPS, 2, GROUP, LANES)
    real, imag = parted[:, 0], parted[:, 1]
    amplitude = jnp.sqrt(real * real + imag * imag).reshape(BINS, LANES)
    high, low = split(amplitude)
    wide = mm(band_ref[...], jnp.concatenate([high, low], axis=1))
    smoothed = (wide[:, :LANES] + wide[:, LANES:]) * share_ref[...]
    level = jnp.sum(amplitude, axis=0, keepdims=True) * (1.0 / BINS)
    scale = 1.0 / (smoothed + (WATER * level + 1e-06))
    white = parted * scale.reshape(GROUPS, 1, GROUP, LANES)
    white_ref[...] = white.astype(BF16)
    flat = white.reshape(2 * BINS, LANES)
    turned = pltpu.roll(flat, SPAN, 1)
    lane = lax.broadcasted_iota(jnp.int32, (BINS, LANES), 1)
    up_ref[...] = jnp.where(lane < SPAN, turned[:BINS], flat[BINS:]).astype(BF16)
    down_ref[...] = jnp.where(lane < SPAN, flat[:BINS], turned[BINS:]).astype(BF16)


def offset_moves(offs_ref):
    row = lax.broadcasted_iota(jnp.int32, (2 * LANES, LANES), 0)
    channel = lax.broadcasted_iota(jnp.int32, (2 * LANES, LANES), 1)
    distance = jnp.where(row < LANES + SPAN, row, row - 2 * LANES) - channel
    hits = [(distance == offs_ref[o]).astype(F32) for o in range(offs_ref.shape[0])]
    return jnp.concatenate(hits, axis=1).astype(BF16)


def pack_matrix(owners):
    share = LANES // owners
    matrix = np.zeros((owners, owners, share, owners, owners, share), np.float32)
    for group in range(owners):
        for owner in range(owners):
            matrix[group, owner, :, owner, group, :] = np.eye(share)
    return matrix.reshape(owners * LANES, owners * LANES).astype(jnp.bfloat16)


def partner_of(place, r, owners):
    return place ^ r if owners & (owners - 1) == 0 else (place + r) % owners


def near_kernel(offs_ref, white_ref, before_ref, after_ref, inv_ref, *refs):
    out_refs, lags_ref = refs[:-1], refs[-1]
    rows = white_ref.shape[0] * 2 * GROUP
    half = rows // 2
    noff = lags_ref.shape[0]
    before, after = before_ref[...].astype(F32), after_ref[...].astype(F32)
    lane = lax.broadcasted_iota(jnp.int32, (half, LANES), 1)
    upper = jnp.where(lane < SPAN, after, pltpu.roll(before, SPAN, 1))
    lower = jnp.where(lane < SPAN, pltpu.roll(after, SPAN, 1), before)
    edge = jnp.concatenate([upper, lower], axis=0).astype(BF16)
    own = white_ref[...].reshape(rows, LANES)
    far = mm(jnp.concatenate([own, edge], axis=1), offset_moves(offs_ref))
    own = own.astype(F32).reshape(-1, 2, GROUP, LANES)
    columns = []
    for o in range(noff):
        other = far[:, o * LANES : (o + 1) * LANES].reshape(own.shape)
        real = own[:, 0] * other[:, 0] + own[:, 1] * other[:, 1]
        imag = own[:, 1] * other[:, 0] - own[:, 0] * other[:, 1]
        columns.append(jnp.stack([real, imag], axis=1).reshape(rows, LANES).astype(BF16))
    both = mm(inv_ref[...], jnp.concatenate(columns, axis=1))
    lags = both[:LAGS] + both[LAGS:]
    for o in range(noff):
        lags_ref[o] = lags[:, o * LANES : (o + 1) * LANES]
    owners = len(out_refs)
    each = noff // owners
    place = lax.axis_index("seg")
    for r in range(owners):
        first = partner_of(place, r, owners) * each
        out_refs[r][...] = lags_ref[pl.ds(first, each)].astype(BF16)


def turn_kernel(*refs):
    near_ref = refs[-1]
    total = sum(ref[...].astype(F32) for ref in refs[:-1])
    for t in range(near_ref.shape[1]):
        near_ref[:, t, :] = total[t].T


def loop_kernel(partner_ref, count_ref, flip_ref, pack_ref, white_ref, out_ref, turned_ref):
    blocks, segs, _, bins, _ = white_ref.shape
    owners = out_ref.shape[1]
    slots = partner_ref.shape[0]
    rows = segs * 2 * bins
    packed_rows = 2 * bins // owners
    flats = [white_ref[b].reshape(rows, LANES) for b in range(blocks)]
    turned_ref[...] = mm(jnp.concatenate(flats, axis=0), flip_ref[...]).reshape(turned_ref.shape)
    loops = []
    for b in range(blocks):
        own = flats[b].astype(F32).reshape(segs, 2, bins, LANES)
        for k in range(slots):
            partner = jnp.clip(partner_ref[k, b], 0, blocks - 1)
            live = (k < count_ref[b]).astype(F32)
            far = turned_ref[partner].reshape(segs, 2, bins, LANES)
            real = jnp.sum(own[:, 0] * far[:, 0] + own[:, 1] * far[:, 1], axis=0)
            imag = jnp.sum(own[:, 1] * far[:, 0] - own[:, 0] * far[:, 1], axis=0)
            pair = jnp.concatenate([real, imag], axis=0) * live
            groups = [pair[g * packed_rows : (g + 1) * packed_rows] for g in range(owners)]
            loops.append(jnp.concatenate(groups, axis=1))
    packed = mm(jnp.concatenate(loops, axis=0).astype(BF16), pack_ref[...])
    depth = slots * packed_rows
    for b in range(blocks):
        for q in range(owners):
            tile = packed[b * depth : (b + 1) * depth, q * LANES : (q + 1) * LANES]
            out_ref[b, q] = tile.astype(BF16)


def loop_lag_kernel(slots, spec_ref, inv_ref, loop_ref):
    sources = spec_ref.shape[0]
    step = spec_ref.shape[1] // slots
    share = loop_ref.shape[0] // slots
    loop = spec_ref[...].astype(F32)
    rows = []
    for k in range(slots):
        turned = loop[:, k * step : (k + 1) * step].reshape(sources * step, LANES).T
        groups = [turned[g * share : (g + 1) * share] for g in range(LANES // share)]
        rows.append(jnp.concatenate(groups, axis=1))
    both = mm(jnp.concatenate(rows, axis=0).astype(BF16), inv_ref[...])
    loop_ref[...] = both[:, :LAGS] + both[:, LAGS:]


def vmem(count):
    return [pl.BlockSpec(memory_space=pltpu.VMEM)] * count


def smem(count):
    return [pl.BlockSpec(memory_space=pltpu.SMEM)] * count


def hbm(count):
    return [pl.BlockSpec(memory_space=pltpu.HBM)] * count


def in_hbm(array):
    return pltpu.with_memory_space_constraint(jnp.asarray(array), pltpu.HBM)


def loops_plain(white, loop_partner, loop_count, owners, inverse):
    blocks, _, _, bins, chans = white.shape
    devices = blocks * owners
    slots = loop_partner.shape[1]
    share = chans // owners
    wide = white.astype(F32)
    loops = []
    for k in range(slots):
        far = jnp.flip(wide[loop_partner[:, k]], axis=4)
        live = (k < loop_count).astype(F32)[:, None, None]
        real = jnp.sum(wide[:, :, 0] * far[:, :, 0] + wide[:, :, 1] * far[:, :, 1], axis=1)
        imag = jnp.sum(wide[:, :, 1] * far[:, :, 0] - wide[:, :, 0] * far[:, :, 1], axis=1)
        pair = (jnp.stack([real, imag]) * live[None]).astype(BF16)
        loops.append(pair.reshape(2, blocks, bins, owners, share))
    loop = jnp.transpose(jnp.stack(loops), (2, 4, 0, 1, 3, 5))
    loop = loop.reshape(devices, slots, 2 * bins, share)
    summed = lax.all_to_all(loop, ("chan", "seg"), 0, 0, tiled=True).astype(F32)
    table = inverse.astype(np.float32).reshape(LAGS, devices, 2 * bins)
    lags = jnp.einsum("dtvc,ldv->tcl", summed, table, precision=lax.Precision.HIGHEST)
    return lags[None]


def body(recording, filter_taps, offsets, loop_partner, loop_count):
    chan_count = lax.axis_size("chan")
    seg_count = lax.axis_size("seg")
    devices = chan_count * seg_count
    bins = BINS // devices
    chans, length = recording.shape
    noff, slots = offsets.shape[0], loop_partner.shape[1]
    share = chans // seg_count
    near_each = noff // seg_count
    assert length == NFFT * DECIM and chans == LANES and noff % seg_count == 0

    route = [(i, i + 1) for i in range(seg_count - 1)]
    rim = pl.pallas_call(
        rim_kernel,
        out_shape=jax.ShapeDtypeStruct((chans // 2, LANES), F32),
        in_specs=hbm(1),
        out_specs=pl.BlockSpec(memory_space=pltpu.VMEM),
        scratch_shapes=[pltpu.VMEM((chans, LANES), F32), pltpu.SemaphoreType.DMA],
        compiler_params=PARAMS,
        cost_estimate=pl.CostEstimate(
            flops=10_000_000_000, bytes_accessed=20_000_000, transcendentals=0
        ),
        name="history",
    )(in_hbm(recording))
    rim = lax.ppermute(rim, "seg", route)
    taps = filter_taps.reshape(1, TAPS)
    spec, mean, head = pl.pallas_call(
        spectrum_kernel,
        out_shape=[
            jax.ShapeDtypeStruct((2 * BINS, LANES), F32),
            jax.ShapeDtypeStruct((LANES, LANES), F32),
            jax.ShapeDtypeStruct((GROUP, LANES), F32),
        ],
        in_specs=vmem(4),
        out_specs=vmem(3),
        compiler_params=PARAMS,
        cost_estimate=pl.CostEstimate(
            flops=1_000_000_000, bytes_accessed=5_000_000, transcendentals=0
        ),
        name="filter_and_transform",
    )(taps, recording, short_table(), twiddle_table())

    band, band_share = band_tables()
    half = jax.ShapeDtypeStruct((BINS, LANES), BF16)
    white, up, down = pl.pallas_call(
        whiten_kernel,
        out_shape=[jax.ShapeDtypeStruct((GROUPS, 2, GROUP, LANES), BF16), half, half],
        in_specs=vmem(7),
        out_specs=vmem(3),
        compiler_params=PARAMS,
        name="whiten",
    )(spec, rim, mean, head, edge_table(), band, band_share)

    spread = white
    if bins != GROUP:
        spread = jnp.moveaxis(white, 1, 0).reshape(2, devices, bins, LANES)
        spread = jnp.moveaxis(spread, 0, 1)
    moved = lax.all_to_all(spread, ("chan", "seg"), 0, 0, tiled=True)
    moved = moved.reshape(chan_count, seg_count, 2, bins, LANES)

    ring = [(i, (i + 1) % chan_count) for i in range(chan_count)]
    before = lax.ppermute(up, "chan", ring)
    after = lax.ppermute(down, "chan", [(j, i) for i, j in ring])
    order = np.repeat(bin_order().reshape(GROUPS, 1, GROUP), 2, axis=1).reshape(-1)
    part = np.broadcast_to(np.arange(2).reshape(1, 2, 1), (GROUPS, 2, GROUP)).reshape(-1)
    inverse = np.concatenate(split_np(inverse_table(seg_count, order, part)), axis=0)
    lags = pl.pallas_call(
        near_kernel,
        out_shape=[jax.ShapeDtypeStruct((near_each, LAGS, LANES), BF16)] * seg_count,
        in_specs=smem(1) + vmem(4),
        out_specs=vmem(seg_count),
        scratch_shapes=[pltpu.VMEM((noff, LAGS, LANES), F32)],
        compiler_params=PARAMS,
        cost_estimate=pl.CostEstimate(
            flops=20_000_000_000, bytes_accessed=20_000_000, transcendentals=0
        ),
        name="near_lags",
    )(offsets, white, before, after, inverse)
    moved, *lags = lax.optimization_barrier((moved, *lags))

    if bins % GROUP or 2 * bins % (8 * seg_count):
        order = np.repeat(bin_order().reshape(devices, 1, bins), 2, axis=1).reshape(-1)
        part = np.broadcast_to(np.arange(2).reshape(1, 2, 1), (devices, 2, bins)).reshape(-1)
        loop_inverse = inverse_table(seg_count, order, part)
        loop = loops_plain(moved, loop_partner, loop_count, seg_count, loop_inverse)
    else:
        flip = np.eye(LANES, dtype=np.float32)[::-1].astype(jnp.bfloat16)
        out_rows = slots * (2 * bins // seg_count)
        crossed = pl.pallas_call(
            loop_kernel,
            out_shape=jax.ShapeDtypeStruct((chan_count, seg_count, out_rows, LANES), BF16),
            in_specs=smem(2) + vmem(3),
            out_specs=pl.BlockSpec(memory_space=pltpu.VMEM),
            scratch_shapes=[pltpu.VMEM((chan_count, seg_count * 2 * bins, LANES), F32)],
            compiler_params=PARAMS,
            name="loop_spectra",
        )(loop_partner.T, loop_count, flip, pack_matrix(seg_count), moved)
        crossed = crossed.reshape(devices, out_rows, LANES)
        summed = lax.all_to_all(crossed, ("chan", "seg"), 0, 0, tiled=True)
        columns = np.arange(2 * BINS).reshape(devices, seg_count, -1).swapaxes(0, 1).reshape(-1)
        loop_inverse = inverse_table(seg_count, order[columns], part[columns]).T
        loop_inverse = np.concatenate(split_np(loop_inverse), axis=1)
        loop = pl.pallas_call(
            functools.partial(loop_lag_kernel, slots),
            out_shape=jax.ShapeDtypeStruct((slots * share, LAGS), F32),
            in_specs=vmem(2),
            out_specs=pl.BlockSpec(memory_space=pltpu.VMEM),
            compiler_params=PARAMS,
            name="loop_lags",
        )(summed, loop_inverse)
        loop = loop.reshape(1, slots, share, LAGS)
    for r in range(seg_count - 1, 0, -1):
        route = [(i, partner_of(i, r, seg_count)) for i in range(seg_count)]
        lags[r] = lax.ppermute(lags[r], "seg", route)
    near = pl.pallas_call(
        turn_kernel,
        out_shape=jax.ShapeDtypeStruct((chans, near_each, LAGS), F32),
        in_specs=vmem(seg_count),
        out_specs=pl.BlockSpec(memory_space=pltpu.VMEM),
        compiler_params=PARAMS,
        name="near_turn",
    )(*lags)
    return near, loop


def solution(mesh):
    in_specs = (P("chan", "seg"), P(), P(), P(), P())
    out_specs = (P("chan", "seg", None), P("chan", None, "seg", None))
    return jax.shard_map(body, mesh=mesh, in_specs=in_specs, out_specs=out_specs, check_vma=False)
```

```python
import functools
import math

import jax
import jax.numpy as jnp
import numpy as np
from jax import lax
from jax.experimental import pallas as pl
from jax.experimental.pallas import tpu as pltpu
from jax.sharding import PartitionSpec as P

NFFT = 1024
LAGS = 256
TAPS = 64
DECIM = 4
HALFBAND = 10
SPAN = 64
BINS = 512
WATER = 0.2

LANES = 128
GROUP = 16
GROUPS = BINS // GROUP
OUT_BLOCK = 128
STEP = OUT_BLOCK * DECIM
RADIX = 4
DEPTH = NFFT // RADIX
FAR_BINS = BINS // RADIX

F32 = jnp.float32
BF16 = jnp.bfloat16
MIB = 1024 * 1024
PARAMS = pltpu.CompilerParams(vmem_limit_bytes=32 * MIB)


def bin_order():
    return np.concatenate([np.arange(r, BINS, RADIX) for r in range(RADIX)])


def split_np(table):
    high = table.astype(jnp.bfloat16)
    low = (table - high.astype(np.float64)).astype(jnp.bfloat16)
    return high, low


def short_table():
    bins = np.arange(FAR_BINS).reshape(-1, 1, GROUP, 1)
    angles = (bins * np.arange(DEPTH) % DEPTH) * (2.0 * np.pi / DEPTH)
    rows = np.concatenate([np.cos(angles), np.sin(angles)], axis=1).reshape(-1, DEPTH)
    high, low = split_np(rows)
    return np.concatenate([high, high, low], axis=1)


def twiddle_table():
    angles = np.arange(DEPTH)[:, None] * np.arange(1, RADIX) * (2.0 * np.pi / NFFT)
    columns = np.stack([np.cos(angles), np.sin(angles)], axis=2).reshape(DEPTH, -1)
    return np.pad(columns, ((0, 0), (0, LANES - columns.shape[1]))).astype(np.float32)


def edge_table():
    bins = bin_order().reshape(GROUPS, 1, GROUP, 1)
    angles = (bins * np.arange(GROUP) % NFFT) * (2.0 * np.pi / NFFT)
    rows = np.concatenate([np.cos(angles), -np.sin(angles)], axis=1) * (bins != 0)
    high, low = split_np(rows.reshape(2 * BINS, GROUP))
    table = np.concatenate([high, high, low], axis=1)
    return np.pad(table.astype(np.float32), ((0, 0), (0, LANES - 3 * GROUP))).astype(jnp.bfloat16)


def inverse_table(total_segs, bins, part):
    lag = np.arange(LAGS) - LAGS // 2
    angles = (bins[None, :] * lag[:, None] % NFFT) * (2.0 * np.pi / NFFT)
    weights = np.where(bins == 0, 1.0, 2.0) / math.sqrt(2.0 * BINS * total_segs)
    return np.where(part[None, :] == 1, -np.sin(angles), np.cos(angles)) * weights[None, :]


def band_tables():
    bins = bin_order()
    inside = np.abs(bins[:, None] - bins[None, :]) <= HALFBAND
    share = np.broadcast_to(1.0 / inside.sum(axis=1, keepdims=True), (BINS, LANES))
    return inside.astype(jnp.bfloat16), share.astype(np.float32)


def split(value):
    high = value.astype(BF16)
    return high, (value - high.astype(F32)).astype(BF16)


def mm(a, b):
    return jnp.dot(a, b, preferred_element_type=F32)


def mm_nt(a, b):
    return lax.dot_general(a, b, (((1,), (1,)), ((), ())), preferred_element_type=F32)


def tap_rows(taps):
    width = LANES + STEP
    square = (TAPS, TAPS)
    diagonal = lax.broadcasted_iota(jnp.int32, square, 0) == lax.broadcasted_iota(jnp.int32, square, 1)
    column_taps = jnp.sum(jnp.where(diagonal, taps, 0.0), axis=1, keepdims=True)
    tap = lax.broadcasted_iota(jnp.int32, (TAPS, width), 0)
    column = lax.broadcasted_iota(jnp.int32, (TAPS, width), 1)
    placed = jnp.where(column == LANES + DECIM - 1 - tap, column_taps, 0.0)
    spread = jnp.broadcast_to(jnp.sum(placed, axis=0, keepdims=True), (OUT_BLOCK, width))
    return pltpu.roll(spread, 0, 1, stride=DECIM, stride_axis=0)


def rim_kernel(rec_hbm, rim_ref, tail_ref, sem):
    length = rec_hbm.shape[1]
    copy = pltpu.make_async_copy(rec_hbm.at[:, pl.ds(length - LANES, LANES)], tail_ref, sem)
    copy.start()
    copy.wait()
    upper, lower = tail_ref[: LANES // 2], tail_ref[LANES // 2 :]
    lane = lax.broadcasted_iota(jnp.int32, lower.shape, 1)
    rim_ref[...] = jnp.where(lane < TAPS, pltpu.roll(upper, LANES - TAPS, 1), lower)


def spectrum_kernel(taps_ref, rec_ref, tab_ref, twist_ref, spec_ref, mean_ref, head_ref):
    blocks = rec_ref.shape[1] // STEP
    table = tap_rows(taps_ref[...])
    head_ref[...] = table[:GROUP, :LANES]
    taps_high, taps_low = split(table.T)
    taps_both = jnp.concatenate([taps_high, taps_low], axis=1)
    before = [jnp.zeros((LANES, LANES), BF16)] * 2
    outputs = []
    for first in range(0, blocks, blocks // 2):
        windows = ([], [])
        for j in range(first, first + blocks // 2):
            chunk = rec_ref[:, j * STEP : (j + 1) * STEP]
            if j == 0:
                mean = jnp.sum(chunk, axis=1, keepdims=True) * (1.0 / STEP)
            for i, value in enumerate(split(chunk - mean)):
                windows[i].append(jnp.concatenate([before[i], value], axis=1))
                before[i] = value[:, STEP - LANES :]
        wide = mm(jnp.concatenate(windows[0], axis=0), taps_both)
        rest = mm(jnp.concatenate(windows[1], axis=0), taps_high)
        total = wide[:, :LANES] + wide[:, LANES:] + rest
        outputs += [total[t * LANES : (t + 1) * LANES].T for t in range(blocks // 2)]
    pieces = [jnp.concatenate(outputs[j : j + 2], axis=0) for j in range(0, blocks, 2)]
    mean_ref[...] = jnp.broadcast_to(mean, mean_ref.shape)
    even, odd = pieces[0] + pieces[2], pieces[1] + pieces[3]
    a, b = pieces[0] - pieces[2], pieces[1] - pieces[3]
    whole, half = even + odd, even - odd
    whole = whole - jnp.sum(whole, axis=0, keepdims=True) * (1.0 / DEPTH)
    c1, s1, c2, s2, c3, s3 = [twist_ref[:, i : i + 1] for i in range(6)]
    inputs = [
        whole,
        a * c1 - b * s1,
        -(a * s1 + b * c1),
        half * c2,
        -(half * s2),
        a * c3 + b * s3,
        b * c3 - a * s3,
    ]
    parts = [split(value) for value in inputs]
    high = jnp.concatenate([p[0] for p in parts], axis=1)
    low = jnp.concatenate([p[1] for p in parts], axis=1)
    out = mm(tab_ref[...], jnp.concatenate([high, low, high], axis=0))
    out = out.reshape(FAR_BINS // GROUP, 2, GROUP, out.shape[1])
    rows = 2 * FAR_BINS
    for r in range(RADIX):
        first = max(2 * r - 1, 0) * LANES
        real_in = out[..., first : first + LANES]
        if r == 0:
            real, imag = real_in[:, 0], -real_in[:, 1]
        else:
            imag_in = out[..., first + LANES : first + 2 * LANES]
            real, imag = real_in[:, 0] + imag_in[:, 1], imag_in[:, 0] - real_in[:, 1]
        both = jnp.stack([real, imag], axis=1).reshape(rows, LANES)
        spec_ref[r * rows : (r + 1) * rows, :] = both


def whiten_kernel(
    spec_ref,
    rim_ref,
    mean_ref,
    head_ref,
    edge_ref,
    band_ref,
    share_ref,
    white_hbm,
    up_ref,
    down_ref,
    white_ref,
    sems,
):
    head_high, head_low = split(head_ref[...])
    rim = jnp.concatenate([pltpu.roll(rim_ref[...], LANES - TAPS, 1), rim_ref[...]], axis=0)
    rim_high, rim_low = split(rim - mean_ref[...])
    history = mm_nt(
        jnp.concatenate([head_high, head_high, head_low], axis=1),
        jnp.concatenate([rim_high, rim_low, rim_high], axis=1),
    )
    high, low = split(history)
    stacked = jnp.concatenate([high, low, high], axis=0)
    spec = spec_ref[...] + mm(edge_ref[:, : 3 * GROUP], stacked)
    parted = spec.reshape(GROUPS, 2, GROUP, LANES)
    real, imag = parted[:, 0], parted[:, 1]
    amplitude = jnp.sqrt(real * real + imag * imag).reshape(BINS, LANES)
    high, low = split(amplitude)
    wide = mm(band_ref[...], jnp.concatenate([high, low], axis=1))
    smoothed = (wide[:, :LANES] + wide[:, LANES:]) * share_ref[...]
    level = jnp.sum(amplitude, axis=0, keepdims=True) * (1.0 / BINS)
    scale = 1.0 / (smoothed + (WATER * level + 1e-06))
    scale = scale.reshape(GROUPS, 1, GROUP, LANES)
    halves, copies = [], []
    for i in range(2):
        part = slice(i * GROUPS // 2, (i + 1) * GROUPS // 2)
        white = parted[part] * scale[part]
        white_ref[part] = white.astype(BF16)
        copies.append(pltpu.make_async_copy(white_ref.at[part], white_hbm.at[part], sems.at[i]))
        copies[i].start()
        halves.append(white.reshape(BINS, LANES))
    lane = lax.broadcasted_iota(jnp.int32, (BINS, LANES), 1)
    up_ref[...] = jnp.where(lane < SPAN, pltpu.roll(halves[0], SPAN, 1), halves[1]).astype(BF16)
    down_ref[...] = jnp.where(lane < SPAN, halves[0], pltpu.roll(halves[1], SPAN, 1)).astype(BF16)
    for copy in copies:
        copy.wait()


def offset_moves(offs_ref):
    row = lax.broadcasted_iota(jnp.int32, (2 * LANES, LANES), 0)
    channel = lax.broadcasted_iota(jnp.int32, (2 * LANES, LANES), 1)
    distance = jnp.where(row < LANES + SPAN, row, row - 2 * LANES) - channel
    hits = [(distance == offs_ref[o]).astype(F32) for o in range(offs_ref.shape[0])]
    return jnp.concatenate(hits, axis=1).astype(BF16)


def pack_matrix(owners):
    share = LANES // owners
    matrix = np.zeros((owners, owners, share, owners, owners, share), np.float32)
    for group in range(owners):
        for owner in range(owners):
            matrix[group, owner, :, owner, group, :] = np.eye(share)
    return matrix.reshape(owners * LANES, owners * LANES).astype(jnp.bfloat16)


def partner_of(place, r, owners):
    return place ^ r if owners & (owners - 1) == 0 else (place + r) % owners


def near_kernel(offs_ref, white_ref, before_ref, after_ref, inv_ref, *refs):
    out_refs, lags_ref = refs[:-1], refs[-1]
    rows = white_ref.shape[0] * 2 * GROUP
    half = rows // 2
    noff = lags_ref.shape[0]
    before, after = before_ref[...].astype(F32), after_ref[...].astype(F32)
    lane = lax.broadcasted_iota(jnp.int32, (half, LANES), 1)
    upper = jnp.where(lane < SPAN, after, pltpu.roll(before, SPAN, 1))
    lower = jnp.where(lane < SPAN, pltpu.roll(after, SPAN, 1), before)
    edge = jnp.concatenate([upper, lower], axis=0).astype(BF16)
    own = white_ref[...].reshape(rows, LANES)
    far = mm(jnp.concatenate([own, edge], axis=1), offset_moves(offs_ref))
    own = own.astype(F32).reshape(-1, 2, GROUP, LANES)
    columns = []
    for o in range(noff):
        other = far[:, o * LANES : (o + 1) * LANES].reshape(own.shape)
        real = own[:, 0] * other[:, 0] + own[:, 1] * other[:, 1]
        imag = own[:, 1] * other[:, 0] - own[:, 0] * other[:, 1]
        columns.append(jnp.stack([real, imag], axis=1).reshape(rows, LANES).astype(BF16))
    both = mm(inv_ref[...], jnp.concatenate(columns, axis=1))
    lags = both[:LAGS] + both[LAGS:]
    for o in range(noff):
        lags_ref[o] = lags[:, o * LANES : (o + 1) * LANES]
    owners = len(out_refs)
    each = noff // owners
    place = lax.axis_index("seg")
    for r in range(owners):
        first = partner_of(place, r, owners) * each
        out_refs[r][...] = lags_ref[pl.ds(first, each)].astype(BF16)


def turn_kernel(*refs):
    near_ref = refs[-1]
    total = sum(ref[...].astype(F32) for ref in refs[:-1])
    for t in range(near_ref.shape[1]):
        near_ref[:, t, :] = total[t].T


def loop_kernel(
    partner_ref, count_ref, flip_ref, pack_ref, white_ref, out_hbm, out_ref, turned_ref, sems
):
    blocks, segs, _, bins, _ = white_ref.shape
    owners = out_ref.shape[1]
    slots = partner_ref.shape[0]
    rows = segs * 2 * bins
    packed_rows = 2 * bins // owners
    flats = [white_ref[b].reshape(rows, LANES) for b in range(blocks)]
    turned_ref[...] = mm(jnp.concatenate(flats, axis=0), flip_ref[...]).reshape(turned_ref.shape)
    depth = slots * packed_rows
    copies = []
    for i in range(2):
        part = range(i * blocks // 2, (i + 1) * blocks // 2)
        loops = []
        for b in part:
            own = flats[b].astype(F32).reshape(segs, 2, bins, LANES)
            for k in range(slots):
                partner = jnp.clip(partner_ref[k, b], 0, blocks - 1)
                live = (k < count_ref[b]).astype(F32)
                far = turned_ref[partner].reshape(segs, 2, bins, LANES)
                real = jnp.sum(own[:, 0] * far[:, 0] + own[:, 1] * far[:, 1], axis=0)
                imag = jnp.sum(own[:, 1] * far[:, 0] - own[:, 0] * far[:, 1], axis=0)
                pair = jnp.concatenate([real, imag], axis=0) * live
                groups = [pair[g * packed_rows : (g + 1) * packed_rows] for g in range(owners)]
                loops.append(jnp.concatenate(groups, axis=1))
        packed = mm(jnp.concatenate(loops, axis=0).astype(BF16), pack_ref[...])
        for n, b in enumerate(part):
            for q in range(owners):
                tile = packed[n * depth : (n + 1) * depth, q * LANES : (q + 1) * LANES]
                out_ref[b, q] = tile.astype(BF16)
        place = slice(part[0], part[-1] + 1)
        copies.append(pltpu.make_async_copy(out_ref.at[place], out_hbm.at[place], sems.at[i]))
        copies[i].start()
    for copy in copies:
        copy.wait()


def loop_lag_kernel(slots, spec_ref, inv_ref, loop_ref):
    sources = spec_ref.shape[0]
    step = spec_ref.shape[1] // slots
    share = loop_ref.shape[0] // slots
    loop = spec_ref[...].astype(F32)
    rows = []
    for k in range(slots):
        turned = loop[:, k * step : (k + 1) * step].reshape(sources * step, LANES).T
        groups = [turned[g * share : (g + 1) * share] for g in range(LANES // share)]
        rows.append(jnp.concatenate(groups, axis=1))
    both = mm(jnp.concatenate(rows, axis=0).astype(BF16), inv_ref[...])
    loop_ref[...] = both[:, :LAGS] + both[:, LAGS:]


def vmem(count):
    return [pl.BlockSpec(memory_space=pltpu.VMEM)] * count


def smem(count):
    return [pl.BlockSpec(memory_space=pltpu.SMEM)] * count


def hbm(count):
    return [pl.BlockSpec(memory_space=pltpu.HBM)] * count


def in_hbm(array):
    return pltpu.with_memory_space_constraint(jnp.asarray(array), pltpu.HBM)


def loops_plain(white, loop_partner, loop_count, owners, inverse):
    blocks, _, _, bins, chans = white.shape
    devices = blocks * owners
    slots = loop_partner.shape[1]
    share = chans // owners
    wide = white.astype(F32)
    loops = []
    for k in range(slots):
        far = jnp.flip(wide[loop_partner[:, k]], axis=4)
        live = (k < loop_count).astype(F32)[:, None, None]
        real = jnp.sum(wide[:, :, 0] * far[:, :, 0] + wide[:, :, 1] * far[:, :, 1], axis=1)
        imag = jnp.sum(wide[:, :, 1] * far[:, :, 0] - wide[:, :, 0] * far[:, :, 1], axis=1)
        pair = (jnp.stack([real, imag]) * live[None]).astype(BF16)
        loops.append(pair.reshape(2, blocks, bins, owners, share))
    loop = jnp.transpose(jnp.stack(loops), (2, 4, 0, 1, 3, 5))
    loop = loop.reshape(devices, slots, 2 * bins, share)
    summed = lax.all_to_all(loop, ("chan", "seg"), 0, 0, tiled=True).astype(F32)
    table = inverse.astype(np.float32).reshape(LAGS, devices, 2 * bins)
    lags = jnp.einsum("dtvc,ldv->tcl", summed, table, precision=lax.Precision.HIGHEST)
    return lags[None]


def body(recording, filter_taps, offsets, loop_partner, loop_count):
    chan_count = lax.axis_size("chan")
    seg_count = lax.axis_size("seg")
    devices = chan_count * seg_count
    bins = BINS // devices
    chans, length = recording.shape
    noff, slots = offsets.shape[0], loop_partner.shape[1]
    share = chans // seg_count
    near_each = noff // seg_count
    assert length == NFFT * DECIM and chans == LANES and noff % seg_count == 0

    route = [(i, i + 1) for i in range(seg_count - 1)]
    rim = pl.pallas_call(
        rim_kernel,
        out_shape=jax.ShapeDtypeStruct((chans // 2, LANES), F32),
        in_specs=hbm(1),
        out_specs=pl.BlockSpec(memory_space=pltpu.VMEM),
        scratch_shapes=[pltpu.VMEM((chans, LANES), F32), pltpu.SemaphoreType.DMA],
        compiler_params=PARAMS,
        cost_estimate=pl.CostEstimate(
            flops=10_000_000_000, bytes_accessed=20_000_000, transcendentals=0
        ),
        name="history",
    )(in_hbm(recording))
    rim = lax.ppermute(rim, "seg", route)
    taps = filter_taps.reshape(1, TAPS)
    spec, mean, head = pl.pallas_call(
        spectrum_kernel,
        out_shape=[
            jax.ShapeDtypeStruct((2 * BINS, LANES), F32),
            jax.ShapeDtypeStruct((LANES, LANES), F32),
            jax.ShapeDtypeStruct((GROUP, LANES), F32),
        ],
        in_specs=vmem(4),
        out_specs=vmem(3),
        compiler_params=PARAMS,
        cost_estimate=pl.CostEstimate(
            flops=1_000_000_000, bytes_accessed=5_000_000, transcendentals=0
        ),
        name="filter_and_transform",
    )(taps, recording, short_table(), twiddle_table())

    band, band_share = band_tables()
    half = jax.ShapeDtypeStruct((BINS, LANES), BF16)
    white, up, down = pl.pallas_call(
        whiten_kernel,
        out_shape=[jax.ShapeDtypeStruct((GROUPS, 2, GROUP, LANES), BF16), half, half],
        in_specs=vmem(7),
        out_specs=hbm(1) + vmem(2),
        scratch_shapes=[
            pltpu.VMEM((GROUPS, 2, GROUP, LANES), BF16),
            pltpu.SemaphoreType.DMA((2,)),
        ],
        compiler_params=PARAMS,
        name="whiten",
    )(spec, rim, mean, head, edge_table(), band, band_share)

    spread = white
    if bins != GROUP:
        spread = jnp.moveaxis(white, 1, 0).reshape(2, devices, bins, LANES)
        spread = jnp.moveaxis(spread, 0, 1)
    moved = lax.all_to_all(spread, ("chan", "seg"), 0, 0, tiled=True)
    moved = moved.reshape(chan_count, seg_count, 2, bins, LANES)

    ring = [(i, (i + 1) % chan_count) for i in range(chan_count)]
    before = lax.ppermute(up, "chan", ring)
    after = lax.ppermute(down, "chan", [(j, i) for i, j in ring])
    order = np.repeat(bin_order().reshape(GROUPS, 1, GROUP), 2, axis=1).reshape(-1)
    part = np.broadcast_to(np.arange(2).reshape(1, 2, 1), (GROUPS, 2, GROUP)).reshape(-1)
    inverse = np.concatenate(split_np(inverse_table(seg_count, order, part)), axis=0)
    lags = pl.pallas_call(
        near_kernel,
        out_shape=[jax.ShapeDtypeStruct((near_each, LAGS, LANES), BF16)] * seg_count,
        in_specs=smem(1) + vmem(4),
        out_specs=vmem(seg_count),
        scratch_shapes=[pltpu.VMEM((noff, LAGS, LANES), F32)],
        compiler_params=PARAMS,
        cost_estimate=pl.CostEstimate(
            flops=20_000_000_000, bytes_accessed=20_000_000, transcendentals=0
        ),
        name="near_lags",
    )(offsets, white, before, after, inverse)
    moved, *lags = lax.optimization_barrier((moved, *lags))

    if bins % GROUP or 2 * bins % (8 * seg_count):
        order = np.repeat(bin_order().reshape(devices, 1, bins), 2, axis=1).reshape(-1)
        part = np.broadcast_to(np.arange(2).reshape(1, 2, 1), (devices, 2, bins)).reshape(-1)
        loop_inverse = inverse_table(seg_count, order, part)
        loop = loops_plain(moved, loop_partner, loop_count, seg_count, loop_inverse)
    else:
        flip = np.eye(LANES, dtype=np.float32)[::-1].astype(jnp.bfloat16)
        out_rows = slots * (2 * bins // seg_count)
        crossed = pl.pallas_call(
            loop_kernel,
            out_shape=jax.ShapeDtypeStruct((chan_count, seg_count, out_rows, LANES), BF16),
            in_specs=smem(2) + vmem(3),
            out_specs=pl.BlockSpec(memory_space=pltpu.HBM),
            scratch_shapes=[
                pltpu.VMEM((chan_count, seg_count, out_rows, LANES), BF16),
                pltpu.VMEM((chan_count, seg_count * 2 * bins, LANES), F32),
                pltpu.SemaphoreType.DMA((2,)),
            ],
            compiler_params=PARAMS,
            name="loop_spectra",
        )(loop_partner.T, loop_count, flip, pack_matrix(seg_count), moved)
        crossed = crossed.reshape(devices, out_rows, LANES)
        summed = lax.all_to_all(crossed, ("chan", "seg"), 0, 0, tiled=True)
        columns = np.arange(2 * BINS).reshape(devices, seg_count, -1).swapaxes(0, 1).reshape(-1)
        loop_inverse = inverse_table(seg_count, order[columns], part[columns]).T
        loop_inverse = np.concatenate(split_np(loop_inverse), axis=1)
        loop = pl.pallas_call(
            functools.partial(loop_lag_kernel, slots),
            out_shape=jax.ShapeDtypeStruct((slots * share, LAGS), F32),
            in_specs=vmem(2),
            out_specs=pl.BlockSpec(memory_space=pltpu.VMEM),
            compiler_params=PARAMS,
            name="loop_lags",
        )(summed, loop_inverse)
        loop = loop.reshape(1, slots, share, LAGS)
    for r in range(seg_count - 1, 0, -1):
        route = [(i, partner_of(i, r, seg_count)) for i in range(seg_count)]
        lags[r] = lax.ppermute(lags[r], "seg", route)
    near = pl.pallas_call(
        turn_kernel,
        out_shape=jax.ShapeDtypeStruct((chans, near_each, LAGS), F32),
        in_specs=vmem(seg_count),
        out_specs=pl.BlockSpec(memory_space=pltpu.VMEM),
        compiler_params=PARAMS,
        cost_estimate=pl.CostEstimate(
            flops=20_000_000_000, bytes_accessed=20_000_000, transcendentals=0
        ),
        name="near_turn",
    )(*lags)
    return near, loop


def solution(mesh):
    in_specs = (P("chan", "seg"), P(), P(), P(), P())
    out_specs = (P("chan", "seg", None), P("chan", None, "seg", None))
    return jax.shard_map(body, mesh=mesh, in_specs=in_specs, out_specs=out_specs, check_vma=False)
```

```python
import functools
import math

import jax
import jax.numpy as jnp
import numpy as np
from jax import lax
from jax.experimental import pallas as pl
from jax.experimental.pallas import tpu as pltpu
from jax.sharding import PartitionSpec as P

NFFT = 1024
LAGS = 256
TAPS = 64
DECIM = 4
HALFBAND = 10
SPAN = 64
BINS = 512
WATER = 0.2

LANES = 128
GROUP = 16
GROUPS = BINS // GROUP
OUT_BLOCK = 128
STEP = OUT_BLOCK * DECIM
RADIX = 4
DEPTH = NFFT // RADIX
FAR_BINS = BINS // RADIX

F32 = jnp.float32
BF16 = jnp.bfloat16
MIB = 1024 * 1024
PARAMS = pltpu.CompilerParams(vmem_limit_bytes=32 * MIB)


def bin_order():
    return np.concatenate([np.arange(r, BINS, RADIX) for r in range(RADIX)])


def split_np(table):
    high = table.astype(jnp.bfloat16)
    low = (table - high.astype(np.float64)).astype(jnp.bfloat16)
    return high, low


def short_table():
    bins = np.arange(FAR_BINS).reshape(-1, 1, GROUP, 1)
    angles = (bins * np.arange(DEPTH) % DEPTH) * (2.0 * np.pi / DEPTH)
    rows = np.concatenate([np.cos(angles), np.sin(angles)], axis=1).reshape(-1, DEPTH)
    high, low = split_np(rows)
    return np.concatenate([high, high, low], axis=1)


def twiddle_table():
    angles = np.arange(DEPTH)[:, None] * np.arange(1, RADIX) * (2.0 * np.pi / NFFT)
    columns = np.stack([np.cos(angles), np.sin(angles)], axis=2).reshape(DEPTH, -1)
    return np.pad(columns, ((0, 0), (0, LANES - columns.shape[1]))).astype(np.float32)


def edge_table():
    bins = bin_order().reshape(GROUPS, 1, GROUP, 1)
    angles = (bins * np.arange(GROUP) % NFFT) * (2.0 * np.pi / NFFT)
    rows = np.concatenate([np.cos(angles), -np.sin(angles)], axis=1) * (bins != 0)
    high, low = split_np(rows.reshape(2 * BINS, GROUP))
    table = np.concatenate([high, high, low], axis=1)
    return np.pad(table.astype(np.float32), ((0, 0), (0, LANES - 3 * GROUP))).astype(jnp.bfloat16)


def inverse_table(total_segs, bins, part):
    lag = np.arange(LAGS) - LAGS // 2
    angles = (bins[None, :] * lag[:, None] % NFFT) * (2.0 * np.pi / NFFT)
    weights = np.where(bins == 0, 1.0, 2.0) / math.sqrt(2.0 * BINS * total_segs)
    return np.where(part[None, :] == 1, -np.sin(angles), np.cos(angles)) * weights[None, :]


def band_tables():
    bins = bin_order()
    inside = np.abs(bins[:, None] - bins[None, :]) <= HALFBAND
    share = np.broadcast_to(1.0 / inside.sum(axis=1, keepdims=True), (BINS, LANES))
    return inside.astype(jnp.bfloat16), share.astype(np.float32)


def split(value):
    high = value.astype(BF16)
    return high, (value - high.astype(F32)).astype(BF16)


def mm(a, b):
    return jnp.dot(a, b, preferred_element_type=F32)


def mm_nt(a, b):
    return lax.dot_general(a, b, (((1,), (1,)), ((), ())), preferred_element_type=F32)


def tap_rows(taps):
    width = LANES + STEP
    square = (TAPS, TAPS)
    diagonal = lax.broadcasted_iota(jnp.int32, square, 0) == lax.broadcasted_iota(jnp.int32, square, 1)
    column_taps = jnp.sum(jnp.where(diagonal, taps, 0.0), axis=1, keepdims=True)
    tap = lax.broadcasted_iota(jnp.int32, (TAPS, width), 0)
    column = lax.broadcasted_iota(jnp.int32, (TAPS, width), 1)
    placed = jnp.where(column == LANES + DECIM - 1 - tap, column_taps, 0.0)
    spread = jnp.broadcast_to(jnp.sum(placed, axis=0, keepdims=True), (OUT_BLOCK, width))
    return pltpu.roll(spread, 0, 1, stride=DECIM, stride_axis=0)


def rim_kernel(rec_hbm, rim_ref, tail_ref, sem):
    length = rec_hbm.shape[1]
    copy = pltpu.make_async_copy(rec_hbm.at[:, pl.ds(length - LANES, LANES)], tail_ref, sem)
    copy.start()
    copy.wait()
    upper, lower = tail_ref[: LANES // 2], tail_ref[LANES // 2 :]
    lane = lax.broadcasted_iota(jnp.int32, lower.shape, 1)
    rim_ref[...] = jnp.where(lane < TAPS, pltpu.roll(upper, LANES - TAPS, 1), lower)


def spectrum_kernel(taps_ref, rec_ref, tab_ref, twist_ref, spec_ref, mean_ref, head_ref):
    blocks = rec_ref.shape[1] // STEP
    table = tap_rows(taps_ref[...])
    head_ref[...] = table[:GROUP, :LANES]
    taps_high, taps_low = split(table.T)
    taps_both = jnp.concatenate([taps_high, taps_low], axis=1)
    before = [jnp.zeros((LANES, LANES), BF16)] * 2
    outputs = []
    for first in range(0, blocks, blocks // 2):
        windows = ([], [])
        for j in range(first, first + blocks // 2):
            chunk = rec_ref[:, j * STEP : (j + 1) * STEP]
            if j == 0:
                mean = jnp.sum(chunk, axis=1, keepdims=True) * (1.0 / STEP)
            for i, value in enumerate(split(chunk - mean)):
                windows[i].append(jnp.concatenate([before[i], value], axis=1))
                before[i] = value[:, STEP - LANES :]
        wide = mm(jnp.concatenate(windows[0], axis=0), taps_both)
        rest = mm(jnp.concatenate(windows[1], axis=0), taps_high)
        total = wide[:, :LANES] + wide[:, LANES:] + rest
        outputs += [total[t * LANES : (t + 1) * LANES].T for t in range(blocks // 2)]
    pieces = [jnp.concatenate(outputs[j : j + 2], axis=0) for j in range(0, blocks, 2)]
    mean_ref[...] = jnp.broadcast_to(mean, mean_ref.shape)
    even, odd = pieces[0] + pieces[2], pieces[1] + pieces[3]
    a, b = pieces[0] - pieces[2], pieces[1] - pieces[3]
    whole, half = even + odd, even - odd
    whole = whole - jnp.sum(whole, axis=0, keepdims=True) * (1.0 / DEPTH)
    c1, s1, c2, s2, c3, s3 = [twist_ref[:, i : i + 1] for i in range(6)]
    inputs = [
        whole,
        a * c1 - b * s1,
        -(a * s1 + b * c1),
        half * c2,
        -(half * s2),
        a * c3 + b * s3,
        b * c3 - a * s3,
    ]
    parts = [split(value) for value in inputs]
    high = jnp.concatenate([p[0] for p in parts], axis=1)
    low = jnp.concatenate([p[1] for p in parts], axis=1)
    out = mm(tab_ref[...], jnp.concatenate([high, low, high], axis=0))
    out = out.reshape(FAR_BINS // GROUP, 2, GROUP, out.shape[1])
    rows = 2 * FAR_BINS
    for r in range(RADIX):
        first = max(2 * r - 1, 0) * LANES
        real_in = out[..., first : first + LANES]
        if r == 0:
            real, imag = real_in[:, 0], -real_in[:, 1]
        else:
            imag_in = out[..., first + LANES : first + 2 * LANES]
            real, imag = real_in[:, 0] + imag_in[:, 1], imag_in[:, 0] - real_in[:, 1]
        both = jnp.stack([real, imag], axis=1).reshape(rows, LANES)
        spec_ref[r * rows : (r + 1) * rows, :] = both


def whiten_kernel(
    spec_ref,
    rim_ref,
    mean_ref,
    head_ref,
    edge_ref,
    band_ref,
    share_ref,
    white_ref,
    up_ref,
    down_ref,
):
    head_high, head_low = split(head_ref[...])
    rim = jnp.concatenate([pltpu.roll(rim_ref[...], LANES - TAPS, 1), rim_ref[...]], axis=0)
    rim_high, rim_low = split(rim - mean_ref[...])
    history = mm_nt(
        jnp.concatenate([head_high, head_high, head_low], axis=1),
        jnp.concatenate([rim_high, rim_low, rim_high], axis=1),
    )
    high, low = split(history)
    stacked = jnp.concatenate([high, low, high], axis=0)
    spec = spec_ref[...] + mm(edge_ref[:, : 3 * GROUP], stacked)
    parted = spec.reshape(GROUPS, 2, GROUP, LANES)
    real, imag = parted[:, 0], parted[:, 1]
    amplitude = jnp.sqrt(real * real + imag * imag).reshape(BINS, LANES)
    high, low = split(amplitude)
    wide = mm(band_ref[...], jnp.concatenate([high, low], axis=1))
    smoothed = (wide[:, :LANES] + wide[:, LANES:]) * share_ref[...]
    level = jnp.sum(amplitude, axis=0, keepdims=True) * (1.0 / BINS)
    scale = 1.0 / (smoothed + (WATER * level + 1e-06))
    white = parted * scale.reshape(GROUPS, 1, GROUP, LANES)
    white_ref[...] = white.astype(BF16)
    flat = white.reshape(2 * BINS, LANES)
    turned = pltpu.roll(flat, SPAN, 1)
    lane = lax.broadcasted_iota(jnp.int32, (BINS, LANES), 1)
    up_ref[...] = jnp.where(lane < SPAN, turned[:BINS], flat[BINS:]).astype(BF16)
    down_ref[...] = jnp.where(lane < SPAN, flat[:BINS], turned[BINS:]).astype(BF16)


def offset_moves(offs_ref):
    row = lax.broadcasted_iota(jnp.int32, (2 * LANES, LANES), 0)
    channel = lax.broadcasted_iota(jnp.int32, (2 * LANES, LANES), 1)
    distance = jnp.where(row < LANES + SPAN, row, row - 2 * LANES) - channel
    hits = [(distance == offs_ref[o]).astype(F32) for o in range(offs_ref.shape[0])]
    return jnp.concatenate(hits, axis=1).astype(BF16)


def pack_matrix(owners):
    share = LANES // owners
    matrix = np.zeros((owners, owners, share, owners, owners, share), np.float32)
    for group in range(owners):
        for owner in range(owners):
            matrix[group, owner, :, owner, group, :] = np.eye(share)
    return matrix.reshape(owners * LANES, owners * LANES).astype(jnp.bfloat16)


def partner_of(place, r, owners):
    return place ^ r if owners & (owners - 1) == 0 else (place + r) % owners


def near_kernel(offs_ref, white_ref, before_ref, after_ref, inv_ref, *refs):
    out_refs, lags_ref = refs[:-1], refs[-1]
    rows = white_ref.shape[0] * 2 * GROUP
    half = rows // 2
    noff = lags_ref.shape[0]
    before, after = before_ref[...].astype(F32), after_ref[...].astype(F32)
    lane = lax.broadcasted_iota(jnp.int32, (half, LANES), 1)
    upper = jnp.where(lane < SPAN, after, pltpu.roll(before, SPAN, 1))
    lower = jnp.where(lane < SPAN, pltpu.roll(after, SPAN, 1), before)
    edge = jnp.concatenate([upper, lower], axis=0).astype(BF16)
    own = white_ref[...].reshape(rows, LANES)
    far = mm(jnp.concatenate([own, edge], axis=1), offset_moves(offs_ref))
    own = own.astype(F32).reshape(-1, 2, GROUP, LANES)
    columns = []
    for o in range(noff):
        other = far[:, o * LANES : (o + 1) * LANES].reshape(own.shape)
        real = own[:, 0] * other[:, 0] + own[:, 1] * other[:, 1]
        imag = own[:, 1] * other[:, 0] - own[:, 0] * other[:, 1]
        columns.append(jnp.stack([real, imag], axis=1).reshape(rows, LANES).astype(BF16))
    both = mm(inv_ref[...], jnp.concatenate(columns, axis=1))
    lags = both[:LAGS] + both[LAGS:]
    for o in range(noff):
        lags_ref[o] = lags[:, o * LANES : (o + 1) * LANES]
    owners = len(out_refs)
    each = noff // owners
    place = lax.axis_index("seg")
    for r in range(owners):
        first = partner_of(place, r, owners) * each
        out_refs[r][...] = lags_ref[pl.ds(first, each)].astype(BF16)


def turn_kernel(*refs):
    near_ref = refs[-1]
    total = sum(ref[...].astype(F32) for ref in refs[:-1])
    for t in range(near_ref.shape[1]):
        near_ref[:, t, :] = total[t].T


def loop_kernel(partner_ref, count_ref, flip_ref, pack_ref, white_ref, out_ref, turned_ref):
    blocks, segs, _, bins, _ = white_ref.shape
    owners = out_ref.shape[1]
    slots = partner_ref.shape[0]
    rows = segs * 2 * bins
    packed_rows = 2 * bins // owners
    flats = [white_ref[b].reshape(rows, LANES) for b in range(blocks)]
    turned_ref[...] = mm(jnp.concatenate(flats, axis=0), flip_ref[...]).reshape(turned_ref.shape)
    loops = []
    for b in range(blocks):
        own = flats[b].astype(F32).reshape(segs, 2, bins, LANES)
        for k in range(slots):
            partner = jnp.clip(partner_ref[k, b], 0, blocks - 1)
            live = (k < count_ref[b]).astype(F32)
            far = turned_ref[partner].reshape(segs, 2, bins, LANES)
            real = jnp.sum(own[:, 0] * far[:, 0] + own[:, 1] * far[:, 1], axis=0)
            imag = jnp.sum(own[:, 1] * far[:, 0] - own[:, 0] * far[:, 1], axis=0)
            pair = jnp.concatenate([real, imag], axis=0) * live
            groups = [pair[g * packed_rows : (g + 1) * packed_rows] for g in range(owners)]
            loops.append(jnp.concatenate(groups, axis=1))
    packed = mm(jnp.concatenate(loops, axis=0).astype(BF16), pack_ref[...])
    depth = slots * packed_rows
    for b in range(blocks):
        for q in range(owners):
            tile = packed[b * depth : (b + 1) * depth, q * LANES : (q + 1) * LANES]
            out_ref[b, q] = tile.astype(BF16)


def loop_lag_kernel(slots, spec_ref, inv_ref, loop_ref):
    sources = spec_ref.shape[0]
    step = spec_ref.shape[1] // slots
    share = loop_ref.shape[0] // slots
    loop = spec_ref[...].astype(F32)
    rows = []
    for k in range(slots):
        turned = loop[:, k * step : (k + 1) * step].reshape(sources * step, LANES).T
        groups = [turned[g * share : (g + 1) * share] for g in range(LANES // share)]
        rows.append(jnp.concatenate(groups, axis=1))
    both = mm(jnp.concatenate(rows, axis=0).astype(BF16), inv_ref[...])
    loop_ref[...] = both[:, :LAGS] + both[:, LAGS:]


def last_kernel(slots, spec_ref, inv_ref, *refs):
    turn_kernel(*refs[:-1])
    loop_lag_kernel(slots, spec_ref, inv_ref, refs[-1])


def vmem(count):
    return [pl.BlockSpec(memory_space=pltpu.VMEM)] * count


def smem(count):
    return [pl.BlockSpec(memory_space=pltpu.SMEM)] * count


def hbm(count):
    return [pl.BlockSpec(memory_space=pltpu.HBM)] * count


def in_hbm(array):
    return pltpu.with_memory_space_constraint(jnp.asarray(array), pltpu.HBM)


def loops_plain(white, loop_partner, loop_count, owners, inverse):
    blocks, _, _, bins, chans = white.shape
    devices = blocks * owners
    slots = loop_partner.shape[1]
    share = chans // owners
    wide = white.astype(F32)
    loops = []
    for k in range(slots):
        far = jnp.flip(wide[loop_partner[:, k]], axis=4)
        live = (k < loop_count).astype(F32)[:, None, None]
        real = jnp.sum(wide[:, :, 0] * far[:, :, 0] + wide[:, :, 1] * far[:, :, 1], axis=1)
        imag = jnp.sum(wide[:, :, 1] * far[:, :, 0] - wide[:, :, 0] * far[:, :, 1], axis=1)
        pair = (jnp.stack([real, imag]) * live[None]).astype(BF16)
        loops.append(pair.reshape(2, blocks, bins, owners, share))
    loop = jnp.transpose(jnp.stack(loops), (2, 4, 0, 1, 3, 5))
    loop = loop.reshape(devices, slots, 2 * bins, share)
    summed = lax.all_to_all(loop, ("chan", "seg"), 0, 0, tiled=True).astype(F32)
    table = inverse.astype(np.float32).reshape(LAGS, devices, 2 * bins)
    lags = jnp.einsum("dtvc,ldv->tcl", summed, table, precision=lax.Precision.HIGHEST)
    return lags[None]


def body(recording, filter_taps, offsets, loop_partner, loop_count):
    chan_count = lax.axis_size("chan")
    seg_count = lax.axis_size("seg")
    devices = chan_count * seg_count
    bins = BINS // devices
    chans, length = recording.shape
    noff, slots = offsets.shape[0], loop_partner.shape[1]
    share = chans // seg_count
    near_each = noff // seg_count
    assert length == NFFT * DECIM and chans == LANES and noff % seg_count == 0

    route = [(i, i + 1) for i in range(seg_count - 1)]
    rim = pl.pallas_call(
        rim_kernel,
        out_shape=jax.ShapeDtypeStruct((chans // 2, LANES), F32),
        in_specs=hbm(1),
        out_specs=pl.BlockSpec(memory_space=pltpu.VMEM),
        scratch_shapes=[pltpu.VMEM((chans, LANES), F32), pltpu.SemaphoreType.DMA],
        compiler_params=PARAMS,
        cost_estimate=pl.CostEstimate(
            flops=10_000_000_000, bytes_accessed=20_000_000, transcendentals=0
        ),
        name="history",
    )(in_hbm(recording))
    rim = lax.ppermute(rim, "seg", route)
    taps = filter_taps.reshape(1, TAPS)
    spec, mean, head = pl.pallas_call(
        spectrum_kernel,
        out_shape=[
            jax.ShapeDtypeStruct((2 * BINS, LANES), F32),
            jax.ShapeDtypeStruct((LANES, LANES), F32),
            jax.ShapeDtypeStruct((GROUP, LANES), F32),
        ],
        in_specs=vmem(4),
        out_specs=vmem(3),
        compiler_params=PARAMS,
        cost_estimate=pl.CostEstimate(
            flops=1_000_000_000, bytes_accessed=5_000_000, transcendentals=0
        ),
        name="filter_and_transform",
    )(taps, recording, short_table(), twiddle_table())

    band, band_share = band_tables()
    half = jax.ShapeDtypeStruct((BINS, LANES), BF16)
    white, up, down = pl.pallas_call(
        whiten_kernel,
        out_shape=[jax.ShapeDtypeStruct((GROUPS, 2, GROUP, LANES), BF16), half, half],
        in_specs=vmem(7),
        out_specs=vmem(3),
        compiler_params=PARAMS,
        name="whiten",
    )(spec, rim, mean, head, edge_table(), band, band_share)

    spread = white
    if bins != GROUP:
        spread = jnp.moveaxis(white, 1, 0).reshape(2, devices, bins, LANES)
        spread = jnp.moveaxis(spread, 0, 1)
    moved = lax.all_to_all(spread, ("chan", "seg"), 0, 0, tiled=True)
    moved = moved.reshape(chan_count, seg_count, 2, bins, LANES)

    ring = [(i, (i + 1) % chan_count) for i in range(chan_count)]
    before = lax.ppermute(up, "chan", ring)
    after = lax.ppermute(down, "chan", [(j, i) for i, j in ring])
    order = np.repeat(bin_order().reshape(GROUPS, 1, GROUP), 2, axis=1).reshape(-1)
    part = np.broadcast_to(np.arange(2).reshape(1, 2, 1), (GROUPS, 2, GROUP)).reshape(-1)
    inverse = np.concatenate(split_np(inverse_table(seg_count, order, part)), axis=0)
    lags = pl.pallas_call(
        near_kernel,
        out_shape=[jax.ShapeDtypeStruct((near_each, LAGS, LANES), BF16)] * seg_count,
        in_specs=smem(1) + vmem(4),
        out_specs=vmem(seg_count),
        scratch_shapes=[pltpu.VMEM((noff, LAGS, LANES), F32)],
        compiler_params=PARAMS,
        cost_estimate=pl.CostEstimate(
            flops=20_000_000_000, bytes_accessed=20_000_000, transcendentals=0
        ),
        name="near_lags",
    )(offsets, white, before, after, inverse)
    lags = list(lags)
    for r in range(seg_count - 1, 0, -1):
        route = [(i, partner_of(i, r, seg_count)) for i in range(seg_count)]
        lags[r] = lax.ppermute(lags[r], "seg", route)
    moved, lags[0] = lax.optimization_barrier((moved, lags[0]))

    near_shape = jax.ShapeDtypeStruct((chans, near_each, LAGS), F32)
    if bins % GROUP or 2 * bins % (8 * seg_count):
        order = np.repeat(bin_order().reshape(devices, 1, bins), 2, axis=1).reshape(-1)
        part = np.broadcast_to(np.arange(2).reshape(1, 2, 1), (devices, 2, bins)).reshape(-1)
        loop_inverse = inverse_table(seg_count, order, part)
        loop = loops_plain(moved, loop_partner, loop_count, seg_count, loop_inverse)
        near = pl.pallas_call(
            turn_kernel,
            out_shape=near_shape,
            in_specs=vmem(seg_count),
            out_specs=pl.BlockSpec(memory_space=pltpu.VMEM),
            compiler_params=PARAMS,
            name="near_turn",
        )(*lags)
        return near, loop

    flip = np.eye(LANES, dtype=np.float32)[::-1].astype(jnp.bfloat16)
    out_rows = slots * (2 * bins // seg_count)
    crossed = pl.pallas_call(
        loop_kernel,
        out_shape=jax.ShapeDtypeStruct((chan_count, seg_count, out_rows, LANES), BF16),
        in_specs=smem(2) + vmem(3),
        out_specs=pl.BlockSpec(memory_space=pltpu.VMEM),
        scratch_shapes=[pltpu.VMEM((chan_count, seg_count * 2 * bins, LANES), F32)],
        compiler_params=PARAMS,
        name="loop_spectra",
    )(loop_partner.T, loop_count, flip, pack_matrix(seg_count), moved)
    crossed, *lags[1:] = lax.optimization_barrier((crossed, *lags[1:]))
    crossed = crossed.reshape(devices, out_rows, LANES)
    summed = lax.all_to_all(crossed, ("chan", "seg"), 0, 0, tiled=True)
    columns = np.arange(2 * BINS).reshape(devices, seg_count, -1).swapaxes(0, 1).reshape(-1)
    loop_inverse = inverse_table(seg_count, order[columns], part[columns]).T
    loop_inverse = np.concatenate(split_np(loop_inverse), axis=1)
    near, loop = pl.pallas_call(
        functools.partial(last_kernel, slots),
        out_shape=[near_shape, jax.ShapeDtypeStruct((slots * share, LAGS), F32)],
        in_specs=vmem(2 + seg_count),
        out_specs=vmem(2),
        compiler_params=PARAMS,
        name="lags",
    )(summed, loop_inverse, *lags)
    return near, loop.reshape(1, slots, share, LAGS)


def solution(mesh):
    in_specs = (P("chan", "seg"), P(), P(), P(), P())
    out_specs = (P("chan", "seg", None), P("chan", None, "seg", None))
    return jax.shard_map(body, mesh=mesh, in_specs=in_specs, out_specs=out_specs, check_vma=False)
```

```python
import functools
import math

import jax
import jax.numpy as jnp
import numpy as np
from jax import lax
from jax.experimental import pallas as pl
from jax.experimental.pallas import tpu as pltpu
from jax.sharding import PartitionSpec as P

NFFT = 1024
LAGS = 256
TAPS = 64
DECIM = 4
HALFBAND = 10
SPAN = 64
BINS = 512
WATER = 0.2

LANES = 128
GROUP = 16
GROUPS = BINS // GROUP
OUT_BLOCK = 128
STEP = OUT_BLOCK * DECIM
RADIX = 4
DEPTH = NFFT // RADIX
FAR_BINS = BINS // RADIX

F32 = jnp.float32
BF16 = jnp.bfloat16
MIB = 1024 * 1024
PARAMS = pltpu.CompilerParams(vmem_limit_bytes=32 * MIB)


def bin_order():
    return np.concatenate([np.arange(r, BINS, RADIX) for r in range(RADIX)])


def split_np(table):
    high = table.astype(jnp.bfloat16)
    low = (table - high.astype(np.float64)).astype(jnp.bfloat16)
    return high, low


def short_table():
    bins = np.arange(FAR_BINS).reshape(-1, 1, GROUP, 1)
    angles = (bins * np.arange(DEPTH) % DEPTH) * (2.0 * np.pi / DEPTH)
    rows = np.concatenate([np.cos(angles), np.sin(angles)], axis=1).reshape(-1, DEPTH)
    high, low = split_np(rows)
    return np.concatenate([high, high, low], axis=1)


def twiddle_table():
    angles = np.arange(DEPTH)[:, None] * np.arange(1, RADIX) * (2.0 * np.pi / NFFT)
    columns = np.stack([np.cos(angles), np.sin(angles)], axis=2).reshape(DEPTH, -1)
    return np.pad(columns, ((0, 0), (0, LANES - columns.shape[1]))).astype(np.float32)


def edge_table():
    bins = bin_order().reshape(GROUPS, 1, GROUP, 1)
    angles = (bins * np.arange(GROUP) % NFFT) * (2.0 * np.pi / NFFT)
    rows = np.concatenate([np.cos(angles), -np.sin(angles)], axis=1) * (bins != 0)
    high, low = split_np(rows.reshape(2 * BINS, GROUP))
    table = np.concatenate([high, high, low], axis=1)
    return np.pad(table.astype(np.float32), ((0, 0), (0, LANES - 3 * GROUP))).astype(jnp.bfloat16)


def inverse_table(total_segs, bins, part):
    lag = np.arange(LAGS) - LAGS // 2
    angles = (bins[None, :] * lag[:, None] % NFFT) * (2.0 * np.pi / NFFT)
    weights = np.where(bins == 0, 1.0, 2.0) / math.sqrt(2.0 * BINS * total_segs)
    return np.where(part[None, :] == 1, -np.sin(angles), np.cos(angles)) * weights[None, :]


def band_tables():
    bins = bin_order()
    inside = np.abs(bins[:, None] - bins[None, :]) <= HALFBAND
    share = np.broadcast_to(1.0 / inside.sum(axis=1, keepdims=True), (BINS, LANES))
    return inside.astype(jnp.bfloat16), share.astype(np.float32)


def split(value):
    high = value.astype(BF16)
    return high, (value - high.astype(F32)).astype(BF16)


def mm(a, b):
    return jnp.dot(a, b, preferred_element_type=F32)


def mm_nt(a, b):
    return lax.dot_general(a, b, (((1,), (1,)), ((), ())), preferred_element_type=F32)


def tap_rows(taps):
    width, period = 2 * LANES, LANES // DECIM
    square = (TAPS, TAPS)
    diagonal = lax.broadcasted_iota(jnp.int32, square, 0) == lax.broadcasted_iota(jnp.int32, square, 1)
    column_taps = jnp.sum(jnp.where(diagonal, taps, 0.0), axis=1, keepdims=True)
    tap = lax.broadcasted_iota(jnp.int32, (TAPS, width), 0)
    column = lax.broadcasted_iota(jnp.int32, (TAPS, width), 1)
    placed = jnp.where(column == LANES + DECIM - 1 - tap, column_taps, 0.0)
    spread = jnp.broadcast_to(jnp.sum(placed, axis=0, keepdims=True), (period, width))
    piece = pltpu.roll(spread, 0, 1, stride=DECIM, stride_axis=0)
    rows = []
    for t in range(OUT_BLOCK // period):
        left = jnp.zeros((period, t * LANES), F32)
        right = jnp.zeros((period, STEP - LANES - t * LANES), F32)
        rows.append(jnp.concatenate([p for p in (left, piece, right) if p.shape[1]], axis=1))
    return jnp.concatenate(rows, axis=0)


def rim_kernel(rec_hbm, rim_ref, tail_ref, sem):
    length = rec_hbm.shape[1]
    copy = pltpu.make_async_copy(rec_hbm.at[:, pl.ds(length - LANES, LANES)], tail_ref, sem)
    copy.start()
    copy.wait()
    rim_ref[...] = tail_ref[...].T[LANES - TAPS :]


def spectrum_kernel(taps_ref, rec_ref, tab_ref, twist_ref, spec_ref, mean_ref, head_ref):
    blocks = rec_ref.shape[1] // STEP
    table = tap_rows(taps_ref[...])
    head_ref[...] = table[:GROUP, :LANES]
    taps_high, taps_low = split(table.T)
    taps_both = jnp.concatenate([taps_high, taps_low], axis=1)
    before = [jnp.zeros((LANES, LANES), BF16)] * 2
    outputs = []
    for first in range(0, blocks, blocks // 2):
        windows = ([], [])
        for j in range(first, first + blocks // 2):
            chunk = rec_ref[:, j * STEP : (j + 1) * STEP]
            if j == 0:
                mean = jnp.sum(chunk, axis=1, keepdims=True) * (1.0 / STEP)
            for i, value in enumerate(split(chunk - mean)):
                windows[i].append(jnp.concatenate([before[i], value], axis=1))
                before[i] = value[:, STEP - LANES :]
        wide = mm(jnp.concatenate(windows[0], axis=0), taps_both)
        rest = mm(jnp.concatenate(windows[1], axis=0), taps_high)
        total = wide[:, :LANES] + wide[:, LANES:] + rest
        outputs += [total[t * LANES : (t + 1) * LANES].T for t in range(blocks // 2)]
    pieces = [jnp.concatenate(outputs[j : j + 2], axis=0) for j in range(0, blocks, 2)]
    mean_ref[...] = jnp.broadcast_to(mean, (LANES, LANES)).T[: mean_ref.shape[0]]
    even, odd = pieces[0] + pieces[2], pieces[1] + pieces[3]
    a, b = pieces[0] - pieces[2], pieces[1] - pieces[3]
    whole, half = even + odd, even - odd
    whole = whole - jnp.sum(whole, axis=0, keepdims=True) * (1.0 / DEPTH)
    c1, s1, c2, s2, c3, s3 = [twist_ref[:, i : i + 1] for i in range(6)]
    inputs = [
        whole,
        a * c1 - b * s1,
        -(a * s1 + b * c1),
        half * c2,
        -(half * s2),
        a * c3 + b * s3,
        b * c3 - a * s3,
    ]
    parts = [split(value) for value in inputs]
    high = jnp.concatenate([p[0] for p in parts], axis=1)
    low = jnp.concatenate([p[1] for p in parts], axis=1)
    out = mm(tab_ref[...], jnp.concatenate([high, low, high], axis=0))
    out = out.reshape(FAR_BINS // GROUP, 2, GROUP, out.shape[1])
    rows = 2 * FAR_BINS
    for r in range(RADIX):
        first = max(2 * r - 1, 0) * LANES
        real_in = out[..., first : first + LANES]
        if r == 0:
            real, imag = real_in[:, 0], -real_in[:, 1]
        else:
            imag_in = out[..., first + LANES : first + 2 * LANES]
            real, imag = real_in[:, 0] + imag_in[:, 1], imag_in[:, 0] - real_in[:, 1]
        both = jnp.stack([real, imag], axis=1).reshape(rows, LANES)
        spec_ref[r * rows : (r + 1) * rows, :] = both


def whiten_kernel(
    spec_ref,
    rim_ref,
    mean_ref,
    head_ref,
    edge_ref,
    band_ref,
    share_ref,
    white_ref,
    up_ref,
    down_ref,
):
    head_high, head_low = split(head_ref[:, LANES - TAPS :])
    rim_high, rim_low = split(rim_ref[...] - mean_ref[0:1, :])
    history = mm(
        jnp.concatenate([head_high, head_high, head_low], axis=1),
        jnp.concatenate([rim_high, rim_low, rim_high], axis=0),
    )
    high, low = split(history)
    stacked = jnp.concatenate([high, low, high], axis=0)
    spec = spec_ref[...] + mm(edge_ref[:, : 3 * GROUP], stacked)
    parted = spec.reshape(GROUPS, 2, GROUP, LANES)
    real, imag = parted[:, 0], parted[:, 1]
    amplitude = jnp.sqrt(real * real + imag * imag).reshape(BINS, LANES)
    high, low = split(amplitude)
    wide = mm(band_ref[...], jnp.concatenate([high, low], axis=1))
    smoothed = (wide[:, :LANES] + wide[:, LANES:]) * share_ref[...]
    level = jnp.sum(amplitude, axis=0, keepdims=True) * (1.0 / BINS)
    scale = 1.0 / (smoothed + (WATER * level + 1e-06))
    white = parted * scale.reshape(GROUPS, 1, GROUP, LANES)
    white_ref[...] = white.astype(BF16)
    flat = white.reshape(2 * BINS, LANES)
    turned = pltpu.roll(flat, SPAN, 1)
    lane = lax.broadcasted_iota(jnp.int32, (BINS, LANES), 1)
    up_ref[...] = jnp.where(lane < SPAN, turned[:BINS], flat[BINS:]).astype(BF16)
    down_ref[...] = jnp.where(lane < SPAN, flat[:BINS], turned[BINS:]).astype(BF16)


def offset_moves(offs_ref):
    row = lax.broadcasted_iota(jnp.int32, (2 * LANES, LANES), 0)
    channel = lax.broadcasted_iota(jnp.int32, (2 * LANES, LANES), 1)
    distance = jnp.where(row < LANES + SPAN, row, row - 2 * LANES) - channel
    hits = [(distance == offs_ref[o]).astype(F32) for o in range(offs_ref.shape[0])]
    return jnp.concatenate(hits, axis=1).astype(BF16)


def pack_matrix(owners):
    share = LANES // owners
    matrix = np.zeros((owners, owners, share, owners, owners, share), np.float32)
    for group in range(owners):
        for owner in range(owners):
            matrix[group, owner, :, owner, group, :] = np.eye(share)
    matrix = matrix.reshape(owners, LANES, owners * LANES)[:, ::-1]
    return matrix.reshape(owners * LANES, owners * LANES).astype(jnp.bfloat16)


def partner_of(place, r, owners):
    return place ^ r if owners & (owners - 1) == 0 else (place + r) % owners


def near_kernel(offs_ref, white_ref, before_ref, after_ref, inv_ref, *refs):
    out_refs, lags_ref = refs[:-1], refs[-1]
    rows = white_ref.shape[0] * 2 * GROUP
    half = rows // 2
    noff = lags_ref.shape[0]
    before, after = before_ref[...].astype(F32), after_ref[...].astype(F32)
    lane = lax.broadcasted_iota(jnp.int32, (half, LANES), 1)
    upper = jnp.where(lane < SPAN, after, pltpu.roll(before, SPAN, 1))
    lower = jnp.where(lane < SPAN, pltpu.roll(after, SPAN, 1), before)
    edge = jnp.concatenate([upper, lower], axis=0).astype(BF16)
    own = white_ref[...].reshape(rows, LANES)
    far = mm(jnp.concatenate([own, edge], axis=1), offset_moves(offs_ref))
    own = own.astype(F32).reshape(-1, 2, GROUP, LANES)
    columns = []
    for o in range(noff):
        other = far[:, o * LANES : (o + 1) * LANES].reshape(own.shape)
        real = own[:, 0] * other[:, 0] + own[:, 1] * other[:, 1]
        imag = own[:, 1] * other[:, 0] - own[:, 0] * other[:, 1]
        columns.append(jnp.stack([real, imag], axis=1).reshape(rows, LANES).astype(BF16))
    both = mm(inv_ref[...], jnp.concatenate(columns, axis=1))
    lags = both[:LAGS] + both[LAGS:]
    for o in range(noff):
        lags_ref[o] = lags[:, o * LANES : (o + 1) * LANES]
    owners = len(out_refs)
    each = noff // owners
    place = lax.axis_index("seg")
    for r in range(owners):
        first = partner_of(place, r, owners) * each
        out_refs[r][...] = lags_ref[pl.ds(first, each)].astype(BF16)


def turn_kernel(*refs):
    near_ref = refs[-1]
    total = sum(ref[...].astype(F32) for ref in refs[:-1])
    for t in range(near_ref.shape[1]):
        near_ref[:, t, :] = total[t].T


def loop_kernel(partner_ref, count_ref, flip_ref, pack_ref, white_ref, out_ref):
    blocks, segs, _, bins, _ = white_ref.shape
    owners = out_ref.shape[1]
    slots = partner_ref.shape[0]
    rows = segs * 2 * bins
    packed_rows = 2 * bins // owners
    turned = mm(white_ref[...].reshape(blocks * rows, LANES), flip_ref[...])
    loops = []
    for b in range(blocks):
        own = turned[b * rows : (b + 1) * rows].reshape(segs, 2, bins, LANES)
        for k in range(slots):
            partner = jnp.clip(partner_ref[k, b], 0, blocks - 1)
            live = (k < count_ref[b]).astype(F32)
            far = white_ref[partner].astype(F32)
            real = jnp.sum(own[:, 0] * far[:, 0] + own[:, 1] * far[:, 1], axis=0)
            imag = jnp.sum(own[:, 1] * far[:, 0] - own[:, 0] * far[:, 1], axis=0)
            pair = jnp.concatenate([real, imag], axis=0) * live
            groups = [pair[g * packed_rows : (g + 1) * packed_rows] for g in range(owners)]
            loops.append(jnp.concatenate(groups, axis=1))
    packed = mm(jnp.concatenate(loops, axis=0).astype(BF16), pack_ref[...])
    depth = slots * packed_rows
    for b in range(blocks):
        for q in range(owners):
            tile = packed[b * depth : (b + 1) * depth, q * LANES : (q + 1) * LANES]
            out_ref[b, q] = tile.astype(BF16)


def loop_lag_kernel(slots, spec_ref, inv_ref, loop_ref):
    sources = spec_ref.shape[0]
    step = spec_ref.shape[1] // slots
    share = loop_ref.shape[0] // slots
    loop = spec_ref[...].astype(F32)
    rows = []
    for k in range(slots):
        turned = loop[:, k * step : (k + 1) * step].reshape(sources * step, LANES).T
        groups = [turned[g * share : (g + 1) * share] for g in range(LANES // share)]
        rows.append(jnp.concatenate(groups, axis=1))
    both = mm(jnp.concatenate(rows, axis=0).astype(BF16), inv_ref[...])
    loop_ref[...] = both[:, :LAGS] + both[:, LAGS:]


def last_kernel(slots, spec_ref, inv_ref, *refs):
    turn_kernel(*refs[:-1])
    loop_lag_kernel(slots, spec_ref, inv_ref, refs[-1])


def vmem(count):
    return [pl.BlockSpec(memory_space=pltpu.VMEM)] * count


def smem(count):
    return [pl.BlockSpec(memory_space=pltpu.SMEM)] * count


def hbm(count):
    return [pl.BlockSpec(memory_space=pltpu.HBM)] * count


def in_hbm(array):
    return pltpu.with_memory_space_constraint(jnp.asarray(array), pltpu.HBM)


def loops_plain(white, loop_partner, loop_count, owners, inverse):
    blocks, _, _, bins, chans = white.shape
    devices = blocks * owners
    slots = loop_partner.shape[1]
    share = chans // owners
    wide = white.astype(F32)
    loops = []
    for k in range(slots):
        far = jnp.flip(wide[loop_partner[:, k]], axis=4)
        live = (k < loop_count).astype(F32)[:, None, None]
        real = jnp.sum(wide[:, :, 0] * far[:, :, 0] + wide[:, :, 1] * far[:, :, 1], axis=1)
        imag = jnp.sum(wide[:, :, 1] * far[:, :, 0] - wide[:, :, 0] * far[:, :, 1], axis=1)
        pair = (jnp.stack([real, imag]) * live[None]).astype(BF16)
        loops.append(pair.reshape(2, blocks, bins, owners, share))
    loop = jnp.transpose(jnp.stack(loops), (2, 4, 0, 1, 3, 5))
    loop = loop.reshape(devices, slots, 2 * bins, share)
    summed = lax.all_to_all(loop, ("chan", "seg"), 0, 0, tiled=True).astype(F32)
    table = inverse.astype(np.float32).reshape(LAGS, devices, 2 * bins)
    lags = jnp.einsum("dtvc,ldv->tcl", summed, table, precision=lax.Precision.HIGHEST)
    return lags[None]


def body(recording, filter_taps, offsets, loop_partner, loop_count):
    chan_count = lax.axis_size("chan")
    seg_count = lax.axis_size("seg")
    devices = chan_count * seg_count
    bins = BINS // devices
    chans, length = recording.shape
    noff, slots = offsets.shape[0], loop_partner.shape[1]
    share = chans // seg_count
    near_each = noff // seg_count
    assert length == NFFT * DECIM and chans == LANES and noff % seg_count == 0

    route = [(i, i + 1) for i in range(seg_count - 1)]
    rim = pl.pallas_call(
        rim_kernel,
        out_shape=jax.ShapeDtypeStruct((TAPS, chans), F32),
        in_specs=hbm(1),
        out_specs=pl.BlockSpec(memory_space=pltpu.VMEM),
        scratch_shapes=[pltpu.VMEM((chans, LANES), F32), pltpu.SemaphoreType.DMA],
        compiler_params=PARAMS,
        cost_estimate=pl.CostEstimate(
            flops=10_000_000_000, bytes_accessed=20_000_000, transcendentals=0
        ),
        name="history",
    )(in_hbm(recording))
    rim = lax.ppermute(rim, "seg", route)
    taps = filter_taps.reshape(1, TAPS)
    spec, mean, head = pl.pallas_call(
        spectrum_kernel,
        out_shape=[
            jax.ShapeDtypeStruct((2 * BINS, LANES), F32),
            jax.ShapeDtypeStruct((8, LANES), F32),
            jax.ShapeDtypeStruct((GROUP, LANES), F32),
        ],
        in_specs=vmem(4),
        out_specs=vmem(3),
        compiler_params=PARAMS,
        cost_estimate=pl.CostEstimate(
            flops=1_000_000_000, bytes_accessed=5_000_000, transcendentals=0
        ),
        name="filter_and_transform",
    )(taps, recording, short_table(), twiddle_table())

    band, band_share = band_tables()
    half = jax.ShapeDtypeStruct((BINS, LANES), BF16)
    white, up, down = pl.pallas_call(
        whiten_kernel,
        out_shape=[jax.ShapeDtypeStruct((GROUPS, 2, GROUP, LANES), BF16), half, half],
        in_specs=vmem(7),
        out_specs=vmem(3),
        compiler_params=PARAMS,
        name="whiten",
    )(spec, rim, mean, head, edge_table(), band, band_share)

    spread = white
    if bins != GROUP:
        spread = jnp.moveaxis(white, 1, 0).reshape(2, devices, bins, LANES)
        spread = jnp.moveaxis(spread, 0, 1)
    moved = lax.all_to_all(spread, ("chan", "seg"), 0, 0, tiled=True)
    moved = moved.reshape(chan_count, seg_count, 2, bins, LANES)

    ring = [(i, (i + 1) % chan_count) for i in range(chan_count)]
    before = lax.ppermute(up, "chan", ring)
    after = lax.ppermute(down, "chan", [(j, i) for i, j in ring])
    order = np.repeat(bin_order().reshape(GROUPS, 1, GROUP), 2, axis=1).reshape(-1)
    part = np.broadcast_to(np.arange(2).reshape(1, 2, 1), (GROUPS, 2, GROUP)).reshape(-1)
    inverse = np.concatenate(split_np(inverse_table(seg_count, order, part)), axis=0)
    lags = pl.pallas_call(
        near_kernel,
        out_shape=[jax.ShapeDtypeStruct((near_each, LAGS, LANES), BF16)] * seg_count,
        in_specs=smem(1) + vmem(4),
        out_specs=vmem(seg_count),
        scratch_shapes=[pltpu.VMEM((noff, LAGS, LANES), F32)],
        compiler_params=PARAMS,
        cost_estimate=pl.CostEstimate(
            flops=20_000_000_000, bytes_accessed=20_000_000, transcendentals=0
        ),
        name="near_lags",
    )(offsets, white, before, after, inverse)
    lags = list(lags)
    for r in range(seg_count - 1, 0, -1):
        route = [(i, partner_of(i, r, seg_count)) for i in range(seg_count)]
        lags[r] = lax.ppermute(lags[r], "seg", route)
    moved, lags[0] = lax.optimization_barrier((moved, lags[0]))

    near_shape = jax.ShapeDtypeStruct((chans, near_each, LAGS), F32)
    if bins % GROUP or 2 * bins % (8 * seg_count):
        order = np.repeat(bin_order().reshape(devices, 1, bins), 2, axis=1).reshape(-1)
        part = np.broadcast_to(np.arange(2).reshape(1, 2, 1), (devices, 2, bins)).reshape(-1)
        loop_inverse = inverse_table(seg_count, order, part)
        loop = loops_plain(moved, loop_partner, loop_count, seg_count, loop_inverse)
        near = pl.pallas_call(
            turn_kernel,
            out_shape=near_shape,
            in_specs=vmem(seg_count),
            out_specs=pl.BlockSpec(memory_space=pltpu.VMEM),
            compiler_params=PARAMS,
            name="near_turn",
        )(*lags)
        return near, loop

    flip = np.eye(LANES, dtype=np.float32)[::-1].astype(jnp.bfloat16)
    out_rows = slots * (2 * bins // seg_count)
    crossed = pl.pallas_call(
        loop_kernel,
        out_shape=jax.ShapeDtypeStruct((chan_count, seg_count, out_rows, LANES), BF16),
        in_specs=smem(2) + vmem(3),
        out_specs=pl.BlockSpec(memory_space=pltpu.VMEM),
        compiler_params=PARAMS,
        name="loop_spectra",
    )(loop_partner.T, loop_count, flip, pack_matrix(seg_count), moved)
    crossed, *lags[1:] = lax.optimization_barrier((crossed, *lags[1:]))
    crossed = crossed.reshape(devices, out_rows, LANES)
    summed = lax.all_to_all(crossed, ("chan", "seg"), 0, 0, tiled=True)
    columns = np.arange(2 * BINS).reshape(devices, seg_count, -1).swapaxes(0, 1).reshape(-1)
    loop_inverse = inverse_table(seg_count, order[columns], part[columns]).T
    loop_inverse = np.concatenate(split_np(loop_inverse), axis=1)
    near, loop = pl.pallas_call(
        functools.partial(last_kernel, slots),
        out_shape=[near_shape, jax.ShapeDtypeStruct((slots * share, LAGS), F32)],
        in_specs=vmem(2 + seg_count),
        out_specs=vmem(2),
        compiler_params=PARAMS,
        name="lags",
    )(summed, loop_inverse, *lags)
    return near, loop.reshape(1, slots, share, LAGS)


def solution(mesh):
    in_specs = (P("chan", "seg"), P(), P(), P(), P())
    out_specs = (P("chan", "seg", None), P("chan", None, "seg", None))
    return jax.shard_map(body, mesh=mesh, in_specs=in_specs, out_specs=out_specs, check_vma=False)
```

```python
import functools
import math

import jax
import jax.numpy as jnp
import numpy as np
from jax import lax
from jax.experimental import pallas as pl
from jax.experimental.pallas import tpu as pltpu
from jax.sharding import PartitionSpec as P

NFFT = 1024
LAGS = 256
TAPS = 64
DECIM = 4
HALFBAND = 10
SPAN = 64
BINS = 512
WATER = 0.2

LANES = 128
GROUP = 16
GROUPS = BINS // GROUP
OUT_BLOCK = 128
STEP = OUT_BLOCK * DECIM
RADIX = 4
DEPTH = NFFT // RADIX
FAR_BINS = BINS // RADIX

F32 = jnp.float32
BF16 = jnp.bfloat16
MIB = 1024 * 1024
PARAMS = pltpu.CompilerParams(vmem_limit_bytes=32 * MIB)


def bin_order():
    return np.concatenate([np.arange(r, BINS, RADIX) for r in range(RADIX)])


def split_np(table):
    high = table.astype(jnp.bfloat16)
    low = (table - high.astype(np.float64)).astype(jnp.bfloat16)
    return high, low


def short_table():
    bins = np.arange(FAR_BINS).reshape(-1, 1, GROUP, 1)
    angles = (bins * np.arange(DEPTH) % DEPTH) * (2.0 * np.pi / DEPTH)
    rows = np.concatenate([np.cos(angles), np.sin(angles)], axis=1).reshape(-1, DEPTH)
    high, low = split_np(rows)
    return np.concatenate([high, high, low], axis=1)


def twiddle_table():
    angles = np.arange(DEPTH)[:, None] * np.arange(1, RADIX) * (2.0 * np.pi / NFFT)
    columns = np.stack([np.cos(angles), np.sin(angles)], axis=2).reshape(DEPTH, -1)
    return np.pad(columns, ((0, 0), (0, LANES - columns.shape[1]))).astype(np.float32)


def edge_table():
    bins = bin_order().reshape(GROUPS, 1, GROUP, 1)
    angles = (bins * np.arange(GROUP) % NFFT) * (2.0 * np.pi / NFFT)
    rows = np.concatenate([np.cos(angles), -np.sin(angles)], axis=1) * (bins != 0)
    high, low = split_np(rows.reshape(2 * BINS, GROUP))
    table = np.concatenate([high, high, low], axis=1)
    return np.pad(table.astype(np.float32), ((0, 0), (0, LANES - 3 * GROUP))).astype(jnp.bfloat16)


def inverse_table(total_segs, bins, part):
    lag = np.arange(LAGS) - LAGS // 2
    angles = (bins[None, :] * lag[:, None] % NFFT) * (2.0 * np.pi / NFFT)
    weights = np.where(bins == 0, 1.0, 2.0) / math.sqrt(2.0 * BINS * total_segs)
    return np.where(part[None, :] == 1, -np.sin(angles), np.cos(angles)) * weights[None, :]


def band_tables():
    bins = bin_order()
    inside = np.abs(bins[:, None] - bins[None, :]) <= HALFBAND
    share = np.broadcast_to(1.0 / inside.sum(axis=1, keepdims=True), (BINS, LANES))
    return inside.astype(jnp.bfloat16), share.astype(np.float32)


def split(value):
    high = value.astype(BF16)
    return high, (value - high.astype(F32)).astype(BF16)


def mm(a, b):
    return jnp.dot(a, b, preferred_element_type=F32)


def mm_nt(a, b):
    return lax.dot_general(a, b, (((1,), (1,)), ((), ())), preferred_element_type=F32)


def tap_rows(taps):
    width, period = 2 * LANES, LANES // DECIM
    square = (TAPS, TAPS)
    diagonal = lax.broadcasted_iota(jnp.int32, square, 0) == lax.broadcasted_iota(jnp.int32, square, 1)
    column_taps = jnp.sum(jnp.where(diagonal, taps, 0.0), axis=1, keepdims=True)
    tap = lax.broadcasted_iota(jnp.int32, (TAPS, width), 0)
    column = lax.broadcasted_iota(jnp.int32, (TAPS, width), 1)
    placed = jnp.where(column == LANES + DECIM - 1 - tap, column_taps, 0.0)
    spread = jnp.broadcast_to(jnp.sum(placed, axis=0, keepdims=True), (period, width))
    piece = pltpu.roll(spread, 0, 1, stride=DECIM, stride_axis=0)
    rows = []
    for t in range(OUT_BLOCK // period):
        left = jnp.zeros((period, t * LANES), F32)
        right = jnp.zeros((period, STEP - LANES - t * LANES), F32)
        rows.append(jnp.concatenate([p for p in (left, piece, right) if p.shape[1]], axis=1))
    return jnp.concatenate(rows, axis=0)


def rim_kernel(rec_hbm, rim_ref, tail_ref, sem):
    length = rec_hbm.shape[1]
    copy = pltpu.make_async_copy(rec_hbm.at[:, pl.ds(length - LANES, LANES)], tail_ref, sem)
    copy.start()
    copy.wait()
    rim_ref[...] = tail_ref[...].T[LANES - TAPS :]


def spectrum_kernel(taps_ref, rec_ref, tab_ref, twist_ref, spec_ref, mean_ref, head_ref):
    blocks = rec_ref.shape[1] // STEP
    table = tap_rows(taps_ref[...])
    head_ref[...] = table[:GROUP, :LANES]
    taps_high, taps_low = split(table.T)
    taps_both = jnp.concatenate([taps_high, taps_low], axis=1)
    before = [jnp.zeros((LANES, LANES), BF16)] * 2
    outputs = []
    for first in range(0, blocks, blocks // 2):
        windows = ([], [])
        for j in range(first, first + blocks // 2):
            chunk = rec_ref[:, j * STEP : (j + 1) * STEP]
            if j == 0:
                mean = jnp.sum(chunk, axis=1, keepdims=True) * (1.0 / STEP)
            for i, value in enumerate(split(chunk - mean)):
                windows[i].append(jnp.concatenate([before[i], value], axis=1))
                before[i] = value[:, STEP - LANES :]
        wide = mm(jnp.concatenate(windows[0], axis=0), taps_both)
        rest = mm(jnp.concatenate(windows[1], axis=0), taps_high)
        total = wide[:, :LANES] + wide[:, LANES:] + rest
        outputs += [total[t * LANES : (t + 1) * LANES].T for t in range(blocks // 2)]
    pieces = [jnp.concatenate(outputs[j : j + 2], axis=0) for j in range(0, blocks, 2)]
    mean_ref[...] = jnp.broadcast_to(mean, (LANES, LANES)).T[: mean_ref.shape[0]]
    even, odd = pieces[0] + pieces[2], pieces[1] + pieces[3]
    a, b = pieces[0] - pieces[2], pieces[1] - pieces[3]
    whole, half = even + odd, even - odd
    whole = whole - jnp.sum(whole, axis=0, keepdims=True) * (1.0 / DEPTH)
    c1, s1, c2, s2, c3, s3 = [twist_ref[:, i : i + 1] for i in range(6)]
    inputs = [
        whole,
        a * c1 - b * s1,
        -(a * s1 + b * c1),
        half * c2,
        -(half * s2),
        a * c3 + b * s3,
        b * c3 - a * s3,
    ]
    parts = [split(value) for value in inputs]
    high = jnp.concatenate([p[0] for p in parts], axis=1)
    low = jnp.concatenate([p[1] for p in parts], axis=1)
    out = mm(tab_ref[...], jnp.concatenate([high, low, high], axis=0))
    out = out.reshape(FAR_BINS // GROUP, 2, GROUP, out.shape[1])
    rows = 2 * FAR_BINS
    for r in range(RADIX):
        first = max(2 * r - 1, 0) * LANES
        real_in = out[..., first : first + LANES]
        if r == 0:
            real, imag = real_in[:, 0], -real_in[:, 1]
        else:
            imag_in = out[..., first + LANES : first + 2 * LANES]
            real, imag = real_in[:, 0] + imag_in[:, 1], imag_in[:, 0] - real_in[:, 1]
        both = jnp.stack([real, imag], axis=1).reshape(rows, LANES)
        spec_ref[r * rows : (r + 1) * rows, :] = both


def whiten_kernel(
    spec_ref,
    rim_ref,
    mean_ref,
    head_ref,
    edge_ref,
    band_ref,
    share_ref,
    white_ref,
    up_ref,
    down_ref,
):
    head_high, head_low = split(head_ref[:, LANES - TAPS :])
    rim_high, rim_low = split(rim_ref[...] - mean_ref[0:1, :])
    history = mm(
        jnp.concatenate([head_high, head_high, head_low], axis=1),
        jnp.concatenate([rim_high, rim_low, rim_high], axis=0),
    )
    high, low = split(history)
    stacked = jnp.concatenate([high, low, high], axis=0)
    spec = spec_ref[...] + mm(edge_ref[:, : 3 * GROUP], stacked)
    parted = spec.reshape(GROUPS, 2, GROUP, LANES)
    real, imag = parted[:, 0], parted[:, 1]
    amplitude = jnp.sqrt(real * real + imag * imag).reshape(BINS, LANES)
    high, low = split(amplitude)
    wide = mm(band_ref[...], jnp.concatenate([high, low], axis=1))
    smoothed = (wide[:, :LANES] + wide[:, LANES:]) * share_ref[...]
    level = jnp.sum(amplitude, axis=0, keepdims=True) * (1.0 / BINS)
    scale = 1.0 / (smoothed + (WATER * level + 1e-06))
    white = parted * scale.reshape(GROUPS, 1, GROUP, LANES)
    white_ref[...] = white.astype(BF16)
    flat = white.reshape(2 * BINS, LANES)
    turned = pltpu.roll(flat, SPAN, 1)
    lane = lax.broadcasted_iota(jnp.int32, (BINS, LANES), 1)
    up_ref[...] = jnp.where(lane < SPAN, turned[:BINS], flat[BINS:]).astype(BF16)
    down_ref[...] = jnp.where(lane < SPAN, flat[:BINS], turned[BINS:]).astype(BF16)


def offset_moves(offs_ref):
    row = lax.broadcasted_iota(jnp.int32, (2 * LANES, LANES), 0)
    channel = lax.broadcasted_iota(jnp.int32, (2 * LANES, LANES), 1)
    distance = jnp.where(row < LANES + SPAN, row, row - 2 * LANES) - channel
    hits = [(distance == offs_ref[o]).astype(F32) for o in range(offs_ref.shape[0])]
    return jnp.concatenate(hits, axis=1).astype(BF16)


def pack_matrix(owners):
    share = LANES // owners
    matrix = np.zeros((owners, owners, share, owners, owners, share), np.float32)
    for group in range(owners):
        for owner in range(owners):
            matrix[group, owner, :, owner, group, :] = np.eye(share)
    matrix = matrix.reshape(owners, LANES, owners * LANES)[:, ::-1]
    return matrix.reshape(owners * LANES, owners * LANES).astype(jnp.bfloat16)


def partner_of(place, r, owners):
    return place ^ r if owners & (owners - 1) == 0 else (place + r) % owners


def near_kernel(offs_ref, white_ref, before_ref, after_ref, inv_ref, *refs):
    out_refs, lags_ref = refs[:-1], refs[-1]
    rows = white_ref.shape[0] * 2 * GROUP
    half = rows // 2
    noff = lags_ref.shape[0]
    before, after = before_ref[...].astype(F32), after_ref[...].astype(F32)
    lane = lax.broadcasted_iota(jnp.int32, (half, LANES), 1)
    upper = jnp.where(lane < SPAN, after, pltpu.roll(before, SPAN, 1))
    lower = jnp.where(lane < SPAN, pltpu.roll(after, SPAN, 1), before)
    edge = jnp.concatenate([upper, lower], axis=0).astype(BF16)
    own = white_ref[...].reshape(rows, LANES)
    far = mm(jnp.concatenate([own, edge], axis=1), offset_moves(offs_ref))
    own = own.astype(F32).reshape(-1, 2, GROUP, LANES)
    columns = []
    for o in range(noff):
        other = far[:, o * LANES : (o + 1) * LANES].reshape(own.shape)
        real = own[:, 0] * other[:, 0] + own[:, 1] * other[:, 1]
        imag = own[:, 1] * other[:, 0] - own[:, 0] * other[:, 1]
        columns.append(jnp.stack([real, imag], axis=1).reshape(rows, LANES).astype(BF16))
    both = mm(inv_ref[...], jnp.concatenate(columns, axis=1))
    lags = both[:LAGS] + both[LAGS:]
    for o in range(noff):
        lags_ref[o] = lags[:, o * LANES : (o + 1) * LANES]
    owners = len(out_refs)
    each = noff // owners
    place = lax.axis_index("seg")
    for r in range(owners):
        first = partner_of(place, r, owners) * each
        out_refs[r][...] = lags_ref[pl.ds(first, each)].astype(BF16)


def turn_kernel(*refs):
    near_ref = refs[-1]
    total = sum(ref[...].astype(F32) for ref in refs[:-1])
    for t in range(near_ref.shape[1]):
        near_ref[:, t, :] = total[t].T


def loop_kernel(partner_ref, count_ref, flip_ref, pack_ref, white_ref, out_ref):
    segs, blocks, _, bins, _ = white_ref.shape
    owners = out_ref.shape[0]
    slots = partner_ref.shape[0]
    rows = segs * 2 * bins
    packed_rows = 2 * bins // owners
    turned = mm(white_ref[...].reshape(blocks * rows, LANES), flip_ref[...])
    turned = turned.reshape(white_ref.shape)
    loops = []
    for b in range(blocks):
        own = turned[:, b]
        for k in range(slots):
            partner = jnp.clip(partner_ref[k, b], 0, blocks - 1)
            live = (k < count_ref[b]).astype(F32)
            far = white_ref[:, partner].astype(F32)
            real = jnp.sum(own[:, 0] * far[:, 0] + own[:, 1] * far[:, 1], axis=0)
            imag = jnp.sum(own[:, 1] * far[:, 0] - own[:, 0] * far[:, 1], axis=0)
            pair = jnp.concatenate([real, imag], axis=0) * live
            groups = [pair[g * packed_rows : (g + 1) * packed_rows] for g in range(owners)]
            loops.append(jnp.concatenate(groups, axis=1))
    packed = mm(jnp.concatenate(loops, axis=0).astype(BF16), pack_ref[...])
    depth = slots * packed_rows
    for b in range(blocks):
        for q in range(owners):
            tile = packed[b * depth : (b + 1) * depth, q * LANES : (q + 1) * LANES]
            out_ref[q, b] = tile.astype(BF16)


def loop_lag_kernel(slots, spec_ref, inv_ref, loop_ref):
    sources = spec_ref.shape[0]
    step = spec_ref.shape[1] // slots
    share = loop_ref.shape[0] // slots
    loop = spec_ref[...].astype(F32)
    rows = []
    for k in range(slots):
        turned = loop[:, k * step : (k + 1) * step].reshape(sources * step, LANES).T
        groups = [turned[g * share : (g + 1) * share] for g in range(LANES // share)]
        rows.append(jnp.concatenate(groups, axis=1))
    both = mm(jnp.concatenate(rows, axis=0).astype(BF16), inv_ref[...])
    loop_ref[...] = both[:, :LAGS] + both[:, LAGS:]


def last_kernel(slots, spec_ref, inv_ref, *refs):
    turn_kernel(*refs[:-1])
    loop_lag_kernel(slots, spec_ref, inv_ref, refs[-1])


def vmem(count):
    return [pl.BlockSpec(memory_space=pltpu.VMEM)] * count


def smem(count):
    return [pl.BlockSpec(memory_space=pltpu.SMEM)] * count


def hbm(count):
    return [pl.BlockSpec(memory_space=pltpu.HBM)] * count


def in_hbm(array):
    return pltpu.with_memory_space_constraint(jnp.asarray(array), pltpu.HBM)


def loops_plain(white, loop_partner, loop_count, owners, inverse):
    _, blocks, _, bins, chans = white.shape
    devices = blocks * owners
    slots = loop_partner.shape[1]
    share = chans // owners
    wide = white.astype(F32).swapaxes(0, 1)
    loops = []
    for k in range(slots):
        far = jnp.flip(wide[loop_partner[:, k]], axis=4)
        live = (k < loop_count).astype(F32)[:, None, None]
        real = jnp.sum(wide[:, :, 0] * far[:, :, 0] + wide[:, :, 1] * far[:, :, 1], axis=1)
        imag = jnp.sum(wide[:, :, 1] * far[:, :, 0] - wide[:, :, 0] * far[:, :, 1], axis=1)
        pair = (jnp.stack([real, imag]) * live[None]).astype(BF16)
        loops.append(pair.reshape(2, blocks, bins, owners, share))
    loop = jnp.transpose(jnp.stack(loops), (4, 2, 0, 1, 3, 5))
    loop = loop.reshape(devices, slots, 2 * bins, share)
    summed = lax.all_to_all(loop, ("seg", "chan"), 0, 0, tiled=True).astype(F32)
    table = inverse.astype(np.float32).reshape(LAGS, devices, 2 * bins)
    lags = jnp.einsum("dtvc,ldv->tcl", summed, table, precision=lax.Precision.HIGHEST)
    return lags[None]


def body(recording, filter_taps, offsets, loop_partner, loop_count):
    chan_count = lax.axis_size("chan")
    seg_count = lax.axis_size("seg")
    devices = chan_count * seg_count
    bins = BINS // devices
    chans, length = recording.shape
    noff, slots = offsets.shape[0], loop_partner.shape[1]
    share = chans // seg_count
    near_each = noff // seg_count
    assert length == NFFT * DECIM and chans == LANES and noff % seg_count == 0

    route = [(i, i + 1) for i in range(seg_count - 1)]
    rim = pl.pallas_call(
        rim_kernel,
        out_shape=jax.ShapeDtypeStruct((TAPS, chans), F32),
        in_specs=hbm(1),
        out_specs=pl.BlockSpec(memory_space=pltpu.VMEM),
        scratch_shapes=[pltpu.VMEM((chans, LANES), F32), pltpu.SemaphoreType.DMA],
        compiler_params=PARAMS,
        cost_estimate=pl.CostEstimate(
            flops=10_000_000_000, bytes_accessed=20_000_000, transcendentals=0
        ),
        name="history",
    )(in_hbm(recording))
    rim = lax.ppermute(rim, "seg", route)
    taps = filter_taps.reshape(1, TAPS)
    spec, mean, head = pl.pallas_call(
        spectrum_kernel,
        out_shape=[
            jax.ShapeDtypeStruct((2 * BINS, LANES), F32),
            jax.ShapeDtypeStruct((8, LANES), F32),
            jax.ShapeDtypeStruct((GROUP, LANES), F32),
        ],
        in_specs=vmem(4),
        out_specs=vmem(3),
        compiler_params=PARAMS,
        cost_estimate=pl.CostEstimate(
            flops=1_000_000_000, bytes_accessed=5_000_000, transcendentals=0
        ),
        name="filter_and_transform",
    )(taps, recording, short_table(), twiddle_table())

    band, band_share = band_tables()
    half = jax.ShapeDtypeStruct((BINS, LANES), BF16)
    white, up, down = pl.pallas_call(
        whiten_kernel,
        out_shape=[jax.ShapeDtypeStruct((GROUPS, 2, GROUP, LANES), BF16), half, half],
        in_specs=vmem(7),
        out_specs=vmem(3),
        compiler_params=PARAMS,
        name="whiten",
    )(spec, rim, mean, head, edge_table(), band, band_share)

    spread = white
    if bins != GROUP:
        spread = jnp.moveaxis(white, 1, 0).reshape(2, devices, bins, LANES)
        spread = jnp.moveaxis(spread, 0, 1)
    moved = lax.all_to_all(spread, ("seg", "chan"), 0, 0, tiled=True)
    moved = moved.reshape(seg_count, chan_count, 2, bins, LANES)

    ring = [(i, (i + 1) % chan_count) for i in range(chan_count)]
    before = lax.ppermute(up, "chan", ring)
    after = lax.ppermute(down, "chan", [(j, i) for i, j in ring])
    order = np.repeat(bin_order().reshape(GROUPS, 1, GROUP), 2, axis=1).reshape(-1)
    part = np.broadcast_to(np.arange(2).reshape(1, 2, 1), (GROUPS, 2, GROUP)).reshape(-1)
    inverse = np.concatenate(split_np(inverse_table(seg_count, order, part)), axis=0)
    lags = pl.pallas_call(
        near_kernel,
        out_shape=[jax.ShapeDtypeStruct((near_each, LAGS, LANES), BF16)] * seg_count,
        in_specs=smem(1) + vmem(4),
        out_specs=vmem(seg_count),
        scratch_shapes=[pltpu.VMEM((noff, LAGS, LANES), F32)],
        compiler_params=PARAMS,
        cost_estimate=pl.CostEstimate(
            flops=20_000_000_000, bytes_accessed=20_000_000, transcendentals=0
        ),
        name="near_lags",
    )(offsets, white, before, after, inverse)
    lags = list(lags)
    for r in range(seg_count - 1, 0, -1):
        route = [(i, partner_of(i, r, seg_count)) for i in range(seg_count)]
        lags[r] = lax.ppermute(lags[r], "seg", route)
    moved, lags[0] = lax.optimization_barrier((moved, lags[0]))

    near_shape = jax.ShapeDtypeStruct((chans, near_each, LAGS), F32)
    if bins % GROUP or 2 * bins % (8 * seg_count):
        order = np.repeat(bin_order().reshape(devices, 1, bins), 2, axis=1).reshape(-1)
        part = np.broadcast_to(np.arange(2).reshape(1, 2, 1), (devices, 2, bins)).reshape(-1)
        loop_inverse = inverse_table(seg_count, order, part)
        loop = loops_plain(moved, loop_partner, loop_count, seg_count, loop_inverse)
        near = pl.pallas_call(
            turn_kernel,
            out_shape=near_shape,
            in_specs=vmem(seg_count),
            out_specs=pl.BlockSpec(memory_space=pltpu.VMEM),
            compiler_params=PARAMS,
            name="near_turn",
        )(*lags)
        return near, loop

    flip = np.eye(LANES, dtype=np.float32)[::-1].astype(jnp.bfloat16)
    out_rows = slots * (2 * bins // seg_count)
    crossed = pl.pallas_call(
        loop_kernel,
        out_shape=jax.ShapeDtypeStruct((seg_count, chan_count, out_rows, LANES), BF16),
        in_specs=smem(2) + vmem(3),
        out_specs=pl.BlockSpec(memory_space=pltpu.VMEM),
        compiler_params=PARAMS,
        name="loop_spectra",
    )(loop_partner.T, loop_count, flip, pack_matrix(seg_count), moved)
    crossed, *lags[1:] = lax.optimization_barrier((crossed, *lags[1:]))
    crossed = crossed.reshape(devices, out_rows, LANES)
    summed = lax.all_to_all(crossed, ("seg", "chan"), 0, 0, tiled=True)
    columns = np.arange(2 * BINS).reshape(devices, seg_count, -1).swapaxes(0, 1).reshape(-1)
    loop_inverse = inverse_table(seg_count, order[columns], part[columns]).T
    loop_inverse = np.concatenate(split_np(loop_inverse), axis=1)
    near, loop = pl.pallas_call(
        functools.partial(last_kernel, slots),
        out_shape=[near_shape, jax.ShapeDtypeStruct((slots * share, LAGS), F32)],
        in_specs=vmem(2 + seg_count),
        out_specs=vmem(2),
        compiler_params=PARAMS,
        name="lags",
    )(summed, loop_inverse, *lags)
    return near, loop.reshape(1, slots, share, LAGS)


def solution(mesh):
    in_specs = (P("chan", "seg"), P(), P(), P(), P())
    out_specs = (P("chan", "seg", None), P("chan", None, "seg", None))
    return jax.shard_map(body, mesh=mesh, in_specs=in_specs, out_specs=out_specs, check_vma=False)
```

```python
import functools
import math

import jax
import jax.numpy as jnp
import numpy as np
from jax import lax
from jax.experimental import pallas as pl
from jax.experimental.pallas import tpu as pltpu
from jax.sharding import PartitionSpec as P

NFFT = 1024
LAGS = 256
TAPS = 64
DECIM = 4
HALFBAND = 10
SPAN = 64
BINS = 512
WATER = 0.2

LANES = 128
GROUP = 16
GROUPS = BINS // GROUP
OUT_BLOCK = 128
STEP = OUT_BLOCK * DECIM
RADIX = 4
DEPTH = NFFT // RADIX
FAR_BINS = BINS // RADIX

F32 = jnp.float32
BF16 = jnp.bfloat16
MIB = 1024 * 1024
PARAMS = pltpu.CompilerParams(vmem_limit_bytes=32 * MIB)


def bin_order():
    return np.concatenate([np.arange(r, BINS, RADIX) for r in range(RADIX)])


def split_np(table):
    high = table.astype(jnp.bfloat16)
    low = (table - high.astype(np.float64)).astype(jnp.bfloat16)
    return high, low


def short_table():
    bins = np.arange(FAR_BINS).reshape(-1, 1, GROUP, 1)
    angles = (bins * np.arange(DEPTH) % DEPTH) * (2.0 * np.pi / DEPTH)
    rows = np.concatenate([np.cos(angles), np.sin(angles)], axis=1).reshape(-1, DEPTH)
    high, low = split_np(rows)
    return np.concatenate([high, high, low], axis=1)


def twiddle_table():
    angles = np.arange(DEPTH)[:, None] * np.arange(1, RADIX) * (2.0 * np.pi / NFFT)
    columns = np.stack([np.cos(angles), np.sin(angles)], axis=2).reshape(DEPTH, -1)
    return np.repeat(columns, LANES, axis=1).astype(np.float32)


def edge_table():
    bins = bin_order().reshape(GROUPS, 1, GROUP, 1)
    angles = (bins * np.arange(GROUP) % NFFT) * (2.0 * np.pi / NFFT)
    rows = np.concatenate([np.cos(angles), -np.sin(angles)], axis=1) * (bins != 0)
    high, low = split_np(rows.reshape(2 * BINS, GROUP))
    table = np.concatenate([high, high, low], axis=1)
    return np.pad(table.astype(np.float32), ((0, 0), (0, LANES - 3 * GROUP))).astype(jnp.bfloat16)


def inverse_table(total_segs, bins, part):
    lag = np.arange(LAGS) - LAGS // 2
    angles = (bins[None, :] * lag[:, None] % NFFT) * (2.0 * np.pi / NFFT)
    weights = np.where(bins == 0, 1.0, 2.0) / math.sqrt(2.0 * BINS * total_segs)
    return np.where(part[None, :] == 1, -np.sin(angles), np.cos(angles)) * weights[None, :]


def band_tables():
    bins = bin_order()
    inside = np.abs(bins[:, None] - bins[None, :]) <= HALFBAND
    share = np.broadcast_to(1.0 / inside.sum(axis=1, keepdims=True), (BINS, LANES))
    return inside.astype(jnp.bfloat16), share.astype(np.float32)


def split(value):
    high = value.astype(BF16)
    return high, (value - high.astype(F32)).astype(BF16)


def mm(a, b):
    return jnp.dot(a, b, preferred_element_type=F32)


def mm_nt(a, b):
    return lax.dot_general(a, b, (((1,), (1,)), ((), ())), preferred_element_type=F32)


def tap_rows(taps):
    width, period = 2 * LANES, LANES // DECIM
    square = (TAPS, TAPS)
    diagonal = lax.broadcasted_iota(jnp.int32, square, 0) == lax.broadcasted_iota(jnp.int32, square, 1)
    column_taps = jnp.sum(jnp.where(diagonal, taps, 0.0), axis=1, keepdims=True)
    tap = lax.broadcasted_iota(jnp.int32, (TAPS, width), 0)
    column = lax.broadcasted_iota(jnp.int32, (TAPS, width), 1)
    placed = jnp.where(column == LANES + DECIM - 1 - tap, column_taps, 0.0)
    spread = jnp.broadcast_to(jnp.sum(placed, axis=0, keepdims=True), (period, width))
    piece = pltpu.roll(spread, 0, 1, stride=DECIM, stride_axis=0)
    rows = []
    for t in range(OUT_BLOCK // period):
        left = jnp.zeros((period, t * LANES), F32)
        right = jnp.zeros((period, STEP - LANES - t * LANES), F32)
        rows.append(jnp.concatenate([p for p in (left, piece, right) if p.shape[1]], axis=1))
    return jnp.concatenate(rows, axis=0)


def rim_kernel(rec_hbm, rim_ref, tail_ref, sem):
    length = rec_hbm.shape[1]
    copy = pltpu.make_async_copy(rec_hbm.at[:, pl.ds(length - LANES, LANES)], tail_ref, sem)
    copy.start()
    copy.wait()
    rim_ref[...] = tail_ref[...].T[LANES - TAPS :]


def spectrum_kernel(taps_ref, rec_ref, tab_ref, twist_ref, spec_ref, mean_ref, head_ref):
    blocks = rec_ref.shape[1] // STEP
    table = tap_rows(taps_ref[...])
    head_ref[...] = table[:GROUP, :LANES]
    taps_high, taps_low = split(table.T)
    taps_both = jnp.concatenate([taps_high, taps_low], axis=1)
    before = [jnp.zeros((LANES, LANES), BF16)] * 2
    windows = ([], [])
    for j in range(blocks):
        chunk = rec_ref[:, j * STEP : (j + 1) * STEP]
        if j == 0:
            mean = jnp.sum(chunk, axis=1, keepdims=True) * (1.0 / STEP)
        for i, value in enumerate(split(chunk - mean)):
            windows[i].append(jnp.concatenate([before[i], value], axis=1))
            before[i] = value[:, STEP - LANES :]
    wide = mm(jnp.concatenate(windows[0], axis=0), taps_both)
    rest = mm(jnp.concatenate(windows[1], axis=0), taps_high)
    total = wide[:, :LANES] + wide[:, LANES:] + rest
    outputs = [total[t * LANES : (t + 1) * LANES].T for t in range(blocks)]
    pieces = [jnp.concatenate(outputs[j : j + 2], axis=0) for j in range(0, blocks, 2)]
    mean_ref[...] = jnp.broadcast_to(mean, (LANES, LANES)).T[: mean_ref.shape[0]]
    even, odd = pieces[0] + pieces[2], pieces[1] + pieces[3]
    a, b = pieces[0] - pieces[2], pieces[1] - pieces[3]
    whole, half = even + odd, even - odd
    whole = whole - jnp.sum(whole, axis=0, keepdims=True) * (1.0 / DEPTH)
    c1, s1, c2, s2, c3, s3 = [twist_ref[:, i * LANES : (i + 1) * LANES] for i in range(6)]
    inputs = [
        whole,
        a * c1 - b * s1,
        -(a * s1 + b * c1),
        half * c2,
        -(half * s2),
        a * c3 + b * s3,
        b * c3 - a * s3,
    ]
    parts = [split(value) for value in inputs]
    high = jnp.concatenate([p[0] for p in parts], axis=1)
    low = jnp.concatenate([p[1] for p in parts], axis=1)
    out = mm(tab_ref[...], jnp.concatenate([high, low, high], axis=0))
    out = out.reshape(FAR_BINS // GROUP, 2, GROUP, out.shape[1])
    rows = 2 * FAR_BINS
    for r in range(RADIX):
        first = max(2 * r - 1, 0) * LANES
        real_in = out[..., first : first + LANES]
        if r == 0:
            real, imag = real_in[:, 0], -real_in[:, 1]
        else:
            imag_in = out[..., first + LANES : first + 2 * LANES]
            real, imag = real_in[:, 0] + imag_in[:, 1], imag_in[:, 0] - real_in[:, 1]
        both = jnp.stack([real, imag], axis=1).reshape(rows, LANES)
        spec_ref[r * rows : (r + 1) * rows, :] = both


def whiten_kernel(
    spec_ref,
    rim_ref,
    mean_ref,
    head_ref,
    edge_ref,
    band_ref,
    share_ref,
    white_ref,
    up_ref,
    down_ref,
):
    head_high, head_low = split(head_ref[:, LANES - TAPS :])
    rim_high, rim_low = split(rim_ref[...] - mean_ref[0:1, :])
    history = mm(
        jnp.concatenate([head_high, head_high, head_low], axis=1),
        jnp.concatenate([rim_high, rim_low, rim_high], axis=0),
    )
    high, low = split(history)
    stacked = jnp.concatenate([high, low, high], axis=0)
    spec = spec_ref[...] + mm(edge_ref[:, : 3 * GROUP], stacked)
    parted = spec.reshape(GROUPS, 2, GROUP, LANES)
    real, imag = parted[:, 0], parted[:, 1]
    amplitude = jnp.sqrt(real * real + imag * imag).reshape(BINS, LANES)
    high, low = split(amplitude)
    wide = mm(band_ref[...], jnp.concatenate([high, low], axis=1))
    smoothed = (wide[:, :LANES] + wide[:, LANES:]) * share_ref[...]
    level = jnp.sum(amplitude, axis=0, keepdims=True) * (1.0 / BINS)
    scale = 1.0 / (smoothed + (WATER * level + 1e-06))
    white = parted * scale.reshape(GROUPS, 1, GROUP, LANES)
    white_ref[...] = white.astype(BF16)
    flat = white.reshape(2 * BINS, LANES)
    turned = pltpu.roll(flat, SPAN, 1)
    lane = lax.broadcasted_iota(jnp.int32, (BINS, LANES), 1)
    up_ref[...] = jnp.where(lane < SPAN, turned[:BINS], flat[BINS:]).astype(BF16)
    down_ref[...] = jnp.where(lane < SPAN, flat[:BINS], turned[BINS:]).astype(BF16)


def offset_moves(offs_ref):
    row = lax.broadcasted_iota(jnp.int32, (2 * LANES, LANES), 0)
    channel = lax.broadcasted_iota(jnp.int32, (2 * LANES, LANES), 1)
    distance = jnp.where(row < LANES + SPAN, row, row - 2 * LANES) - channel
    hits = [(distance == offs_ref[o]).astype(F32) for o in range(offs_ref.shape[0])]
    return jnp.concatenate(hits, axis=1).astype(BF16)


def pack_matrix(owners):
    share = LANES // owners
    matrix = np.zeros((owners, owners, share, owners, owners, share), np.float32)
    for group in range(owners):
        for owner in range(owners):
            matrix[group, owner, :, owner, group, :] = np.eye(share)
    matrix = matrix.reshape(owners, LANES, owners * LANES)[:, ::-1]
    return matrix.reshape(owners * LANES, owners * LANES).astype(jnp.bfloat16)


def partner_of(place, r, owners):
    return place ^ r if owners & (owners - 1) == 0 else (place + r) % owners


def near_kernel(offs_ref, white_ref, before_ref, after_ref, inv_ref, *refs):
    out_refs, lags_ref = refs[:-1], refs[-1]
    rows = white_ref.shape[0] * 2 * GROUP
    half = rows // 2
    noff = lags_ref.shape[0]
    before, after = before_ref[...].astype(F32), after_ref[...].astype(F32)
    lane = lax.broadcasted_iota(jnp.int32, (half, LANES), 1)
    upper = jnp.where(lane < SPAN, after, pltpu.roll(before, SPAN, 1))
    lower = jnp.where(lane < SPAN, pltpu.roll(after, SPAN, 1), before)
    edge = jnp.concatenate([upper, lower], axis=0).astype(BF16)
    own = white_ref[...].reshape(rows, LANES)
    far = mm(jnp.concatenate([own, edge], axis=1), offset_moves(offs_ref))
    own = own.astype(F32).reshape(-1, 2, GROUP, LANES)
    columns = []
    for o in range(noff):
        other = far[:, o * LANES : (o + 1) * LANES].reshape(own.shape)
        real = own[:, 0] * other[:, 0] + own[:, 1] * other[:, 1]
        imag = own[:, 1] * other[:, 0] - own[:, 0] * other[:, 1]
        columns.append(jnp.stack([real, imag], axis=1).reshape(rows, LANES).astype(BF16))
    both = mm(inv_ref[...], jnp.concatenate(columns, axis=1))
    lags = both[:LAGS] + both[LAGS:]
    for o in range(noff):
        lags_ref[o] = lags[:, o * LANES : (o + 1) * LANES]
    owners = len(out_refs)
    each = noff // owners
    place = lax.axis_index("seg")
    for r in range(owners):
        first = partner_of(place, r, owners) * each
        out_refs[r][...] = lags_ref[pl.ds(first, each)].astype(BF16)


def turn_kernel(*refs):
    near_ref = refs[-1]
    total = sum(ref[...].astype(F32) for ref in refs[:-1])
    for t in range(near_ref.shape[1]):
        near_ref[:, t, :] = total[t].T


def loop_kernel(partner_ref, count_ref, flip_ref, pack_ref, white_ref, out_ref):
    segs, blocks, _, bins, _ = white_ref.shape
    owners = out_ref.shape[0]
    slots = partner_ref.shape[0]
    rows = segs * 2 * bins
    packed_rows = 2 * bins // owners
    turned = mm(white_ref[...].reshape(blocks * rows, LANES), flip_ref[...])
    turned = turned.reshape(white_ref.shape)
    loops = []
    for b in range(blocks):
        own = turned[:, b]
        for k in range(slots):
            partner = jnp.clip(partner_ref[k, b], 0, blocks - 1)
            live = (k < count_ref[b]).astype(F32)
            far = white_ref[:, partner].astype(F32)
            real = jnp.sum(own[:, 0] * far[:, 0] + own[:, 1] * far[:, 1], axis=0)
            imag = jnp.sum(own[:, 1] * far[:, 0] - own[:, 0] * far[:, 1], axis=0)
            pair = jnp.concatenate([real, imag], axis=0) * live
            groups = [pair[g * packed_rows : (g + 1) * packed_rows] for g in range(owners)]
            loops.append(jnp.concatenate(groups, axis=1))
    packed = mm(jnp.concatenate(loops, axis=0).astype(BF16), pack_ref[...])
    depth = slots * packed_rows
    for b in range(blocks):
        for q in range(owners):
            tile = packed[b * depth : (b + 1) * depth, q * LANES : (q + 1) * LANES]
            out_ref[q, b] = tile.astype(BF16)


def loop_lag_kernel(slots, spec_ref, inv_ref, loop_ref):
    sources = spec_ref.shape[0]
    step = spec_ref.shape[1] // slots
    share = loop_ref.shape[0] // slots
    loop = spec_ref[...].astype(F32)
    rows = []
    for k in range(slots):
        turned = loop[:, k * step : (k + 1) * step].reshape(sources * step, LANES).T
        groups = [turned[g * share : (g + 1) * share] for g in range(LANES // share)]
        rows.append(jnp.concatenate(groups, axis=1))
    both = mm(jnp.concatenate(rows, axis=0).astype(BF16), inv_ref[...])
    loop_ref[...] = both[:, :LAGS] + both[:, LAGS:]


def last_kernel(slots, spec_ref, inv_ref, *refs):
    turn_kernel(*refs[:-1])
    loop_lag_kernel(slots, spec_ref, inv_ref, refs[-1])


def vmem(count):
    return [pl.BlockSpec(memory_space=pltpu.VMEM)] * count


def smem(count):
    return [pl.BlockSpec(memory_space=pltpu.SMEM)] * count


def hbm(count):
    return [pl.BlockSpec(memory_space=pltpu.HBM)] * count


def in_hbm(array):
    return pltpu.with_memory_space_constraint(jnp.asarray(array), pltpu.HBM)


def loops_plain(white, loop_partner, loop_count, owners, inverse):
    _, blocks, _, bins, chans = white.shape
    devices = blocks * owners
    slots = loop_partner.shape[1]
    share = chans // owners
    wide = white.astype(F32).swapaxes(0, 1)
    loops = []
    for k in range(slots):
        far = jnp.flip(wide[loop_partner[:, k]], axis=4)
        live = (k < loop_count).astype(F32)[:, None, None]
        real = jnp.sum(wide[:, :, 0] * far[:, :, 0] + wide[:, :, 1] * far[:, :, 1], axis=1)
        imag = jnp.sum(wide[:, :, 1] * far[:, :, 0] - wide[:, :, 0] * far[:, :, 1], axis=1)
        pair = (jnp.stack([real, imag]) * live[None]).astype(BF16)
        loops.append(pair.reshape(2, blocks, bins, owners, share))
    loop = jnp.transpose(jnp.stack(loops), (4, 2, 0, 1, 3, 5))
    loop = loop.reshape(devices, slots, 2 * bins, share)
    summed = lax.all_to_all(loop, ("seg", "chan"), 0, 0, tiled=True).astype(F32)
    table = inverse.astype(np.float32).reshape(LAGS, devices, 2 * bins)
    lags = jnp.einsum("dtvc,ldv->tcl", summed, table, precision=lax.Precision.HIGHEST)
    return lags[None]


def body(recording, filter_taps, offsets, loop_partner, loop_count):
    chan_count = lax.axis_size("chan")
    seg_count = lax.axis_size("seg")
    devices = chan_count * seg_count
    bins = BINS // devices
    chans, length = recording.shape
    noff, slots = offsets.shape[0], loop_partner.shape[1]
    share = chans // seg_count
    near_each = noff // seg_count
    assert length == NFFT * DECIM and chans == LANES and noff % seg_count == 0

    route = [(i, i + 1) for i in range(seg_count - 1)]
    rim = pl.pallas_call(
        rim_kernel,
        out_shape=jax.ShapeDtypeStruct((TAPS, chans), F32),
        in_specs=hbm(1),
        out_specs=pl.BlockSpec(memory_space=pltpu.VMEM),
        scratch_shapes=[pltpu.VMEM((chans, LANES), F32), pltpu.SemaphoreType.DMA],
        compiler_params=PARAMS,
        cost_estimate=pl.CostEstimate(
            flops=10_000_000_000, bytes_accessed=20_000_000, transcendentals=0
        ),
        name="history",
    )(in_hbm(recording))
    rim = lax.ppermute(rim, "seg", route)
    taps = filter_taps.reshape(1, TAPS)
    spec, mean, head = pl.pallas_call(
        spectrum_kernel,
        out_shape=[
            jax.ShapeDtypeStruct((2 * BINS, LANES), F32),
            jax.ShapeDtypeStruct((8, LANES), F32),
            jax.ShapeDtypeStruct((GROUP, LANES), F32),
        ],
        in_specs=vmem(4),
        out_specs=vmem(3),
        compiler_params=PARAMS,
        cost_estimate=pl.CostEstimate(
            flops=1_000_000_000, bytes_accessed=5_000_000, transcendentals=0
        ),
        name="filter_and_transform",
    )(taps, recording, short_table(), twiddle_table())

    band, band_share = band_tables()
    half = jax.ShapeDtypeStruct((BINS, LANES), BF16)
    white, up, down = pl.pallas_call(
        whiten_kernel,
        out_shape=[jax.ShapeDtypeStruct((GROUPS, 2, GROUP, LANES), BF16), half, half],
        in_specs=vmem(7),
        out_specs=vmem(3),
        compiler_params=PARAMS,
        name="whiten",
    )(spec, rim, mean, head, edge_table(), band, band_share)

    spread = white
    if bins != GROUP:
        spread = jnp.moveaxis(white, 1, 0).reshape(2, devices, bins, LANES)
        spread = jnp.moveaxis(spread, 0, 1)
    moved = lax.all_to_all(spread, ("seg", "chan"), 0, 0, tiled=True)
    moved = moved.reshape(seg_count, chan_count, 2, bins, LANES)

    ring = [(i, (i + 1) % chan_count) for i in range(chan_count)]
    before = lax.ppermute(up, "chan", ring)
    after = lax.ppermute(down, "chan", [(j, i) for i, j in ring])
    order = np.repeat(bin_order().reshape(GROUPS, 1, GROUP), 2, axis=1).reshape(-1)
    part = np.broadcast_to(np.arange(2).reshape(1, 2, 1), (GROUPS, 2, GROUP)).reshape(-1)
    inverse = np.concatenate(split_np(inverse_table(seg_count, order, part)), axis=0)
    lags = pl.pallas_call(
        near_kernel,
        out_shape=[jax.ShapeDtypeStruct((near_each, LAGS, LANES), BF16)] * seg_count,
        in_specs=smem(1) + vmem(4),
        out_specs=vmem(seg_count),
        scratch_shapes=[pltpu.VMEM((noff, LAGS, LANES), F32)],
        compiler_params=PARAMS,
        cost_estimate=pl.CostEstimate(
            flops=20_000_000_000, bytes_accessed=20_000_000, transcendentals=0
        ),
        name="near_lags",
    )(offsets, white, before, after, inverse)
    lags = list(lags)
    for r in range(seg_count - 1, 0, -1):
        route = [(i, partner_of(i, r, seg_count)) for i in range(seg_count)]
        lags[r] = lax.ppermute(lags[r], "seg", route)
    moved, lags[0] = lax.optimization_barrier((moved, lags[0]))

    near_shape = jax.ShapeDtypeStruct((chans, near_each, LAGS), F32)
    if bins % GROUP or 2 * bins % (8 * seg_count):
        order = np.repeat(bin_order().reshape(devices, 1, bins), 2, axis=1).reshape(-1)
        part = np.broadcast_to(np.arange(2).reshape(1, 2, 1), (devices, 2, bins)).reshape(-1)
        loop_inverse = inverse_table(seg_count, order, part)
        loop = loops_plain(moved, loop_partner, loop_count, seg_count, loop_inverse)
        near = pl.pallas_call(
            turn_kernel,
            out_shape=near_shape,
            in_specs=vmem(seg_count),
            out_specs=pl.BlockSpec(memory_space=pltpu.VMEM),
            compiler_params=PARAMS,
            name="near_turn",
        )(*lags)
        return near, loop

    flip = np.eye(LANES, dtype=np.float32)[::-1].astype(jnp.bfloat16)
    out_rows = slots * (2 * bins // seg_count)
    crossed = pl.pallas_call(
        loop_kernel,
        out_shape=jax.ShapeDtypeStruct((seg_count, chan_count, out_rows, LANES), BF16),
        in_specs=smem(2) + vmem(3),
        out_specs=pl.BlockSpec(memory_space=pltpu.VMEM),
        compiler_params=PARAMS,
        name="loop_spectra",
    )(loop_partner.T, loop_count, flip, pack_matrix(seg_count), moved)
    crossed, *lags[1:] = lax.optimization_barrier((crossed, *lags[1:]))
    crossed = crossed.reshape(devices, out_rows, LANES)
    summed = lax.all_to_all(crossed, ("seg", "chan"), 0, 0, tiled=True)
    columns = np.arange(2 * BINS).reshape(devices, seg_count, -1).swapaxes(0, 1).reshape(-1)
    loop_inverse = inverse_table(seg_count, order[columns], part[columns]).T
    loop_inverse = np.concatenate(split_np(loop_inverse), axis=1)
    near, loop = pl.pallas_call(
        functools.partial(last_kernel, slots),
        out_shape=[near_shape, jax.ShapeDtypeStruct((slots * share, LAGS), F32)],
        in_specs=vmem(2 + seg_count),
        out_specs=vmem(2),
        compiler_params=PARAMS,
        name="lags",
    )(summed, loop_inverse, *lags)
    return near, loop.reshape(1, slots, share, LAGS)


def solution(mesh):
    in_specs = (P("chan", "seg"), P(), P(), P(), P())
    out_specs = (P("chan", "seg", None), P("chan", None, "seg", None))
    return jax.shard_map(body, mesh=mesh, in_specs=in_specs, out_specs=out_specs, check_vma=False)
```

```python
import functools
import math

import jax
import jax.numpy as jnp
import numpy as np
from jax import lax
from jax.experimental import pallas as pl
from jax.experimental.pallas import tpu as pltpu
from jax.sharding import PartitionSpec as P

NFFT = 1024
LAGS = 256
TAPS = 64
DECIM = 4
HALFBAND = 10
SPAN = 64
BINS = 512
WATER = 0.2

LANES = 128
GROUP = 16
GROUPS = BINS // GROUP
OUT_BLOCK = 128
STEP = OUT_BLOCK * DECIM
RADIX = 4
DEPTH = NFFT // RADIX
FAR_BINS = BINS // RADIX

F32 = jnp.float32
BF16 = jnp.bfloat16
MIB = 1024 * 1024
PARAMS = pltpu.CompilerParams(vmem_limit_bytes=32 * MIB)


def bin_order():
    return np.concatenate([np.arange(r, BINS, RADIX) for r in range(RADIX)])


def split_np(table):
    high = table.astype(jnp.bfloat16)
    low = (table - high.astype(np.float64)).astype(jnp.bfloat16)
    return high, low


def short_table():
    bins = np.arange(FAR_BINS).reshape(-1, 1, GROUP, 1)
    angles = (bins * np.arange(DEPTH) % DEPTH) * (2.0 * np.pi / DEPTH)
    rows = np.concatenate([np.cos(angles), np.sin(angles)], axis=1).reshape(-1, DEPTH)
    high, low = split_np(rows)
    return np.concatenate([high, high, low], axis=1)


def twiddle_table():
    angles = np.arange(DEPTH)[:, None] * np.arange(1, RADIX) * (2.0 * np.pi / NFFT)
    columns = np.stack([np.cos(angles), np.sin(angles)], axis=2).reshape(DEPTH, -1)
    return np.pad(columns, ((0, 0), (0, LANES - columns.shape[1]))).astype(np.float32)


def edge_table():
    bins = bin_order().reshape(GROUPS, 1, GROUP, 1)
    angles = (bins * np.arange(GROUP) % NFFT) * (2.0 * np.pi / NFFT)
    rows = np.concatenate([np.cos(angles), -np.sin(angles)], axis=1) * (bins != 0)
    high, low = split_np(rows.reshape(2 * BINS, GROUP))
    table = np.concatenate([high, high, low], axis=1)
    return np.pad(table.astype(np.float32), ((0, 0), (0, LANES - 3 * GROUP))).astype(jnp.bfloat16)


def inverse_table(total_segs, bins, part):
    lag = np.arange(LAGS) - LAGS // 2
    angles = (bins[None, :] * lag[:, None] % NFFT) * (2.0 * np.pi / NFFT)
    weights = np.where(bins == 0, 1.0, 2.0) / math.sqrt(2.0 * BINS * total_segs)
    return np.where(part[None, :] == 1, -np.sin(angles), np.cos(angles)) * weights[None, :]


def band_tables():
    bins = bin_order()
    inside = np.abs(bins[:, None] - bins[None, :]) <= HALFBAND
    share = np.broadcast_to(1.0 / inside.sum(axis=1, keepdims=True), (BINS, LANES))
    return inside.astype(jnp.bfloat16), share.astype(np.float32)


def split(value):
    high = value.astype(BF16)
    return high, (value - high.astype(F32)).astype(BF16)


def mm(a, b):
    return jnp.dot(a, b, preferred_element_type=F32)


def mm_nt(a, b):
    return lax.dot_general(a, b, (((1,), (1,)), ((), ())), preferred_element_type=F32)


def tap_rows(taps):
    width, period = 2 * LANES, LANES // DECIM
    square = (TAPS, TAPS)
    diagonal = lax.broadcasted_iota(jnp.int32, square, 0) == lax.broadcasted_iota(jnp.int32, square, 1)
    column_taps = jnp.sum(jnp.where(diagonal, taps, 0.0), axis=1, keepdims=True)
    tap = lax.broadcasted_iota(jnp.int32, (TAPS, width), 0)
    column = lax.broadcasted_iota(jnp.int32, (TAPS, width), 1)
    placed = jnp.where(column == LANES + DECIM - 1 - tap, column_taps, 0.0)
    spread = jnp.broadcast_to(jnp.sum(placed, axis=0, keepdims=True), (period, width))
    piece = pltpu.roll(spread, 0, 1, stride=DECIM, stride_axis=0)
    rows = []
    for t in range(OUT_BLOCK // period):
        left = jnp.zeros((period, t * LANES), F32)
        right = jnp.zeros((period, STEP - LANES - t * LANES), F32)
        rows.append(jnp.concatenate([p for p in (left, piece, right) if p.shape[1]], axis=1))
    return jnp.concatenate(rows, axis=0)


def rim_kernel(rec_hbm, rim_ref, tail_ref, sem):
    length = rec_hbm.shape[1]
    copy = pltpu.make_async_copy(rec_hbm.at[:, pl.ds(length - LANES, LANES)], tail_ref, sem)
    copy.start()
    copy.wait()
    tail = tail_ref[...].T[LANES - TAPS :]
    mean = jnp.sum(tail, axis=0, keepdims=True) * (1.0 / TAPS)
    high, _ = split(mean)
    middle, low = split(mean - high.astype(F32))
    parts = [high, middle, low]
    row = lax.broadcasted_iota(jnp.int32, (GROUP, LANES), 0)
    means = jnp.zeros((GROUP, LANES), F32)
    for i, part in enumerate(parts):
        means = jnp.where(row == i, part.astype(F32), means)
    rim_ref[...] = jnp.concatenate([tail - mean, means], axis=0).astype(BF16)


def spectrum_kernel(taps_ref, rec_ref, tab_ref, twist_ref, spec_ref, mean_ref, head_ref):
    blocks = rec_ref.shape[1] // STEP
    table = tap_rows(taps_ref[...])
    head_ref[...] = table[:GROUP, :LANES]
    taps_high, taps_low = split(table.T)
    taps_both = jnp.concatenate([taps_high, taps_low], axis=1)
    before = [jnp.zeros((LANES, LANES), BF16)] * 2
    outputs = []
    for first in range(0, blocks, blocks // 2):
        windows = ([], [])
        for j in range(first, first + blocks // 2):
            chunk = rec_ref[:, j * STEP : (j + 1) * STEP]
            if j == 0:
                mean = jnp.sum(chunk, axis=1, keepdims=True) * (1.0 / STEP)
            for i, value in enumerate(split(chunk - mean)):
                windows[i].append(jnp.concatenate([before[i], value], axis=1))
                before[i] = value[:, STEP - LANES :]
        wide = mm(jnp.concatenate(windows[0], axis=0), taps_both)
        rest = mm(jnp.concatenate(windows[1], axis=0), taps_high)
        total = wide[:, :LANES] + wide[:, LANES:] + rest
        outputs += [total[t * LANES : (t + 1) * LANES].T for t in range(blocks // 2)]
    pieces = [jnp.concatenate(outputs[j : j + 2], axis=0) for j in range(0, blocks, 2)]
    mean_ref[...] = jnp.broadcast_to(mean, (LANES, LANES)).T[: mean_ref.shape[0]]
    even, odd = pieces[0] + pieces[2], pieces[1] + pieces[3]
    a, b = pieces[0] - pieces[2], pieces[1] - pieces[3]
    whole, half = even + odd, even - odd
    whole = whole - jnp.sum(whole, axis=0, keepdims=True) * (1.0 / DEPTH)
    c1, s1, c2, s2, c3, s3 = [twist_ref[:, i : i + 1] for i in range(6)]
    inputs = [
        whole,
        a * c1 - b * s1,
        -(a * s1 + b * c1),
        half * c2,
        -(half * s2),
        a * c3 + b * s3,
        b * c3 - a * s3,
    ]
    parts = [split(value) for value in inputs]
    high = jnp.concatenate([p[0] for p in parts], axis=1)
    low = jnp.concatenate([p[1] for p in parts], axis=1)
    out = mm(tab_ref[...], jnp.concatenate([high, low, high], axis=0))
    out = out.reshape(FAR_BINS // GROUP, 2, GROUP, out.shape[1])
    rows = 2 * FAR_BINS
    for r in range(RADIX):
        first = max(2 * r - 1, 0) * LANES
        real_in = out[..., first : first + LANES]
        if r == 0:
            real, imag = real_in[:, 0], -real_in[:, 1]
        else:
            imag_in = out[..., first + LANES : first + 2 * LANES]
            real, imag = real_in[:, 0] + imag_in[:, 1], imag_in[:, 0] - real_in[:, 1]
        both = jnp.stack([real, imag], axis=1).reshape(rows, LANES)
        spec_ref[r * rows : (r + 1) * rows, :] = both


def whiten_kernel(
    spec_ref,
    rim_ref,
    mean_ref,
    head_ref,
    edge_ref,
    band_ref,
    share_ref,
    white_ref,
    up_ref,
    down_ref,
):
    head_high, head_low = split(head_ref[:, LANES - TAPS :])
    rim = rim_ref[...].astype(F32)
    offset = jnp.sum(rim[TAPS:], axis=0, keepdims=True) - mean_ref[0:1, :]
    rim_high, rim_low = split(rim[:TAPS] + offset)
    history = mm(
        jnp.concatenate([head_high, head_high, head_low], axis=1),
        jnp.concatenate([rim_high, rim_low, rim_high], axis=0),
    )
    high, low = split(history)
    stacked = jnp.concatenate([high, low, high], axis=0)
    spec = spec_ref[...] + mm(edge_ref[:, : 3 * GROUP], stacked)
    parted = spec.reshape(GROUPS, 2, GROUP, LANES)
    real, imag = parted[:, 0], parted[:, 1]
    amplitude = jnp.sqrt(real * real + imag * imag).reshape(BINS, LANES)
    high, low = split(amplitude)
    wide = mm(band_ref[...], jnp.concatenate([high, low], axis=1))
    smoothed = (wide[:, :LANES] + wide[:, LANES:]) * share_ref[...]
    level = jnp.sum(amplitude, axis=0, keepdims=True) * (1.0 / BINS)
    scale = 1.0 / (smoothed + (WATER * level + 1e-06))
    white = parted * scale.reshape(GROUPS, 1, GROUP, LANES)
    white_ref[...] = white.astype(BF16)
    flat = white.reshape(2 * BINS, LANES)
    turned = pltpu.roll(flat, SPAN, 1)
    lane = lax.broadcasted_iota(jnp.int32, (BINS, LANES), 1)
    up_ref[...] = jnp.where(lane < SPAN, turned[:BINS], flat[BINS:]).astype(BF16)
    down_ref[...] = jnp.where(lane < SPAN, flat[:BINS], turned[BINS:]).astype(BF16)


def offset_moves(offs_ref):
    row = lax.broadcasted_iota(jnp.int32, (2 * LANES, LANES), 0)
    channel = lax.broadcasted_iota(jnp.int32, (2 * LANES, LANES), 1)
    distance = jnp.where(row < LANES + SPAN, row, row - 2 * LANES) - channel
    hits = [(distance == offs_ref[o]).astype(F32) for o in range(offs_ref.shape[0])]
    return jnp.concatenate(hits, axis=1).astype(BF16)


def pack_matrix(owners):
    share = LANES // owners
    matrix = np.zeros((owners, owners, share, owners, owners, share), np.float32)
    for group in range(owners):
        for owner in range(owners):
            matrix[group, owner, :, owner, group, :] = np.eye(share)
    matrix = matrix.reshape(owners, LANES, owners * LANES)[:, ::-1]
    return matrix.reshape(owners * LANES, owners * LANES).astype(jnp.bfloat16)


def partner_of(place, r, owners):
    return place ^ r if owners & (owners - 1) == 0 else (place + r) % owners


def near_kernel(offs_ref, white_ref, before_ref, after_ref, inv_ref, *refs):
    out_refs, lags_ref = refs[:-1], refs[-1]
    rows = white_ref.shape[0] * 2 * GROUP
    half = rows // 2
    noff = lags_ref.shape[0]
    before, after = before_ref[...].astype(F32), after_ref[...].astype(F32)
    lane = lax.broadcasted_iota(jnp.int32, (half, LANES), 1)
    upper = jnp.where(lane < SPAN, after, pltpu.roll(before, SPAN, 1))
    lower = jnp.where(lane < SPAN, pltpu.roll(after, SPAN, 1), before)
    edge = jnp.concatenate([upper, lower], axis=0).astype(BF16)
    own = white_ref[...].reshape(rows, LANES)
    far = mm(jnp.concatenate([own, edge], axis=1), offset_moves(offs_ref))
    own = own.astype(F32).reshape(-1, 2, GROUP, LANES)
    columns = []
    for o in range(noff):
        other = far[:, o * LANES : (o + 1) * LANES].reshape(own.shape)
        real = own[:, 0] * other[:, 0] + own[:, 1] * other[:, 1]
        imag = own[:, 1] * other[:, 0] - own[:, 0] * other[:, 1]
        columns.append(jnp.stack([real, imag], axis=1).reshape(rows, LANES).astype(BF16))
    both = mm(inv_ref[...], jnp.concatenate(columns, axis=1))
    lags = both[:LAGS] + both[LAGS:]
    for o in range(noff):
        lags_ref[o] = lags[:, o * LANES : (o + 1) * LANES]
    owners = len(out_refs)
    each = noff // owners
    place = lax.axis_index("seg")
    for r in range(owners):
        first = partner_of(place, r, owners) * each
        out_refs[r][...] = lags_ref[pl.ds(first, each)].astype(BF16)


def turn_kernel(*refs):
    near_ref = refs[-1]
    total = sum(ref[...].astype(F32) for ref in refs[:-1])
    for t in range(near_ref.shape[1]):
        near_ref[:, t, :] = total[t].T


def loop_kernel(partner_ref, count_ref, flip_ref, pack_ref, white_ref, out_ref):
    segs, blocks, _, bins, _ = white_ref.shape
    owners = out_ref.shape[0]
    slots = partner_ref.shape[0]
    rows = segs * 2 * bins
    packed_rows = 2 * bins // owners
    turned = mm(white_ref[...].reshape(blocks * rows, LANES), flip_ref[...])
    turned = turned.reshape(white_ref.shape)
    loops = []
    for b in range(blocks):
        own = turned[:, b]
        for k in range(slots):
            partner = jnp.clip(partner_ref[k, b], 0, blocks - 1)
            live = (k < count_ref[b]).astype(F32)
            far = white_ref[:, partner].astype(F32)
            real = jnp.sum(own[:, 0] * far[:, 0] + own[:, 1] * far[:, 1], axis=0)
            imag = jnp.sum(own[:, 1] * far[:, 0] - own[:, 0] * far[:, 1], axis=0)
            pair = jnp.concatenate([real, imag], axis=0) * live
            groups = [pair[g * packed_rows : (g + 1) * packed_rows] for g in range(owners)]
            loops.append(jnp.concatenate(groups, axis=1))
    packed = mm(jnp.concatenate(loops, axis=0).astype(BF16), pack_ref[...])
    depth = slots * packed_rows
    for b in range(blocks):
        for q in range(owners):
            tile = packed[b * depth : (b + 1) * depth, q * LANES : (q + 1) * LANES]
            out_ref[q, b] = tile.astype(BF16)


def loop_lag_kernel(slots, spec_ref, inv_ref, loop_ref):
    sources = spec_ref.shape[0]
    step = spec_ref.shape[1] // slots
    share = loop_ref.shape[0] // slots
    loop = spec_ref[...].astype(F32)
    rows = []
    for k in range(slots):
        turned = loop[:, k * step : (k + 1) * step].reshape(sources * step, LANES).T
        groups = [turned[g * share : (g + 1) * share] for g in range(LANES // share)]
        rows.append(jnp.concatenate(groups, axis=1))
    both = mm(jnp.concatenate(rows, axis=0).astype(BF16), inv_ref[...])
    loop_ref[...] = both[:, :LAGS] + both[:, LAGS:]


def last_kernel(slots, spec_ref, inv_ref, *refs):
    turn_kernel(*refs[:-1])
    loop_lag_kernel(slots, spec_ref, inv_ref, refs[-1])


def vmem(count):
    return [pl.BlockSpec(memory_space=pltpu.VMEM)] * count


def smem(count):
    return [pl.BlockSpec(memory_space=pltpu.SMEM)] * count


def hbm(count):
    return [pl.BlockSpec(memory_space=pltpu.HBM)] * count


def in_hbm(array):
    return pltpu.with_memory_space_constraint(jnp.asarray(array), pltpu.HBM)


def loops_plain(white, loop_partner, loop_count, owners, inverse):
    _, blocks, _, bins, chans = white.shape
    devices = blocks * owners
    slots = loop_partner.shape[1]
    share = chans // owners
    wide = white.astype(F32).swapaxes(0, 1)
    loops = []
    for k in range(slots):
        far = jnp.flip(wide[loop_partner[:, k]], axis=4)
        live = (k < loop_count).astype(F32)[:, None, None]
        real = jnp.sum(wide[:, :, 0] * far[:, :, 0] + wide[:, :, 1] * far[:, :, 1], axis=1)
        imag = jnp.sum(wide[:, :, 1] * far[:, :, 0] - wide[:, :, 0] * far[:, :, 1], axis=1)
        pair = (jnp.stack([real, imag]) * live[None]).astype(BF16)
        loops.append(pair.reshape(2, blocks, bins, owners, share))
    loop = jnp.transpose(jnp.stack(loops), (4, 2, 0, 1, 3, 5))
    loop = loop.reshape(devices, slots, 2 * bins, share)
    summed = lax.all_to_all(loop, ("seg", "chan"), 0, 0, tiled=True).astype(F32)
    table = inverse.astype(np.float32).reshape(LAGS, devices, 2 * bins)
    lags = jnp.einsum("dtvc,ldv->tcl", summed, table, precision=lax.Precision.HIGHEST)
    return lags[None]


def body(recording, filter_taps, offsets, loop_partner, loop_count):
    chan_count = lax.axis_size("chan")
    seg_count = lax.axis_size("seg")
    devices = chan_count * seg_count
    bins = BINS // devices
    chans, length = recording.shape
    noff, slots = offsets.shape[0], loop_partner.shape[1]
    share = chans // seg_count
    near_each = noff // seg_count
    assert length == NFFT * DECIM and chans == LANES and noff % seg_count == 0

    route = [(i, i + 1) for i in range(seg_count - 1)]
    rim = pl.pallas_call(
        rim_kernel,
        out_shape=jax.ShapeDtypeStruct((TAPS + GROUP, chans), BF16),
        in_specs=hbm(1),
        out_specs=pl.BlockSpec(memory_space=pltpu.VMEM),
        scratch_shapes=[pltpu.VMEM((chans, LANES), F32), pltpu.SemaphoreType.DMA],
        compiler_params=PARAMS,
        cost_estimate=pl.CostEstimate(
            flops=10_000_000_000, bytes_accessed=20_000_000, transcendentals=0
        ),
        name="history",
    )(in_hbm(recording))
    rim = lax.ppermute(rim, "seg", route)
    taps = filter_taps.reshape(1, TAPS)
    spec, mean, head = pl.pallas_call(
        spectrum_kernel,
        out_shape=[
            jax.ShapeDtypeStruct((2 * BINS, LANES), F32),
            jax.ShapeDtypeStruct((8, LANES), F32),
            jax.ShapeDtypeStruct((GROUP, LANES), F32),
        ],
        in_specs=vmem(4),
        out_specs=vmem(3),
        compiler_params=PARAMS,
        cost_estimate=pl.CostEstimate(
            flops=1_000_000_000, bytes_accessed=5_000_000, transcendentals=0
        ),
        name="filter_and_transform",
    )(taps, recording, short_table(), twiddle_table())

    band, band_share = band_tables()
    half = jax.ShapeDtypeStruct((BINS, LANES), BF16)
    white, up, down = pl.pallas_call(
        whiten_kernel,
        out_shape=[jax.ShapeDtypeStruct((GROUPS, 2, GROUP, LANES), BF16), half, half],
        in_specs=vmem(7),
        out_specs=vmem(3),
        compiler_params=PARAMS,
        name="whiten",
    )(spec, rim, mean, head, edge_table(), band, band_share)

    spread = white
    if bins != GROUP:
        spread = jnp.moveaxis(white, 1, 0).reshape(2, devices, bins, LANES)
        spread = jnp.moveaxis(spread, 0, 1)
    moved = lax.all_to_all(spread, ("seg", "chan"), 0, 0, tiled=True)
    moved = moved.reshape(seg_count, chan_count, 2, bins, LANES)

    ring = [(i, (i + 1) % chan_count) for i in range(chan_count)]
    before = lax.ppermute(up, "chan", ring)
    after = lax.ppermute(down, "chan", [(j, i) for i, j in ring])
    order = np.repeat(bin_order().reshape(GROUPS, 1, GROUP), 2, axis=1).reshape(-1)
    part = np.broadcast_to(np.arange(2).reshape(1, 2, 1), (GROUPS, 2, GROUP)).reshape(-1)
    inverse = np.concatenate(split_np(inverse_table(seg_count, order, part)), axis=0)
    lags = pl.pallas_call(
        near_kernel,
        out_shape=[jax.ShapeDtypeStruct((near_each, LAGS, LANES), BF16)] * seg_count,
        in_specs=smem(1) + vmem(4),
        out_specs=vmem(seg_count),
        scratch_shapes=[pltpu.VMEM((noff, LAGS, LANES), F32)],
        compiler_params=PARAMS,
        cost_estimate=pl.CostEstimate(
            flops=20_000_000_000, bytes_accessed=20_000_000, transcendentals=0
        ),
        name="near_lags",
    )(offsets, white, before, after, inverse)
    lags = list(lags)
    for r in range(seg_count - 1, 0, -1):
        route = [(i, partner_of(i, r, seg_count)) for i in range(seg_count)]
        lags[r] = lax.ppermute(lags[r], "seg", route)
    moved, lags[0] = lax.optimization_barrier((moved, lags[0]))

    near_shape = jax.ShapeDtypeStruct((chans, near_each, LAGS), F32)
    if bins % GROUP or 2 * bins % (8 * seg_count):
        order = np.repeat(bin_order().reshape(devices, 1, bins), 2, axis=1).reshape(-1)
        part = np.broadcast_to(np.arange(2).reshape(1, 2, 1), (devices, 2, bins)).reshape(-1)
        loop_inverse = inverse_table(seg_count, order, part)
        loop = loops_plain(moved, loop_partner, loop_count, seg_count, loop_inverse)
        near = pl.pallas_call(
            turn_kernel,
            out_shape=near_shape,
            in_specs=vmem(seg_count),
            out_specs=pl.BlockSpec(memory_space=pltpu.VMEM),
            compiler_params=PARAMS,
            name="near_turn",
        )(*lags)
        return near, loop

    flip = np.eye(LANES, dtype=np.float32)[::-1].astype(jnp.bfloat16)
    out_rows = slots * (2 * bins // seg_count)
    crossed = pl.pallas_call(
        loop_kernel,
        out_shape=jax.ShapeDtypeStruct((seg_count, chan_count, out_rows, LANES), BF16),
        in_specs=smem(2) + vmem(3),
        out_specs=pl.BlockSpec(memory_space=pltpu.VMEM),
        compiler_params=PARAMS,
        name="loop_spectra",
    )(loop_partner.T, loop_count, flip, pack_matrix(seg_count), moved)
    crossed, *lags[1:] = lax.optimization_barrier((crossed, *lags[1:]))
    crossed = crossed.reshape(devices, out_rows, LANES)
    summed = lax.all_to_all(crossed, ("seg", "chan"), 0, 0, tiled=True)
    columns = np.arange(2 * BINS).reshape(devices, seg_count, -1).swapaxes(0, 1).reshape(-1)
    loop_inverse = inverse_table(seg_count, order[columns], part[columns]).T
    loop_inverse = np.concatenate(split_np(loop_inverse), axis=1)
    near, loop = pl.pallas_call(
        functools.partial(last_kernel, slots),
        out_shape=[near_shape, jax.ShapeDtypeStruct((slots * share, LAGS), F32)],
        in_specs=vmem(2 + seg_count),
        out_specs=vmem(2),
        compiler_params=PARAMS,
        name="lags",
    )(summed, loop_inverse, *lags)
    return near, loop.reshape(1, slots, share, LAGS)


def solution(mesh):
    in_specs = (P("chan", "seg"), P(), P(), P(), P())
    out_specs = (P("chan", "seg", None), P("chan", None, "seg", None))
    return jax.shard_map(body, mesh=mesh, in_specs=in_specs, out_specs=out_specs, check_vma=False)
```

```python
import functools
import math

import jax
import jax.numpy as jnp
import numpy as np
from jax import lax
from jax.experimental import pallas as pl
from jax.experimental.pallas import tpu as pltpu
from jax.sharding import PartitionSpec as P

NFFT = 1024
LAGS = 256
TAPS = 64
DECIM = 4
HALFBAND = 10
SPAN = 64
BINS = 512
WATER = 0.2

LANES = 128
GROUP = 16
GROUPS = BINS // GROUP
OUT_BLOCK = 128
STEP = OUT_BLOCK * DECIM
RADIX = 4
DEPTH = NFFT // RADIX
FAR_BINS = BINS // RADIX

F32 = jnp.float32
BF16 = jnp.bfloat16
MIB = 1024 * 1024
PARAMS = pltpu.CompilerParams(vmem_limit_bytes=32 * MIB)


def bin_order():
    return np.concatenate([np.arange(r, BINS, RADIX) for r in range(RADIX)])


def split_np(table):
    high = table.astype(jnp.bfloat16)
    low = (table - high.astype(np.float64)).astype(jnp.bfloat16)
    return high, low


def short_table():
    bins = np.arange(FAR_BINS).reshape(-1, 1, GROUP, 1)
    angles = (bins * np.arange(DEPTH) % DEPTH) * (2.0 * np.pi / DEPTH)
    rows = np.concatenate([np.cos(angles), np.sin(angles)], axis=1).reshape(-1, DEPTH)
    high, low = split_np(rows)
    return np.concatenate([high, high, low], axis=1)


def twiddle_table():
    angles = np.arange(DEPTH)[:, None] * np.arange(1, RADIX) * (2.0 * np.pi / NFFT)
    columns = np.stack([np.cos(angles), np.sin(angles)], axis=2).reshape(DEPTH, -1)
    return np.pad(columns, ((0, 0), (0, LANES - columns.shape[1]))).astype(np.float32)


def edge_table():
    bins = bin_order().reshape(GROUPS, 1, GROUP, 1)
    angles = (bins * np.arange(GROUP) % NFFT) * (2.0 * np.pi / NFFT)
    rows = np.concatenate([np.cos(angles), -np.sin(angles)], axis=1) * (bins != 0)
    high, low = split_np(rows.reshape(2 * BINS, GROUP))
    table = np.concatenate([high, high, low], axis=1)
    return np.pad(table.astype(np.float32), ((0, 0), (0, LANES - 3 * GROUP))).astype(jnp.bfloat16)


def inverse_table(total_segs, bins, part):
    lag = np.arange(LAGS) - LAGS // 2
    angles = (bins[None, :] * lag[:, None] % NFFT) * (2.0 * np.pi / NFFT)
    weights = np.where(bins == 0, 1.0, 2.0) / math.sqrt(2.0 * BINS * total_segs)
    return np.where(part[None, :] == 1, -np.sin(angles), np.cos(angles)) * weights[None, :]


def band_tables():
    bins = bin_order()
    inside = np.abs(bins[:, None] - bins[None, :]) <= HALFBAND
    share = np.broadcast_to(1.0 / inside.sum(axis=1, keepdims=True), (BINS, LANES))
    return inside.astype(jnp.bfloat16), share.astype(np.float32)


def split(value):
    high = value.astype(BF16)
    return high, (value - high.astype(F32)).astype(BF16)


def mm(a, b):
    return jnp.dot(a, b, preferred_element_type=F32)


def mm_nt(a, b):
    return lax.dot_general(a, b, (((1,), (1,)), ((), ())), preferred_element_type=F32)


def tap_rows(taps):
    width, period = 2 * LANES, LANES // DECIM
    square = (TAPS, TAPS)
    diagonal = lax.broadcasted_iota(jnp.int32, square, 0) == lax.broadcasted_iota(jnp.int32, square, 1)
    column_taps = jnp.sum(jnp.where(diagonal, taps, 0.0), axis=1, keepdims=True)
    tap = lax.broadcasted_iota(jnp.int32, (TAPS, width), 0)
    column = lax.broadcasted_iota(jnp.int32, (TAPS, width), 1)
    placed = jnp.where(column == LANES + DECIM - 1 - tap, column_taps, 0.0)
    spread = jnp.broadcast_to(jnp.sum(placed, axis=0, keepdims=True), (period, width))
    piece = pltpu.roll(spread, 0, 1, stride=DECIM, stride_axis=0)
    rows = []
    for t in range(OUT_BLOCK // period):
        left = jnp.zeros((period, t * LANES), F32)
        right = jnp.zeros((period, STEP - LANES - t * LANES), F32)
        rows.append(jnp.concatenate([p for p in (left, piece, right) if p.shape[1]], axis=1))
    return jnp.concatenate(rows, axis=0)


def rim_kernel(rec_hbm, rim_ref, tail_ref, sem):
    length = rec_hbm.shape[1]
    copy = pltpu.make_async_copy(rec_hbm.at[:, pl.ds(length - LANES, LANES)], tail_ref, sem)
    copy.start()
    copy.wait()
    rim_ref[...] = tail_ref[...].T[LANES - TAPS :]


def spectrum_kernel(taps_ref, rec_ref, tab_ref, twist_ref, spec_ref, mean_ref, head_ref):
    blocks = rec_ref.shape[1] // STEP
    table = tap_rows(taps_ref[...])
    head_ref[...] = table[:GROUP, :LANES]
    taps_high, taps_low = split(table.T)
    taps_both = jnp.concatenate([taps_high, taps_low], axis=1)
    before = [jnp.zeros((LANES, LANES), BF16)] * 2
    outputs = []
    for first in range(0, blocks, blocks // 2):
        windows = ([], [])
        for j in range(first, first + blocks // 2):
            chunk = rec_ref[:, j * STEP : (j + 1) * STEP]
            if j == 0:
                mean = jnp.sum(chunk, axis=1, keepdims=True) * (1.0 / STEP)
            for i, value in enumerate(split(chunk - mean)):
                windows[i].append(jnp.concatenate([before[i], value], axis=1))
                before[i] = value[:, STEP - LANES :]
        wide = mm(jnp.concatenate(windows[0], axis=0), taps_both)
        rest = mm(jnp.concatenate(windows[1], axis=0), taps_high)
        total = wide[:, :LANES] + wide[:, LANES:] + rest
        outputs += [total[t * LANES : (t + 1) * LANES].T for t in range(blocks // 2)]
    pieces = [jnp.concatenate(outputs[j : j + 2], axis=0) for j in range(0, blocks, 2)]
    mean_ref[...] = jnp.broadcast_to(mean, (LANES, LANES)).T[: mean_ref.shape[0]]
    even, odd = pieces[0] + pieces[2], pieces[1] + pieces[3]
    a, b = pieces[0] - pieces[2], pieces[1] - pieces[3]
    whole, half = even + odd, even - odd
    whole = whole - jnp.sum(whole, axis=0, keepdims=True) * (1.0 / DEPTH)
    c1, s1, c2, s2, c3, s3 = [twist_ref[:, i : i + 1] for i in range(6)]
    inputs = [
        whole,
        a * c1 - b * s1,
        -(a * s1 + b * c1),
        half * c2,
        -(half * s2),
        a * c3 + b * s3,
        b * c3 - a * s3,
    ]
    parts = [split(value) for value in inputs]
    high = jnp.concatenate([p[0] for p in parts], axis=1)
    low = jnp.concatenate([p[1] for p in parts], axis=1)
    out = mm(tab_ref[...], jnp.concatenate([high, low, high], axis=0))
    out = out.reshape(FAR_BINS // GROUP, 2, GROUP, out.shape[1])
    rows = 2 * FAR_BINS
    for r in range(RADIX):
        first = max(2 * r - 1, 0) * LANES
        real_in = out[..., first : first + LANES]
        if r == 0:
            real, imag = real_in[:, 0], -real_in[:, 1]
        else:
            imag_in = out[..., first + LANES : first + 2 * LANES]
            real, imag = real_in[:, 0] + imag_in[:, 1], imag_in[:, 0] - real_in[:, 1]
        both = jnp.stack([real, imag], axis=1).reshape(rows, LANES)
        spec_ref[r * rows : (r + 1) * rows, :] = both


def whiten_kernel(
    spec_ref,
    rim_ref,
    mean_ref,
    head_ref,
    edge_ref,
    band_ref,
    share_ref,
    white_ref,
):
    head_high, head_low = split(head_ref[:, LANES - TAPS :])
    rim_high, rim_low = split(rim_ref[...] - mean_ref[0:1, :])
    history = mm(
        jnp.concatenate([head_high, head_high, head_low], axis=1),
        jnp.concatenate([rim_high, rim_low, rim_high], axis=0),
    )
    high, low = split(history)
    stacked = jnp.concatenate([high, low, high], axis=0)
    spec = spec_ref[...] + mm(edge_ref[:, : 3 * GROUP], stacked)
    parted = spec.reshape(GROUPS, 2, GROUP, LANES)
    real, imag = parted[:, 0], parted[:, 1]
    amplitude = jnp.sqrt(real * real + imag * imag).reshape(BINS, LANES)
    high, low = split(amplitude)
    wide = mm(band_ref[...], jnp.concatenate([high, low], axis=1))
    smoothed = (wide[:, :LANES] + wide[:, LANES:]) * share_ref[...]
    level = jnp.sum(amplitude, axis=0, keepdims=True) * (1.0 / BINS)
    scale = 1.0 / (smoothed + (WATER * level + 1e-06))
    white = parted * scale.reshape(GROUPS, 1, GROUP, LANES)
    white_ref[...] = white.astype(BF16)


def offset_moves(offs_ref):
    row = lax.broadcasted_iota(jnp.int32, (2 * LANES, LANES), 0)
    channel = lax.broadcasted_iota(jnp.int32, (2 * LANES, LANES), 1)
    distance = row - (channel + SPAN)
    offsets = [0] + [offs_ref[o] for o in range(offs_ref.shape[0])]
    hits = [(distance == offset).astype(F32) for offset in offsets]
    return jnp.concatenate(hits, axis=1).astype(BF16)


def pack_matrix(owners):
    share = LANES // owners
    matrix = np.zeros((owners, owners, share, owners, owners, share), np.float32)
    for group in range(owners):
        for owner in range(owners):
            matrix[group, owner, :, owner, group, :] = np.eye(share)
    matrix = matrix.reshape(owners, LANES, owners * LANES)[:, ::-1]
    return matrix.reshape(owners * LANES, owners * LANES).astype(jnp.bfloat16)


def partner_of(place, r, owners):
    return place ^ r if owners & (owners - 1) == 0 else (place + r) % owners


def near_kernel(offs_ref, white_ref, before_ref, inv_ref, *refs):
    out_refs, lags_ref = refs[:-1], refs[-1]
    rows = white_ref.shape[0] * 2 * GROUP
    noff = lags_ref.shape[0]
    blocks = [ref[...].reshape(rows, LANES) for ref in (before_ref, white_ref)]
    far = mm(jnp.concatenate(blocks, axis=1), offset_moves(offs_ref))
    own = far[:, :LANES].reshape(-1, 2, GROUP, LANES)
    columns = []
    for o in range(noff):
        other = far[:, (o + 1) * LANES : (o + 2) * LANES].reshape(own.shape)
        real = own[:, 0] * other[:, 0] + own[:, 1] * other[:, 1]
        imag = own[:, 1] * other[:, 0] - own[:, 0] * other[:, 1]
        columns.append(jnp.stack([real, imag], axis=1).reshape(rows, LANES).astype(BF16))
    both = mm(inv_ref[...], jnp.concatenate(columns, axis=1))
    lags = both[:LAGS] + both[LAGS:]
    for o in range(noff):
        lags_ref[o] = lags[:, o * LANES : (o + 1) * LANES]
    owners = len(out_refs) // 2
    each = noff // owners
    place = lax.axis_index("seg")
    half = LAGS // 2
    lane = lax.broadcasted_iota(jnp.int32, (half, LANES), 1)
    for r in range(owners):
        first = partner_of(place, r, owners) * each
        for t in range(each):
            upper, lower = lags_ref[first + t, :half], lags_ref[first + t, half:]
            mine = jnp.where(lane < SPAN, pltpu.roll(upper, SPAN, 1), lower)
            theirs = jnp.where(lane < SPAN, upper, pltpu.roll(lower, SPAN, 1))
            out_refs[r][t] = mine.astype(BF16)
            out_refs[owners + r][t] = theirs.astype(BF16)


def turn_kernel(*refs):
    near_ref = refs[-1]
    owners = (len(refs) - 1) // 2
    first = sum(ref[...].astype(F32) for ref in refs[:owners])
    second = sum(ref[...].astype(F32) for ref in refs[owners:-1])
    lane = lax.broadcasted_iota(jnp.int32, first.shape[1:], 1)
    for t in range(near_ref.shape[1]):
        upper = jnp.where(lane < SPAN, first[t], pltpu.roll(second[t], SPAN, 1))
        lower = jnp.where(lane < SPAN, pltpu.roll(first[t], SPAN, 1), second[t])
        near_ref[:, t, :] = jnp.concatenate([upper, lower], axis=0).T


def loop_kernel(partner_ref, count_ref, flip_ref, pack_ref, white_ref, out_ref):
    segs, blocks, _, bins, _ = white_ref.shape
    owners = out_ref.shape[0]
    slots = partner_ref.shape[0]
    rows = segs * 2 * bins
    packed_rows = 2 * bins // owners
    turned = mm(white_ref[...].reshape(blocks * rows, LANES), flip_ref[...])
    turned = turned.reshape(white_ref.shape)
    loops = []
    for b in range(blocks):
        own = turned[:, b]
        for k in range(slots):
            partner = jnp.clip(partner_ref[k, b], 0, blocks - 1)
            live = (k < count_ref[b]).astype(F32)
            far = white_ref[:, partner].astype(F32)
            real = jnp.sum(own[:, 0] * far[:, 0] + own[:, 1] * far[:, 1], axis=0)
            imag = jnp.sum(own[:, 1] * far[:, 0] - own[:, 0] * far[:, 1], axis=0)
            pair = jnp.concatenate([real, imag], axis=0) * live
            groups = [pair[g * packed_rows : (g + 1) * packed_rows] for g in range(owners)]
            loops.append(jnp.concatenate(groups, axis=1))
    packed = mm(jnp.concatenate(loops, axis=0).astype(BF16), pack_ref[...])
    depth = slots * packed_rows
    for b in range(blocks):
        for q in range(owners):
            tile = packed[b * depth : (b + 1) * depth, q * LANES : (q + 1) * LANES]
            out_ref[q, b] = tile.astype(BF16)


def loop_lag_kernel(slots, spec_ref, inv_ref, loop_ref):
    sources = spec_ref.shape[0]
    step = spec_ref.shape[1] // slots
    share = loop_ref.shape[0] // slots
    loop = spec_ref[...].astype(F32)
    rows = []
    for k in range(slots):
        turned = loop[:, k * step : (k + 1) * step].reshape(sources * step, LANES).T
        groups = [turned[g * share : (g + 1) * share] for g in range(LANES // share)]
        rows.append(jnp.concatenate(groups, axis=1))
    both = mm(jnp.concatenate(rows, axis=0).astype(BF16), inv_ref[...])
    loop_ref[...] = both[:, :LAGS] + both[:, LAGS:]


def last_kernel(slots, spec_ref, inv_ref, *refs):
    turn_kernel(*refs[:-1])
    loop_lag_kernel(slots, spec_ref, inv_ref, refs[-1])


def vmem(count):
    return [pl.BlockSpec(memory_space=pltpu.VMEM)] * count


def smem(count):
    return [pl.BlockSpec(memory_space=pltpu.SMEM)] * count


def hbm(count):
    return [pl.BlockSpec(memory_space=pltpu.HBM)] * count


def in_hbm(array):
    return pltpu.with_memory_space_constraint(jnp.asarray(array), pltpu.HBM)


def loops_plain(white, loop_partner, loop_count, owners, inverse):
    _, blocks, _, bins, chans = white.shape
    devices = blocks * owners
    slots = loop_partner.shape[1]
    share = chans // owners
    wide = white.astype(F32).swapaxes(0, 1)
    loops = []
    for k in range(slots):
        far = jnp.flip(wide[loop_partner[:, k]], axis=4)
        live = (k < loop_count).astype(F32)[:, None, None]
        real = jnp.sum(wide[:, :, 0] * far[:, :, 0] + wide[:, :, 1] * far[:, :, 1], axis=1)
        imag = jnp.sum(wide[:, :, 1] * far[:, :, 0] - wide[:, :, 0] * far[:, :, 1], axis=1)
        pair = (jnp.stack([real, imag]) * live[None]).astype(BF16)
        loops.append(pair.reshape(2, blocks, bins, owners, share))
    loop = jnp.transpose(jnp.stack(loops), (4, 2, 0, 1, 3, 5))
    loop = loop.reshape(devices, slots, 2 * bins, share)
    summed = lax.all_to_all(loop, ("seg", "chan"), 0, 0, tiled=True).astype(F32)
    table = inverse.astype(np.float32).reshape(LAGS, devices, 2 * bins)
    lags = jnp.einsum("dtvc,ldv->tcl", summed, table, precision=lax.Precision.HIGHEST)
    return lags[None]


def body(recording, filter_taps, offsets, loop_partner, loop_count):
    chan_count = lax.axis_size("chan")
    seg_count = lax.axis_size("seg")
    devices = chan_count * seg_count
    bins = BINS // devices
    chans, length = recording.shape
    noff, slots = offsets.shape[0], loop_partner.shape[1]
    share = chans // seg_count
    near_each = noff // seg_count
    assert length == NFFT * DECIM and chans == LANES and noff % seg_count == 0

    route = [(i, i + 1) for i in range(seg_count - 1)]
    rim = pl.pallas_call(
        rim_kernel,
        out_shape=jax.ShapeDtypeStruct((TAPS, chans), F32),
        in_specs=hbm(1),
        out_specs=pl.BlockSpec(memory_space=pltpu.VMEM),
        scratch_shapes=[pltpu.VMEM((chans, LANES), F32), pltpu.SemaphoreType.DMA],
        compiler_params=PARAMS,
        cost_estimate=pl.CostEstimate(
            flops=10_000_000_000, bytes_accessed=20_000_000, transcendentals=0
        ),
        name="history",
    )(in_hbm(recording))
    rim = lax.ppermute(rim, "seg", route)
    taps = filter_taps.reshape(1, TAPS)
    spec, mean, head = pl.pallas_call(
        spectrum_kernel,
        out_shape=[
            jax.ShapeDtypeStruct((2 * BINS, LANES), F32),
            jax.ShapeDtypeStruct((8, LANES), F32),
            jax.ShapeDtypeStruct((GROUP, LANES), F32),
        ],
        in_specs=vmem(4),
        out_specs=vmem(3),
        compiler_params=PARAMS,
        cost_estimate=pl.CostEstimate(
            flops=1_000_000_000, bytes_accessed=5_000_000, transcendentals=0
        ),
        name="filter_and_transform",
    )(taps, recording, short_table(), twiddle_table())

    band, band_share = band_tables()
    white = pl.pallas_call(
        whiten_kernel,
        out_shape=jax.ShapeDtypeStruct((GROUPS, 2, GROUP, LANES), BF16),
        in_specs=vmem(7),
        out_specs=pl.BlockSpec(memory_space=pltpu.VMEM),
        compiler_params=PARAMS,
        name="whiten",
    )(spec, rim, mean, head, edge_table(), band, band_share)

    spread = white
    if bins != GROUP:
        spread = jnp.moveaxis(white, 1, 0).reshape(2, devices, bins, LANES)
        spread = jnp.moveaxis(spread, 0, 1)
    moved = lax.all_to_all(spread, ("seg", "chan"), 0, 0, tiled=True)
    moved = moved.reshape(seg_count, chan_count, 2, bins, LANES)

    ring = [(i, (i + 1) % chan_count) for i in range(chan_count)]
    before = lax.ppermute(white, "chan", ring)
    order = np.repeat(bin_order().reshape(GROUPS, 1, GROUP), 2, axis=1).reshape(-1)
    part = np.broadcast_to(np.arange(2).reshape(1, 2, 1), (GROUPS, 2, GROUP)).reshape(-1)
    inverse = np.concatenate(split_np(inverse_table(seg_count, order, part)), axis=0)
    lags = pl.pallas_call(
        near_kernel,
        out_shape=[jax.ShapeDtypeStruct((near_each, LAGS // 2, LANES), BF16)] * (2 * seg_count),
        in_specs=smem(1) + vmem(3),
        out_specs=vmem(2 * seg_count),
        scratch_shapes=[pltpu.VMEM((noff, LAGS, LANES), F32)],
        compiler_params=PARAMS,
        cost_estimate=pl.CostEstimate(
            flops=20_000_000_000, bytes_accessed=20_000_000, transcendentals=0
        ),
        name="near_lags",
    )(offsets, white, before, inverse)
    lags = list(lags)
    for r in range(seg_count - 1, 0, -1):
        route = [(i, partner_of(i, r, seg_count)) for i in range(seg_count)]
        lags[r] = lax.ppermute(lags[r], "seg", route)
    for r in range(seg_count - 1, -1, -1):
        route = [
            (c * seg_count + i, (c - 1) % chan_count * seg_count + partner_of(i, r, seg_count))
            for c in range(chan_count)
            for i in range(seg_count)
        ]
        lags[seg_count + r] = lax.ppermute(lags[seg_count + r], ("chan", "seg"), route)
    moved, lags[0] = lax.optimization_barrier((moved, lags[0]))

    near_shape = jax.ShapeDtypeStruct((chans, near_each, LAGS), F32)
    if bins % GROUP or 2 * bins % (8 * seg_count):
        order = np.repeat(bin_order().reshape(devices, 1, bins), 2, axis=1).reshape(-1)
        part = np.broadcast_to(np.arange(2).reshape(1, 2, 1), (devices, 2, bins)).reshape(-1)
        loop_inverse = inverse_table(seg_count, order, part)
        loop = loops_plain(moved, loop_partner, loop_count, seg_count, loop_inverse)
        near = pl.pallas_call(
            turn_kernel,
            out_shape=near_shape,
            in_specs=vmem(2 * seg_count),
            out_specs=pl.BlockSpec(memory_space=pltpu.VMEM),
            compiler_params=PARAMS,
            name="near_turn",
        )(*lags)
        return near, loop

    flip = np.eye(LANES, dtype=np.float32)[::-1].astype(jnp.bfloat16)
    out_rows = slots * (2 * bins // seg_count)
    crossed = pl.pallas_call(
        loop_kernel,
        out_shape=jax.ShapeDtypeStruct((seg_count, chan_count, out_rows, LANES), BF16),
        in_specs=smem(2) + vmem(3),
        out_specs=pl.BlockSpec(memory_space=pltpu.VMEM),
        compiler_params=PARAMS,
        name="loop_spectra",
    )(loop_partner.T, loop_count, flip, pack_matrix(seg_count), moved)
    crossed, *lags[1:] = lax.optimization_barrier((crossed, *lags[1:]))
    crossed = crossed.reshape(devices, out_rows, LANES)
    summed = lax.all_to_all(crossed, ("seg", "chan"), 0, 0, tiled=True)
    columns = np.arange(2 * BINS).reshape(devices, seg_count, -1).swapaxes(0, 1).reshape(-1)
    loop_inverse = inverse_table(seg_count, order[columns], part[columns]).T
    loop_inverse = np.concatenate(split_np(loop_inverse), axis=1)
    near, loop = pl.pallas_call(
        functools.partial(last_kernel, slots),
        out_shape=[near_shape, jax.ShapeDtypeStruct((slots * share, LAGS), F32)],
        in_specs=vmem(2 + 2 * seg_count),
        out_specs=vmem(2),
        compiler_params=PARAMS,
        name="lags",
    )(summed, loop_inverse, *lags)
    return near, loop.reshape(1, slots, share, LAGS)


def solution(mesh):
    in_specs = (P("chan", "seg"), P(), P(), P(), P())
    out_specs = (P("chan", "seg", None), P("chan", None, "seg", None))
    return jax.shard_map(body, mesh=mesh, in_specs=in_specs, out_specs=out_specs, check_vma=False)
```

```python
import functools
import math

import jax
import jax.numpy as jnp
import numpy as np
from jax import lax
from jax.experimental import pallas as pl
from jax.experimental.pallas import tpu as pltpu
from jax.sharding import PartitionSpec as P

NFFT = 1024
LAGS = 256
TAPS = 64
DECIM = 4
HALFBAND = 10
SPAN = 64
BINS = 512
WATER = 0.2

LANES = 128
GROUP = 16
GROUPS = BINS // GROUP
OUT_BLOCK = 128
STEP = OUT_BLOCK * DECIM
RADIX = 4
DEPTH = NFFT // RADIX
FAR_BINS = BINS // RADIX

F32 = jnp.float32
BF16 = jnp.bfloat16
MIB = 1024 * 1024
PARAMS = pltpu.CompilerParams(vmem_limit_bytes=32 * MIB)


def bin_order():
    return np.concatenate([np.arange(r, BINS, RADIX) for r in range(RADIX)])


def split_np(table):
    high = table.astype(jnp.bfloat16)
    low = (table - high.astype(np.float64)).astype(jnp.bfloat16)
    return high, low


def short_table():
    bins = np.arange(FAR_BINS).reshape(-1, 1, GROUP, 1)
    angles = (bins * np.arange(DEPTH) % DEPTH) * (2.0 * np.pi / DEPTH)
    rows = np.concatenate([np.cos(angles), np.sin(angles)], axis=1).reshape(-1, DEPTH)
    high, low = split_np(rows)
    return np.concatenate([high, high, low], axis=1)


def twiddle_table():
    angles = np.arange(DEPTH)[:, None] * np.arange(1, RADIX) * (2.0 * np.pi / NFFT)
    columns = np.stack([np.cos(angles), np.sin(angles)], axis=2).reshape(DEPTH, -1)
    return np.pad(columns, ((0, 0), (0, LANES - columns.shape[1]))).astype(np.float32)


def edge_table():
    bins = bin_order().reshape(GROUPS, 1, GROUP, 1)
    angles = (bins * np.arange(GROUP) % NFFT) * (2.0 * np.pi / NFFT)
    rows = np.concatenate([np.cos(angles), -np.sin(angles)], axis=1) * (bins != 0)
    high, low = split_np(rows.reshape(2 * BINS, GROUP))
    table = np.concatenate([high, high, low], axis=1)
    return np.pad(table.astype(np.float32), ((0, 0), (0, LANES - 3 * GROUP))).astype(jnp.bfloat16)


def inverse_table(total_segs, bins, part):
    lag = np.arange(LAGS) - LAGS // 2
    angles = (bins[None, :] * lag[:, None] % NFFT) * (2.0 * np.pi / NFFT)
    weights = np.where(bins == 0, 1.0, 2.0) / math.sqrt(2.0 * BINS * total_segs)
    return np.where(part[None, :] == 1, -np.sin(angles), np.cos(angles)) * weights[None, :]


def band_tables():
    bins = bin_order()
    inside = np.abs(bins[:, None] - bins[None, :]) <= HALFBAND
    share = np.broadcast_to(1.0 / inside.sum(axis=1, keepdims=True), (BINS, LANES))
    return inside.astype(jnp.bfloat16), share.astype(np.float32)


def split(value):
    high = value.astype(BF16)
    return high, (value - high.astype(F32)).astype(BF16)


def mm(a, b):
    return jnp.dot(a, b, preferred_element_type=F32)


def mm_nt(a, b):
    return lax.dot_general(a, b, (((1,), (1,)), ((), ())), preferred_element_type=F32)


def tap_rows(taps):
    width, period = 2 * LANES, LANES // DECIM
    square = (TAPS, TAPS)
    diagonal = lax.broadcasted_iota(jnp.int32, square, 0) == lax.broadcasted_iota(jnp.int32, square, 1)
    column_taps = jnp.sum(jnp.where(diagonal, taps, 0.0), axis=1, keepdims=True)
    tap = lax.broadcasted_iota(jnp.int32, (TAPS, width), 0)
    column = lax.broadcasted_iota(jnp.int32, (TAPS, width), 1)
    placed = jnp.where(column == LANES + DECIM - 1 - tap, column_taps, 0.0)
    spread = jnp.broadcast_to(jnp.sum(placed, axis=0, keepdims=True), (period, width))
    piece = pltpu.roll(spread, 0, 1, stride=DECIM, stride_axis=0)
    rows = []
    for t in range(OUT_BLOCK // period):
        left = jnp.zeros((period, t * LANES), F32)
        right = jnp.zeros((period, STEP - LANES - t * LANES), F32)
        rows.append(jnp.concatenate([p for p in (left, piece, right) if p.shape[1]], axis=1))
    return jnp.concatenate(rows, axis=0)


def rim_kernel(rec_hbm, rim_ref, tail_ref, sem):
    length = rec_hbm.shape[1]
    copy = pltpu.make_async_copy(rec_hbm.at[:, pl.ds(length - LANES, LANES)], tail_ref, sem)
    copy.start()
    copy.wait()
    rim_ref[...] = tail_ref[...].T[LANES - TAPS :]


def spectrum_kernel(taps_ref, rec_ref, tab_ref, twist_ref, spec_ref, mean_ref, head_ref):
    blocks = rec_ref.shape[1] // STEP
    table = tap_rows(taps_ref[...])
    head_ref[...] = table[:GROUP, :LANES]
    taps_high, taps_low = split(table.T)
    taps_both = jnp.concatenate([taps_high, taps_low], axis=1)
    before = [jnp.zeros((LANES, LANES), BF16)] * 2
    outputs = []
    for first in range(0, blocks, blocks // 2):
        windows = ([], [])
        for j in range(first, first + blocks // 2):
            chunk = rec_ref[:, j * STEP : (j + 1) * STEP]
            if j == 0:
                mean = jnp.sum(chunk, axis=1, keepdims=True) * (1.0 / STEP)
            for i, value in enumerate(split(chunk - mean)):
                windows[i].append(jnp.concatenate([before[i], value], axis=1))
                before[i] = value[:, STEP - LANES :]
        wide = mm(jnp.concatenate(windows[0], axis=0), taps_both)
        rest = mm(jnp.concatenate(windows[1], axis=0), taps_high)
        total = wide[:, :LANES] + wide[:, LANES:] + rest
        outputs += [total[t * LANES : (t + 1) * LANES].T for t in range(blocks // 2)]
    pieces = [jnp.concatenate(outputs[j : j + 2], axis=0) for j in range(0, blocks, 2)]
    mean_ref[...] = jnp.broadcast_to(mean, (LANES, LANES)).T[: mean_ref.shape[0]]
    even, odd = pieces[0] + pieces[2], pieces[1] + pieces[3]
    a, b = pieces[0] - pieces[2], pieces[1] - pieces[3]
    whole, half = even + odd, even - odd
    whole = whole - jnp.sum(whole, axis=0, keepdims=True) * (1.0 / DEPTH)
    c1, s1, c2, s2, c3, s3 = [twist_ref[:, i : i + 1] for i in range(6)]
    inputs = [
        whole,
        a * c1 - b * s1,
        -(a * s1 + b * c1),
        half * c2,
        -(half * s2),
        a * c3 + b * s3,
        b * c3 - a * s3,
    ]
    parts = [split(value) for value in inputs]
    high = jnp.concatenate([p[0] for p in parts], axis=1)
    low = jnp.concatenate([p[1] for p in parts], axis=1)
    out = mm(tab_ref[...], jnp.concatenate([high, low, high], axis=0))
    out = out.reshape(FAR_BINS // GROUP, 2, GROUP, out.shape[1])
    rows = 2 * FAR_BINS
    for r in range(RADIX):
        first = max(2 * r - 1, 0) * LANES
        real_in = out[..., first : first + LANES]
        if r == 0:
            real, imag = real_in[:, 0], -real_in[:, 1]
        else:
            imag_in = out[..., first + LANES : first + 2 * LANES]
            real, imag = real_in[:, 0] + imag_in[:, 1], imag_in[:, 0] - real_in[:, 1]
        both = jnp.stack([real, imag], axis=1).reshape(rows, LANES)
        spec_ref[r * rows : (r + 1) * rows, :] = both


def whiten_kernel(
    spec_ref,
    rim_ref,
    mean_ref,
    head_ref,
    edge_ref,
    band_ref,
    share_ref,
    white_ref,
    first_ref,
    second_ref,
):
    head_high, head_low = split(head_ref[:, LANES - TAPS :])
    rim_high, rim_low = split(rim_ref[...] - mean_ref[0:1, :])
    history = mm(
        jnp.concatenate([head_high, head_high, head_low], axis=1),
        jnp.concatenate([rim_high, rim_low, rim_high], axis=0),
    )
    high, low = split(history)
    stacked = jnp.concatenate([high, low, high], axis=0)
    spec = spec_ref[...] + mm(edge_ref[:, : 3 * GROUP], stacked)
    parted = spec.reshape(GROUPS, 2, GROUP, LANES)
    real, imag = parted[:, 0], parted[:, 1]
    amplitude = jnp.sqrt(real * real + imag * imag).reshape(BINS, LANES)
    high, low = split(amplitude)
    wide = mm(band_ref[...], jnp.concatenate([high, low], axis=1))
    smoothed = (wide[:, :LANES] + wide[:, LANES:]) * share_ref[...]
    level = jnp.sum(amplitude, axis=0, keepdims=True) * (1.0 / BINS)
    scale = 1.0 / (smoothed + (WATER * level + 1e-06))
    white = parted * scale.reshape(GROUPS, 1, GROUP, LANES)
    white_ref[...] = white.astype(BF16)
    flat = white.reshape(2 * BINS, LANES)
    turned = pltpu.roll(flat, SPAN, 1)
    lane = lax.broadcasted_iota(jnp.int32, (BINS, LANES), 1)
    up = jnp.where(lane < SPAN, turned[:BINS], flat[BINS:])
    down = jnp.where(lane < SPAN, flat[:BINS], turned[BINS:])
    place = lax.axis_index("chan")
    up_first = halo_order(place, lax.axis_size("chan"))[0]
    first_ref[...] = jnp.where(up_first, up, down).astype(BF16)
    second_ref[...] = jnp.where(up_first, down, up).astype(BF16)


def halo_order(place, count):
    if count % 2:
        return place >= 0, place >= 0
    return place % 2 == 0, place % 2 == 1


def halo_routes(count):
    if count % 2:
        ring = [(i, (i + 1) % count) for i in range(count)]
        return ring, [(j, i) for i, j in ring]
    first = [(i, i + 1 - 2 * (i % 2)) for i in range(count)]
    second = [(i, (i - 1 + 2 * (i % 2)) % count) for i in range(count)]
    return first, second


def offset_moves(offs_ref):
    row = lax.broadcasted_iota(jnp.int32, (2 * LANES, LANES), 0)
    channel = lax.broadcasted_iota(jnp.int32, (2 * LANES, LANES), 1)
    distance = jnp.where(row < LANES + SPAN, row, row - 2 * LANES) - channel
    hits = [(distance == offs_ref[o]).astype(F32) for o in range(offs_ref.shape[0])]
    return jnp.concatenate(hits, axis=1).astype(BF16)


def pack_matrix(owners):
    share = LANES // owners
    matrix = np.zeros((owners, owners, share, owners, owners, share), np.float32)
    for group in range(owners):
        for owner in range(owners):
            matrix[group, owner, :, owner, group, :] = np.eye(share)
    matrix = matrix.reshape(owners, LANES, owners * LANES)[:, ::-1]
    return matrix.reshape(owners * LANES, owners * LANES).astype(jnp.bfloat16)


def partner_of(place, r, owners):
    return place ^ r if owners & (owners - 1) == 0 else (place + r) % owners


def near_kernel(offs_ref, white_ref, first_ref, second_ref, inv_ref, *refs):
    out_refs, lags_ref = refs[:-1], refs[-1]
    rows = white_ref.shape[0] * 2 * GROUP
    half = rows // 2
    noff = lags_ref.shape[0]
    before_first = halo_order(lax.axis_index("chan"), lax.axis_size("chan"))[1]
    first, second = first_ref[...].astype(F32), second_ref[...].astype(F32)
    before = jnp.where(before_first, first, second)
    after = jnp.where(before_first, second, first)
    lane = lax.broadcasted_iota(jnp.int32, (half, LANES), 1)
    upper = jnp.where(lane < SPAN, after, pltpu.roll(before, SPAN, 1))
    lower = jnp.where(lane < SPAN, pltpu.roll(after, SPAN, 1), before)
    edge = jnp.concatenate([upper, lower], axis=0).astype(BF16)
    own = white_ref[...].reshape(rows, LANES)
    far = mm(jnp.concatenate([own, edge], axis=1), offset_moves(offs_ref))
    own = own.astype(F32).reshape(-1, 2, GROUP, LANES)
    columns = []
    for o in range(noff):
        other = far[:, o * LANES : (o + 1) * LANES].reshape(own.shape)
        real = own[:, 0] * other[:, 0] + own[:, 1] * other[:, 1]
        imag = own[:, 1] * other[:, 0] - own[:, 0] * other[:, 1]
        columns.append(jnp.stack([real, imag], axis=1).reshape(rows, LANES).astype(BF16))
    both = mm(inv_ref[...], jnp.concatenate(columns, axis=1))
    lags = both[:LAGS] + both[LAGS:]
    for o in range(noff):
        lags_ref[o] = lags[:, o * LANES : (o + 1) * LANES]
    owners = len(out_refs)
    each = noff // owners
    place = lax.axis_index("seg")
    for r in range(owners):
        first = partner_of(place, r, owners) * each
        out_refs[r][...] = lags_ref[pl.ds(first, each)].astype(BF16)


def turn_kernel(*refs):
    near_ref = refs[-1]
    total = sum(ref[...].astype(F32) for ref in refs[:-1])
    for t in range(near_ref.shape[1]):
        near_ref[:, t, :] = total[t].T


def loop_kernel(partner_ref, count_ref, flip_ref, pack_ref, white_ref, out_ref):
    segs, blocks, _, bins, _ = white_ref.shape
    owners = out_ref.shape[0]
    slots = partner_ref.shape[0]
    rows = segs * 2 * bins
    packed_rows = 2 * bins // owners
    turned = mm(white_ref[...].reshape(blocks * rows, LANES), flip_ref[...])
    turned = turned.reshape(white_ref.shape)
    loops = []
    for b in range(blocks):
        own = turned[:, b]
        for k in range(slots):
            partner = jnp.clip(partner_ref[k, b], 0, blocks - 1)
            live = (k < count_ref[b]).astype(F32)
            far = white_ref[:, partner].astype(F32)
            real = jnp.sum(own[:, 0] * far[:, 0] + own[:, 1] * far[:, 1], axis=0)
            imag = jnp.sum(own[:, 1] * far[:, 0] - own[:, 0] * far[:, 1], axis=0)
            pair = jnp.concatenate([real, imag], axis=0) * live
            groups = [pair[g * packed_rows : (g + 1) * packed_rows] for g in range(owners)]
            loops.append(jnp.concatenate(groups, axis=1))
    packed = mm(jnp.concatenate(loops, axis=0).astype(BF16), pack_ref[...])
    depth = slots * packed_rows
    for b in range(blocks):
        for q in range(owners):
            tile = packed[b * depth : (b + 1) * depth, q * LANES : (q + 1) * LANES]
            out_ref[q, b] = tile.astype(BF16)


def loop_lag_kernel(slots, spec_ref, inv_ref, loop_ref):
    sources = spec_ref.shape[0]
    step = spec_ref.shape[1] // slots
    share = loop_ref.shape[0] // slots
    loop = spec_ref[...].astype(F32)
    rows = []
    for k in range(slots):
        turned = loop[:, k * step : (k + 1) * step].reshape(sources * step, LANES).T
        groups = [turned[g * share : (g + 1) * share] for g in range(LANES // share)]
        rows.append(jnp.concatenate(groups, axis=1))
    both = mm(jnp.concatenate(rows, axis=0).astype(BF16), inv_ref[...])
    loop_ref[...] = both[:, :LAGS] + both[:, LAGS:]


def last_kernel(slots, spec_ref, inv_ref, *refs):
    turn_kernel(*refs[:-1])
    loop_lag_kernel(slots, spec_ref, inv_ref, refs[-1])


def vmem(count):
    return [pl.BlockSpec(memory_space=pltpu.VMEM)] * count


def smem(count):
    return [pl.BlockSpec(memory_space=pltpu.SMEM)] * count


def hbm(count):
    return [pl.BlockSpec(memory_space=pltpu.HBM)] * count


def in_hbm(array):
    return pltpu.with_memory_space_constraint(jnp.asarray(array), pltpu.HBM)


def loops_plain(white, loop_partner, loop_count, owners, inverse):
    _, blocks, _, bins, chans = white.shape
    devices = blocks * owners
    slots = loop_partner.shape[1]
    share = chans // owners
    wide = white.astype(F32).swapaxes(0, 1)
    loops = []
    for k in range(slots):
        far = jnp.flip(wide[loop_partner[:, k]], axis=4)
        live = (k < loop_count).astype(F32)[:, None, None]
        real = jnp.sum(wide[:, :, 0] * far[:, :, 0] + wide[:, :, 1] * far[:, :, 1], axis=1)
        imag = jnp.sum(wide[:, :, 1] * far[:, :, 0] - wide[:, :, 0] * far[:, :, 1], axis=1)
        pair = (jnp.stack([real, imag]) * live[None]).astype(BF16)
        loops.append(pair.reshape(2, blocks, bins, owners, share))
    loop = jnp.transpose(jnp.stack(loops), (4, 2, 0, 1, 3, 5))
    loop = loop.reshape(devices, slots, 2 * bins, share)
    summed = lax.all_to_all(loop, ("seg", "chan"), 0, 0, tiled=True).astype(F32)
    table = inverse.astype(np.float32).reshape(LAGS, devices, 2 * bins)
    lags = jnp.einsum("dtvc,ldv->tcl", summed, table, precision=lax.Precision.HIGHEST)
    return lags[None]


def body(recording, filter_taps, offsets, loop_partner, loop_count):
    chan_count = lax.axis_size("chan")
    seg_count = lax.axis_size("seg")
    devices = chan_count * seg_count
    bins = BINS // devices
    chans, length = recording.shape
    noff, slots = offsets.shape[0], loop_partner.shape[1]
    share = chans // seg_count
    near_each = noff // seg_count
    assert length == NFFT * DECIM and chans == LANES and noff % seg_count == 0

    route = [(i, i + 1) for i in range(seg_count - 1)]
    rim = pl.pallas_call(
        rim_kernel,
        out_shape=jax.ShapeDtypeStruct((TAPS, chans), F32),
        in_specs=hbm(1),
        out_specs=pl.BlockSpec(memory_space=pltpu.VMEM),
        scratch_shapes=[pltpu.VMEM((chans, LANES), F32), pltpu.SemaphoreType.DMA],
        compiler_params=PARAMS,
        cost_estimate=pl.CostEstimate(
            flops=10_000_000_000, bytes_accessed=20_000_000, transcendentals=0
        ),
        name="history",
    )(in_hbm(recording))
    rim = lax.ppermute(rim, "seg", route)
    taps = filter_taps.reshape(1, TAPS)
    spec, mean, head = pl.pallas_call(
        spectrum_kernel,
        out_shape=[
            jax.ShapeDtypeStruct((2 * BINS, LANES), F32),
            jax.ShapeDtypeStruct((8, LANES), F32),
            jax.ShapeDtypeStruct((GROUP, LANES), F32),
        ],
        in_specs=vmem(4),
        out_specs=vmem(3),
        compiler_params=PARAMS,
        cost_estimate=pl.CostEstimate(
            flops=1_000_000_000, bytes_accessed=5_000_000, transcendentals=0
        ),
        name="filter_and_transform",
    )(taps, recording, short_table(), twiddle_table())

    band, band_share = band_tables()
    half = jax.ShapeDtypeStruct((BINS, LANES), BF16)
    white, first, second = pl.pallas_call(
        whiten_kernel,
        out_shape=[jax.ShapeDtypeStruct((GROUPS, 2, GROUP, LANES), BF16), half, half],
        in_specs=vmem(7),
        out_specs=vmem(3),
        compiler_params=PARAMS,
        name="whiten",
    )(spec, rim, mean, head, edge_table(), band, band_share)

    spread = white
    if bins != GROUP:
        spread = jnp.moveaxis(white, 1, 0).reshape(2, devices, bins, LANES)
        spread = jnp.moveaxis(spread, 0, 1)
    moved = lax.all_to_all(spread, ("seg", "chan"), 0, 0, tiled=True)
    moved = moved.reshape(seg_count, chan_count, 2, bins, LANES)

    routes = halo_routes(chan_count)
    first = lax.ppermute(first, "chan", routes[0])
    second = lax.ppermute(second, "chan", routes[1])
    order = np.repeat(bin_order().reshape(GROUPS, 1, GROUP), 2, axis=1).reshape(-1)
    part = np.broadcast_to(np.arange(2).reshape(1, 2, 1), (GROUPS, 2, GROUP)).reshape(-1)
    inverse = np.concatenate(split_np(inverse_table(seg_count, order, part)), axis=0)
    lags = pl.pallas_call(
        near_kernel,
        out_shape=[jax.ShapeDtypeStruct((near_each, LAGS, LANES), BF16)] * seg_count,
        in_specs=smem(1) + vmem(4),
        out_specs=vmem(seg_count),
        scratch_shapes=[pltpu.VMEM((noff, LAGS, LANES), F32)],
        compiler_params=PARAMS,
        cost_estimate=pl.CostEstimate(
            flops=20_000_000_000, bytes_accessed=20_000_000, transcendentals=0
        ),
        name="near_lags",
    )(offsets, white, first, second, inverse)
    lags = list(lags)
    for r in range(seg_count - 1, 0, -1):
        route = [(i, partner_of(i, r, seg_count)) for i in range(seg_count)]
        lags[r] = lax.ppermute(lags[r], "seg", route)
    moved, lags[0] = lax.optimization_barrier((moved, lags[0]))

    near_shape = jax.ShapeDtypeStruct((chans, near_each, LAGS), F32)
    if bins % GROUP or 2 * bins % (8 * seg_count):
        order = np.repeat(bin_order().reshape(devices, 1, bins), 2, axis=1).reshape(-1)
        part = np.broadcast_to(np.arange(2).reshape(1, 2, 1), (devices, 2, bins)).reshape(-1)
        loop_inverse = inverse_table(seg_count, order, part)
        loop = loops_plain(moved, loop_partner, loop_count, seg_count, loop_inverse)
        near = pl.pallas_call(
            turn_kernel,
            out_shape=near_shape,
            in_specs=vmem(seg_count),
            out_specs=pl.BlockSpec(memory_space=pltpu.VMEM),
            compiler_params=PARAMS,
            name="near_turn",
        )(*lags)
        return near, loop

    flip = np.eye(LANES, dtype=np.float32)[::-1].astype(jnp.bfloat16)
    out_rows = slots * (2 * bins // seg_count)
    crossed = pl.pallas_call(
        loop_kernel,
        out_shape=jax.ShapeDtypeStruct((seg_count, chan_count, out_rows, LANES), BF16),
        in_specs=smem(2) + vmem(3),
        out_specs=pl.BlockSpec(memory_space=pltpu.VMEM),
        compiler_params=PARAMS,
        name="loop_spectra",
    )(loop_partner.T, loop_count, flip, pack_matrix(seg_count), moved)
    crossed, *lags[1:] = lax.optimization_barrier((crossed, *lags[1:]))
    crossed = crossed.reshape(devices, out_rows, LANES)
    summed = lax.all_to_all(crossed, ("seg", "chan"), 0, 0, tiled=True)
    columns = np.arange(2 * BINS).reshape(devices, seg_count, -1).swapaxes(0, 1).reshape(-1)
    loop_inverse = inverse_table(seg_count, order[columns], part[columns]).T
    loop_inverse = np.concatenate(split_np(loop_inverse), axis=1)
    near, loop = pl.pallas_call(
        functools.partial(last_kernel, slots),
        out_shape=[near_shape, jax.ShapeDtypeStruct((slots * share, LAGS), F32)],
        in_specs=vmem(2 + seg_count),
        out_specs=vmem(2),
        compiler_params=PARAMS,
        name="lags",
    )(summed, loop_inverse, *lags)
    return near, loop.reshape(1, slots, share, LAGS)


def solution(mesh):
    in_specs = (P("chan", "seg"), P(), P(), P(), P())
    out_specs = (P("chan", "seg", None), P("chan", None, "seg", None))
    return jax.shard_map(body, mesh=mesh, in_specs=in_specs, out_specs=out_specs, check_vma=False)
```

```python
import functools
import math

import jax
import jax.numpy as jnp
import numpy as np
from jax import lax
from jax.experimental import pallas as pl
from jax.experimental.pallas import tpu as pltpu
from jax.sharding import PartitionSpec as P

NFFT = 1024
LAGS = 256
TAPS = 64
DECIM = 4
HALFBAND = 10
SPAN = 64
BINS = 512
WATER = 0.2

LANES = 128
GROUP = 16
GROUPS = BINS // GROUP
OUT_BLOCK = 128
STEP = OUT_BLOCK * DECIM
RADIX = 4
DEPTH = NFFT // RADIX
FAR_BINS = BINS // RADIX

F32 = jnp.float32
BF16 = jnp.bfloat16
MIB = 1024 * 1024
PARAMS = pltpu.CompilerParams(vmem_limit_bytes=32 * MIB)


def bin_order():
    return np.concatenate([np.arange(r, BINS, RADIX) for r in range(RADIX)])


def split_np(table):
    high = table.astype(jnp.bfloat16)
    low = (table - high.astype(np.float64)).astype(jnp.bfloat16)
    return high, low


def short_table():
    bins = np.arange(FAR_BINS).reshape(-1, 1, GROUP, 1)
    angles = (bins * np.arange(DEPTH) % DEPTH) * (2.0 * np.pi / DEPTH)
    rows = np.concatenate([np.cos(angles), np.sin(angles)], axis=1).reshape(-1, DEPTH)
    high, low = split_np(rows)
    return np.concatenate([high, high, low], axis=1)


def twiddle_table():
    angles = np.arange(DEPTH)[:, None] * np.arange(1, RADIX) * (2.0 * np.pi / NFFT)
    columns = np.stack([np.cos(angles), np.sin(angles)], axis=2).reshape(DEPTH, -1)
    return np.pad(columns, ((0, 0), (0, LANES - columns.shape[1]))).astype(np.float32)


def edge_table():
    bins = bin_order().reshape(GROUPS, 1, GROUP, 1)
    angles = (bins * np.arange(GROUP) % NFFT) * (2.0 * np.pi / NFFT)
    rows = np.concatenate([np.cos(angles), -np.sin(angles)], axis=1) * (bins != 0)
    high, low = split_np(rows.reshape(2 * BINS, GROUP))
    table = np.concatenate([high, high, low], axis=1)
    return np.pad(table.astype(np.float32), ((0, 0), (0, LANES - 3 * GROUP))).astype(jnp.bfloat16)


def inverse_table(total_segs, bins, part):
    lag = np.arange(LAGS) - LAGS // 2
    angles = (bins[None, :] * lag[:, None] % NFFT) * (2.0 * np.pi / NFFT)
    weights = np.where(bins == 0, 1.0, 2.0) / math.sqrt(2.0 * BINS * total_segs)
    return np.where(part[None, :] == 1, -np.sin(angles), np.cos(angles)) * weights[None, :]


def band_tables():
    bins = bin_order()
    inside = np.abs(bins[:, None] - bins[None, :]) <= HALFBAND
    share = np.broadcast_to(1.0 / inside.sum(axis=1, keepdims=True), (BINS, LANES))
    return inside.astype(jnp.bfloat16), share.astype(np.float32)


def split(value):
    high = value.astype(BF16)
    return high, (value - high.astype(F32)).astype(BF16)


def mm(a, b):
    return jnp.dot(a, b, preferred_element_type=F32)


def mm_nt(a, b):
    return lax.dot_general(a, b, (((1,), (1,)), ((), ())), preferred_element_type=F32)


def tap_rows(taps):
    width, period = 2 * LANES, LANES // DECIM
    square = (TAPS, TAPS)
    diagonal = lax.broadcasted_iota(jnp.int32, square, 0) == lax.broadcasted_iota(jnp.int32, square, 1)
    column_taps = jnp.sum(jnp.where(diagonal, taps, 0.0), axis=1, keepdims=True)
    tap = lax.broadcasted_iota(jnp.int32, (TAPS, width), 0)
    column = lax.broadcasted_iota(jnp.int32, (TAPS, width), 1)
    placed = jnp.where(column == LANES + DECIM - 1 - tap, column_taps, 0.0)
    spread = jnp.broadcast_to(jnp.sum(placed, axis=0, keepdims=True), (period, width))
    piece = pltpu.roll(spread, 0, 1, stride=DECIM, stride_axis=0)
    rows = []
    for t in range(OUT_BLOCK // period):
        left = jnp.zeros((period, t * LANES), F32)
        right = jnp.zeros((period, STEP - LANES - t * LANES), F32)
        rows.append(jnp.concatenate([p for p in (left, piece, right) if p.shape[1]], axis=1))
    return jnp.concatenate(rows, axis=0)


def rim_kernel(rec_hbm, rim_ref, tail_ref, sem):
    length = rec_hbm.shape[1]
    copy = pltpu.make_async_copy(rec_hbm.at[:, pl.ds(length - LANES, LANES)], tail_ref, sem)
    copy.start()
    copy.wait()
    rim_ref[...] = tail_ref[...].T[LANES - TAPS :]


def spectrum_kernel(taps_ref, rec_ref, tab_ref, twist_ref, spec_ref, mean_ref, head_ref):
    blocks = rec_ref.shape[1] // STEP
    table = tap_rows(taps_ref[...])
    head_ref[...] = table[:GROUP, :LANES]
    taps_high, taps_low = split(table.T)
    taps_both = jnp.concatenate([taps_high, taps_low], axis=1)
    before = [jnp.zeros((LANES, LANES), BF16)] * 2
    outputs = []
    for first in range(0, blocks, blocks // 2):
        windows = ([], [])
        for j in range(first, first + blocks // 2):
            chunk = rec_ref[:, j * STEP : (j + 1) * STEP]
            if j == 0:
                mean = jnp.sum(chunk, axis=1, keepdims=True) * (1.0 / STEP)
            for i, value in enumerate(split(chunk - mean)):
                windows[i].append(jnp.concatenate([before[i], value], axis=1))
                before[i] = value[:, STEP - LANES :]
        wide = mm(jnp.concatenate(windows[0], axis=0), taps_both)
        rest = mm(jnp.concatenate(windows[1], axis=0), taps_high)
        total = wide[:, :LANES] + wide[:, LANES:] + rest
        outputs += [total[t * LANES : (t + 1) * LANES].T for t in range(blocks // 2)]
    pieces = [jnp.concatenate(outputs[j : j + 2], axis=0) for j in range(0, blocks, 2)]
    mean_ref[...] = jnp.broadcast_to(mean, (LANES, LANES)).T[: mean_ref.shape[0]]
    even, odd = pieces[0] + pieces[2], pieces[1] + pieces[3]
    a, b = pieces[0] - pieces[2], pieces[1] - pieces[3]
    whole, half = even + odd, even - odd
    whole = whole - jnp.sum(whole, axis=0, keepdims=True) * (1.0 / DEPTH)
    c1, s1, c2, s2, c3, s3 = [twist_ref[:, i : i + 1] for i in range(6)]
    inputs = [
        whole,
        a * c1 - b * s1,
        -(a * s1 + b * c1),
        half * c2,
        -(half * s2),
        a * c3 + b * s3,
        b * c3 - a * s3,
    ]
    parts = [split(value) for value in inputs]
    high = jnp.concatenate([p[0] for p in parts], axis=1)
    low = jnp.concatenate([p[1] for p in parts], axis=1)
    out = mm(tab_ref[...], jnp.concatenate([high, low, high], axis=0))
    out = out.reshape(FAR_BINS // GROUP, 2, GROUP, out.shape[1])
    rows = 2 * FAR_BINS
    for r in range(RADIX):
        first = max(2 * r - 1, 0) * LANES
        real_in = out[..., first : first + LANES]
        if r == 0:
            real, imag = real_in[:, 0], -real_in[:, 1]
        else:
            imag_in = out[..., first + LANES : first + 2 * LANES]
            real, imag = real_in[:, 0] + imag_in[:, 1], imag_in[:, 0] - real_in[:, 1]
        both = jnp.stack([real, imag], axis=1).reshape(rows, LANES)
        spec_ref[r * rows : (r + 1) * rows, :] = both


def whiten_kernel(
    spec_ref,
    rim_ref,
    mean_ref,
    head_ref,
    edge_ref,
    band_ref,
    share_ref,
    white_ref,
    first_ref,
    second_ref,
):
    head_high, head_low = split(head_ref[:, LANES - TAPS :])
    rim_high, rim_low = split(rim_ref[...] - mean_ref[0:1, :])
    history = mm(
        jnp.concatenate([head_high, head_high, head_low], axis=1),
        jnp.concatenate([rim_high, rim_low, rim_high], axis=0),
    )
    high, low = split(history)
    stacked = jnp.concatenate([high, low, high], axis=0)
    spec = spec_ref[...] + mm(edge_ref[:, : 3 * GROUP], stacked)
    parted = spec.reshape(GROUPS, 2, GROUP, LANES)
    real, imag = parted[:, 0], parted[:, 1]
    amplitude = jnp.sqrt(real * real + imag * imag).reshape(BINS, LANES)
    high, low = split(amplitude)
    wide = mm(band_ref[...], jnp.concatenate([high, low], axis=1))
    smoothed = (wide[:, :LANES] + wide[:, LANES:]) * share_ref[...]
    level = jnp.sum(amplitude, axis=0, keepdims=True) * (1.0 / BINS)
    scale = 1.0 / (smoothed + (WATER * level + 1e-06))
    white = parted * scale.reshape(GROUPS, 1, GROUP, LANES)
    white_ref[...] = white.astype(BF16)
    flat = white.reshape(2 * BINS, LANES)
    turned = pltpu.roll(flat, SPAN, 1)
    lane = lax.broadcasted_iota(jnp.int32, (BINS, LANES), 1)
    up = jnp.where(lane < SPAN, turned[:BINS], flat[BINS:])
    down = jnp.where(lane < SPAN, flat[:BINS], turned[BINS:])
    place = lax.axis_index("chan")
    up_first = halo_order(place, lax.axis_size("chan"))[0]
    first_ref[...] = jnp.where(up_first, up, down).astype(BF16)
    second_ref[...] = jnp.where(up_first, down, up).astype(BF16)


def halo_order(place, count):
    if count % 2:
        return place >= 0, place >= 0
    return place % 2 == 1, place % 2 == 0


def halo_routes(count):
    if count % 2:
        ring = [(i, (i + 1) % count) for i in range(count)]
        return ring, [(j, i) for i, j in ring]
    first = [(i, (i - 1 + 2 * (i % 2)) % count) for i in range(count)]
    second = [(i, i + 1 - 2 * (i % 2)) for i in range(count)]
    return first, second


def offset_moves(offs_ref):
    row = lax.broadcasted_iota(jnp.int32, (2 * LANES, LANES), 0)
    channel = lax.broadcasted_iota(jnp.int32, (2 * LANES, LANES), 1)
    distance = jnp.where(row < LANES + SPAN, row, row - 2 * LANES) - channel
    hits = [(distance == offs_ref[o]).astype(F32) for o in range(offs_ref.shape[0])]
    return jnp.concatenate(hits, axis=1).astype(BF16)


def pack_matrix(owners):
    share = LANES // owners
    matrix = np.zeros((owners, owners, share, owners, owners, share), np.float32)
    for group in range(owners):
        for owner in range(owners):
            matrix[group, owner, :, owner, group, :] = np.eye(share)
    matrix = matrix.reshape(owners, LANES, owners * LANES)[:, ::-1]
    return matrix.reshape(owners * LANES, owners * LANES).astype(jnp.bfloat16)


def partner_of(place, r, owners):
    return place ^ r if owners & (owners - 1) == 0 else (place + r) % owners


def near_kernel(offs_ref, white_ref, first_ref, second_ref, inv_ref, *refs):
    out_refs, lags_ref = refs[:-1], refs[-1]
    rows = white_ref.shape[0] * 2 * GROUP
    half = rows // 2
    noff = lags_ref.shape[0]
    before_first = halo_order(lax.axis_index("chan"), lax.axis_size("chan"))[1]
    first, second = first_ref[...].astype(F32), second_ref[...].astype(F32)
    before = jnp.where(before_first, first, second)
    after = jnp.where(before_first, second, first)
    lane = lax.broadcasted_iota(jnp.int32, (half, LANES), 1)
    upper = jnp.where(lane < SPAN, after, pltpu.roll(before, SPAN, 1))
    lower = jnp.where(lane < SPAN, pltpu.roll(after, SPAN, 1), before)
    edge = jnp.concatenate([upper, lower], axis=0).astype(BF16)
    own = white_ref[...].reshape(rows, LANES)
    far = mm(jnp.concatenate([own, edge], axis=1), offset_moves(offs_ref))
    own = own.astype(F32).reshape(-1, 2, GROUP, LANES)
    columns = []
    for o in range(noff):
        other = far[:, o * LANES : (o + 1) * LANES].reshape(own.shape)
        real = own[:, 0] * other[:, 0] + own[:, 1] * other[:, 1]
        imag = own[:, 1] * other[:, 0] - own[:, 0] * other[:, 1]
        columns.append(jnp.stack([real, imag], axis=1).reshape(rows, LANES).astype(BF16))
    both = mm(inv_ref[...], jnp.concatenate(columns, axis=1))
    lags = both[:LAGS] + both[LAGS:]
    for o in range(noff):
        lags_ref[o] = lags[:, o * LANES : (o + 1) * LANES]
    owners = len(out_refs)
    each = noff // owners
    place = lax.axis_index("seg")
    for r in range(owners):
        first = partner_of(place, r, owners) * each
        out_refs[r][...] = lags_ref[pl.ds(first, each)].astype(BF16)


def turn_kernel(*refs):
    near_ref = refs[-1]
    total = sum(ref[...].astype(F32) for ref in refs[:-1])
    for t in range(near_ref.shape[1]):
        near_ref[:, t, :] = total[t].T


def loop_kernel(partner_ref, count_ref, flip_ref, pack_ref, white_ref, out_ref):
    segs, blocks, _, bins, _ = white_ref.shape
    owners = out_ref.shape[0]
    slots = partner_ref.shape[0]
    rows = segs * 2 * bins
    packed_rows = 2 * bins // owners
    turned = mm(white_ref[...].reshape(blocks * rows, LANES), flip_ref[...])
    turned = turned.reshape(white_ref.shape)
    loops = []
    for b in range(blocks):
        own = turned[:, b]
        for k in range(slots):
            partner = jnp.clip(partner_ref[k, b], 0, blocks - 1)
            live = (k < count_ref[b]).astype(F32)
            far = white_ref[:, partner].astype(F32)
            real = jnp.sum(own[:, 0] * far[:, 0] + own[:, 1] * far[:, 1], axis=0)
            imag = jnp.sum(own[:, 1] * far[:, 0] - own[:, 0] * far[:, 1], axis=0)
            pair = jnp.concatenate([real, imag], axis=0) * live
            groups = [pair[g * packed_rows : (g + 1) * packed_rows] for g in range(owners)]
            loops.append(jnp.concatenate(groups, axis=1))
    packed = mm(jnp.concatenate(loops, axis=0).astype(BF16), pack_ref[...])
    depth = slots * packed_rows
    for b in range(blocks):
        for q in range(owners):
            tile = packed[b * depth : (b + 1) * depth, q * LANES : (q + 1) * LANES]
            out_ref[q, b] = tile.astype(BF16)


def loop_lag_kernel(slots, spec_ref, inv_ref, loop_ref):
    sources = spec_ref.shape[0]
    step = spec_ref.shape[1] // slots
    share = loop_ref.shape[0] // slots
    loop = spec_ref[...].astype(F32)
    rows = []
    for k in range(slots):
        turned = loop[:, k * step : (k + 1) * step].reshape(sources * step, LANES).T
        groups = [turned[g * share : (g + 1) * share] for g in range(LANES // share)]
        rows.append(jnp.concatenate(groups, axis=1))
    both = mm(jnp.concatenate(rows, axis=0).astype(BF16), inv_ref[...])
    loop_ref[...] = both[:, :LAGS] + both[:, LAGS:]


def last_kernel(slots, spec_ref, inv_ref, *refs):
    turn_kernel(*refs[:-1])
    loop_lag_kernel(slots, spec_ref, inv_ref, refs[-1])


def vmem(count):
    return [pl.BlockSpec(memory_space=pltpu.VMEM)] * count


def smem(count):
    return [pl.BlockSpec(memory_space=pltpu.SMEM)] * count


def hbm(count):
    return [pl.BlockSpec(memory_space=pltpu.HBM)] * count


def in_hbm(array):
    return pltpu.with_memory_space_constraint(jnp.asarray(array), pltpu.HBM)


def loops_plain(white, loop_partner, loop_count, owners, inverse):
    _, blocks, _, bins, chans = white.shape
    devices = blocks * owners
    slots = loop_partner.shape[1]
    share = chans // owners
    wide = white.astype(F32).swapaxes(0, 1)
    loops = []
    for k in range(slots):
        far = jnp.flip(wide[loop_partner[:, k]], axis=4)
        live = (k < loop_count).astype(F32)[:, None, None]
        real = jnp.sum(wide[:, :, 0] * far[:, :, 0] + wide[:, :, 1] * far[:, :, 1], axis=1)
        imag = jnp.sum(wide[:, :, 1] * far[:, :, 0] - wide[:, :, 0] * far[:, :, 1], axis=1)
        pair = (jnp.stack([real, imag]) * live[None]).astype(BF16)
        loops.append(pair.reshape(2, blocks, bins, owners, share))
    loop = jnp.transpose(jnp.stack(loops), (4, 2, 0, 1, 3, 5))
    loop = loop.reshape(devices, slots, 2 * bins, share)
    summed = lax.all_to_all(loop, ("seg", "chan"), 0, 0, tiled=True).astype(F32)
    table = inverse.astype(np.float32).reshape(LAGS, devices, 2 * bins)
    lags = jnp.einsum("dtvc,ldv->tcl", summed, table, precision=lax.Precision.HIGHEST)
    return lags[None]


def body(recording, filter_taps, offsets, loop_partner, loop_count):
    chan_count = lax.axis_size("chan")
    seg_count = lax.axis_size("seg")
    devices = chan_count * seg_count
    bins = BINS // devices
    chans, length = recording.shape
    noff, slots = offsets.shape[0], loop_partner.shape[1]
    share = chans // seg_count
    near_each = noff // seg_count
    assert length == NFFT * DECIM and chans == LANES and noff % seg_count == 0

    route = [(i, i + 1) for i in range(seg_count - 1)]
    rim = pl.pallas_call(
        rim_kernel,
        out_shape=jax.ShapeDtypeStruct((TAPS, chans), F32),
        in_specs=hbm(1),
        out_specs=pl.BlockSpec(memory_space=pltpu.VMEM),
        scratch_shapes=[pltpu.VMEM((chans, LANES), F32), pltpu.SemaphoreType.DMA],
        compiler_params=PARAMS,
        cost_estimate=pl.CostEstimate(
            flops=10_000_000_000, bytes_accessed=20_000_000, transcendentals=0
        ),
        name="history",
    )(in_hbm(recording))
    rim = lax.ppermute(rim, "seg", route)
    taps = filter_taps.reshape(1, TAPS)
    spec, mean, head = pl.pallas_call(
        spectrum_kernel,
        out_shape=[
            jax.ShapeDtypeStruct((2 * BINS, LANES), F32),
            jax.ShapeDtypeStruct((8, LANES), F32),
            jax.ShapeDtypeStruct((GROUP, LANES), F32),
        ],
        in_specs=vmem(4),
        out_specs=vmem(3),
        compiler_params=PARAMS,
        cost_estimate=pl.CostEstimate(
            flops=1_000_000_000, bytes_accessed=5_000_000, transcendentals=0
        ),
        name="filter_and_transform",
    )(taps, recording, short_table(), twiddle_table())

    band, band_share = band_tables()
    half = jax.ShapeDtypeStruct((BINS, LANES), BF16)
    white, first, second = pl.pallas_call(
        whiten_kernel,
        out_shape=[jax.ShapeDtypeStruct((GROUPS, 2, GROUP, LANES), BF16), half, half],
        in_specs=vmem(7),
        out_specs=vmem(3),
        compiler_params=PARAMS,
        name="whiten",
    )(spec, rim, mean, head, edge_table(), band, band_share)

    spread = white
    if bins != GROUP:
        spread = jnp.moveaxis(white, 1, 0).reshape(2, devices, bins, LANES)
        spread = jnp.moveaxis(spread, 0, 1)
    moved = lax.all_to_all(spread, ("seg", "chan"), 0, 0, tiled=True)
    moved = moved.reshape(seg_count, chan_count, 2, bins, LANES)

    routes = halo_routes(chan_count)
    first = lax.ppermute(first, "chan", routes[0])
    second = lax.ppermute(second, "chan", routes[1])
    order = np.repeat(bin_order().reshape(GROUPS, 1, GROUP), 2, axis=1).reshape(-1)
    part = np.broadcast_to(np.arange(2).reshape(1, 2, 1), (GROUPS, 2, GROUP)).reshape(-1)
    inverse = np.concatenate(split_np(inverse_table(seg_count, order, part)), axis=0)
    lags = pl.pallas_call(
        near_kernel,
        out_shape=[jax.ShapeDtypeStruct((near_each, LAGS, LANES), BF16)] * seg_count,
        in_specs=smem(1) + vmem(4),
        out_specs=vmem(seg_count),
        scratch_shapes=[pltpu.VMEM((noff, LAGS, LANES), F32)],
        compiler_params=PARAMS,
        cost_estimate=pl.CostEstimate(
            flops=20_000_000_000, bytes_accessed=20_000_000, transcendentals=0
        ),
        name="near_lags",
    )(offsets, white, first, second, inverse)
    lags = list(lags)
    for r in range(seg_count - 1, 0, -1):
        route = [(i, partner_of(i, r, seg_count)) for i in range(seg_count)]
        lags[r] = lax.ppermute(lags[r], "seg", route)
    moved, lags[0] = lax.optimization_barrier((moved, lags[0]))

    near_shape = jax.ShapeDtypeStruct((chans, near_each, LAGS), F32)
    if bins % GROUP or 2 * bins % (8 * seg_count):
        order = np.repeat(bin_order().reshape(devices, 1, bins), 2, axis=1).reshape(-1)
        part = np.broadcast_to(np.arange(2).reshape(1, 2, 1), (devices, 2, bins)).reshape(-1)
        loop_inverse = inverse_table(seg_count, order, part)
        loop = loops_plain(moved, loop_partner, loop_count, seg_count, loop_inverse)
        near = pl.pallas_call(
            turn_kernel,
            out_shape=near_shape,
            in_specs=vmem(seg_count),
            out_specs=pl.BlockSpec(memory_space=pltpu.VMEM),
            compiler_params=PARAMS,
            name="near_turn",
        )(*lags)
        return near, loop

    flip = np.eye(LANES, dtype=np.float32)[::-1].astype(jnp.bfloat16)
    out_rows = slots * (2 * bins // seg_count)
    crossed = pl.pallas_call(
        loop_kernel,
        out_shape=jax.ShapeDtypeStruct((seg_count, chan_count, out_rows, LANES), BF16),
        in_specs=smem(2) + vmem(3),
        out_specs=pl.BlockSpec(memory_space=pltpu.VMEM),
        compiler_params=PARAMS,
        name="loop_spectra",
    )(loop_partner.T, loop_count, flip, pack_matrix(seg_count), moved)
    crossed, *lags[1:] = lax.optimization_barrier((crossed, *lags[1:]))
    crossed = crossed.reshape(devices, out_rows, LANES)
    summed = lax.all_to_all(crossed, ("seg", "chan"), 0, 0, tiled=True)
    columns = np.arange(2 * BINS).reshape(devices, seg_count, -1).swapaxes(0, 1).reshape(-1)
    loop_inverse = inverse_table(seg_count, order[columns], part[columns]).T
    loop_inverse = np.concatenate(split_np(loop_inverse), axis=1)
    near, loop = pl.pallas_call(
        functools.partial(last_kernel, slots),
        out_shape=[near_shape, jax.ShapeDtypeStruct((slots * share, LAGS), F32)],
        in_specs=vmem(2 + seg_count),
        out_specs=vmem(2),
        compiler_params=PARAMS,
        name="lags",
    )(summed, loop_inverse, *lags)
    return near, loop.reshape(1, slots, share, LAGS)


def solution(mesh):
    in_specs = (P("chan", "seg"), P(), P(), P(), P())
    out_specs = (P("chan", "seg", None), P("chan", None, "seg", None))
    return jax.shard_map(body, mesh=mesh, in_specs=in_specs, out_specs=out_specs, check_vma=False)
```

```python
import functools
import math

import jax
import jax.numpy as jnp
import numpy as np
from jax import lax
from jax.experimental import pallas as pl
from jax.experimental.pallas import tpu as pltpu
from jax.sharding import PartitionSpec as P

NFFT = 1024
LAGS = 256
TAPS = 64
DECIM = 4
HALFBAND = 10
SPAN = 64
BINS = 512
WATER = 0.2

LANES = 128
GROUP = 16
GROUPS = BINS // GROUP
OUT_BLOCK = 128
STEP = OUT_BLOCK * DECIM
RADIX = 4
DEPTH = NFFT // RADIX
FAR_BINS = BINS // RADIX

F32 = jnp.float32
BF16 = jnp.bfloat16
MIB = 1024 * 1024
PARAMS = pltpu.CompilerParams(vmem_limit_bytes=32 * MIB)


def bin_order():
    return np.concatenate([np.arange(r, BINS, RADIX) for r in range(RADIX)])


def split_np(table):
    high = table.astype(jnp.bfloat16)
    low = (table - high.astype(np.float64)).astype(jnp.bfloat16)
    return high, low


def short_table():
    bins = np.arange(FAR_BINS).reshape(-1, 1, GROUP, 1)
    angles = (bins * np.arange(DEPTH) % DEPTH) * (2.0 * np.pi / DEPTH)
    rows = np.concatenate([np.cos(angles), np.sin(angles)], axis=1).reshape(-1, DEPTH)
    high, low = split_np(rows)
    return np.concatenate([high, high, low], axis=1)


def twiddle_table():
    angles = np.arange(DEPTH)[:, None] * np.arange(1, RADIX) * (2.0 * np.pi / NFFT)
    columns = np.stack([np.cos(angles), np.sin(angles)], axis=2).reshape(DEPTH, -1)
    return np.pad(columns, ((0, 0), (0, LANES - columns.shape[1]))).astype(np.float32)


def edge_table():
    bins = bin_order().reshape(GROUPS, 1, GROUP, 1)
    angles = (bins * np.arange(GROUP) % NFFT) * (2.0 * np.pi / NFFT)
    rows = np.concatenate([np.cos(angles), -np.sin(angles)], axis=1) * (bins != 0)
    high, low = split_np(rows.reshape(2 * BINS, GROUP))
    table = np.concatenate([high, high, low], axis=1)
    return np.pad(table.astype(np.float32), ((0, 0), (0, LANES - 3 * GROUP))).astype(jnp.bfloat16)


def inverse_table(total_segs, bins, part):
    lag = np.arange(LAGS) - LAGS // 2
    angles = (bins[None, :] * lag[:, None] % NFFT) * (2.0 * np.pi / NFFT)
    weights = np.where(bins == 0, 1.0, 2.0) / math.sqrt(2.0 * BINS * total_segs)
    return np.where(part[None, :] == 1, -np.sin(angles), np.cos(angles)) * weights[None, :]


def band_tables():
    bins = bin_order()
    inside = np.abs(bins[:, None] - bins[None, :]) <= HALFBAND
    share = np.broadcast_to(1.0 / inside.sum(axis=1, keepdims=True), (BINS, LANES))
    return inside.astype(jnp.bfloat16), share.astype(np.float32)


def split(value):
    high = value.astype(BF16)
    return high, (value - high.astype(F32)).astype(BF16)


def mm(a, b):
    return jnp.dot(a, b, preferred_element_type=F32)


def mm_nt(a, b):
    return lax.dot_general(a, b, (((1,), (1,)), ((), ())), preferred_element_type=F32)


def tap_rows(taps):
    width, period = 2 * LANES, LANES // DECIM
    square = (TAPS, TAPS)
    diagonal = lax.broadcasted_iota(jnp.int32, square, 0) == lax.broadcasted_iota(jnp.int32, square, 1)
    column_taps = jnp.sum(jnp.where(diagonal, taps, 0.0), axis=1, keepdims=True)
    tap = lax.broadcasted_iota(jnp.int32, (TAPS, width), 0)
    column = lax.broadcasted_iota(jnp.int32, (TAPS, width), 1)
    placed = jnp.where(column == LANES + DECIM - 1 - tap, column_taps, 0.0)
    spread = jnp.broadcast_to(jnp.sum(placed, axis=0, keepdims=True), (period, width))
    piece = pltpu.roll(spread, 0, 1, stride=DECIM, stride_axis=0)
    rows = []
    for t in range(OUT_BLOCK // period):
        left = jnp.zeros((period, t * LANES), F32)
        right = jnp.zeros((period, STEP - LANES - t * LANES), F32)
        rows.append(jnp.concatenate([p for p in (left, piece, right) if p.shape[1]], axis=1))
    return jnp.concatenate(rows, axis=0)


def rim_kernel(rec_hbm, rim_ref, tail_ref, sem):
    length = rec_hbm.shape[1]
    copy = pltpu.make_async_copy(rec_hbm.at[:, pl.ds(length - LANES, LANES)], tail_ref, sem)
    copy.start()
    copy.wait()
    rim_ref[...] = tail_ref[...].T[LANES - TAPS :]


def spectrum_kernel(taps_ref, rec_ref, tab_ref, twist_ref, spec_ref, mean_ref, head_ref):
    blocks = rec_ref.shape[1] // STEP
    table = tap_rows(taps_ref[...])
    head_ref[...] = table[:GROUP, :LANES]
    taps_high, taps_low = split(table.T)
    taps_both = jnp.concatenate([taps_high, taps_low], axis=1)
    before = [jnp.zeros((LANES, LANES), BF16)] * 2
    outputs = []
    for first in range(0, blocks, blocks // 2):
        windows = ([], [])
        for j in range(first, first + blocks // 2):
            chunk = rec_ref[:, j * STEP : (j + 1) * STEP]
            if j == 0:
                mean = jnp.sum(chunk, axis=1, keepdims=True) * (1.0 / STEP)
            for i, value in enumerate(split(chunk - mean)):
                windows[i].append(jnp.concatenate([before[i], value], axis=1))
                before[i] = value[:, STEP - LANES :]
        wide = mm(jnp.concatenate(windows[0], axis=0), taps_both)
        rest = mm(jnp.concatenate(windows[1], axis=0), taps_high)
        total = wide[:, :LANES] + wide[:, LANES:] + rest
        outputs += [total[t * LANES : (t + 1) * LANES].T for t in range(blocks // 2)]
    pieces = [jnp.concatenate(outputs[j : j + 2], axis=0) for j in range(0, blocks, 2)]
    mean_ref[...] = jnp.broadcast_to(mean, (LANES, LANES)).T[: mean_ref.shape[0]]
    even, odd = pieces[0] + pieces[2], pieces[1] + pieces[3]
    a, b = pieces[0] - pieces[2], pieces[1] - pieces[3]
    whole, half = even + odd, even - odd
    whole = whole - jnp.sum(whole, axis=0, keepdims=True) * (1.0 / DEPTH)
    c1, s1, c2, s2, c3, s3 = [twist_ref[:, i : i + 1] for i in range(6)]
    inputs = [
        whole,
        a * c1 - b * s1,
        -(a * s1 + b * c1),
        half * c2,
        -(half * s2),
        a * c3 + b * s3,
        b * c3 - a * s3,
    ]
    parts = [split(value) for value in inputs]
    high = jnp.concatenate([p[0] for p in parts], axis=1)
    low = jnp.concatenate([p[1] for p in parts], axis=1)
    out = mm(tab_ref[...], jnp.concatenate([high, low, high], axis=0))
    out = out.reshape(FAR_BINS // GROUP, 2, GROUP, out.shape[1])
    rows = 2 * FAR_BINS
    for r in range(RADIX):
        first = max(2 * r - 1, 0) * LANES
        real_in = out[..., first : first + LANES]
        if r == 0:
            real, imag = real_in[:, 0], -real_in[:, 1]
        else:
            imag_in = out[..., first + LANES : first + 2 * LANES]
            real, imag = real_in[:, 0] + imag_in[:, 1], imag_in[:, 0] - real_in[:, 1]
        both = jnp.stack([real, imag], axis=1).reshape(rows, LANES)
        spec_ref[r * rows : (r + 1) * rows, :] = both


def whiten_kernel(
    spec_ref,
    rim_ref,
    mean_ref,
    head_ref,
    edge_ref,
    band_ref,
    share_ref,
    white_ref,
    up_ref,
    down_ref,
):
    head_high, head_low = split(head_ref[:, LANES - TAPS :])
    rim_high, rim_low = split(rim_ref[...] - mean_ref[0:1, :])
    history = mm(
        jnp.concatenate([head_high, head_high, head_low], axis=1),
        jnp.concatenate([rim_high, rim_low, rim_high], axis=0),
    )
    high, low = split(history)
    stacked = jnp.concatenate([high, low, high], axis=0)
    spec = spec_ref[...] + mm(edge_ref[:, : 3 * GROUP], stacked)
    parted = spec.reshape(GROUPS, 2, GROUP, LANES)
    real, imag = parted[:, 0], parted[:, 1]
    amplitude = jnp.sqrt(real * real + imag * imag).reshape(BINS, LANES)
    high, low = split(amplitude)
    wide = mm(band_ref[...], jnp.concatenate([high, low], axis=1))
    smoothed = (wide[:, :LANES] + wide[:, LANES:]) * share_ref[...]
    level = jnp.sum(amplitude, axis=0, keepdims=True) * (1.0 / BINS)
    scale = 1.0 / (smoothed + (WATER * level + 1e-06))
    white = parted * scale.reshape(GROUPS, 1, GROUP, LANES)
    white_ref[...] = white.astype(BF16)
    flat = white.reshape(2 * BINS, LANES)
    turned = pltpu.roll(flat, SPAN, 1)
    lane = lax.broadcasted_iota(jnp.int32, (BINS, LANES), 1)
    up_ref[...] = jnp.where(lane < SPAN, turned[:BINS], flat[BINS:]).astype(BF16)
    down_ref[...] = jnp.where(lane < SPAN, flat[:BINS], turned[BINS:]).astype(BF16)


def offset_moves(offs_ref):
    row = lax.broadcasted_iota(jnp.int32, (2 * LANES, LANES), 0)
    channel = lax.broadcasted_iota(jnp.int32, (2 * LANES, LANES), 1)
    distance = jnp.where(row < LANES + SPAN, row, row - 2 * LANES) - channel
    hits = [(distance == offs_ref[o]).astype(F32) for o in range(offs_ref.shape[0])]
    return jnp.concatenate(hits, axis=1).astype(BF16)


def pack_matrix(owners):
    share = LANES // owners
    matrix = np.zeros((owners, owners, share, owners, owners, share), np.float32)
    for group in range(owners):
        for owner in range(owners):
            matrix[group, owner, :, owner, group, :] = np.eye(share)
    matrix = matrix.reshape(owners, LANES, owners * LANES)[:, ::-1]
    return matrix.reshape(owners * LANES, owners * LANES).astype(jnp.bfloat16)


def partner_of(place, r, owners):
    return place ^ r if owners & (owners - 1) == 0 else (place + r) % owners


def near_kernel(offs_ref, white_ref, before_ref, after_ref, inv_ref, *refs):
    out_refs, lags_ref = refs[:-1], refs[-1]
    rows = white_ref.shape[0] * 2 * GROUP
    half = rows // 2
    noff = lags_ref.shape[0]
    before, after = before_ref[...].astype(F32), after_ref[...].astype(F32)
    lane = lax.broadcasted_iota(jnp.int32, (half, LANES), 1)
    upper = jnp.where(lane < SPAN, after, pltpu.roll(before, SPAN, 1))
    lower = jnp.where(lane < SPAN, pltpu.roll(after, SPAN, 1), before)
    edge = jnp.concatenate([upper, lower], axis=0).astype(BF16)
    own = white_ref[...].reshape(rows, LANES)
    far = mm(jnp.concatenate([own, edge], axis=1), offset_moves(offs_ref))
    own = own.astype(F32).reshape(-1, 2, GROUP, LANES)
    columns = []
    for o in range(noff):
        other = far[:, o * LANES : (o + 1) * LANES].reshape(own.shape)
        real = own[:, 0] * other[:, 0] + own[:, 1] * other[:, 1]
        imag = own[:, 1] * other[:, 0] - own[:, 0] * other[:, 1]
        columns.append(jnp.stack([real, imag], axis=1).reshape(rows, LANES).astype(BF16))
    both = mm(inv_ref[...], jnp.concatenate(columns, axis=1))
    lags = both[:LAGS] + both[LAGS:]
    for o in range(noff):
        lags_ref[o] = lags[:, o * LANES : (o + 1) * LANES]
    owners = len(out_refs)
    each = noff // owners
    place = lax.axis_index("seg")
    for r in range(owners):
        first = partner_of(place, r, owners) * each
        out_refs[r][...] = lags_ref[pl.ds(first, each)].astype(BF16)


def turn_kernel(*refs):
    near_ref = refs[-1]
    total = sum(ref[...].astype(F32) for ref in refs[:-1])
    for t in range(near_ref.shape[1]):
        near_ref[:, t, :] = total[t].T


def loop_kernel(partner_ref, count_ref, flip_ref, pack_ref, white_ref, out_ref):
    segs, blocks, _, bins, _ = white_ref.shape
    owners = out_ref.shape[0]
    slots = partner_ref.shape[0]
    rows = segs * 2 * bins
    packed_rows = 2 * bins // owners
    turned = mm(white_ref[...].reshape(blocks * rows, LANES), flip_ref[...])
    turned = turned.reshape(white_ref.shape)
    loops = []
    for b in range(blocks):
        own = turned[:, b]
        for k in range(slots):
            partner = jnp.clip(partner_ref[k, b], 0, blocks - 1)
            live = (k < count_ref[b]).astype(F32)
            far = white_ref[:, partner].astype(F32)
            real = jnp.sum(own[:, 0] * far[:, 0] + own[:, 1] * far[:, 1], axis=0)
            imag = jnp.sum(own[:, 1] * far[:, 0] - own[:, 0] * far[:, 1], axis=0)
            pair = jnp.concatenate([real, imag], axis=0) * live
            groups = [pair[g * packed_rows : (g + 1) * packed_rows] for g in range(owners)]
            loops.append(jnp.concatenate(groups, axis=1))
    packed = mm(jnp.concatenate(loops, axis=0).astype(BF16), pack_ref[...])
    depth = slots * packed_rows
    for b in range(blocks):
        for q in range(owners):
            tile = packed[b * depth : (b + 1) * depth, q * LANES : (q + 1) * LANES]
            out_ref[q, b] = tile.astype(BF16)


def loop_lag_kernel(slots, spec_ref, inv_ref, loop_ref):
    sources = spec_ref.shape[0]
    step = spec_ref.shape[1] // slots
    share = loop_ref.shape[0] // slots
    loop = spec_ref[...].astype(F32)
    rows = []
    for k in range(slots):
        turned = loop[:, k * step : (k + 1) * step].reshape(sources * step, LANES).T
        groups = [turned[g * share : (g + 1) * share] for g in range(LANES // share)]
        rows.append(jnp.concatenate(groups, axis=1))
    loop_ref[...] = mm(jnp.concatenate(rows, axis=0).astype(BF16), inv_ref[...])


def last_kernel(slots, spec_ref, inv_ref, *refs):
    turn_kernel(*refs[:-1])
    loop_lag_kernel(slots, spec_ref, inv_ref, refs[-1])


def vmem(count):
    return [pl.BlockSpec(memory_space=pltpu.VMEM)] * count


def smem(count):
    return [pl.BlockSpec(memory_space=pltpu.SMEM)] * count


def hbm(count):
    return [pl.BlockSpec(memory_space=pltpu.HBM)] * count


def in_hbm(array):
    return pltpu.with_memory_space_constraint(jnp.asarray(array), pltpu.HBM)


def loops_plain(white, loop_partner, loop_count, owners, inverse):
    _, blocks, _, bins, chans = white.shape
    devices = blocks * owners
    slots = loop_partner.shape[1]
    share = chans // owners
    wide = white.astype(F32).swapaxes(0, 1)
    loops = []
    for k in range(slots):
        far = jnp.flip(wide[loop_partner[:, k]], axis=4)
        live = (k < loop_count).astype(F32)[:, None, None]
        real = jnp.sum(wide[:, :, 0] * far[:, :, 0] + wide[:, :, 1] * far[:, :, 1], axis=1)
        imag = jnp.sum(wide[:, :, 1] * far[:, :, 0] - wide[:, :, 0] * far[:, :, 1], axis=1)
        pair = (jnp.stack([real, imag]) * live[None]).astype(BF16)
        loops.append(pair.reshape(2, blocks, bins, owners, share))
    loop = jnp.transpose(jnp.stack(loops), (4, 2, 0, 1, 3, 5))
    loop = loop.reshape(devices, slots, 2 * bins, share)
    summed = lax.all_to_all(loop, ("seg", "chan"), 0, 0, tiled=True).astype(F32)
    table = inverse.astype(np.float32).reshape(LAGS, devices, 2 * bins)
    lags = jnp.einsum("dtvc,ldv->tcl", summed, table, precision=lax.Precision.HIGHEST)
    return lags[None]


def body(recording, filter_taps, offsets, loop_partner, loop_count):
    chan_count = lax.axis_size("chan")
    seg_count = lax.axis_size("seg")
    devices = chan_count * seg_count
    bins = BINS // devices
    chans, length = recording.shape
    noff, slots = offsets.shape[0], loop_partner.shape[1]
    share = chans // seg_count
    near_each = noff // seg_count
    assert length == NFFT * DECIM and chans == LANES and noff % seg_count == 0

    route = [(i, i + 1) for i in range(seg_count - 1)]
    rim = pl.pallas_call(
        rim_kernel,
        out_shape=jax.ShapeDtypeStruct((TAPS, chans), F32),
        in_specs=hbm(1),
        out_specs=pl.BlockSpec(memory_space=pltpu.VMEM),
        scratch_shapes=[pltpu.VMEM((chans, LANES), F32), pltpu.SemaphoreType.DMA],
        compiler_params=PARAMS,
        cost_estimate=pl.CostEstimate(
            flops=10_000_000_000, bytes_accessed=20_000_000, transcendentals=0
        ),
        name="history",
    )(in_hbm(recording))
    rim = lax.ppermute(rim, "seg", route)
    taps = filter_taps.reshape(1, TAPS)
    spec, mean, head = pl.pallas_call(
        spectrum_kernel,
        out_shape=[
            jax.ShapeDtypeStruct((2 * BINS, LANES), F32),
            jax.ShapeDtypeStruct((8, LANES), F32),
            jax.ShapeDtypeStruct((GROUP, LANES), F32),
        ],
        in_specs=vmem(4),
        out_specs=vmem(3),
        compiler_params=PARAMS,
        cost_estimate=pl.CostEstimate(
            flops=1_000_000_000, bytes_accessed=5_000_000, transcendentals=0
        ),
        name="filter_and_transform",
    )(taps, recording, short_table(), twiddle_table())

    band, band_share = band_tables()
    half = jax.ShapeDtypeStruct((BINS, LANES), BF16)
    white, up, down = pl.pallas_call(
        whiten_kernel,
        out_shape=[jax.ShapeDtypeStruct((GROUPS, 2, GROUP, LANES), BF16), half, half],
        in_specs=vmem(7),
        out_specs=vmem(3),
        compiler_params=PARAMS,
        name="whiten",
    )(spec, rim, mean, head, edge_table(), band, band_share)

    spread = white
    if bins != GROUP:
        spread = jnp.moveaxis(white, 1, 0).reshape(2, devices, bins, LANES)
        spread = jnp.moveaxis(spread, 0, 1)
    moved = lax.all_to_all(spread, ("seg", "chan"), 0, 0, tiled=True)
    moved = moved.reshape(seg_count, chan_count, 2, bins, LANES)

    ring = [(i, (i + 1) % chan_count) for i in range(chan_count)]
    before = lax.ppermute(up, "chan", ring)
    after = lax.ppermute(down, "chan", [(j, i) for i, j in ring])
    order = np.repeat(bin_order().reshape(GROUPS, 1, GROUP), 2, axis=1).reshape(-1)
    part = np.broadcast_to(np.arange(2).reshape(1, 2, 1), (GROUPS, 2, GROUP)).reshape(-1)
    inverse = np.concatenate(split_np(inverse_table(seg_count, order, part)), axis=0)
    lags = pl.pallas_call(
        near_kernel,
        out_shape=[jax.ShapeDtypeStruct((near_each, LAGS, LANES), BF16)] * seg_count,
        in_specs=smem(1) + vmem(4),
        out_specs=vmem(seg_count),
        scratch_shapes=[pltpu.VMEM((noff, LAGS, LANES), F32)],
        compiler_params=PARAMS,
        cost_estimate=pl.CostEstimate(
            flops=20_000_000_000, bytes_accessed=20_000_000, transcendentals=0
        ),
        name="near_lags",
    )(offsets, white, before, after, inverse)
    lags = list(lags)
    for r in range(seg_count - 1, 0, -1):
        route = [(i, partner_of(i, r, seg_count)) for i in range(seg_count)]
        lags[r] = lax.ppermute(lags[r], "seg", route)
    moved, lags[0] = lax.optimization_barrier((moved, lags[0]))

    near_shape = jax.ShapeDtypeStruct((chans, near_each, LAGS), F32)
    if bins % GROUP or 2 * bins % (8 * seg_count):
        order = np.repeat(bin_order().reshape(devices, 1, bins), 2, axis=1).reshape(-1)
        part = np.broadcast_to(np.arange(2).reshape(1, 2, 1), (devices, 2, bins)).reshape(-1)
        loop_inverse = inverse_table(seg_count, order, part)
        loop = loops_plain(moved, loop_partner, loop_count, seg_count, loop_inverse)
        near = pl.pallas_call(
            turn_kernel,
            out_shape=near_shape,
            in_specs=vmem(seg_count),
            out_specs=pl.BlockSpec(memory_space=pltpu.VMEM),
            compiler_params=PARAMS,
            name="near_turn",
        )(*lags)
        return near, loop

    flip = np.eye(LANES, dtype=np.float32)[::-1].astype(jnp.bfloat16)
    out_rows = slots * (2 * bins // seg_count)
    crossed = pl.pallas_call(
        loop_kernel,
        out_shape=jax.ShapeDtypeStruct((seg_count, chan_count, out_rows, LANES), BF16),
        in_specs=smem(2) + vmem(3),
        out_specs=pl.BlockSpec(memory_space=pltpu.VMEM),
        compiler_params=PARAMS,
        name="loop_spectra",
    )(loop_partner.T, loop_count, flip, pack_matrix(seg_count), moved)
    crossed, *lags[1:] = lax.optimization_barrier((crossed, *lags[1:]))
    crossed = crossed.reshape(devices, out_rows, LANES)
    summed = lax.all_to_all(crossed, ("seg", "chan"), 0, 0, tiled=True)
    columns = np.arange(2 * BINS).reshape(devices, seg_count, -1).swapaxes(0, 1).reshape(-1)
    loop_inverse = inverse_table(seg_count, order[columns], part[columns]).T
    loop_inverse = loop_inverse.astype(jnp.bfloat16)
    near, loop = pl.pallas_call(
        functools.partial(last_kernel, slots),
        out_shape=[near_shape, jax.ShapeDtypeStruct((slots * share, LAGS), F32)],
        in_specs=vmem(2 + seg_count),
        out_specs=vmem(2),
        compiler_params=PARAMS,
        name="lags",
    )(summed, loop_inverse, *lags)
    return near, loop.reshape(1, slots, share, LAGS)


def solution(mesh):
    in_specs = (P("chan", "seg"), P(), P(), P(), P())
    out_specs = (P("chan", "seg", None), P("chan", None, "seg", None))
    return jax.shard_map(body, mesh=mesh, in_specs=in_specs, out_specs=out_specs, check_vma=False)
```

```python
import functools
import math

import jax
import jax.numpy as jnp
import numpy as np
from jax import lax
from jax.experimental import pallas as pl
from jax.experimental.pallas import tpu as pltpu
from jax.sharding import PartitionSpec as P

NFFT = 1024
LAGS = 256
TAPS = 64
DECIM = 4
HALFBAND = 10
SPAN = 64
BINS = 512
WATER = 0.2

LANES = 128
GROUP = 16
GROUPS = BINS // GROUP
OUT_BLOCK = 128
STEP = OUT_BLOCK * DECIM
RADIX = 4
DEPTH = NFFT // RADIX
FAR_BINS = BINS // RADIX

F32 = jnp.float32
BF16 = jnp.bfloat16
MIB = 1024 * 1024
PARAMS = pltpu.CompilerParams(vmem_limit_bytes=32 * MIB)


def bin_order():
    return np.concatenate([np.arange(r, BINS, RADIX) for r in range(RADIX)])


def split_np(table):
    high = table.astype(jnp.bfloat16)
    low = (table - high.astype(np.float64)).astype(jnp.bfloat16)
    return high, low


def short_table():
    bins = np.arange(FAR_BINS).reshape(-1, 1, GROUP, 1)
    angles = (bins * np.arange(DEPTH) % DEPTH) * (2.0 * np.pi / DEPTH)
    rows = np.concatenate([np.cos(angles), np.sin(angles)], axis=1).reshape(-1, DEPTH)
    high, low = split_np(rows)
    return np.concatenate([high, high, low], axis=1)


def twiddle_table():
    angles = np.arange(DEPTH)[:, None] * np.arange(1, RADIX) * (2.0 * np.pi / NFFT)
    columns = np.stack([np.cos(angles), np.sin(angles)], axis=2).reshape(DEPTH, -1)
    return np.pad(columns, ((0, 0), (0, LANES - columns.shape[1]))).astype(np.float32)


def edge_table():
    bins = bin_order().reshape(GROUPS, 1, GROUP, 1)
    angles = (bins * np.arange(GROUP) % NFFT) * (2.0 * np.pi / NFFT)
    rows = np.concatenate([np.cos(angles), -np.sin(angles)], axis=1) * (bins != 0)
    high, low = split_np(rows.reshape(2 * BINS, GROUP))
    table = np.concatenate([high, high, low], axis=1)
    return np.pad(table.astype(np.float32), ((0, 0), (0, LANES - 3 * GROUP))).astype(jnp.bfloat16)


def inverse_table(total_segs, bins, part):
    lag = np.arange(LAGS) - LAGS // 2
    angles = (bins[None, :] * lag[:, None] % NFFT) * (2.0 * np.pi / NFFT)
    weights = np.where(bins == 0, 1.0, 2.0) / math.sqrt(2.0 * BINS * total_segs)
    return np.where(part[None, :] == 1, -np.sin(angles), np.cos(angles)) * weights[None, :]


def band_tables():
    bins = bin_order()
    inside = np.abs(bins[:, None] - bins[None, :]) <= HALFBAND
    share = np.broadcast_to(1.0 / inside.sum(axis=1, keepdims=True), (BINS, LANES))
    return inside.astype(jnp.bfloat16), share.astype(np.float32)


def split(value):
    high = value.astype(BF16)
    return high, (value - high.astype(F32)).astype(BF16)


def mm(a, b):
    return jnp.dot(a, b, preferred_element_type=F32)


def mm_nt(a, b):
    return lax.dot_general(a, b, (((1,), (1,)), ((), ())), preferred_element_type=F32)


def tap_rows(taps):
    width, period = 2 * LANES, LANES // DECIM
    square = (TAPS, TAPS)
    diagonal = lax.broadcasted_iota(jnp.int32, square, 0) == lax.broadcasted_iota(jnp.int32, square, 1)
    column_taps = jnp.sum(jnp.where(diagonal, taps, 0.0), axis=1, keepdims=True)
    tap = lax.broadcasted_iota(jnp.int32, (TAPS, width), 0)
    column = lax.broadcasted_iota(jnp.int32, (TAPS, width), 1)
    placed = jnp.where(column == LANES + DECIM - 1 - tap, column_taps, 0.0)
    spread = jnp.broadcast_to(jnp.sum(placed, axis=0, keepdims=True), (period, width))
    piece = pltpu.roll(spread, 0, 1, stride=DECIM, stride_axis=0)
    rows = []
    for t in range(OUT_BLOCK // period):
        left = jnp.zeros((period, t * LANES), F32)
        right = jnp.zeros((period, STEP - LANES - t * LANES), F32)
        rows.append(jnp.concatenate([p for p in (left, piece, right) if p.shape[1]], axis=1))
    return jnp.concatenate(rows, axis=0)


def rim_kernel(rec_hbm, rim_ref, tail_ref, sem):
    length = rec_hbm.shape[1]
    copies = []
    for i in range(4):
        part = pl.ds(i * LANES // 4, LANES // 4)
        source = rec_hbm.at[part, pl.ds(length - LANES, LANES)]
        copies.append(pltpu.make_async_copy(source, tail_ref.at[part], sem.at[i]))
        copies[i].start()
    for copy in copies:
        copy.wait()
    rim_ref[...] = tail_ref[...].T[LANES - TAPS :]


def spectrum_kernel(taps_ref, rec_ref, tab_ref, twist_ref, spec_ref, mean_ref, head_ref):
    blocks = rec_ref.shape[1] // STEP
    table = tap_rows(taps_ref[...])
    head_ref[...] = table[:GROUP, :LANES]
    taps_high, taps_low = split(table.T)
    taps_both = jnp.concatenate([taps_high, taps_low], axis=1)
    before = [jnp.zeros((LANES, LANES), BF16)] * 2
    outputs = []
    for first in range(0, blocks, blocks // 2):
        windows = ([], [])
        for j in range(first, first + blocks // 2):
            chunk = rec_ref[:, j * STEP : (j + 1) * STEP]
            if j == 0:
                mean = jnp.sum(chunk, axis=1, keepdims=True) * (1.0 / STEP)
            for i, value in enumerate(split(chunk - mean)):
                windows[i].append(jnp.concatenate([before[i], value], axis=1))
                before[i] = value[:, STEP - LANES :]
        wide = mm(jnp.concatenate(windows[0], axis=0), taps_both)
        rest = mm(jnp.concatenate(windows[1], axis=0), taps_high)
        total = wide[:, :LANES] + wide[:, LANES:] + rest
        outputs += [total[t * LANES : (t + 1) * LANES].T for t in range(blocks // 2)]
    pieces = [jnp.concatenate(outputs[j : j + 2], axis=0) for j in range(0, blocks, 2)]
    mean_ref[...] = jnp.broadcast_to(mean, (LANES, LANES)).T[: mean_ref.shape[0]]
    even, odd = pieces[0] + pieces[2], pieces[1] + pieces[3]
    a, b = pieces[0] - pieces[2], pieces[1] - pieces[3]
    whole, half = even + odd, even - odd
    whole = whole - jnp.sum(whole, axis=0, keepdims=True) * (1.0 / DEPTH)
    c1, s1, c2, s2, c3, s3 = [twist_ref[:, i : i + 1] for i in range(6)]
    inputs = [
        whole,
        a * c1 - b * s1,
        -(a * s1 + b * c1),
        half * c2,
        -(half * s2),
        a * c3 + b * s3,
        b * c3 - a * s3,
    ]
    parts = [split(value) for value in inputs]
    high = jnp.concatenate([p[0] for p in parts], axis=1)
    low = jnp.concatenate([p[1] for p in parts], axis=1)
    out = mm(tab_ref[...], jnp.concatenate([high, low, high], axis=0))
    out = out.reshape(FAR_BINS // GROUP, 2, GROUP, out.shape[1])
    rows = 2 * FAR_BINS
    for r in range(RADIX):
        first = max(2 * r - 1, 0) * LANES
        real_in = out[..., first : first + LANES]
        if r == 0:
            real, imag = real_in[:, 0], -real_in[:, 1]
        else:
            imag_in = out[..., first + LANES : first + 2 * LANES]
            real, imag = real_in[:, 0] + imag_in[:, 1], imag_in[:, 0] - real_in[:, 1]
        both = jnp.stack([real, imag], axis=1).reshape(rows, LANES)
        spec_ref[r * rows : (r + 1) * rows, :] = both


def whiten_kernel(
    spec_ref,
    rim_ref,
    mean_ref,
    head_ref,
    edge_ref,
    band_ref,
    share_ref,
    white_ref,
    up_ref,
    down_ref,
):
    head_high, head_low = split(head_ref[:, LANES - TAPS :])
    rim_high, rim_low = split(rim_ref[...] - mean_ref[0:1, :])
    history = mm(
        jnp.concatenate([head_high, head_high, head_low], axis=1),
        jnp.concatenate([rim_high, rim_low, rim_high], axis=0),
    )
    high, low = split(history)
    stacked = jnp.concatenate([high, low, high], axis=0)
    spec = spec_ref[...] + mm(edge_ref[:, : 3 * GROUP], stacked)
    parted = spec.reshape(GROUPS, 2, GROUP, LANES)
    real, imag = parted[:, 0], parted[:, 1]
    amplitude = jnp.sqrt(real * real + imag * imag).reshape(BINS, LANES)
    high, low = split(amplitude)
    wide = mm(band_ref[...], jnp.concatenate([high, low], axis=1))
    smoothed = (wide[:, :LANES] + wide[:, LANES:]) * share_ref[...]
    level = jnp.sum(amplitude, axis=0, keepdims=True) * (1.0 / BINS)
    scale = 1.0 / (smoothed + (WATER * level + 1e-06))
    white = parted * scale.reshape(GROUPS, 1, GROUP, LANES)
    white_ref[...] = white.astype(BF16)
    flat = white.reshape(2 * BINS, LANES)
    turned = pltpu.roll(flat, SPAN, 1)
    lane = lax.broadcasted_iota(jnp.int32, (BINS, LANES), 1)
    up_ref[...] = jnp.where(lane < SPAN, turned[:BINS], flat[BINS:]).astype(BF16)
    down_ref[...] = jnp.where(lane < SPAN, flat[:BINS], turned[BINS:]).astype(BF16)


def offset_moves(offs_ref):
    row = lax.broadcasted_iota(jnp.int32, (2 * LANES, LANES), 0)
    channel = lax.broadcasted_iota(jnp.int32, (2 * LANES, LANES), 1)
    distance = jnp.where(row < LANES + SPAN, row, row - 2 * LANES) - channel
    hits = [(distance == offs_ref[o]).astype(F32) for o in range(offs_ref.shape[0])]
    return jnp.concatenate(hits, axis=1).astype(BF16)


def pack_matrix(owners):
    share = LANES // owners
    matrix = np.zeros((owners, owners, share, owners, owners, share), np.float32)
    for group in range(owners):
        for owner in range(owners):
            matrix[group, owner, :, owner, group, :] = np.eye(share)
    matrix = matrix.reshape(owners, LANES, owners * LANES)[:, ::-1]
    return matrix.reshape(owners * LANES, owners * LANES).astype(jnp.bfloat16)


def partner_of(place, r, owners):
    return place ^ r if owners & (owners - 1) == 0 else (place + r) % owners


def near_kernel(offs_ref, white_ref, before_ref, after_ref, inv_ref, *refs):
    out_refs, lags_ref = refs[:-1], refs[-1]
    rows = white_ref.shape[0] * 2 * GROUP
    half = rows // 2
    noff = lags_ref.shape[0]
    before, after = before_ref[...].astype(F32), after_ref[...].astype(F32)
    lane = lax.broadcasted_iota(jnp.int32, (half, LANES), 1)
    upper = jnp.where(lane < SPAN, after, pltpu.roll(before, SPAN, 1))
    lower = jnp.where(lane < SPAN, pltpu.roll(after, SPAN, 1), before)
    edge = jnp.concatenate([upper, lower], axis=0).astype(BF16)
    own = white_ref[...].reshape(rows, LANES)
    far = mm(jnp.concatenate([own, edge], axis=1), offset_moves(offs_ref))
    own = own.astype(F32).reshape(-1, 2, GROUP, LANES)
    columns = []
    for o in range(noff):
        other = far[:, o * LANES : (o + 1) * LANES].reshape(own.shape)
        real = own[:, 0] * other[:, 0] + own[:, 1] * other[:, 1]
        imag = own[:, 1] * other[:, 0] - own[:, 0] * other[:, 1]
        columns.append(jnp.stack([real, imag], axis=1).reshape(rows, LANES).astype(BF16))
    both = mm(inv_ref[...], jnp.concatenate(columns, axis=1))
    lags = both[:LAGS] + both[LAGS:]
    for o in range(noff):
        lags_ref[o] = lags[:, o * LANES : (o + 1) * LANES]
    owners = len(out_refs)
    each = noff // owners
    place = lax.axis_index("seg")
    for r in range(owners):
        first = partner_of(place, r, owners) * each
        out_refs[r][...] = lags_ref[pl.ds(first, each)].astype(BF16)


def turn_kernel(*refs):
    near_ref = refs[-1]
    total = sum(ref[...].astype(F32) for ref in refs[:-1])
    for t in range(near_ref.shape[1]):
        near_ref[:, t, :] = total[t].T


def loop_kernel(partner_ref, count_ref, flip_ref, pack_ref, white_ref, out_ref):
    segs, blocks, _, bins, _ = white_ref.shape
    owners = out_ref.shape[0]
    slots = partner_ref.shape[0]
    rows = segs * 2 * bins
    packed_rows = 2 * bins // owners
    turned = mm(white_ref[...].reshape(blocks * rows, LANES), flip_ref[...])
    turned = turned.reshape(white_ref.shape)
    loops = []
    for b in range(blocks):
        own = turned[:, b]
        for k in range(slots):
            partner = jnp.clip(partner_ref[k, b], 0, blocks - 1)
            live = (k < count_ref[b]).astype(F32)
            far = white_ref[:, partner].astype(F32)
            real = jnp.sum(own[:, 0] * far[:, 0] + own[:, 1] * far[:, 1], axis=0)
            imag = jnp.sum(own[:, 1] * far[:, 0] - own[:, 0] * far[:, 1], axis=0)
            pair = jnp.concatenate([real, imag], axis=0) * live
            groups = [pair[g * packed_rows : (g + 1) * packed_rows] for g in range(owners)]
            loops.append(jnp.concatenate(groups, axis=1))
    packed = mm(jnp.concatenate(loops, axis=0).astype(BF16), pack_ref[...])
    depth = slots * packed_rows
    for b in range(blocks):
        for q in range(owners):
            tile = packed[b * depth : (b + 1) * depth, q * LANES : (q + 1) * LANES]
            out_ref[q, b] = tile.astype(BF16)


def loop_lag_kernel(slots, spec_ref, inv_ref, loop_ref):
    sources = spec_ref.shape[0]
    step = spec_ref.shape[1] // slots
    share = loop_ref.shape[0] // slots
    loop = spec_ref[...].astype(F32)
    rows = []
    for k in range(slots):
        turned = loop[:, k * step : (k + 1) * step].reshape(sources * step, LANES).T
        groups = [turned[g * share : (g + 1) * share] for g in range(LANES // share)]
        rows.append(jnp.concatenate(groups, axis=1))
    loop_ref[...] = mm(jnp.concatenate(rows, axis=0).astype(BF16), inv_ref[...])


def last_kernel(slots, spec_ref, inv_ref, *refs):
    lag_refs, (near_hbm, loop_ref, near_ref, sem) = refs[:-4], refs[-4:]
    turn_kernel(*lag_refs, near_ref)
    copy = pltpu.make_async_copy(near_ref, near_hbm, sem)
    copy.start()
    loop_lag_kernel(slots, spec_ref, inv_ref, loop_ref)
    copy.wait()


def vmem(count):
    return [pl.BlockSpec(memory_space=pltpu.VMEM)] * count


def smem(count):
    return [pl.BlockSpec(memory_space=pltpu.SMEM)] * count


def hbm(count):
    return [pl.BlockSpec(memory_space=pltpu.HBM)] * count


def in_hbm(array):
    return pltpu.with_memory_space_constraint(jnp.asarray(array), pltpu.HBM)


def loops_plain(white, loop_partner, loop_count, owners, inverse):
    _, blocks, _, bins, chans = white.shape
    devices = blocks * owners
    slots = loop_partner.shape[1]
    share = chans // owners
    wide = white.astype(F32).swapaxes(0, 1)
    loops = []
    for k in range(slots):
        far = jnp.flip(wide[loop_partner[:, k]], axis=4)
        live = (k < loop_count).astype(F32)[:, None, None]
        real = jnp.sum(wide[:, :, 0] * far[:, :, 0] + wide[:, :, 1] * far[:, :, 1], axis=1)
        imag = jnp.sum(wide[:, :, 1] * far[:, :, 0] - wide[:, :, 0] * far[:, :, 1], axis=1)
        pair = (jnp.stack([real, imag]) * live[None]).astype(BF16)
        loops.append(pair.reshape(2, blocks, bins, owners, share))
    loop = jnp.transpose(jnp.stack(loops), (4, 2, 0, 1, 3, 5))
    loop = loop.reshape(devices, slots, 2 * bins, share)
    summed = lax.all_to_all(loop, ("seg", "chan"), 0, 0, tiled=True).astype(F32)
    table = inverse.astype(np.float32).reshape(LAGS, devices, 2 * bins)
    lags = jnp.einsum("dtvc,ldv->tcl", summed, table, precision=lax.Precision.HIGHEST)
    return lags[None]


def body(recording, filter_taps, offsets, loop_partner, loop_count):
    chan_count = lax.axis_size("chan")
    seg_count = lax.axis_size("seg")
    devices = chan_count * seg_count
    bins = BINS // devices
    chans, length = recording.shape
    noff, slots = offsets.shape[0], loop_partner.shape[1]
    share = chans // seg_count
    near_each = noff // seg_count
    assert length == NFFT * DECIM and chans == LANES and noff % seg_count == 0

    route = [(i, i + 1) for i in range(seg_count - 1)]
    rim = pl.pallas_call(
        rim_kernel,
        out_shape=jax.ShapeDtypeStruct((TAPS, chans), F32),
        in_specs=hbm(1),
        out_specs=pl.BlockSpec(memory_space=pltpu.VMEM),
        scratch_shapes=[pltpu.VMEM((chans, LANES), F32), pltpu.SemaphoreType.DMA((4,))],
        compiler_params=PARAMS,
        cost_estimate=pl.CostEstimate(
            flops=10_000_000_000, bytes_accessed=20_000_000, transcendentals=0
        ),
        name="history",
    )(in_hbm(recording))
    rim = lax.ppermute(rim, "seg", route)
    taps = filter_taps.reshape(1, TAPS)
    spec, mean, head = pl.pallas_call(
        spectrum_kernel,
        out_shape=[
            jax.ShapeDtypeStruct((2 * BINS, LANES), F32),
            jax.ShapeDtypeStruct((8, LANES), F32),
            jax.ShapeDtypeStruct((GROUP, LANES), F32),
        ],
        in_specs=vmem(4),
        out_specs=vmem(3),
        compiler_params=PARAMS,
        cost_estimate=pl.CostEstimate(
            flops=1_000_000_000, bytes_accessed=5_000_000, transcendentals=0
        ),
        name="filter_and_transform",
    )(taps, recording, short_table(), twiddle_table())

    band, band_share = band_tables()
    half = jax.ShapeDtypeStruct((BINS, LANES), BF16)
    white, up, down = pl.pallas_call(
        whiten_kernel,
        out_shape=[jax.ShapeDtypeStruct((GROUPS, 2, GROUP, LANES), BF16), half, half],
        in_specs=vmem(7),
        out_specs=vmem(3),
        compiler_params=PARAMS,
        name="whiten",
    )(spec, rim, mean, head, edge_table(), band, band_share)

    spread = white
    if bins != GROUP:
        spread = jnp.moveaxis(white, 1, 0).reshape(2, devices, bins, LANES)
        spread = jnp.moveaxis(spread, 0, 1)
    moved = lax.all_to_all(spread, ("seg", "chan"), 0, 0, tiled=True)
    moved = moved.reshape(seg_count, chan_count, 2, bins, LANES)

    ring = [(i, (i + 1) % chan_count) for i in range(chan_count)]
    before = lax.ppermute(up, "chan", ring)
    after = lax.ppermute(down, "chan", [(j, i) for i, j in ring])
    order = np.repeat(bin_order().reshape(GROUPS, 1, GROUP), 2, axis=1).reshape(-1)
    part = np.broadcast_to(np.arange(2).reshape(1, 2, 1), (GROUPS, 2, GROUP)).reshape(-1)
    inverse = np.concatenate(split_np(inverse_table(seg_count, order, part)), axis=0)
    lags = pl.pallas_call(
        near_kernel,
        out_shape=[jax.ShapeDtypeStruct((near_each, LAGS, LANES), BF16)] * seg_count,
        in_specs=smem(1) + vmem(4),
        out_specs=vmem(seg_count),
        scratch_shapes=[pltpu.VMEM((noff, LAGS, LANES), F32)],
        compiler_params=PARAMS,
        cost_estimate=pl.CostEstimate(
            flops=20_000_000_000, bytes_accessed=20_000_000, transcendentals=0
        ),
        name="near_lags",
    )(offsets, white, before, after, inverse)
    lags = list(lags)
    for r in range(seg_count - 1, 0, -1):
        route = [(i, partner_of(i, r, seg_count)) for i in range(seg_count)]
        lags[r] = lax.ppermute(lags[r], "seg", route)
    moved, lags[0] = lax.optimization_barrier((moved, lags[0]))

    near_shape = jax.ShapeDtypeStruct((chans, near_each, LAGS), F32)
    if bins % GROUP or 2 * bins % (8 * seg_count):
        order = np.repeat(bin_order().reshape(devices, 1, bins), 2, axis=1).reshape(-1)
        part = np.broadcast_to(np.arange(2).reshape(1, 2, 1), (devices, 2, bins)).reshape(-1)
        loop_inverse = inverse_table(seg_count, order, part)
        loop = loops_plain(moved, loop_partner, loop_count, seg_count, loop_inverse)
        near = pl.pallas_call(
            turn_kernel,
            out_shape=near_shape,
            in_specs=vmem(seg_count),
            out_specs=pl.BlockSpec(memory_space=pltpu.VMEM),
            compiler_params=PARAMS,
            name="near_turn",
        )(*lags)
        return near, loop

    flip = np.eye(LANES, dtype=np.float32)[::-1].astype(jnp.bfloat16)
    out_rows = slots * (2 * bins // seg_count)
    crossed = pl.pallas_call(
        loop_kernel,
        out_shape=jax.ShapeDtypeStruct((seg_count, chan_count, out_rows, LANES), BF16),
        in_specs=smem(2) + vmem(3),
        out_specs=pl.BlockSpec(memory_space=pltpu.VMEM),
        compiler_params=PARAMS,
        name="loop_spectra",
    )(loop_partner.T, loop_count, flip, pack_matrix(seg_count), moved)
    crossed, *lags[1:] = lax.optimization_barrier((crossed, *lags[1:]))
    crossed = crossed.reshape(devices, out_rows, LANES)
    summed = lax.all_to_all(crossed, ("seg", "chan"), 0, 0, tiled=True)
    columns = np.arange(2 * BINS).reshape(devices, seg_count, -1).swapaxes(0, 1).reshape(-1)
    loop_inverse = inverse_table(seg_count, order[columns], part[columns]).T
    loop_inverse = loop_inverse.astype(jnp.bfloat16)
    near, loop = pl.pallas_call(
        functools.partial(last_kernel, slots),
        out_shape=[near_shape, jax.ShapeDtypeStruct((slots * share, LAGS), F32)],
        in_specs=vmem(2 + seg_count),
        out_specs=hbm(1) + vmem(1),
        scratch_shapes=[
            pltpu.VMEM((chans, near_each, LAGS), F32),
            pltpu.SemaphoreType.DMA,
        ],
        compiler_params=PARAMS,
        name="lags",
    )(summed, loop_inverse, *lags)
    return near, loop.reshape(1, slots, share, LAGS)


def solution(mesh):
    in_specs = (P("chan", "seg"), P(), P(), P(), P())
    out_specs = (P("chan", "seg", None), P("chan", None, "seg", None))
    return jax.shard_map(body, mesh=mesh, in_specs=in_specs, out_specs=out_specs, check_vma=False)
```

```python
import functools
import math

import jax
import jax.numpy as jnp
import numpy as np
from jax import lax
from jax.experimental import pallas as pl
from jax.experimental.pallas import tpu as pltpu
from jax.sharding import PartitionSpec as P

NFFT = 1024
LAGS = 256
TAPS = 64
DECIM = 4
HALFBAND = 10
SPAN = 64
BINS = 512
WATER = 0.2

LANES = 128
GROUP = 16
GROUPS = BINS // GROUP
OUT_BLOCK = 128
STEP = OUT_BLOCK * DECIM
RADIX = 4
DEPTH = NFFT // RADIX
FAR_BINS = BINS // RADIX

F32 = jnp.float32
BF16 = jnp.bfloat16
MIB = 1024 * 1024
PARAMS = pltpu.CompilerParams(vmem_limit_bytes=32 * MIB)


def bin_order():
    return np.concatenate([np.arange(r, BINS, RADIX) for r in range(RADIX)])


def split_np(table):
    high = table.astype(jnp.bfloat16)
    low = (table - high.astype(np.float64)).astype(jnp.bfloat16)
    return high, low


def short_table():
    bins = np.arange(FAR_BINS).reshape(-1, 1, GROUP, 1)
    angles = (bins * np.arange(DEPTH) % DEPTH) * (2.0 * np.pi / DEPTH)
    rows = np.concatenate([np.cos(angles), np.sin(angles)], axis=1).reshape(-1, DEPTH)
    high, low = split_np(rows)
    return np.concatenate([high, high, low], axis=1)


def twiddle_table():
    angles = np.arange(DEPTH)[:, None] * np.arange(1, RADIX) * (2.0 * np.pi / NFFT)
    columns = np.stack([np.cos(angles), np.sin(angles)], axis=2).reshape(DEPTH, -1)
    return np.pad(columns, ((0, 0), (0, LANES - columns.shape[1]))).astype(np.float32)


def edge_table():
    bins = bin_order().reshape(GROUPS, 1, GROUP, 1)
    angles = (bins * np.arange(GROUP) % NFFT) * (2.0 * np.pi / NFFT)
    rows = np.concatenate([np.cos(angles), -np.sin(angles)], axis=1) * (bins != 0)
    high, low = split_np(rows.reshape(2 * BINS, GROUP))
    table = np.concatenate([high, high, low], axis=1)
    return np.pad(table.astype(np.float32), ((0, 0), (0, LANES - 3 * GROUP))).astype(jnp.bfloat16)


def inverse_table(total_segs, bins, part):
    lag = np.arange(LAGS) - LAGS // 2
    angles = (bins[None, :] * lag[:, None] % NFFT) * (2.0 * np.pi / NFFT)
    weights = np.where(bins == 0, 1.0, 2.0) / math.sqrt(2.0 * BINS * total_segs)
    return np.where(part[None, :] == 1, -np.sin(angles), np.cos(angles)) * weights[None, :]


def band_tables():
    bins = bin_order()
    inside = np.abs(bins[:, None] - bins[None, :]) <= HALFBAND
    share = np.broadcast_to(1.0 / inside.sum(axis=1, keepdims=True), (BINS, LANES))
    return inside.astype(jnp.bfloat16), share.astype(np.float32)


def split(value):
    high = value.astype(BF16)
    return high, (value - high.astype(F32)).astype(BF16)


def mm(a, b):
    return jnp.dot(a, b, preferred_element_type=F32)


def mm_nt(a, b):
    return lax.dot_general(a, b, (((1,), (1,)), ((), ())), preferred_element_type=F32)


def tap_rows(taps):
    width, period = 2 * LANES, LANES // DECIM
    square = (TAPS, TAPS)
    diagonal = lax.broadcasted_iota(jnp.int32, square, 0) == lax.broadcasted_iota(jnp.int32, square, 1)
    column_taps = jnp.sum(jnp.where(diagonal, taps, 0.0), axis=1, keepdims=True)
    tap = lax.broadcasted_iota(jnp.int32, (TAPS, width), 0)
    column = lax.broadcasted_iota(jnp.int32, (TAPS, width), 1)
    placed = jnp.where(column == LANES + DECIM - 1 - tap, column_taps, 0.0)
    spread = jnp.broadcast_to(jnp.sum(placed, axis=0, keepdims=True), (period, width))
    piece = pltpu.roll(spread, 0, 1, stride=DECIM, stride_axis=0)
    rows = []
    for t in range(OUT_BLOCK // period):
        left = jnp.zeros((period, t * LANES), F32)
        right = jnp.zeros((period, STEP - LANES - t * LANES), F32)
        rows.append(jnp.concatenate([p for p in (left, piece, right) if p.shape[1]], axis=1))
    return jnp.concatenate(rows, axis=0)


def rim_kernel(rec_hbm, rim_ref, tail_ref, sem):
    length = rec_hbm.shape[1]
    copies = []
    for i in range(4):
        part = pl.ds(i * LANES // 4, LANES // 4)
        source = rec_hbm.at[part, pl.ds(length - LANES, LANES)]
        copies.append(pltpu.make_async_copy(source, tail_ref.at[part], sem.at[i]))
        copies[i].start()
    for copy in copies:
        copy.wait()
    rim_ref[...] = tail_ref[...].T[LANES - TAPS :]


def spectrum_kernel(taps_ref, rec_ref, tab_ref, twist_ref, spec_ref, mean_ref, head_ref):
    blocks = rec_ref.shape[1] // STEP
    table = tap_rows(taps_ref[...])
    head_ref[...] = table[:GROUP, :LANES]
    taps_high, taps_low = split(table.T)
    taps_both = jnp.concatenate([taps_high, taps_low], axis=1)
    before = [jnp.zeros((LANES, LANES), BF16)] * 2
    outputs = []
    for first in range(0, blocks, blocks // 2):
        windows = ([], [])
        for j in range(first, first + blocks // 2):
            chunk = rec_ref[:, j * STEP : (j + 1) * STEP]
            if j == 0:
                mean = jnp.sum(chunk, axis=1, keepdims=True) * (1.0 / STEP)
            for i, value in enumerate(split(chunk - mean)):
                windows[i].append(jnp.concatenate([before[i], value], axis=1))
                before[i] = value[:, STEP - LANES :]
        wide = mm(jnp.concatenate(windows[0], axis=0), taps_both)
        rest = mm(jnp.concatenate(windows[1], axis=0), taps_high)
        total = wide[:, :LANES] + wide[:, LANES:] + rest
        outputs += [total[t * LANES : (t + 1) * LANES].T for t in range(blocks // 2)]
    pieces = [jnp.concatenate(outputs[j : j + 2], axis=0) for j in range(0, blocks, 2)]
    mean_ref[...] = jnp.broadcast_to(mean, (LANES, LANES)).T[: mean_ref.shape[0]]
    even, odd = pieces[0] + pieces[2], pieces[1] + pieces[3]
    a, b = pieces[0] - pieces[2], pieces[1] - pieces[3]
    whole, half = even + odd, even - odd
    whole = whole - jnp.sum(whole, axis=0, keepdims=True) * (1.0 / DEPTH)
    c1, s1, c2, s2, c3, s3 = [twist_ref[:, i : i + 1] for i in range(6)]
    inputs = [
        whole,
        a * c1 - b * s1,
        -(a * s1 + b * c1),
        half * c2,
        -(half * s2),
        a * c3 + b * s3,
        b * c3 - a * s3,
    ]
    parts = [split(value) for value in inputs]
    high = jnp.concatenate([p[0] for p in parts], axis=1)
    low = jnp.concatenate([p[1] for p in parts], axis=1)
    out = mm(tab_ref[...], jnp.concatenate([high, low, high], axis=0))
    out = out.reshape(FAR_BINS // GROUP, 2, GROUP, out.shape[1])
    rows = 2 * FAR_BINS
    for r in range(RADIX):
        first = max(2 * r - 1, 0) * LANES
        real_in = out[..., first : first + LANES]
        if r == 0:
            real, imag = real_in[:, 0], -real_in[:, 1]
        else:
            imag_in = out[..., first + LANES : first + 2 * LANES]
            real, imag = real_in[:, 0] + imag_in[:, 1], imag_in[:, 0] - real_in[:, 1]
        both = jnp.stack([real, imag], axis=1).reshape(rows, LANES)
        spec_ref[r * rows : (r + 1) * rows, :] = both


def whiten_kernel(
    spec_ref,
    rim_ref,
    mean_ref,
    head_ref,
    edge_ref,
    band_ref,
    share_ref,
    white_ref,
    up_ref,
    down_ref,
):
    head_high, head_low = split(head_ref[:, LANES - TAPS :])
    rim_high, rim_low = split(rim_ref[...] - mean_ref[0:1, :])
    history = mm(
        jnp.concatenate([head_high, head_high, head_low], axis=1),
        jnp.concatenate([rim_high, rim_low, rim_high], axis=0),
    )
    high, low = split(history)
    stacked = jnp.concatenate([high, low, high], axis=0)
    spec = spec_ref[...] + mm(edge_ref[:, : 3 * GROUP], stacked)
    parted = spec.reshape(GROUPS, 2, GROUP, LANES)
    real, imag = parted[:, 0], parted[:, 1]
    amplitude = jnp.sqrt(real * real + imag * imag).reshape(BINS, LANES)
    high, low = split(amplitude)
    wide = mm(band_ref[...], jnp.concatenate([high, low], axis=1))
    smoothed = (wide[:, :LANES] + wide[:, LANES:]) * share_ref[...]
    level = jnp.sum(amplitude, axis=0, keepdims=True) * (1.0 / BINS)
    scale = 1.0 / (smoothed + (WATER * level + 1e-06))
    white = parted * scale.reshape(GROUPS, 1, GROUP, LANES)
    white_ref[...] = white.astype(BF16)
    flat = white.reshape(2 * BINS, LANES)
    turned = pltpu.roll(flat, SPAN, 1)
    lane = lax.broadcasted_iota(jnp.int32, (BINS, LANES), 1)
    up_ref[...] = jnp.where(lane < SPAN, turned[:BINS], flat[BINS:]).astype(BF16)
    down_ref[...] = jnp.where(lane < SPAN, flat[:BINS], turned[BINS:]).astype(BF16)


def offset_moves(offs_ref):
    row = lax.broadcasted_iota(jnp.int32, (2 * LANES, LANES), 0)
    channel = lax.broadcasted_iota(jnp.int32, (2 * LANES, LANES), 1)
    distance = jnp.where(row < LANES + SPAN, row, row - 2 * LANES) - channel
    hits = [(distance == offs_ref[o]).astype(F32) for o in range(offs_ref.shape[0])]
    return jnp.concatenate(hits, axis=1).astype(BF16)


def pack_matrix(owners):
    share = LANES // owners
    matrix = np.zeros((owners, owners, share, owners, owners, share), np.float32)
    for group in range(owners):
        for owner in range(owners):
            matrix[group, owner, :, owner, group, :] = np.eye(share)
    matrix = matrix.reshape(owners, LANES, owners * LANES)[:, ::-1]
    return matrix.reshape(owners * LANES, owners * LANES).astype(jnp.bfloat16)


def partner_of(place, r, owners):
    return place ^ r if owners & (owners - 1) == 0 else (place + r) % owners


def near_kernel(offs_ref, white_ref, before_ref, after_ref, inv_ref, *refs):
    out_refs, lags_ref = refs[:-1], refs[-1]
    rows = white_ref.shape[0] * 2 * GROUP
    half = rows // 2
    noff = lags_ref.shape[0]
    before, after = before_ref[...].astype(F32), after_ref[...].astype(F32)
    lane = lax.broadcasted_iota(jnp.int32, (half, LANES), 1)
    upper = jnp.where(lane < SPAN, after, pltpu.roll(before, SPAN, 1))
    lower = jnp.where(lane < SPAN, pltpu.roll(after, SPAN, 1), before)
    edge = jnp.concatenate([upper, lower], axis=0).astype(BF16)
    own = white_ref[...].reshape(rows, LANES)
    far = mm(jnp.concatenate([own, edge], axis=1), offset_moves(offs_ref))
    own = own.astype(F32).reshape(-1, 2, GROUP, LANES)
    columns = []
    for o in range(noff):
        other = far[:, o * LANES : (o + 1) * LANES].reshape(own.shape)
        real = own[:, 0] * other[:, 0] + own[:, 1] * other[:, 1]
        imag = own[:, 1] * other[:, 0] - own[:, 0] * other[:, 1]
        columns.append(jnp.stack([real, imag], axis=1).reshape(rows, LANES).astype(BF16))
    both = mm(inv_ref[...], jnp.concatenate(columns, axis=1))
    lags = both[:LAGS] + both[LAGS:]
    for o in range(noff):
        lags_ref[o] = lags[:, o * LANES : (o + 1) * LANES]
    owners = len(out_refs)
    each = noff // owners
    place = lax.axis_index("seg")
    for r in range(owners):
        first = partner_of(place, r, owners) * each
        out_refs[r][...] = lags_ref[pl.ds(first, each)].astype(BF16)


def turn_kernel(*refs):
    near_ref = refs[-1]
    total = sum(ref[...].astype(F32) for ref in refs[:-1])
    for t in range(near_ref.shape[1]):
        near_ref[:, t, :] = total[t].T


def loop_kernel(partner_ref, count_ref, flip_ref, pack_ref, white_ref, out_ref):
    segs, blocks, _, bins, _ = white_ref.shape
    owners = out_ref.shape[0]
    slots = partner_ref.shape[0]
    rows = segs * 2 * bins
    packed_rows = 2 * bins // owners
    turned = mm(white_ref[...].reshape(blocks * rows, LANES), flip_ref[...])
    turned = turned.reshape(white_ref.shape)
    loops = []
    for b in range(blocks):
        own = turned[:, b]
        for k in range(slots):
            partner = jnp.clip(partner_ref[k, b], 0, blocks - 1)
            live = (k < count_ref[b]).astype(F32)
            far = white_ref[:, partner].astype(F32)
            real = jnp.sum(own[:, 0] * far[:, 0] + own[:, 1] * far[:, 1], axis=0)
            imag = jnp.sum(own[:, 1] * far[:, 0] - own[:, 0] * far[:, 1], axis=0)
            pair = jnp.concatenate([real, imag], axis=0) * live
            groups = [pair[g * packed_rows : (g + 1) * packed_rows] for g in range(owners)]
            loops.append(jnp.concatenate(groups, axis=1))
    packed = mm(jnp.concatenate(loops, axis=0).astype(BF16), pack_ref[...])
    depth = slots * packed_rows
    for b in range(blocks):
        for q in range(owners):
            tile = packed[b * depth : (b + 1) * depth, q * LANES : (q + 1) * LANES]
            out_ref[q, b] = tile.astype(BF16)


def loop_lag_kernel(slots, spec_ref, inv_ref, loop_ref):
    sources = spec_ref.shape[0]
    step = spec_ref.shape[1] // slots
    share = loop_ref.shape[0] // slots
    loop = spec_ref[...].astype(F32)
    rows = []
    for k in range(slots):
        turned = loop[:, k * step : (k + 1) * step].reshape(sources * step, LANES).T
        groups = [turned[g * share : (g + 1) * share] for g in range(LANES // share)]
        rows.append(jnp.concatenate(groups, axis=1))
    loop_ref[...] = mm(jnp.concatenate(rows, axis=0).astype(BF16), inv_ref[...])


def last_kernel(slots, spec_ref, inv_ref, *refs):
    turn_kernel(*refs[:-1])
    loop_lag_kernel(slots, spec_ref, inv_ref, refs[-1])


def vmem(count):
    return [pl.BlockSpec(memory_space=pltpu.VMEM)] * count


def smem(count):
    return [pl.BlockSpec(memory_space=pltpu.SMEM)] * count


def hbm(count):
    return [pl.BlockSpec(memory_space=pltpu.HBM)] * count


def in_hbm(array):
    return pltpu.with_memory_space_constraint(jnp.asarray(array), pltpu.HBM)


def loops_plain(white, loop_partner, loop_count, owners, inverse):
    _, blocks, _, bins, chans = white.shape
    devices = blocks * owners
    slots = loop_partner.shape[1]
    share = chans // owners
    wide = white.astype(F32).swapaxes(0, 1)
    loops = []
    for k in range(slots):
        far = jnp.flip(wide[loop_partner[:, k]], axis=4)
        live = (k < loop_count).astype(F32)[:, None, None]
        real = jnp.sum(wide[:, :, 0] * far[:, :, 0] + wide[:, :, 1] * far[:, :, 1], axis=1)
        imag = jnp.sum(wide[:, :, 1] * far[:, :, 0] - wide[:, :, 0] * far[:, :, 1], axis=1)
        pair = (jnp.stack([real, imag]) * live[None]).astype(BF16)
        loops.append(pair.reshape(2, blocks, bins, owners, share))
    loop = jnp.transpose(jnp.stack(loops), (4, 2, 0, 1, 3, 5))
    loop = loop.reshape(devices, slots, 2 * bins, share)
    summed = lax.all_to_all(loop, ("seg", "chan"), 0, 0, tiled=True).astype(F32)
    table = inverse.astype(np.float32).reshape(LAGS, devices, 2 * bins)
    lags = jnp.einsum("dtvc,ldv->tcl", summed, table, precision=lax.Precision.HIGHEST)
    return lags[None]


def body(recording, filter_taps, offsets, loop_partner, loop_count):
    chan_count = lax.axis_size("chan")
    seg_count = lax.axis_size("seg")
    devices = chan_count * seg_count
    bins = BINS // devices
    chans, length = recording.shape
    noff, slots = offsets.shape[0], loop_partner.shape[1]
    share = chans // seg_count
    near_each = noff // seg_count
    assert length == NFFT * DECIM and chans == LANES and noff % seg_count == 0

    route = [(i, i + 1) for i in range(seg_count - 1)]
    rim = pl.pallas_call(
        rim_kernel,
        out_shape=jax.ShapeDtypeStruct((TAPS, chans), F32),
        in_specs=hbm(1),
        out_specs=pl.BlockSpec(memory_space=pltpu.VMEM),
        scratch_shapes=[pltpu.VMEM((chans, LANES), F32), pltpu.SemaphoreType.DMA((4,))],
        compiler_params=PARAMS,
        cost_estimate=pl.CostEstimate(
            flops=10_000_000_000, bytes_accessed=20_000_000, transcendentals=0
        ),
        name="history",
    )(in_hbm(recording))
    rim = lax.ppermute(rim, "seg", route)
    taps = filter_taps.reshape(1, TAPS)
    spec, mean, head = pl.pallas_call(
        spectrum_kernel,
        out_shape=[
            jax.ShapeDtypeStruct((2 * BINS, LANES), F32),
            jax.ShapeDtypeStruct((8, LANES), F32),
            jax.ShapeDtypeStruct((GROUP, LANES), F32),
        ],
        in_specs=vmem(4),
        out_specs=vmem(3),
        compiler_params=PARAMS,
        cost_estimate=pl.CostEstimate(
            flops=1_000_000_000, bytes_accessed=5_000_000, transcendentals=0
        ),
        name="filter_and_transform",
    )(taps, recording, short_table(), twiddle_table())

    band, band_share = band_tables()
    half = jax.ShapeDtypeStruct((BINS, LANES), BF16)
    white, up, down = pl.pallas_call(
        whiten_kernel,
        out_shape=[jax.ShapeDtypeStruct((GROUPS, 2, GROUP, LANES), BF16), half, half],
        in_specs=vmem(7),
        out_specs=vmem(3),
        compiler_params=PARAMS,
        name="whiten",
    )(spec, rim, mean, head, edge_table(), band, band_share)

    spread = white
    if bins != GROUP:
        spread = jnp.moveaxis(white, 1, 0).reshape(2, devices, bins, LANES)
        spread = jnp.moveaxis(spread, 0, 1)
    moved = lax.all_to_all(spread, ("seg", "chan"), 0, 0, tiled=True)
    moved = moved.reshape(seg_count, chan_count, 2, bins, LANES)

    ring = [(i, (i + 1) % chan_count) for i in range(chan_count)]
    before = lax.ppermute(up, "chan", ring)
    after = lax.ppermute(down, "chan", [(j, i) for i, j in ring])
    order = np.repeat(bin_order().reshape(GROUPS, 1, GROUP), 2, axis=1).reshape(-1)
    part = np.broadcast_to(np.arange(2).reshape(1, 2, 1), (GROUPS, 2, GROUP)).reshape(-1)
    inverse = np.concatenate(split_np(inverse_table(seg_count, order, part)), axis=0)
    lags = pl.pallas_call(
        near_kernel,
        out_shape=[jax.ShapeDtypeStruct((near_each, LAGS, LANES), BF16)] * seg_count,
        in_specs=smem(1) + vmem(4),
        out_specs=vmem(seg_count),
        scratch_shapes=[pltpu.VMEM((noff, LAGS, LANES), F32)],
        compiler_params=PARAMS,
        cost_estimate=pl.CostEstimate(
            flops=20_000_000_000, bytes_accessed=20_000_000, transcendentals=0
        ),
        name="near_lags",
    )(offsets, white, before, after, inverse)
    lags = list(lags)
    for r in range(seg_count - 1, 0, -1):
        route = [(i, partner_of(i, r, seg_count)) for i in range(seg_count)]
        lags[r] = lax.ppermute(lags[r], "seg", route)
    moved, lags[0] = lax.optimization_barrier((moved, lags[0]))

    near_shape = jax.ShapeDtypeStruct((chans, near_each, LAGS), F32)
    if bins % GROUP or 2 * bins % (8 * seg_count):
        order = np.repeat(bin_order().reshape(devices, 1, bins), 2, axis=1).reshape(-1)
        part = np.broadcast_to(np.arange(2).reshape(1, 2, 1), (devices, 2, bins)).reshape(-1)
        loop_inverse = inverse_table(seg_count, order, part)
        loop = loops_plain(moved, loop_partner, loop_count, seg_count, loop_inverse)
        near = pl.pallas_call(
            turn_kernel,
            out_shape=near_shape,
            in_specs=vmem(seg_count),
            out_specs=pl.BlockSpec(memory_space=pltpu.VMEM),
            compiler_params=PARAMS,
            name="near_turn",
        )(*lags)
        return near, loop

    flip = np.eye(LANES, dtype=np.float32)[::-1].astype(jnp.bfloat16)
    out_rows = slots * (2 * bins // seg_count)
    crossed = pl.pallas_call(
        loop_kernel,
        out_shape=jax.ShapeDtypeStruct((seg_count, chan_count, out_rows, LANES), BF16),
        in_specs=smem(2) + vmem(3),
        out_specs=pl.BlockSpec(memory_space=pltpu.VMEM),
        compiler_params=PARAMS,
        name="loop_spectra",
    )(loop_partner.T, loop_count, flip, pack_matrix(seg_count), moved)
    crossed, *lags[1:] = lax.optimization_barrier((crossed, *lags[1:]))
    crossed = crossed.reshape(devices, out_rows, LANES)
    summed = lax.all_to_all(crossed, ("seg", "chan"), 0, 0, tiled=True)
    columns = np.arange(2 * BINS).reshape(devices, seg_count, -1).swapaxes(0, 1).reshape(-1)
    loop_inverse = inverse_table(seg_count, order[columns], part[columns]).T
    loop_inverse = loop_inverse.astype(jnp.bfloat16)
    near, loop = pl.pallas_call(
        functools.partial(last_kernel, slots),
        out_shape=[near_shape, jax.ShapeDtypeStruct((slots * share, LAGS), F32)],
        in_specs=vmem(2 + seg_count),
        out_specs=vmem(2),
        compiler_params=PARAMS,
        name="lags",
    )(summed, loop_inverse, *lags)
    return near, loop.reshape(1, slots, share, LAGS)


def solution(mesh):
    in_specs = (P("chan", "seg"), P(), P(), P(), P())
    out_specs = (P("chan", "seg", None), P("chan", None, "seg", None))
    return jax.shard_map(body, mesh=mesh, in_specs=in_specs, out_specs=out_specs, check_vma=False)
```

```python
import functools
import math

import jax
import jax.numpy as jnp
import numpy as np
from jax import lax
from jax.experimental import pallas as pl
from jax.experimental.pallas import tpu as pltpu
from jax.sharding import PartitionSpec as P

NFFT = 1024
LAGS = 256
TAPS = 64
DECIM = 4
HALFBAND = 10
SPAN = 64
BINS = 512
WATER = 0.2

LANES = 128
GROUP = 16
GROUPS = BINS // GROUP
OUT_BLOCK = 128
STEP = OUT_BLOCK * DECIM
RADIX = 4
DEPTH = NFFT // RADIX
FAR_BINS = BINS // RADIX

F32 = jnp.float32
BF16 = jnp.bfloat16
MIB = 1024 * 1024
PARAMS = pltpu.CompilerParams(vmem_limit_bytes=32 * MIB)


def bin_order():
    return np.concatenate([np.arange(r, BINS, RADIX) for r in range(RADIX)])


def split_np(table):
    high = table.astype(jnp.bfloat16)
    low = (table - high.astype(np.float64)).astype(jnp.bfloat16)
    return high, low


def short_table():
    bins = np.arange(FAR_BINS).reshape(-1, 1, GROUP, 1)
    angles = (bins * np.arange(DEPTH) % DEPTH) * (2.0 * np.pi / DEPTH)
    rows = np.concatenate([np.cos(angles), np.sin(angles)], axis=1).reshape(-1, DEPTH)
    high, low = split_np(rows)
    return np.concatenate([high, high, low], axis=1)


def twiddle_table():
    angles = np.arange(DEPTH)[:, None] * np.arange(1, RADIX) * (2.0 * np.pi / NFFT)
    columns = np.stack([np.cos(angles), np.sin(angles)], axis=2).reshape(DEPTH, -1)
    return np.pad(columns, ((0, 0), (0, LANES - columns.shape[1]))).astype(np.float32)


def edge_table():
    bins = bin_order().reshape(GROUPS, 1, GROUP, 1)
    angles = (bins * np.arange(GROUP) % NFFT) * (2.0 * np.pi / NFFT)
    rows = np.concatenate([np.cos(angles), -np.sin(angles)], axis=1) * (bins != 0)
    high, low = split_np(rows.reshape(2 * BINS, GROUP))
    table = np.concatenate([high, high, low], axis=1)
    return np.pad(table.astype(np.float32), ((0, 0), (0, LANES - 3 * GROUP))).astype(jnp.bfloat16)


def inverse_table(total_segs, bins, part):
    lag = np.arange(LAGS) - LAGS // 2
    angles = (bins[None, :] * lag[:, None] % NFFT) * (2.0 * np.pi / NFFT)
    weights = np.where(bins == 0, 1.0, 2.0) / math.sqrt(2.0 * BINS * total_segs)
    return np.where(part[None, :] == 1, -np.sin(angles), np.cos(angles)) * weights[None, :]


def band_tables():
    bins = bin_order()
    inside = np.abs(bins[:, None] - bins[None, :]) <= HALFBAND
    share = np.broadcast_to(1.0 / inside.sum(axis=1, keepdims=True), (BINS, LANES))
    return inside.astype(jnp.bfloat16), share.astype(np.float32)


def split(value):
    high = value.astype(BF16)
    return high, (value - high.astype(F32)).astype(BF16)


def mm(a, b):
    return jnp.dot(a, b, preferred_element_type=F32)


def mm_nt(a, b):
    return lax.dot_general(a, b, (((1,), (1,)), ((), ())), preferred_element_type=F32)


def tap_rows(taps):
    width, period = 2 * LANES, LANES // DECIM
    square = (TAPS, TAPS)
    diagonal = lax.broadcasted_iota(jnp.int32, square, 0) == lax.broadcasted_iota(jnp.int32, square, 1)
    column_taps = jnp.sum(jnp.where(diagonal, taps, 0.0), axis=1, keepdims=True)
    tap = lax.broadcasted_iota(jnp.int32, (TAPS, width), 0)
    column = lax.broadcasted_iota(jnp.int32, (TAPS, width), 1)
    placed = jnp.where(column == LANES + DECIM - 1 - tap, column_taps, 0.0)
    spread = jnp.broadcast_to(jnp.sum(placed, axis=0, keepdims=True), (period, width))
    piece = pltpu.roll(spread, 0, 1, stride=DECIM, stride_axis=0)
    rows = []
    for t in range(OUT_BLOCK // period):
        left = jnp.zeros((period, t * LANES), F32)
        right = jnp.zeros((period, STEP - LANES - t * LANES), F32)
        rows.append(jnp.concatenate([p for p in (left, piece, right) if p.shape[1]], axis=1))
    return jnp.concatenate(rows, axis=0)


def rim_kernel(rec_hbm, rim_ref, tail_ref, sem):
    length = rec_hbm.shape[1]
    copies = []
    for i in range(4):
        part = pl.ds(i * LANES // 4, LANES // 4)
        source = rec_hbm.at[part, pl.ds(length - LANES, LANES)]
        copies.append(pltpu.make_async_copy(source, tail_ref.at[part], sem.at[i]))
        copies[i].start()
    for copy in copies:
        copy.wait()
    tail = tail_ref[...].T[LANES - TAPS :]
    mean = jnp.sum(tail, axis=0, keepdims=True) * (1.0 / TAPS)
    high, _ = split(mean)
    middle, low = split(mean - high.astype(F32))
    row = lax.broadcasted_iota(jnp.int32, (GROUP, LANES), 0)
    means = jnp.zeros((GROUP, LANES), F32)
    for i, part in enumerate((high, middle, low)):
        means = jnp.where(row == i, part.astype(F32), means)
    rim_ref[...] = jnp.concatenate([tail - mean, means], axis=0).astype(BF16)


def spectrum_kernel(taps_ref, rec_ref, tab_ref, twist_ref, spec_ref, mean_ref, head_ref):
    blocks = rec_ref.shape[1] // STEP
    table = tap_rows(taps_ref[...])
    head_ref[...] = table[:GROUP, :LANES]
    taps_high, taps_low = split(table.T)
    taps_both = jnp.concatenate([taps_high, taps_low], axis=1)
    before = [jnp.zeros((LANES, LANES), BF16)] * 2
    outputs = []
    for first in range(0, blocks, blocks // 2):
        windows = ([], [])
        for j in range(first, first + blocks // 2):
            chunk = rec_ref[:, j * STEP : (j + 1) * STEP]
            if j == 0:
                mean = jnp.sum(chunk, axis=1, keepdims=True) * (1.0 / STEP)
            for i, value in enumerate(split(chunk - mean)):
                windows[i].append(jnp.concatenate([before[i], value], axis=1))
                before[i] = value[:, STEP - LANES :]
        wide = mm(jnp.concatenate(windows[0], axis=0), taps_both)
        rest = mm(jnp.concatenate(windows[1], axis=0), taps_high)
        total = wide[:, :LANES] + wide[:, LANES:] + rest
        outputs += [total[t * LANES : (t + 1) * LANES].T for t in range(blocks // 2)]
    pieces = [jnp.concatenate(outputs[j : j + 2], axis=0) for j in range(0, blocks, 2)]
    mean_ref[...] = jnp.broadcast_to(mean, (LANES, LANES)).T[: mean_ref.shape[0]]
    even, odd = pieces[0] + pieces[2], pieces[1] + pieces[3]
    a, b = pieces[0] - pieces[2], pieces[1] - pieces[3]
    whole, half = even + odd, even - odd
    whole = whole - jnp.sum(whole, axis=0, keepdims=True) * (1.0 / DEPTH)
    c1, s1, c2, s2, c3, s3 = [twist_ref[:, i : i + 1] for i in range(6)]
    inputs = [
        whole,
        a * c1 - b * s1,
        -(a * s1 + b * c1),
        half * c2,
        -(half * s2),
        a * c3 + b * s3,
        b * c3 - a * s3,
    ]
    parts = [split(value) for value in inputs]
    high = jnp.concatenate([p[0] for p in parts], axis=1)
    low = jnp.concatenate([p[1] for p in parts], axis=1)
    out = mm(tab_ref[...], jnp.concatenate([high, low, high], axis=0))
    out = out.reshape(FAR_BINS // GROUP, 2, GROUP, out.shape[1])
    rows = 2 * FAR_BINS
    for r in range(RADIX):
        first = max(2 * r - 1, 0) * LANES
        real_in = out[..., first : first + LANES]
        if r == 0:
            real, imag = real_in[:, 0], -real_in[:, 1]
        else:
            imag_in = out[..., first + LANES : first + 2 * LANES]
            real, imag = real_in[:, 0] + imag_in[:, 1], imag_in[:, 0] - real_in[:, 1]
        both = jnp.stack([real, imag], axis=1).reshape(rows, LANES)
        spec_ref[r * rows : (r + 1) * rows, :] = both


def whiten_kernel(
    spec_ref,
    rim_ref,
    mean_ref,
    head_ref,
    edge_ref,
    band_ref,
    share_ref,
    white_ref,
    up_ref,
    down_ref,
):
    head_high, head_low = split(head_ref[:, LANES - TAPS :])
    rim = rim_ref[...].astype(F32)
    offset = jnp.sum(rim[TAPS:], axis=0, keepdims=True) - mean_ref[0:1, :]
    rim_high, rim_low = split(rim[:TAPS] + offset)
    history = mm(
        jnp.concatenate([head_high, head_high, head_low], axis=1),
        jnp.concatenate([rim_high, rim_low, rim_high], axis=0),
    )
    high, low = split(history)
    stacked = jnp.concatenate([high, low, high], axis=0)
    spec = spec_ref[...] + mm(edge_ref[:, : 3 * GROUP], stacked)
    parted = spec.reshape(GROUPS, 2, GROUP, LANES)
    real, imag = parted[:, 0], parted[:, 1]
    amplitude = jnp.sqrt(real * real + imag * imag).reshape(BINS, LANES)
    high, low = split(amplitude)
    wide = mm(band_ref[...], jnp.concatenate([high, low], axis=1))
    smoothed = (wide[:, :LANES] + wide[:, LANES:]) * share_ref[...]
    level = jnp.sum(amplitude, axis=0, keepdims=True) * (1.0 / BINS)
    scale = 1.0 / (smoothed + (WATER * level + 1e-06))
    white = parted * scale.reshape(GROUPS, 1, GROUP, LANES)
    white_ref[...] = white.astype(BF16)
    flat = white.reshape(2 * BINS, LANES)
    turned = pltpu.roll(flat, SPAN, 1)
    lane = lax.broadcasted_iota(jnp.int32, (BINS, LANES), 1)
    up_ref[...] = jnp.where(lane < SPAN, turned[:BINS], flat[BINS:]).astype(BF16)
    down_ref[...] = jnp.where(lane < SPAN, flat[:BINS], turned[BINS:]).astype(BF16)


def offset_moves(offs_ref):
    row = lax.broadcasted_iota(jnp.int32, (2 * LANES, LANES), 0)
    channel = lax.broadcasted_iota(jnp.int32, (2 * LANES, LANES), 1)
    distance = jnp.where(row < LANES + SPAN, row, row - 2 * LANES) - channel
    hits = [(distance == offs_ref[o]).astype(F32) for o in range(offs_ref.shape[0])]
    return jnp.concatenate(hits, axis=1).astype(BF16)


def pack_matrix(owners):
    share = LANES // owners
    matrix = np.zeros((owners, owners, share, owners, owners, share), np.float32)
    for group in range(owners):
        for owner in range(owners):
            matrix[group, owner, :, owner, group, :] = np.eye(share)
    matrix = matrix.reshape(owners, LANES, owners * LANES)[:, ::-1]
    return matrix.reshape(owners * LANES, owners * LANES).astype(jnp.bfloat16)


def partner_of(place, r, owners):
    return place ^ r if owners & (owners - 1) == 0 else (place + r) % owners


def near_kernel(offs_ref, white_ref, before_ref, after_ref, inv_ref, *refs):
    out_refs, lags_ref = refs[:-1], refs[-1]
    rows = white_ref.shape[0] * 2 * GROUP
    half = rows // 2
    noff = lags_ref.shape[0]
    before, after = before_ref[...].astype(F32), after_ref[...].astype(F32)
    lane = lax.broadcasted_iota(jnp.int32, (half, LANES), 1)
    upper = jnp.where(lane < SPAN, after, pltpu.roll(before, SPAN, 1))
    lower = jnp.where(lane < SPAN, pltpu.roll(after, SPAN, 1), before)
    edge = jnp.concatenate([upper, lower], axis=0).astype(BF16)
    own = white_ref[...].reshape(rows, LANES)
    far = mm(jnp.concatenate([own, edge], axis=1), offset_moves(offs_ref))
    own = own.astype(F32).reshape(-1, 2, GROUP, LANES)
    columns = []
    for o in range(noff):
        other = far[:, o * LANES : (o + 1) * LANES].reshape(own.shape)
        real = own[:, 0] * other[:, 0] + own[:, 1] * other[:, 1]
        imag = own[:, 1] * other[:, 0] - own[:, 0] * other[:, 1]
        columns.append(jnp.stack([real, imag], axis=1).reshape(rows, LANES).astype(BF16))
    both = mm(inv_ref[...], jnp.concatenate(columns, axis=1))
    lags = both[:LAGS] + both[LAGS:]
    for o in range(noff):
        lags_ref[o] = lags[:, o * LANES : (o + 1) * LANES]
    owners = len(out_refs)
    each = noff // owners
    place = lax.axis_index("seg")
    for r in range(owners):
        first = partner_of(place, r, owners) * each
        out_refs[r][...] = lags_ref[pl.ds(first, each)].astype(BF16)


def turn_kernel(*refs):
    near_ref = refs[-1]
    total = sum(ref[...].astype(F32) for ref in refs[:-1])
    for t in range(near_ref.shape[1]):
        near_ref[:, t, :] = total[t].T


def loop_kernel(partner_ref, count_ref, flip_ref, pack_ref, white_ref, out_ref):
    segs, blocks, _, bins, _ = white_ref.shape
    owners = out_ref.shape[0]
    slots = partner_ref.shape[0]
    rows = segs * 2 * bins
    packed_rows = 2 * bins // owners
    turned = mm(white_ref[...].reshape(blocks * rows, LANES), flip_ref[...])
    turned = turned.reshape(white_ref.shape)
    loops = []
    for b in range(blocks):
        own = turned[:, b]
        for k in range(slots):
            partner = jnp.clip(partner_ref[k, b], 0, blocks - 1)
            live = (k < count_ref[b]).astype(F32)
            far = white_ref[:, partner].astype(F32)
            real = jnp.sum(own[:, 0] * far[:, 0] + own[:, 1] * far[:, 1], axis=0)
            imag = jnp.sum(own[:, 1] * far[:, 0] - own[:, 0] * far[:, 1], axis=0)
            pair = jnp.concatenate([real, imag], axis=0) * live
            groups = [pair[g * packed_rows : (g + 1) * packed_rows] for g in range(owners)]
            loops.append(jnp.concatenate(groups, axis=1))
    packed = mm(jnp.concatenate(loops, axis=0).astype(BF16), pack_ref[...])
    depth = slots * packed_rows
    for b in range(blocks):
        for q in range(owners):
            tile = packed[b * depth : (b + 1) * depth, q * LANES : (q + 1) * LANES]
            out_ref[q, b] = tile.astype(BF16)


def loop_lag_kernel(slots, spec_ref, inv_ref, loop_ref):
    sources = spec_ref.shape[0]
    step = spec_ref.shape[1] // slots
    share = loop_ref.shape[0] // slots
    loop = spec_ref[...].astype(F32)
    rows = []
    for k in range(slots):
        turned = loop[:, k * step : (k + 1) * step].reshape(sources * step, LANES).T
        groups = [turned[g * share : (g + 1) * share] for g in range(LANES // share)]
        rows.append(jnp.concatenate(groups, axis=1))
    loop_ref[...] = mm(jnp.concatenate(rows, axis=0).astype(BF16), inv_ref[...])


def last_kernel(slots, spec_ref, inv_ref, *refs):
    turn_kernel(*refs[:-1])
    loop_lag_kernel(slots, spec_ref, inv_ref, refs[-1])


def vmem(count):
    return [pl.BlockSpec(memory_space=pltpu.VMEM)] * count


def smem(count):
    return [pl.BlockSpec(memory_space=pltpu.SMEM)] * count


def hbm(count):
    return [pl.BlockSpec(memory_space=pltpu.HBM)] * count


def in_hbm(array):
    return pltpu.with_memory_space_constraint(jnp.asarray(array), pltpu.HBM)


def loops_plain(white, loop_partner, loop_count, owners, inverse):
    _, blocks, _, bins, chans = white.shape
    devices = blocks * owners
    slots = loop_partner.shape[1]
    share = chans // owners
    wide = white.astype(F32).swapaxes(0, 1)
    loops = []
    for k in range(slots):
        far = jnp.flip(wide[loop_partner[:, k]], axis=4)
        live = (k < loop_count).astype(F32)[:, None, None]
        real = jnp.sum(wide[:, :, 0] * far[:, :, 0] + wide[:, :, 1] * far[:, :, 1], axis=1)
        imag = jnp.sum(wide[:, :, 1] * far[:, :, 0] - wide[:, :, 0] * far[:, :, 1], axis=1)
        pair = (jnp.stack([real, imag]) * live[None]).astype(BF16)
        loops.append(pair.reshape(2, blocks, bins, owners, share))
    loop = jnp.transpose(jnp.stack(loops), (4, 2, 0, 1, 3, 5))
    loop = loop.reshape(devices, slots, 2 * bins, share)
    summed = lax.all_to_all(loop, ("seg", "chan"), 0, 0, tiled=True).astype(F32)
    table = inverse.astype(np.float32).reshape(LAGS, devices, 2 * bins)
    lags = jnp.einsum("dtvc,ldv->tcl", summed, table, precision=lax.Precision.HIGHEST)
    return lags[None]


def body(recording, filter_taps, offsets, loop_partner, loop_count):
    chan_count = lax.axis_size("chan")
    seg_count = lax.axis_size("seg")
    devices = chan_count * seg_count
    bins = BINS // devices
    chans, length = recording.shape
    noff, slots = offsets.shape[0], loop_partner.shape[1]
    share = chans // seg_count
    near_each = noff // seg_count
    assert length == NFFT * DECIM and chans == LANES and noff % seg_count == 0

    route = [(i, i + 1) for i in range(seg_count - 1)]
    rim = pl.pallas_call(
        rim_kernel,
        out_shape=jax.ShapeDtypeStruct((TAPS + GROUP, chans), BF16),
        in_specs=hbm(1),
        out_specs=pl.BlockSpec(memory_space=pltpu.VMEM),
        scratch_shapes=[pltpu.VMEM((chans, LANES), F32), pltpu.SemaphoreType.DMA((4,))],
        compiler_params=PARAMS,
        cost_estimate=pl.CostEstimate(
            flops=10_000_000_000, bytes_accessed=20_000_000, transcendentals=0
        ),
        name="history",
    )(in_hbm(recording))
    rim = lax.ppermute(rim, "seg", route)
    taps = filter_taps.reshape(1, TAPS)
    spec, mean, head = pl.pallas_call(
        spectrum_kernel,
        out_shape=[
            jax.ShapeDtypeStruct((2 * BINS, LANES), F32),
            jax.ShapeDtypeStruct((8, LANES), F32),
            jax.ShapeDtypeStruct((GROUP, LANES), F32),
        ],
        in_specs=vmem(4),
        out_specs=vmem(3),
        compiler_params=PARAMS,
        cost_estimate=pl.CostEstimate(
            flops=1_000_000_000, bytes_accessed=5_000_000, transcendentals=0
        ),
        name="filter_and_transform",
    )(taps, recording, short_table(), twiddle_table())

    band, band_share = band_tables()
    half = jax.ShapeDtypeStruct((BINS, LANES), BF16)
    white, up, down = pl.pallas_call(
        whiten_kernel,
        out_shape=[jax.ShapeDtypeStruct((GROUPS, 2, GROUP, LANES), BF16), half, half],
        in_specs=vmem(7),
        out_specs=vmem(3),
        compiler_params=PARAMS,
        name="whiten",
    )(spec, rim, mean, head, edge_table(), band, band_share)

    spread = white
    if bins != GROUP:
        spread = jnp.moveaxis(white, 1, 0).reshape(2, devices, bins, LANES)
        spread = jnp.moveaxis(spread, 0, 1)
    moved = lax.all_to_all(spread, ("seg", "chan"), 0, 0, tiled=True)
    moved = moved.reshape(seg_count, chan_count, 2, bins, LANES)

    ring = [(i, (i + 1) % chan_count) for i in range(chan_count)]
    before = lax.ppermute(up, "chan", ring)
    after = lax.ppermute(down, "chan", [(j, i) for i, j in ring])
    order = np.repeat(bin_order().reshape(GROUPS, 1, GROUP), 2, axis=1).reshape(-1)
    part = np.broadcast_to(np.arange(2).reshape(1, 2, 1), (GROUPS, 2, GROUP)).reshape(-1)
    inverse = np.concatenate(split_np(inverse_table(seg_count, order, part)), axis=0)
    lags = pl.pallas_call(
        near_kernel,
        out_shape=[jax.ShapeDtypeStruct((near_each, LAGS, LANES), BF16)] * seg_count,
        in_specs=smem(1) + vmem(4),
        out_specs=vmem(seg_count),
        scratch_shapes=[pltpu.VMEM((noff, LAGS, LANES), F32)],
        compiler_params=PARAMS,
        cost_estimate=pl.CostEstimate(
            flops=20_000_000_000, bytes_accessed=20_000_000, transcendentals=0
        ),
        name="near_lags",
    )(offsets, white, before, after, inverse)
    lags = list(lags)
    for r in range(seg_count - 1, 0, -1):
        route = [(i, partner_of(i, r, seg_count)) for i in range(seg_count)]
        lags[r] = lax.ppermute(lags[r], "seg", route)
    moved, lags[0] = lax.optimization_barrier((moved, lags[0]))

    near_shape = jax.ShapeDtypeStruct((chans, near_each, LAGS), F32)
    if bins % GROUP or 2 * bins % (8 * seg_count):
        order = np.repeat(bin_order().reshape(devices, 1, bins), 2, axis=1).reshape(-1)
        part = np.broadcast_to(np.arange(2).reshape(1, 2, 1), (devices, 2, bins)).reshape(-1)
        loop_inverse = inverse_table(seg_count, order, part)
        loop = loops_plain(moved, loop_partner, loop_count, seg_count, loop_inverse)
        near = pl.pallas_call(
            turn_kernel,
            out_shape=near_shape,
            in_specs=vmem(seg_count),
            out_specs=pl.BlockSpec(memory_space=pltpu.VMEM),
            compiler_params=PARAMS,
            name="near_turn",
        )(*lags)
        return near, loop

    flip = np.eye(LANES, dtype=np.float32)[::-1].astype(jnp.bfloat16)
    out_rows = slots * (2 * bins // seg_count)
    crossed = pl.pallas_call(
        loop_kernel,
        out_shape=jax.ShapeDtypeStruct((seg_count, chan_count, out_rows, LANES), BF16),
        in_specs=smem(2) + vmem(3),
        out_specs=pl.BlockSpec(memory_space=pltpu.VMEM),
        compiler_params=PARAMS,
        name="loop_spectra",
    )(loop_partner.T, loop_count, flip, pack_matrix(seg_count), moved)
    crossed, *lags[1:] = lax.optimization_barrier((crossed, *lags[1:]))
    crossed = crossed.reshape(devices, out_rows, LANES)
    summed = lax.all_to_all(crossed, ("seg", "chan"), 0, 0, tiled=True)
    columns = np.arange(2 * BINS).reshape(devices, seg_count, -1).swapaxes(0, 1).reshape(-1)
    loop_inverse = inverse_table(seg_count, order[columns], part[columns]).T
    loop_inverse = loop_inverse.astype(jnp.bfloat16)
    near, loop = pl.pallas_call(
        functools.partial(last_kernel, slots),
        out_shape=[near_shape, jax.ShapeDtypeStruct((slots * share, LAGS), F32)],
        in_specs=vmem(2 + seg_count),
        out_specs=vmem(2),
        compiler_params=PARAMS,
        name="lags",
    )(summed, loop_inverse, *lags)
    return near, loop.reshape(1, slots, share, LAGS)


def solution(mesh):
    in_specs = (P("chan", "seg"), P(), P(), P(), P())
    out_specs = (P("chan", "seg", None), P("chan", None, "seg", None))
    return jax.shard_map(body, mesh=mesh, in_specs=in_specs, out_specs=out_specs, check_vma=False)
```

```python
import functools
import math

import jax
import jax.numpy as jnp
import numpy as np
from jax import lax
from jax.experimental import pallas as pl
from jax.experimental.pallas import tpu as pltpu
from jax.sharding import PartitionSpec as P

NFFT = 1024
LAGS = 256
TAPS = 64
DECIM = 4
HALFBAND = 10
SPAN = 64
BINS = 512
WATER = 0.2

LANES = 128
GROUP = 16
GROUPS = BINS // GROUP
OUT_BLOCK = 128
STEP = OUT_BLOCK * DECIM
RADIX = 4
DEPTH = NFFT // RADIX
FAR_BINS = BINS // RADIX

F32 = jnp.float32
BF16 = jnp.bfloat16
MIB = 1024 * 1024
PARAMS = pltpu.CompilerParams(vmem_limit_bytes=32 * MIB)


def bin_order():
    return np.concatenate([np.arange(r, BINS, RADIX) for r in range(RADIX)])


def split_np(table):
    high = table.astype(jnp.bfloat16)
    low = (table - high.astype(np.float64)).astype(jnp.bfloat16)
    return high, low


def short_table():
    bins = np.arange(FAR_BINS).reshape(-1, 1, GROUP, 1)
    angles = (bins * np.arange(DEPTH) % DEPTH) * (2.0 * np.pi / DEPTH)
    rows = np.concatenate([np.cos(angles), np.sin(angles)], axis=1).reshape(-1, DEPTH)
    high, low = split_np(rows)
    return np.concatenate([high, high, low], axis=1)


def twiddle_table():
    angles = np.arange(DEPTH)[:, None] * np.arange(1, RADIX) * (2.0 * np.pi / NFFT)
    columns = np.stack([np.cos(angles), np.sin(angles)], axis=2).reshape(DEPTH, -1)
    return np.pad(columns, ((0, 0), (0, LANES - columns.shape[1]))).astype(np.float32)


def edge_table():
    bins = bin_order().reshape(GROUPS, 1, GROUP, 1)
    angles = (bins * np.arange(GROUP) % NFFT) * (2.0 * np.pi / NFFT)
    rows = np.concatenate([np.cos(angles), -np.sin(angles)], axis=1) * (bins != 0)
    high, low = split_np(rows.reshape(2 * BINS, GROUP))
    table = np.concatenate([high, high, low], axis=1)
    return np.pad(table.astype(np.float32), ((0, 0), (0, LANES - 3 * GROUP))).astype(jnp.bfloat16)


def inverse_table(total_segs, bins, part):
    lag = np.arange(LAGS) - LAGS // 2
    angles = (bins[None, :] * lag[:, None] % NFFT) * (2.0 * np.pi / NFFT)
    weights = np.where(bins == 0, 1.0, 2.0) / math.sqrt(2.0 * BINS * total_segs)
    return np.where(part[None, :] == 1, -np.sin(angles), np.cos(angles)) * weights[None, :]


def band_tables():
    bins = bin_order()
    inside = np.abs(bins[:, None] - bins[None, :]) <= HALFBAND
    share = np.broadcast_to(1.0 / inside.sum(axis=1, keepdims=True), (BINS, LANES))
    return inside.astype(jnp.bfloat16), share.astype(np.float32)


def split(value):
    high = value.astype(BF16)
    return high, (value - high.astype(F32)).astype(BF16)


def mm(a, b):
    return jnp.dot(a, b, preferred_element_type=F32)


def mm_nt(a, b):
    return lax.dot_general(a, b, (((1,), (1,)), ((), ())), preferred_element_type=F32)


def tap_rows(taps):
    width, period = 2 * LANES, LANES // DECIM
    square = (TAPS, TAPS)
    diagonal = lax.broadcasted_iota(jnp.int32, square, 0) == lax.broadcasted_iota(jnp.int32, square, 1)
    column_taps = jnp.sum(jnp.where(diagonal, taps, 0.0), axis=1, keepdims=True)
    tap = lax.broadcasted_iota(jnp.int32, (TAPS, width), 0)
    column = lax.broadcasted_iota(jnp.int32, (TAPS, width), 1)
    placed = jnp.where(column == LANES + DECIM - 1 - tap, column_taps, 0.0)
    spread = jnp.broadcast_to(jnp.sum(placed, axis=0, keepdims=True), (period, width))
    piece = pltpu.roll(spread, 0, 1, stride=DECIM, stride_axis=0)
    rows = []
    for t in range(OUT_BLOCK // period):
        left = jnp.zeros((period, t * LANES), F32)
        right = jnp.zeros((period, STEP - LANES - t * LANES), F32)
        rows.append(jnp.concatenate([p for p in (left, piece, right) if p.shape[1]], axis=1))
    return jnp.concatenate(rows, axis=0)


def rim_kernel(rec_hbm, rim_ref, tail_ref, sem):
    length = rec_hbm.shape[1]
    copy = pltpu.make_async_copy(rec_hbm.at[:, pl.ds(length - LANES, LANES)], tail_ref, sem)
    copy.start()
    copy.wait()
    rim_ref[...] = tail_ref[...].T[LANES - TAPS :]


def spectrum_kernel(taps_ref, rec_ref, tab_ref, twist_ref, spec_ref, mean_ref, head_ref):
    blocks = rec_ref.shape[1] // STEP
    table = tap_rows(taps_ref[...])
    head_ref[...] = table[:GROUP, :LANES]
    taps_high, taps_low = split(table.T)
    taps_both = jnp.concatenate([taps_high, taps_low], axis=1)
    before = [jnp.zeros((LANES, LANES), BF16)] * 2
    outputs = []
    for first in range(0, blocks, blocks // 2):
        windows = ([], [])
        for j in range(first, first + blocks // 2):
            chunk = rec_ref[:, j * STEP : (j + 1) * STEP]
            if j == 0:
                mean = jnp.sum(chunk, axis=1, keepdims=True) * (1.0 / STEP)
            for i, value in enumerate(split(chunk - mean)):
                windows[i].append(jnp.concatenate([before[i], value], axis=1))
                before[i] = value[:, STEP - LANES :]
        wide = mm(jnp.concatenate(windows[0], axis=0), taps_both)
        rest = mm(jnp.concatenate(windows[1], axis=0), taps_high)
        total = wide[:, :LANES] + wide[:, LANES:] + rest
        outputs += [total[t * LANES : (t + 1) * LANES].T for t in range(blocks // 2)]
    pieces = [jnp.concatenate(outputs[j : j + 2], axis=0) for j in range(0, blocks, 2)]
    mean_ref[...] = jnp.broadcast_to(mean, (LANES, LANES)).T[: mean_ref.shape[0]]
    even, odd = pieces[0] + pieces[2], pieces[1] + pieces[3]
    a, b = pieces[0] - pieces[2], pieces[1] - pieces[3]
    whole, half = even + odd, even - odd
    whole = whole - jnp.sum(whole, axis=0, keepdims=True) * (1.0 / DEPTH)
    c1, s1, c2, s2, c3, s3 = [twist_ref[:, i : i + 1] for i in range(6)]
    inputs = [
        whole,
        a * c1 - b * s1,
        -(a * s1 + b * c1),
        half * c2,
        -(half * s2),
        a * c3 + b * s3,
        b * c3 - a * s3,
    ]
    parts = [split(value) for value in inputs]
    high = jnp.concatenate([p[0] for p in parts], axis=1)
    low = jnp.concatenate([p[1] for p in parts], axis=1)
    out = mm(tab_ref[...], jnp.concatenate([high, low, high], axis=0))
    out = out.reshape(FAR_BINS // GROUP, 2, GROUP, out.shape[1])
    rows = 2 * FAR_BINS
    for r in range(RADIX):
        first = max(2 * r - 1, 0) * LANES
        real_in = out[..., first : first + LANES]
        if r == 0:
            real, imag = real_in[:, 0], -real_in[:, 1]
        else:
            imag_in = out[..., first + LANES : first + 2 * LANES]
            real, imag = real_in[:, 0] + imag_in[:, 1], imag_in[:, 0] - real_in[:, 1]
        both = jnp.stack([real, imag], axis=1).reshape(rows, LANES)
        spec_ref[r * rows : (r + 1) * rows, :] = both


def whiten_kernel(
    spec_ref,
    rim_ref,
    mean_ref,
    head_ref,
    edge_ref,
    band_ref,
    share_ref,
    white_ref,
    first_ref,
    second_ref,
):
    head_high, head_low = split(head_ref[:, LANES - TAPS :])
    rim_high, rim_low = split(rim_ref[...] - mean_ref[0:1, :])
    history = mm(
        jnp.concatenate([head_high, head_high, head_low], axis=1),
        jnp.concatenate([rim_high, rim_low, rim_high], axis=0),
    )
    high, low = split(history)
    stacked = jnp.concatenate([high, low, high], axis=0)
    spec = spec_ref[...] + mm(edge_ref[:, : 3 * GROUP], stacked)
    parted = spec.reshape(GROUPS, 2, GROUP, LANES)
    real, imag = parted[:, 0], parted[:, 1]
    amplitude = jnp.sqrt(real * real + imag * imag).reshape(BINS, LANES)
    high, low = split(amplitude)
    wide = mm(band_ref[...], jnp.concatenate([high, low], axis=1))
    smoothed = (wide[:, :LANES] + wide[:, LANES:]) * share_ref[...]
    level = jnp.sum(amplitude, axis=0, keepdims=True) * (1.0 / BINS)
    scale = 1.0 / (smoothed + (WATER * level + 1e-06))
    white = parted * scale.reshape(GROUPS, 1, GROUP, LANES)
    white_ref[...] = white.astype(BF16)
    flat = white.reshape(2 * BINS, LANES)
    turned = pltpu.roll(flat, SPAN, 1)
    lane = lax.broadcasted_iota(jnp.int32, (BINS, LANES), 1)
    up = jnp.where(lane < SPAN, turned[:BINS], flat[BINS:])
    down = jnp.where(lane < SPAN, flat[:BINS], turned[BINS:])
    place = lax.axis_index("chan")
    up_first = halo_order(place, lax.axis_size("chan"))[0]
    first_ref[...] = jnp.where(up_first, up, down).astype(BF16)
    second_ref[...] = jnp.where(up_first, down, up).astype(BF16)


def halo_order(place, count):
    if count % 2:
        return place >= 0, place >= 0
    return place % 2 == 0, place % 2 == 1


def halo_routes(count):
    if count % 2:
        ring = [(i, (i + 1) % count) for i in range(count)]
        return ring, [(j, i) for i, j in ring]
    first = [(i, i + 1 - 2 * (i % 2)) for i in range(count)]
    second = [(i, (i - 1 + 2 * (i % 2)) % count) for i in range(count)]
    return first, second


def offset_moves(offs_ref):
    row = lax.broadcasted_iota(jnp.int32, (2 * LANES, LANES), 0)
    channel = lax.broadcasted_iota(jnp.int32, (2 * LANES, LANES), 1)
    distance = jnp.where(row < LANES + SPAN, row, row - 2 * LANES) - channel
    hits = [(distance == offs_ref[o]).astype(F32) for o in range(offs_ref.shape[0])]
    return jnp.concatenate(hits, axis=1).astype(BF16)


def pack_matrix(owners):
    share = LANES // owners
    matrix = np.zeros((owners, owners, share, owners, owners, share), np.float32)
    for group in range(owners):
        for owner in range(owners):
            matrix[group, owner, :, owner, group, :] = np.eye(share)
    matrix = matrix.reshape(owners, LANES, owners * LANES)[:, ::-1]
    return matrix.reshape(owners * LANES, owners * LANES).astype(jnp.bfloat16)


def partner_of(place, r, owners):
    return place ^ r if owners & (owners - 1) == 0 else (place + r) % owners


def near_kernel(offs_ref, white_ref, first_ref, second_ref, inv_ref, *refs):
    out_refs, lags_ref = refs[:-1], refs[-1]
    rows = white_ref.shape[0] * 2 * GROUP
    half = rows // 2
    noff = lags_ref.shape[0]
    before_first = halo_order(lax.axis_index("chan"), lax.axis_size("chan"))[1]
    first, second = first_ref[...].astype(F32), second_ref[...].astype(F32)
    before = jnp.where(before_first, first, second)
    after = jnp.where(before_first, second, first)
    lane = lax.broadcasted_iota(jnp.int32, (half, LANES), 1)
    upper = jnp.where(lane < SPAN, after, pltpu.roll(before, SPAN, 1))
    lower = jnp.where(lane < SPAN, pltpu.roll(after, SPAN, 1), before)
    edge = jnp.concatenate([upper, lower], axis=0).astype(BF16)
    own = white_ref[...].reshape(rows, LANES)
    far = mm(jnp.concatenate([own, edge], axis=1), offset_moves(offs_ref))
    own = own.astype(F32).reshape(-1, 2, GROUP, LANES)
    columns = []
    for o in range(noff):
        other = far[:, o * LANES : (o + 1) * LANES].reshape(own.shape)
        real = own[:, 0] * other[:, 0] + own[:, 1] * other[:, 1]
        imag = own[:, 1] * other[:, 0] - own[:, 0] * other[:, 1]
        columns.append(jnp.stack([real, imag], axis=1).reshape(rows, LANES).astype(BF16))
    both = mm(inv_ref[...], jnp.concatenate(columns, axis=1))
    lags = both[:LAGS] + both[LAGS:]
    for o in range(noff):
        lags_ref[o] = lags[:, o * LANES : (o + 1) * LANES]
    owners = len(out_refs)
    each = noff // owners
    place = lax.axis_index("seg")
    for r in range(owners):
        first = partner_of(place, r, owners) * each
        out_refs[r][...] = lags_ref[pl.ds(first, each)].astype(BF16)


def turn_kernel(*refs):
    near_ref = refs[-1]
    total = sum(ref[...].astype(F32) for ref in refs[:-1])
    for t in range(near_ref.shape[1]):
        near_ref[:, t, :] = total[t].T


def loop_kernel(partner_ref, count_ref, flip_ref, pack_ref, white_ref, out_ref):
    segs, blocks, _, bins, _ = white_ref.shape
    owners = out_ref.shape[0]
    slots = partner_ref.shape[0]
    rows = segs * 2 * bins
    packed_rows = 2 * bins // owners
    turned = mm(white_ref[...].reshape(blocks * rows, LANES), flip_ref[...])
    turned = turned.reshape(white_ref.shape)
    loops = []
    for b in range(blocks):
        own = turned[:, b]
        for k in range(slots):
            partner = jnp.clip(partner_ref[k, b], 0, blocks - 1)
            live = (k < count_ref[b]).astype(F32)
            far = white_ref[:, partner].astype(F32)
            real = jnp.sum(own[:, 0] * far[:, 0] + own[:, 1] * far[:, 1], axis=0)
            imag = jnp.sum(own[:, 1] * far[:, 0] - own[:, 0] * far[:, 1], axis=0)
            pair = jnp.concatenate([real, imag], axis=0) * live
            groups = [pair[g * packed_rows : (g + 1) * packed_rows] for g in range(owners)]
            loops.append(jnp.concatenate(groups, axis=1))
    packed = mm(jnp.concatenate(loops, axis=0).astype(BF16), pack_ref[...])
    depth = slots * packed_rows
    for b in range(blocks):
        for q in range(owners):
            tile = packed[b * depth : (b + 1) * depth, q * LANES : (q + 1) * LANES]
            out_ref[q, b] = tile.astype(BF16)


def loop_lag_kernel(slots, spec_ref, inv_ref, loop_ref):
    sources = spec_ref.shape[0]
    step = spec_ref.shape[1] // slots
    share = loop_ref.shape[0] // slots
    loop = spec_ref[...].astype(F32)
    rows = []
    for k in range(slots):
        turned = loop[:, k * step : (k + 1) * step].reshape(sources * step, LANES).T
        groups = [turned[g * share : (g + 1) * share] for g in range(LANES // share)]
        rows.append(jnp.concatenate(groups, axis=1))
    loop_ref[...] = mm(jnp.concatenate(rows, axis=0).astype(BF16), inv_ref[...])


def last_kernel(slots, spec_ref, inv_ref, *refs):
    turn_kernel(*refs[:-1])
    loop_lag_kernel(slots, spec_ref, inv_ref, refs[-1])


def vmem(count):
    return [pl.BlockSpec(memory_space=pltpu.VMEM)] * count


def smem(count):
    return [pl.BlockSpec(memory_space=pltpu.SMEM)] * count


def hbm(count):
    return [pl.BlockSpec(memory_space=pltpu.HBM)] * count


def in_hbm(array):
    return pltpu.with_memory_space_constraint(jnp.asarray(array), pltpu.HBM)


def loops_plain(white, loop_partner, loop_count, owners, inverse):
    _, blocks, _, bins, chans = white.shape
    devices = blocks * owners
    slots = loop_partner.shape[1]
    share = chans // owners
    wide = white.astype(F32).swapaxes(0, 1)
    loops = []
    for k in range(slots):
        far = jnp.flip(wide[loop_partner[:, k]], axis=4)
        live = (k < loop_count).astype(F32)[:, None, None]
        real = jnp.sum(wide[:, :, 0] * far[:, :, 0] + wide[:, :, 1] * far[:, :, 1], axis=1)
        imag = jnp.sum(wide[:, :, 1] * far[:, :, 0] - wide[:, :, 0] * far[:, :, 1], axis=1)
        pair = (jnp.stack([real, imag]) * live[None]).astype(BF16)
        loops.append(pair.reshape(2, blocks, bins, owners, share))
    loop = jnp.transpose(jnp.stack(loops), (4, 2, 0, 1, 3, 5))
    loop = loop.reshape(devices, slots, 2 * bins, share)
    summed = lax.all_to_all(loop, ("seg", "chan"), 0, 0, tiled=True).astype(F32)
    table = inverse.astype(np.float32).reshape(LAGS, devices, 2 * bins)
    lags = jnp.einsum("dtvc,ldv->tcl", summed, table, precision=lax.Precision.HIGHEST)
    return lags[None]


def body(recording, filter_taps, offsets, loop_partner, loop_count):
    chan_count = lax.axis_size("chan")
    seg_count = lax.axis_size("seg")
    devices = chan_count * seg_count
    bins = BINS // devices
    chans, length = recording.shape
    noff, slots = offsets.shape[0], loop_partner.shape[1]
    share = chans // seg_count
    near_each = noff // seg_count
    assert length == NFFT * DECIM and chans == LANES and noff % seg_count == 0

    route = [(i, i + 1) for i in range(seg_count - 1)]
    rim = pl.pallas_call(
        rim_kernel,
        out_shape=jax.ShapeDtypeStruct((TAPS, chans), F32),
        in_specs=hbm(1),
        out_specs=pl.BlockSpec(memory_space=pltpu.VMEM),
        scratch_shapes=[pltpu.VMEM((chans, LANES), F32), pltpu.SemaphoreType.DMA],
        compiler_params=PARAMS,
        cost_estimate=pl.CostEstimate(
            flops=10_000_000_000, bytes_accessed=20_000_000, transcendentals=0
        ),
        name="history",
    )(in_hbm(recording))
    rim = lax.ppermute(rim, "seg", route)
    taps = filter_taps.reshape(1, TAPS)
    spec, mean, head = pl.pallas_call(
        spectrum_kernel,
        out_shape=[
            jax.ShapeDtypeStruct((2 * BINS, LANES), F32),
            jax.ShapeDtypeStruct((8, LANES), F32),
            jax.ShapeDtypeStruct((GROUP, LANES), F32),
        ],
        in_specs=vmem(4),
        out_specs=vmem(3),
        compiler_params=PARAMS,
        cost_estimate=pl.CostEstimate(
            flops=1_000_000_000, bytes_accessed=5_000_000, transcendentals=0
        ),
        name="filter_and_transform",
    )(taps, recording, short_table(), twiddle_table())

    band, band_share = band_tables()
    half = jax.ShapeDtypeStruct((BINS, LANES), BF16)
    white, first, second = pl.pallas_call(
        whiten_kernel,
        out_shape=[jax.ShapeDtypeStruct((GROUPS, 2, GROUP, LANES), BF16), half, half],
        in_specs=vmem(7),
        out_specs=vmem(3),
        compiler_params=PARAMS,
        name="whiten",
    )(spec, rim, mean, head, edge_table(), band, band_share)

    spread = white
    if bins != GROUP:
        spread = jnp.moveaxis(white, 1, 0).reshape(2, devices, bins, LANES)
        spread = jnp.moveaxis(spread, 0, 1)
    moved = lax.all_to_all(spread, ("seg", "chan"), 0, 0, tiled=True)
    moved = moved.reshape(seg_count, chan_count, 2, bins, LANES)

    routes = halo_routes(chan_count)
    first = lax.ppermute(first, "chan", routes[0])
    second = lax.ppermute(second, "chan", routes[1])
    order = np.repeat(bin_order().reshape(GROUPS, 1, GROUP), 2, axis=1).reshape(-1)
    part = np.broadcast_to(np.arange(2).reshape(1, 2, 1), (GROUPS, 2, GROUP)).reshape(-1)
    inverse = np.concatenate(split_np(inverse_table(seg_count, order, part)), axis=0)
    lags = pl.pallas_call(
        near_kernel,
        out_shape=[jax.ShapeDtypeStruct((near_each, LAGS, LANES), BF16)] * seg_count,
        in_specs=smem(1) + vmem(4),
        out_specs=vmem(seg_count),
        scratch_shapes=[pltpu.VMEM((noff, LAGS, LANES), F32)],
        compiler_params=PARAMS,
        cost_estimate=pl.CostEstimate(
            flops=20_000_000_000, bytes_accessed=20_000_000, transcendentals=0
        ),
        name="near_lags",
    )(offsets, white, first, second, inverse)
    lags = list(lags)
    for r in range(seg_count - 1, 0, -1):
        route = [(i, partner_of(i, r, seg_count)) for i in range(seg_count)]
        lags[r] = lax.ppermute(lags[r], "seg", route)
    moved, lags[0] = lax.optimization_barrier((moved, lags[0]))

    near_shape = jax.ShapeDtypeStruct((chans, near_each, LAGS), F32)
    if bins % GROUP or 2 * bins % (8 * seg_count):
        order = np.repeat(bin_order().reshape(devices, 1, bins), 2, axis=1).reshape(-1)
        part = np.broadcast_to(np.arange(2).reshape(1, 2, 1), (devices, 2, bins)).reshape(-1)
        loop_inverse = inverse_table(seg_count, order, part)
        loop = loops_plain(moved, loop_partner, loop_count, seg_count, loop_inverse)
        near = pl.pallas_call(
            turn_kernel,
            out_shape=near_shape,
            in_specs=vmem(seg_count),
            out_specs=pl.BlockSpec(memory_space=pltpu.VMEM),
            compiler_params=PARAMS,
            name="near_turn",
        )(*lags)
        return near, loop

    flip = np.eye(LANES, dtype=np.float32)[::-1].astype(jnp.bfloat16)
    out_rows = slots * (2 * bins // seg_count)
    crossed = pl.pallas_call(
        loop_kernel,
        out_shape=jax.ShapeDtypeStruct((seg_count, chan_count, out_rows, LANES), BF16),
        in_specs=smem(2) + vmem(3),
        out_specs=pl.BlockSpec(memory_space=pltpu.VMEM),
        compiler_params=PARAMS,
        name="loop_spectra",
    )(loop_partner.T, loop_count, flip, pack_matrix(seg_count), moved)
    crossed, *lags[1:] = lax.optimization_barrier((crossed, *lags[1:]))
    crossed = crossed.reshape(devices, out_rows, LANES)
    summed = lax.all_to_all(crossed, ("seg", "chan"), 0, 0, tiled=True)
    columns = np.arange(2 * BINS).reshape(devices, seg_count, -1).swapaxes(0, 1).reshape(-1)
    loop_inverse = inverse_table(seg_count, order[columns], part[columns]).T
    loop_inverse = loop_inverse.astype(jnp.bfloat16)
    near, loop = pl.pallas_call(
        functools.partial(last_kernel, slots),
        out_shape=[near_shape, jax.ShapeDtypeStruct((slots * share, LAGS), F32)],
        in_specs=vmem(2 + seg_count),
        out_specs=vmem(2),
        compiler_params=PARAMS,
        name="lags",
    )(summed, loop_inverse, *lags)
    return near, loop.reshape(1, slots, share, LAGS)


def solution(mesh):
    in_specs = (P("chan", "seg"), P(), P(), P(), P())
    out_specs = (P("chan", "seg", None), P("chan", None, "seg", None))
    return jax.shard_map(body, mesh=mesh, in_specs=in_specs, out_specs=out_specs, check_vma=False)
```
